32 devices in a mesh: dp: 16 (over z, y, x), sp: 2 (over core).
Axes of the slice: x: 2, y: 2, z: 4, core: 2. Of those that a mesh axis runs over, the one named last changes fastest.
Arguments:
- tokens_in: bfloat16 [16, 512, 1152], P('dp', 'sp'), may hold values from -6 to 6
- segment_ids: int32 [16, 512], P('dp', 'sp'), may hold values from 0 to 3, as said below
- conditions: bfloat16 [16, 4, 1152], P('dp'), may hold values from -6 to 6
- noise_bins: int32 [16, 4], P('dp'), may hold values from 0 to 7
- bin_counts: int32 [16, 8], P('dp'), may hold values from 10 to 90
- cotangent: bfloat16 [16, 512, 1152], P('dp', 'sp'), may hold values from -6 to 6
- ada_weight: bfloat16 [1152, 6912], P(('dp', 'sp')), may hold values from -0.1875 to 0.1875
- qkv_weight: bfloat16 [1152, 3456], P(('dp', 'sp')), may hold values from -0.1875 to 0.1875
- out_weight: bfloat16 [1152, 1152], P(('dp', 'sp')), may hold values from -1.75 to 1.75
- up_weight: bfloat16 [1152, 4608], P(('dp', 'sp')), may hold values from -0.1875 to 0.1875
- down_weight: bfloat16 [4608, 1152], P(('dp', 'sp')), may hold values from -0.09375 to 0.09375
Outputs:
- tokens_out: bfloat16 [16, 512, 1152], P('dp', 'sp')
- tokens_grad: float32 [16, 512, 1152], P('dp', 'sp')
- cond_grad: float32 [16, 4, 1152], P('dp')
- ada_grad: float32 [1152, 6912], P(('dp', 'sp'))
- qkv_grad: float32 [1152, 3456], P(('dp', 'sp'))
- out_grad: float32 [1152, 1152], P(('dp', 'sp'))
- up_grad: float32 [1152, 4608], P(('dp', 'sp'))
- down_grad: float32 [4608, 1152], P(('dp', 'sp'))
The draws below stay inside these ranges and needn't reach their ends.
Inputs may be any that keep to these rules, and one draw needn't show every extreme that they name: `segment_ids`: within each sequence the crop numbers never fall, each of 0 to 3 holds one token or more, and the crop that holds position 256 also holds position 255.
All inputs are finite; a program needn't handle non-finite values.
Results may differ from the reference program's by a relative error of at most 0.012.
The reference program's roundings to bfloat16 on the way count: a program that leaves them out, or rounds other values in their place, can miss the bound.
Values may be sent and summed in bfloat16 or wider, within the bound.
A program may use at most 384 MiB of HBM per device.

```python
import math
import jax
import jax.numpy as jnp
from jax import lax

D = 1152
HEADS = 16
HEAD_DIM = 72
FF = 4608
SEQ_LEN = 512
CROPS = 4
NBINS = 8
SEQS = 1
GROUPS = 16
NSEQ = 16


def draw_segment_ids(key, part):
    row_count = SEQS * GROUPS
    candidates = jnp.arange(1, SEQ_LEN, dtype=jnp.int32)
    positions = jnp.arange(SEQ_LEN, dtype=jnp.int32)

    def one_row(row_key):
        ranking = jax.random.permutation(row_key, SEQ_LEN - 1).astype(jnp.int32)
        ranking = jnp.where(candidates == SEQ_LEN // 2, SEQ_LEN * 4, ranking)
        ordering = jnp.argsort(ranking)
        bounds = candidates[ordering[:CROPS - 1]]
        return jnp.sum((positions[:, None] >= bounds[None, :]).astype(jnp.int32), axis=1)
    return jax.vmap(one_row)(jax.random.split(key, row_count))


def draw_bin_counts(key, part):
    base_counts = jax.random.randint(key, (GROUPS, NBINS), 10, 31).astype(jnp.int32)
    base_counts = base_counts.at[0, 0].set(10).at[GROUPS - 1, NBINS - 1].set(30)
    ramp_factor = (GROUPS - 1 + 2 * jnp.arange(GROUPS, dtype=jnp.int32))[:, None]
    return base_counts * ramp_factor // max(GROUPS - 1, 1)


def place_ends(drawn, rng, low, largest):
    longest = drawn.shape.index(max(drawn.shape))
    spots = []
    for shift in (0, 1):
        where = [jax.random.randint(jax.random.fold_in(rng, axis), (), 0, length) for axis, length in enumerate(drawn.shape)]
        where[longest] = (where[longest] + shift) % drawn.shape[longest]
        spots.append(tuple(where))
    return drawn.at[spots[0]].set(low).at[spots[1]].set(largest)


def block_levels(rng, extent, cuts, smallest, high):
    loudness, own = 1.0, jax.random.fold_in(rng, 6)
    for position, parts in cuts:
        heights = jnp.exp(jax.random.uniform(jax.random.fold_in(own, position), (parts,), jnp.float32, smallest / len(cuts), high / len(cuts)))
        loudness = loudness * jnp.repeat(heights, extent[position] // parts).reshape([-1 if axis == position else 1 for axis in range(len(extent))])
    return loudness


def bell_draw(rng, shape, deviation, limit, pieces=(), held_as=jnp.bfloat16):
    entries = jax.random.normal(rng, shape, jnp.float32) * deviation
    if len(pieces) > 0:
        entries = block_levels(rng, shape, pieces, -0.22, 0.18) * entries
    return jnp.clip(entries, min=-limit, max=limit).astype(held_as)


def setup_inputs(seed: int = 0) -> dict:
    splits = jax.random.split(jax.random.key(seed), 12)
    tokens_in = bell_draw(splits[0], (NSEQ, SEQ_LEN, D), 1.0, 6.0, ((0, 16), (1, 2)))
    segment_ids = draw_segment_ids(jax.random.fold_in(splits[11], 71), 0)
    conditions = bell_draw(splits[2], (NSEQ, CROPS, D), 1.0, 6.0, ((0, 16),))
    noise_bins = place_ends(jax.random.randint(splits[3], (NSEQ, CROPS), 0, NBINS), jax.random.fold_in(splits[3], 1), 0, NBINS - 1).astype(jnp.int32)
    bin_counts = draw_bin_counts(jax.random.fold_in(splits[11], 71), 0)
    cotangent = bell_draw(splits[5], (NSEQ, SEQ_LEN, D), 1.0, 6.0, ((0, 16), (1, 2)))
    ada_weight = bell_draw(splits[6], (D, 6 * D), D ** -0.5, 0.1875, ((0, 32),))
    qkv_weight = bell_draw(splits[7], (D, 3 * D), D ** -0.5, 0.1875, ((0, 32),))
    out_weight = bell_draw(splits[8], (D, D), (D // 96) ** -0.5, 1.75, ((0, 32),))
    up_weight = bell_draw(splits[9], (D, FF), D ** -0.5, 0.1875, ((0, 32),))
    down_weight = bell_draw(splits[10], (FF, D), FF ** -0.5, 0.09375, ((0, 32),))
    return {"tokens_in": tokens_in, "segment_ids": segment_ids, "conditions": conditions, "noise_bins": noise_bins, "bin_counts": bin_counts, "cotangent": cotangent, "ada_weight": ada_weight, "qkv_weight": qkv_weight, "out_weight": out_weight, "up_weight": up_weight, "down_weight": down_weight}


PRECISE = lax.Precision.HIGHEST
EPSILON = 1e-06

@jax.custom_vjp
def low(v):
    return lax.optimization_barrier(v.astype(jnp.bfloat16)).astype(jnp.float32)

@jax.custom_vjp
def low_back(v):
    return v

def low_keep(v):
    return (low(v), None)

def low_pass(kept, grad):
    return (grad,)

def back_keep(v):
    return (v, None)

def back_low(kept, grad):
    return (low(grad),)
low.defvjp(low_keep, low_pass)
low_back.defvjp(back_keep, back_low)

def layer_norm(values):
    center = values - lax.optimization_barrier(jnp.mean(values, axis=-1, keepdims=True))
    return center * lax.rsqrt(lax.optimization_barrier(jnp.mean(center * center, axis=-1, keepdims=True)) + EPSILON)

def forward(tokens, cond_vectors, ada_matrix, qkv_matrix, out_matrix, up_matrix, down_matrix, segments):
    batch_size = tokens.shape[0]
    length = tokens.shape[1]
    model_width = tokens.shape[2]
    modulation = jnp.einsum('bcd,df->bcf', low(jax.nn.silu(cond_vectors)), ada_matrix, precision=PRECISE)
    selector = (segments[..., None] == jnp.arange(CROPS, dtype=jnp.int32)).astype(jnp.float32)
    per_token = jnp.einsum('blc,bcf->blf', selector, modulation, precision=PRECISE)
    shift_one, scale_one, gate_one, shift_two, scale_two, gate_two = jnp.split(per_token, 6, axis=-1)
    hidden_one = low(layer_norm(tokens) * (1.0 + scale_one) + shift_one)
    projected = low(low_back(jnp.einsum('bld,df->blf', hidden_one, qkv_matrix, precision=PRECISE)))
    queries, keys_all, values_all = jnp.split(projected, 3, axis=-1)
    head_shape = (batch_size, length, HEADS, HEAD_DIM)
    scores = low_back(jnp.einsum('bqhd,bkhd->bhqk', queries.reshape(head_shape), keys_all.reshape(head_shape), precision=PRECISE) / math.sqrt(HEAD_DIM))
    same_crop = (segments[:, :, None] == segments[:, None, :])[:, None]
    scores = jnp.where(same_crop, scores, -1e+30)
    row_max = lax.optimization_barrier(jnp.max(scores, axis=-1, keepdims=True))
    raised = jnp.exp(scores - row_max)
    probability = raised / lax.optimization_barrier(jnp.sum(raised, axis=-1, keepdims=True))
    context = jnp.einsum('bhqk,bkhd->bqhd', low(probability), values_all.reshape(head_shape), precision=PRECISE)
    context = low(low_back(context.reshape(batch_size, length, model_width)))
    attended = low_back(jnp.einsum('bld,df->blf', context, out_matrix, precision=PRECISE))
    middle = tokens + gate_one * attended
    hidden_two = low(layer_norm(middle) * (1.0 + scale_two) + shift_two)
    upper_in = low_back(jnp.einsum('bld,df->blf', hidden_two, up_matrix, precision=PRECISE))
    activated = low(jax.nn.gelu(upper_in, approximate=True))
    mlp_out = low_back(jnp.einsum('blf,fd->bld', activated, down_matrix, precision=PRECISE))
    return middle + gate_two * mlp_out

def reference(tokens_in, segment_ids, conditions, noise_bins, bin_counts, cotangent, ada_weight, qkv_weight, out_weight, up_weight, down_weight):
    bin_total = lax.optimization_barrier(jnp.sum(bin_counts, axis=0)).astype(jnp.float32)
    bin_weight = 40.0 * GROUPS / bin_total
    crop_weight = lax.optimization_barrier(jnp.sum(jnp.where(noise_bins[..., None] == jnp.arange(NBINS, dtype=jnp.int32), bin_weight, 0.0), axis=-1))
    matrices = tuple((matrix.astype(jnp.float32) for matrix in (ada_weight, qkv_weight, out_weight, up_weight, down_weight)))
    block_seqs = math.gcd(NSEQ, max(1, 4096 // SEQ_LEN))
    block_count = NSEQ // block_seqs

    def split_blocks(array):
        return array.reshape((block_count, block_seqs) + array.shape[1:])

    def step(carry, item):
        tokens_block, seg_block, cond_block, weight_block, cot_block = item
        token_weight = lax.optimization_barrier(jnp.sum(jnp.where(seg_block[..., None] == jnp.arange(CROPS, dtype=jnp.int32), weight_block[:, None, :], 0.0), axis=-1))

        def apply(tokens_x, cond_x, ada_x, qkv_x, out_x, up_x, down_x):
            return forward(tokens_x, cond_x, ada_x, qkv_x, out_x, up_x, down_x, seg_block)
        result, pull = jax.vjp(apply, tokens_block.astype(jnp.float32), cond_block.astype(jnp.float32), *matrices)
        grads = pull(cot_block.astype(jnp.float32) * token_weight[..., None])
        carry = tuple((running + fresh for running, fresh in zip(carry, grads[2:])))
        return (carry, (result.astype(jnp.bfloat16), grads[0], grads[1]))
    start = tuple((jnp.zeros(matrix.shape, jnp.float32) for matrix in matrices))
    items = (split_blocks(tokens_in), split_blocks(segment_ids), split_blocks(conditions), split_blocks(crop_weight), split_blocks(cotangent))
    grad_totals, (outputs_all, tokens_grads, cond_grads) = lax.scan(step, start, items)
    return (outputs_all.reshape(NSEQ, SEQ_LEN, D), tokens_grads.reshape(NSEQ, SEQ_LEN, D), cond_grads.reshape(NSEQ, CROPS, D), grad_totals[0], grad_totals[1], grad_totals[2], grad_totals[3], grad_totals[4])
```

```python
from functools import partial
import math

import jax
import jax.numpy as jnp
from jax import lax
from jax.experimental import pallas as pl
from jax.experimental.pallas import tpu as pltpu
from jax.sharding import PartitionSpec as P

HEADS = 16
CROPS = 4
NBINS = 8
EPSILON = 1e-06
LARGE_NEGATIVE = -1e30

MESH = pl.DeviceIdType.MESH
PAD = 48
CUT = 80


def position():
    d = lax.axis_index("dp")
    c = lax.axis_index("sp")
    return d // 4, (d // 2) % 2, d % 2, c


def device(z, y, x, c):
    return (z * 4 + y * 2 + x, c)


def slot_of(kind, zy, group):
    return zy * 4 + group if kind == 2 else group * 8 + zy


def greet(z, y, x, c):
    barrier = pltpu.get_barrier_semaphore()
    peers = [device((z + k) % 4, y, x, c) for k in (1, 2, 3)]
    peers += [
        device(z, 1 - y, x, c),
        device(z, y, 1 - x, c),
        device(z, y, x, 1 - c),
        device(z, y, 1 - x, 1 - c),
    ]
    for peer in peers:
        pl.semaphore_signal(barrier, inc=1, device_id=peer, device_id_type=MESH)
    pl.semaphore_wait(barrier, len(peers))


def remote(src, dst, send, recv, target):
    return pltpu.make_async_remote_copy(
        src_ref=src,
        dst_ref=dst,
        send_sem=send,
        recv_sem=recv,
        device_id=target,
        device_id_type=MESH,
    )


def row_selector(rows, share):
    shape = (rows, 4 * PAD)
    row = lax.broadcasted_iota(jnp.int32, shape, 0)
    column = lax.broadcasted_iota(jnp.int32, shape, 1)
    picked = jnp.zeros(shape, jnp.bool_)
    for k in range(4):
        inside = (row >= k * share) & (row < (k + 1) * share)
        picked = picked | (inside & (column == row - k * share + k * PAD))
    return picked.astype(jnp.float32).astype(jnp.bfloat16)


def gather_kernel(share, shards_ref, down_ref, full_ref, stage, piece, *sems):
    (
        group_send, group_recv, own_send, z_send, z_recv, x_send, x_recv, y_send, y_recv,
        dx_send, dx_recv, dy_send, dy_recv, c_send, c_recv,
    ) = sems
    z, y, x, c = position()
    group = x * 2 + c
    zy = z * 2 + y
    halves = (pl.ds(0, CUT), pl.ds(CUT, 4 * share - CUT))
    greet(z, y, x, c)
    sends = []

    def send(*args):
        copy = remote(*args)
        copy.start()
        sends.append(copy)

    def arrive(ref, sem, target):
        remote(ref, ref, sem, sem, target).wait_recv()

    partners = [(x, 1 - c), (1 - x, c), (1 - x, 1 - c)]
    for a in range(2):
        for j, (px, pc) in enumerate(partners):
            send(
                shards_ref.at[a, px * 2 + pc],
                stage.at[a, pl.ds(pl.multiple_of(group * PAD, 16), PAD)],
                group_send.at[a, j],
                group_recv.at[a, j],
                device(z, y, px, pc),
            )
        stage[a, pl.ds(pl.multiple_of(group * PAD, 16), PAD), :] = shards_ref[a, group]

    def slot(a, k, other_y, other_x, core=None):
        zz = (z - k + 4) % 4
        yy = 1 - y if other_y else y
        xx = 1 - x if other_x else x
        cc = c if core is None else core
        return full_ref.at[a, slot_of(a, zz * 2 + yy, xx * 2 + cc)]

    x_peer, y_peer, c_peer = device(z, y, 1 - x, c), device(z, 1 - y, x, c), device(z, y, x, 1 - c)
    keep = []

    def to_core(a, k, pos, src, dst):
        send(src, dst, c_send.at[a, k, pos], c_recv.at[a, k, pos], c_peer)

    def own(a):
        if a < 2:
            for j, (px, pc) in enumerate(partners):
                arrive(
                    stage.at[a, pl.ds(pl.multiple_of((px * 2 + pc) * PAD, 16), PAD)],
                    group_recv.at[a, j],
                    device(z, y, px, pc),
                )
            piece[a] = jnp.dot(
                row_selector(4 * share, share), stage[a], preferred_element_type=jnp.float32
            ).astype(jnp.bfloat16)
        src = piece.at[a] if a < 2 else down_ref
        mine = slot(a, 0, 0, 0)
        for k in (1, 2, 3):
            send(src, mine, z_send.at[a, k - 1], z_recv.at[a, k - 1], device((z + k) % 4, y, x, c))
        local = pltpu.make_async_copy(src, mine, own_send.at[a])
        local.start()
        keep.append(local)

    def spread(a, k):
        if k == 0:
            src = piece.at[a] if a < 2 else down_ref
        else:
            src = slot(a, k, 0, 0)
            arrive(src, z_recv.at[a, k - 1], device((z - k + 4) % 4, y, x, c))
        dst = slot(a, k, 0, 0)
        for h in (0, 1):
            send(src.at[halves[h]], dst.at[halves[h]], x_send.at[a, k, h], x_recv.at[a, k, h], x_peer)
            send(src.at[halves[1 - h]], dst.at[halves[1 - h]], y_send.at[a, k, 1 - h], y_recv.at[a, k, 1 - h], y_peer)
        to_core(a, k, 0, src, dst)

    def forward(a, k):
        from_x, from_y = slot(a, k, 0, 1), slot(a, k, 1, 0)
        top, low = from_x.at[halves[0]], from_y.at[halves[1]]
        arrive(top, x_recv.at[a, k, 0], x_peer)
        send(top, top, dy_send.at[a, k], dy_recv.at[a, k], y_peer)
        arrive(low, y_recv.at[a, k, 1], y_peer)
        send(low, low, dx_send.at[a, k], dx_recv.at[a, k], x_peer)
        arrive(from_x.at[halves[1]], x_recv.at[a, k, 1], x_peer)
        to_core(a, k, 1, from_x, from_x)
        arrive(from_y.at[halves[0]], y_recv.at[a, k, 0], y_peer)
        to_core(a, k, 2, from_y, from_y)

    def finish(a, k):
        far = slot(a, k, 1, 1)
        arrive(far.at[halves[0]], dy_recv.at[a, k], y_peer)
        arrive(far.at[halves[1]], dx_recv.at[a, k], x_peer)
        to_core(a, k, 3, far, far)

    order = [(a, k) for a in range(3) for k in range(4)]
    own(0)
    for i in range(len(order) + 3):
        if i < len(order):
            a, k = order[i]
            if k == 1 and a < 2:
                own(a + 1)
            spread(a, k)
        if 2 <= i < len(order) + 2:
            forward(*order[i - 2])
        if 3 <= i:
            finish(*order[i - 3])
    for a in range(3):
        for k in range(4):
            for pos, (oy, ox) in enumerate(((0, 0), (0, 1), (1, 0), (1, 1))):
                arrive(slot(a, k, oy, ox, 1 - c), c_recv.at[a, k, pos], c_peer)
    for copy in keep:
        copy.wait()
    for copy in sends:
        copy.wait_send()


def gather_weights(shards, down, share):
    width = down.shape[1]
    dma = pltpu.SemaphoreType.DMA
    return pl.pallas_call(
        partial(gather_kernel, share),
        out_shape=jax.ShapeDtypeStruct((3, 32, 4 * share, width), jnp.bfloat16),
        in_specs=[pl.BlockSpec(memory_space=pltpu.VMEM)] * 2,
        out_specs=pl.BlockSpec(memory_space=pl.ANY),
        scratch_shapes=[
            pltpu.VMEM((2, 4 * PAD, width), jnp.bfloat16),
            pltpu.VMEM((2, 4 * share, width), jnp.bfloat16),
            dma((2, 3)), dma((2, 3)), dma((3,)), dma((3, 3)), dma((3, 3)),
            dma((3, 4, 2)), dma((3, 4, 2)), dma((3, 4, 2)), dma((3, 4, 2)),
            dma((3, 4)), dma((3, 4)), dma((3, 4)), dma((3, 4)),
            dma((3, 4, 4)), dma((3, 4, 4)),
        ],
        compiler_params=pltpu.CompilerParams(
            collective_id=0, has_side_effects=True, vmem_limit_bytes=16 * 2**20
        ),
        name="gather_weights",
    )(shards, down)


def add_rows(dst, sources, start, rows):
    def body(i, carry):
        where = pl.ds(pl.multiple_of(start + i * 16, 16), 16)
        total = dst[where, :].astype(jnp.float32)
        for source in sources:
            total = total + source[where, :].astype(jnp.float32)
        dst[where, :] = total.astype(dst.dtype)
        return carry

    lax.fori_loop(0, rows // 16, body, 0)


def scatter_kernel(share, g1_ref, g2_ref, g3_ref, rows_ref, down_ref, held, from_core, diag,
                   from_x, from_y, from_z, spare, *sems):
    (
        load_sem, c_send, c_recv, dx_send, dx_recv, dy_send, dy_recv, x_send, x_recv,
        y_send, y_recv, z_send, z_recv, group_send, group_recv,
    ) = sems
    z, y, x, c = position()
    group = x * 2 + c
    rows = 4 * share
    halves = (pl.ds(0, CUT), pl.ds(CUT, rows - CUT))
    given = (g1_ref, g2_ref, g3_ref)
    greet(z, y, x, c)
    sends = []

    def send(*args):
        copy = remote(*args)
        copy.start()
        sends.append(copy)

    def arrive(ref, sem, target):
        remote(ref, ref, sem, sem, target).wait_recv()

    x_peer, y_peer, c_peer = device(z, y, 1 - x, c), device(z, 1 - y, x, c), device(z, y, x, 1 - c)
    places = ((0, 0), (0, 1), (1, 0), (1, 1))
    loads = {}

    def begin(a, k):
        zz = (z + k) % 4
        for pos, (oy, ox) in enumerate(places):
            yy = 1 - y if oy else y
            xx = 1 - x if ox else x
            send(
                given[a].at[slot_of(a, zz * 2 + yy, xx * 2 + 1 - c)],
                from_core.at[a, k, pos],
                c_send.at[a, k, pos],
                c_recv.at[a, k, pos],
                c_peer,
            )
            loads[a, k, pos] = pltpu.make_async_copy(
                given[a].at[slot_of(a, zz * 2 + yy, xx * 2 + c)],
                held.at[a, k, pos],
                load_sem.at[a, k, pos],
            )
            loads[a, k, pos].start()

    def pair(a, k):
        for pos in (3, 1, 2, 0):
            loads[a, k, pos].wait()
            arrive(from_core.at[a, k, pos], c_recv.at[a, k, pos], c_peer)
            add_rows(held.at[a, k, pos], [from_core.at[a, k, pos]], 0, rows)
            if pos == 3:
                top, low = held.at[a, k, 3, halves[0]], held.at[a, k, 3, halves[1]]
                send(top, diag.at[a, k, halves[0]], dy_send.at[a, k], dy_recv.at[a, k], y_peer)
                send(low, diag.at[a, k, halves[1]], dx_send.at[a, k], dx_recv.at[a, k], x_peer)
            if pos == 1:
                send(held.at[a, k, 1, halves[1]], from_x.at[a, k, halves[1]], x_send.at[a, k, 1], x_recv.at[a, k, 1], x_peer)
            if pos == 2:
                send(held.at[a, k, 2, halves[0]], from_y.at[a, k, halves[0]], y_send.at[a, k, 0], y_recv.at[a, k, 0], y_peer)

    def relay(a, k):
        arrive(diag.at[a, k, halves[0]], dy_recv.at[a, k], y_peer)
        add_rows(held.at[a, k, 1], [diag.at[a, k]], 0, CUT)
        send(held.at[a, k, 1, halves[0]], from_x.at[a, k, halves[0]], x_send.at[a, k, 0], x_recv.at[a, k, 0], x_peer)
        arrive(diag.at[a, k, halves[1]], dx_recv.at[a, k], x_peer)
        add_rows(held.at[a, k, 2], [diag.at[a, k]], CUT, rows - CUT)
        send(held.at[a, k, 2, halves[1]], from_y.at[a, k, halves[1]], y_send.at[a, k, 1], y_recv.at[a, k, 1], y_peer)

    def plane(a, k):
        for h in (0, 1):
            arrive(from_x.at[a, k, halves[h]], x_recv.at[a, k, h], x_peer)
            arrive(from_y.at[a, k, halves[h]], y_recv.at[a, k, h], y_peer)
        if k:
            add_rows(held.at[a, k, 0], [from_x.at[a, k], from_y.at[a, k]], 0, rows)
            send(held.at[a, k, 0], from_z.at[a, k - 1], z_send.at[a, k - 1], z_recv.at[a, k - 1], device((z + k) % 4, y, x, c))
            return
        for j in (1, 2, 3):
            arrive(from_z.at[a, j - 1], z_recv.at[a, j - 1], device((z - j + 4) % 4, y, x, c))

        def body(i, carry):
            where = pl.ds(pl.multiple_of(i * 16, 16), 16)
            total = held[a, 0, 0, where, :].astype(jnp.float32)
            total = total + from_x[a, 0, where, :].astype(jnp.float32)
            total = total + from_y[a, 0, where, :].astype(jnp.float32)
            for j in range(3):
                total = total + from_z[a, j, where, :].astype(jnp.float32)
            if a == 2:
                down_ref[where, :] = total
            else:
                held[a, 0, 0, where, :] = total.astype(jnp.bfloat16)
            return carry

        lax.fori_loop(0, rows // 16, body, 0)
        if a == 2:
            return
        picked = row_selector(rows, share)
        spare[a] = lax.dot_general(
            picked, held[a, 0, 0], (((0,), (0,)), ((), ())), preferred_element_type=jnp.float32
        ).astype(jnp.bfloat16)
        for j, (px, pc) in enumerate(partners):
            send(
                spare.at[a, pl.ds(pl.multiple_of((px * 2 + pc) * PAD, 16), PAD)],
                rows_ref.at[a, group],
                group_send.at[a, j],
                group_recv.at[a, j],
                device(z, y, px, pc),
            )
        rows_ref[a, group] = spare[a, pl.ds(pl.multiple_of(group * PAD, 16), PAD), :]

    partners = [(x, 1 - c), (1 - x, c), (1 - x, 1 - c)]
    order = [(a, k) for a in (2, 1, 0) for k in (1, 2, 3, 0)]
    for i in range(3):
        begin(*order[i])
    for i in range(len(order) + 2):
        if i + 3 < len(order):
            begin(*order[i + 3])
        if i < len(order):
            pair(*order[i])
        if 1 <= i < len(order) + 1:
            relay(*order[i - 1])
        if 2 <= i:
            plane(*order[i - 2])
    for a in range(2):
        for j, (px, pc) in enumerate(partners):
            arrive(rows_ref.at[a, px * 2 + pc], group_recv.at[a, j], device(z, y, px, pc))
    for copy in sends:
        copy.wait_send()


def scatter_grads(first, second, third, share):
    rows, width = third.shape[-2:]
    dma = pltpu.SemaphoreType.DMA
    low = jnp.bfloat16
    return pl.pallas_call(
        partial(scatter_kernel, share),
        out_shape=(
            jax.ShapeDtypeStruct((2, 4, PAD, width), low),
            jax.ShapeDtypeStruct((rows, width), jnp.float32),
        ),
        in_specs=[pl.BlockSpec(memory_space=pl.ANY)] * 3,
        out_specs=[pl.BlockSpec(memory_space=pltpu.VMEM)] * 2,
        scratch_shapes=[
            pltpu.VMEM((3, 4, 4, rows, width), low),
            pltpu.VMEM((3, 4, 4, rows, width), low),
            pltpu.VMEM((3, 4, rows, width), low),
            pltpu.VMEM((3, 4, rows, width), low),
            pltpu.VMEM((3, 4, rows, width), low),
            pltpu.VMEM((3, 3, rows, width), low),
            pltpu.VMEM((2, 4 * PAD, width), low),
            dma((3, 4, 4)), dma((3, 4, 4)), dma((3, 4, 4)),
            dma((3, 4)), dma((3, 4)), dma((3, 4)), dma((3, 4)),
            dma((3, 4, 2)), dma((3, 4, 2)), dma((3, 4, 2)), dma((3, 4, 2)),
            dma((3, 3)), dma((3, 3)), dma((2, 3)), dma((2, 3)),
        ],
        compiler_params=pltpu.CompilerParams(
            collective_id=1, has_side_effects=True, vmem_limit_bytes=58 * 2**20
        ),
        name="scatter_grads",
    )(first, second, third)


def layer_norm(values):
    center = values - jnp.mean(values, axis=-1, keepdims=True)
    inverse = lax.rsqrt(jnp.mean(center * center, axis=-1, keepdims=True) + EPSILON)
    return (center * inverse, inverse)


def norm_back(grad_normed, normed, inverse):
    return inverse * (
        grad_normed
        - jnp.mean(grad_normed, axis=-1, keepdims=True)
        - normed * jnp.mean(grad_normed * normed, axis=-1, keepdims=True)
    )


def to_heads(array):
    return array.reshape(array.shape[0], HEADS, array.shape[1] // HEADS)


def dots(spec, left, right):
    return jnp.einsum(spec, left, right, preferred_element_type=jnp.float32)


def masked_scores(query_heads, key_heads, same_crop):
    scale_factor = 1.0 / math.sqrt(query_heads.shape[-1])
    scores = dots("qhd,khd->hqk", query_heads, key_heads) * scale_factor
    return jnp.where(same_crop[None], scores, LARGE_NEGATIVE)


def attend(query_seq, key_seq, value_seq, same_crop):
    scores = masked_scores(to_heads(query_seq), to_heads(key_seq), same_crop)
    row_max = jnp.max(scores, axis=-1, keepdims=True)
    raised = jnp.exp(scores - row_max)
    row_total = jnp.sum(raised, axis=-1, keepdims=True)
    probability = (raised / row_total).astype(jnp.bfloat16)
    context = dots("hqk,khd->qhd", probability, to_heads(value_seq))
    return (context.reshape(query_seq.shape[0], -1), (row_max + jnp.log(row_total))[..., 0])


def attend_back(query_seq, key_seq, value_seq, same_crop, log_total, grad_seq):
    query_heads = to_heads(query_seq)
    key_heads = to_heads(key_seq)
    value_heads = to_heads(value_seq)
    grad_heads = to_heads(grad_seq)
    scale_factor = 1.0 / math.sqrt(query_heads.shape[-1])
    scores = masked_scores(query_heads, key_heads, same_crop)
    probability = jnp.exp(scores - log_total[..., None])
    grad_prob = dots("qhd,khd->hqk", grad_heads, value_heads)
    inner = jnp.sum(probability * grad_prob, axis=-1, keepdims=True)
    grad_scores = (probability * (grad_prob - inner)).astype(jnp.bfloat16)
    grad_query = dots("hqk,khd->qhd", grad_scores, key_heads) * scale_factor
    grad_key = dots("hqk,qhd->khd", grad_scores, query_heads) * scale_factor
    grad_value = dots("hqk,qhd->khd", probability.astype(jnp.bfloat16), grad_heads)
    rows_here = query_seq.shape[0]
    rows_whole = key_seq.shape[0]
    return (
        grad_query.reshape(rows_here, -1),
        grad_key.reshape(rows_whole, -1),
        grad_value.reshape(rows_whole, -1),
    )


def on_device(
    chips,
    tokens_in,
    segment_ids,
    conditions,
    noise_bins,
    bin_counts,
    cotangent,
    ada_weight,
    qkv_weight,
    out_weight,
    up_weight,
    down_weight,
):
    groups = lax.axis_size("dp")
    cores = lax.axis_size("sp")
    tokens_float = tokens_in[0].astype(jnp.float32)
    segments = segment_ids[0]
    rows_here, width = tokens_float.shape
    share = qkv_weight.shape[0]
    index = lax.axis_index("dp") * cores + lax.axis_index("sp")
    kernels = chips and 4 * share == down_weight.shape[0]

    first = jnp.concatenate([qkv_weight, out_weight], axis=1)
    if kernels:
        shards = jnp.stack([first, up_weight]).reshape(2, share, 4, width)
        shards = jnp.pad(shards.transpose(0, 2, 1, 3), ((0, 0), (0, 0), (0, PAD - share), (0, 0)))
        full = gather_weights(shards, down_weight, share)
        mixers, uppers, downers = full.reshape(3, 4, width, width)
    else:
        mixers = lax.all_gather(first, ("dp", "sp"), axis=0, tiled=True)
        uppers = lax.all_gather(up_weight, ("dp", "sp"), axis=0, tiled=True)
        downers = lax.all_gather(down_weight, ("dp", "sp"), axis=0, tiled=True)
        mixers = mixers.reshape(width, 4, width).transpose(1, 0, 2)
        uppers = uppers.reshape(width, 4, width).transpose(1, 0, 2)
        downers = downers.reshape(4, width, width)

    counts = jnp.zeros((1, width), jnp.bfloat16).at[0, :NBINS].set(bin_counts[0].astype(jnp.bfloat16))
    gathered = lax.all_gather(jnp.concatenate([conditions[0], counts]), "dp", axis=0)
    bin_total = jnp.sum(gathered[:, CROPS, :NBINS].astype(jnp.int32), axis=0)
    bin_weight = 40.0 * groups / bin_total.astype(jnp.float32)
    crop_weight = jnp.sum(
        jnp.where(noise_bins[0][:, None] == jnp.arange(NBINS, dtype=jnp.int32), bin_weight, 0.0),
        axis=-1,
    )
    cond_all = gathered[:, :CROPS].reshape(groups * CROPS, width)
    cond_here = lax.dynamic_slice_in_dim(cond_all, index * share, share, axis=1)
    cond_act = jax.nn.silu(cond_here.astype(jnp.float32)).astype(jnp.bfloat16)
    modulation_part = dots("sd,df->sf", cond_act, ada_weight)
    modulation_part = modulation_part.reshape(groups, CROPS, -1)
    modulation = lax.psum(lax.psum_scatter(modulation_part, "dp", scatter_dimension=0), "sp")
    selector = (segments[:, None] == jnp.arange(CROPS, dtype=jnp.int32)).astype(jnp.float32)
    per_token = jnp.einsum("tc,cf->tf", selector, modulation, precision=lax.Precision.HIGHEST)
    shift_one, scale_one, gate_one, shift_two, scale_two, gate_two = jnp.split(
        per_token, 6, axis=-1
    )

    normed_one, inverse_one = layer_norm(tokens_float)
    hidden_one = (normed_one * (1.0 + scale_one) + shift_one).astype(jnp.bfloat16)
    projected = dots("td,qdf->qtf", hidden_one, mixers[:3]).astype(jnp.bfloat16)
    queries = projected[0]
    sides = lax.all_gather(projected[1:], "sp", axis=1, tiled=True)
    all_segments = lax.all_gather(segments, "sp", axis=0, tiled=True)
    same_crop = segments[:, None] == all_segments[None, :]
    context, log_total = attend(queries, sides[0], sides[1], same_crop)
    context_low = context.astype(jnp.bfloat16)
    attended = dots("td,df->tf", context_low, mixers[3])
    middle = tokens_float + gate_one * attended
    normed_two, inverse_two = layer_norm(middle)
    hidden_two = (normed_two * (1.0 + scale_two) + shift_two).astype(jnp.bfloat16)
    upper_in = dots("td,qdf->qtf", hidden_two, uppers)
    activated = jax.nn.gelu(upper_in, approximate=True).astype(jnp.bfloat16)
    mlp_out = dots("qtf,qfd->td", activated, downers)
    tokens_out = (middle + gate_two * mlp_out).astype(jnp.bfloat16)

    token_weight = jnp.sum(selector * crop_weight[None, :], axis=-1)
    grad_out = cotangent[0].astype(jnp.float32) * token_weight[:, None]
    grad_mlp = (grad_out * gate_two).astype(jnp.bfloat16)
    down_part = dots("qtf,td->qfd", activated, grad_mlp).astype(jnp.bfloat16)
    grad_act = dots("td,qfd->qtf", grad_mlp, downers)
    gelu_pull = jax.vjp(partial(jax.nn.gelu, approximate=True), upper_in)[1]
    grad_upper = gelu_pull(grad_act)[0].astype(jnp.bfloat16)
    up_part = dots("td,qtf->qdf", hidden_two, grad_upper).astype(jnp.bfloat16)
    grad_hidden_two = dots("qtf,qdf->td", grad_upper, uppers)
    grad_middle = grad_out + norm_back(grad_hidden_two * (1.0 + scale_two), normed_two, inverse_two)
    grad_attended = (grad_middle * gate_one).astype(jnp.bfloat16)
    grad_context = dots("tf,df->td", grad_attended, mixers[3]).astype(jnp.bfloat16)
    grad_query, grad_key, grad_value = attend_back(
        queries, sides[0], sides[1], same_crop, log_total, grad_context
    )
    grad_sides = lax.psum_scatter(
        jnp.stack([grad_key, grad_value]).astype(jnp.bfloat16),
        "sp",
        scatter_dimension=1,
        tiled=True,
    )
    grad_projected = jnp.concatenate([grad_query.astype(jnp.bfloat16)[None], grad_sides])
    out_part = dots("td,tf->df", context_low, grad_attended).astype(jnp.bfloat16)
    qkv_part = dots("td,qtf->qdf", hidden_one, grad_projected).astype(jnp.bfloat16)
    first_part = jnp.concatenate([qkv_part, out_part[None]])
    grad_hidden_one = dots("qtf,qdf->td", grad_projected, mixers[:3])
    tokens_grad = grad_middle + norm_back(
        grad_hidden_one * (1.0 + scale_one), normed_one, inverse_one
    )

    if kernels:
        pieces = (32, 4 * share, width)
        rows, down_grad = scatter_grads(
            first_part.reshape(pieces), up_part.reshape(pieces), down_part.reshape(pieces), share
        )
        rows = rows[:, :, :share].astype(jnp.float32).transpose(0, 2, 1, 3).reshape(2, share, 4 * width)
        first_grad, up_grad = rows[0], rows[1]
    else:
        joined = jnp.stack([first_part, up_part]).transpose(2, 0, 1, 3).reshape(width, 8 * width)
        rows = lax.psum_scatter(joined, ("dp", "sp"), scatter_dimension=0, tiled=True)
        rows = rows.astype(jnp.float32)
        first_grad, up_grad = rows[:, : 4 * width], rows[:, 4 * width :]
        down_grad = lax.psum_scatter(
            down_part.reshape(4 * width, width), ("dp", "sp"), scatter_dimension=0, tiled=True
        ).astype(jnp.float32)

    grad_per_token = jnp.concatenate(
        [
            grad_hidden_one,
            grad_hidden_one * normed_one,
            grad_middle * attended,
            grad_hidden_two,
            grad_hidden_two * normed_two,
            grad_out * mlp_out,
        ],
        axis=-1,
    )
    grad_modulation = lax.psum(
        jnp.einsum("tc,tf->cf", selector, grad_per_token, precision=lax.Precision.HIGHEST), "sp"
    )
    grad_rows = lax.all_gather(grad_modulation, "dp", axis=0, tiled=True)
    ada_grad = jnp.einsum(
        "sd,sf->df", cond_act.astype(jnp.float32), grad_rows, precision=lax.Precision.HIGHEST
    )
    silu_part = jnp.einsum(
        "sf,df->sd", grad_rows, ada_weight.astype(jnp.float32), precision=lax.Precision.HIGHEST
    )
    silu_all = lax.all_gather(silu_part, ("dp", "sp"), axis=0)
    silu_here = lax.dynamic_slice_in_dim(silu_all, lax.axis_index("dp") * CROPS, CROPS, axis=1)
    grad_silu = silu_here.transpose(1, 0, 2).reshape(CROPS, width)
    silu_pull = jax.vjp(jax.nn.silu, conditions[0].astype(jnp.float32))[1]
    cond_grad = silu_pull(grad_silu)[0]
    return (
        tokens_out[None],
        tokens_grad[None],
        cond_grad[None],
        ada_grad,
        first_grad[:, : 3 * width],
        first_grad[:, 3 * width :],
        up_grad,
        down_grad,
    )


def solution(mesh):
    placed = (
        P("dp", "sp", None),
        P("dp", "sp"),
        P("dp", None, None),
        P("dp", None),
        P("dp", None),
        P("dp", "sp", None),
        P(("dp", "sp"), None),
        P(("dp", "sp"), None),
        P(("dp", "sp"), None),
        P(("dp", "sp"), None),
        P(("dp", "sp"), None),
    )
    return jax.shard_map(
        partial(on_device, mesh.shape["dp"] == 16 and mesh.shape["sp"] == 2),
        mesh=mesh,
        in_specs=placed,
        out_specs=(
            P("dp", "sp", None),
            P("dp", "sp", None),
            P("dp", None, None),
            P(("dp", "sp"), None),
            P(("dp", "sp"), None),
            P(("dp", "sp"), None),
            P(("dp", "sp"), None),
            P(("dp", "sp"), None),
        ),
        check_vma=False,
    )
```

```python
from functools import partial
import math

import jax
import jax.numpy as jnp
from jax import lax
from jax.experimental import pallas as pl
from jax.experimental.pallas import tpu as pltpu
from jax.sharding import PartitionSpec as P

HEADS = 16
CROPS = 4
NBINS = 8
EPSILON = 1e-06
LARGE_NEGATIVE = -1e30
GELU_SCALE = math.sqrt(2.0 / math.pi)
GELU_CUBE = 0.044715

MESH = pl.DeviceIdType.MESH
PAD = 48
CUT = 80
CHIPS = 16
BAND = 1792
PLACES = ((0, 0), (0, 1), (1, 0), (1, 1))


def position():
    d = lax.axis_index("dp")
    c = lax.axis_index("sp")
    return d // 4, (d // 2) % 2, d % 2, c


def device(z, y, x, c):
    return (z * 4 + y * 2 + x, c)


def block_of(kind, zy, group):
    if kind == 2:
        return zy // 2, (zy % 2) * 4 + group
    return group, zy


def greet(peers):
    barrier = pltpu.get_barrier_semaphore()
    for peer in peers:
        pl.semaphore_signal(barrier, inc=1, device_id=peer, device_id_type=MESH)
    pl.semaphore_wait(barrier, len(peers))


def remote(src, dst, send, recv, target):
    return pltpu.make_async_remote_copy(
        src_ref=src,
        dst_ref=dst,
        send_sem=send,
        recv_sem=recv,
        device_id=target,
        device_id_type=MESH,
    )


def arrive(ref, sem, target):
    remote(ref, ref, sem, sem, target).wait_recv()


def row_selector(rows, share):
    shape = (rows, 4 * PAD)
    row = lax.broadcasted_iota(jnp.int32, shape, 0)
    column = lax.broadcasted_iota(jnp.int32, shape, 1)
    picked = jnp.zeros(shape, jnp.bool_)
    for k in range(4):
        inside = (row >= k * share) & (row < (k + 1) * share)
        picked = picked | (inside & (column == row - k * share + k * PAD))
    return picked.astype(jnp.float32).astype(jnp.bfloat16)


def product(left, right):
    return jnp.dot(left, right, preferred_element_type=jnp.float32)


def product_by_rows(left, right):
    return lax.dot_general(left, right, (((0,), (0,)), ((), ())), preferred_element_type=jnp.float32)


def product_by_columns(left, right):
    return lax.dot_general(left, right, (((1,), (1,)), ((), ())), preferred_element_type=jnp.float32)


def chunks(rows, body, step=16):
    def run(i, carry):
        body(pl.ds(pl.multiple_of(i * step, step), step))
        return carry

    lax.fori_loop(0, rows // step, run, 0)


def normed(values):
    center = values - jnp.mean(values, axis=-1, keepdims=True)
    inverse = lax.rsqrt(jnp.mean(center * center, axis=-1, keepdims=True) + EPSILON)
    return center * inverse, inverse


def pick(segments, table, first, column, width):
    columns = slice(column * width, (column + 1) * width)
    value = table[first + 3 : first + 4, columns]
    for crop in (2, 1, 0):
        value = jnp.where(segments == crop, table[first + crop : first + crop + 1, columns], value)
    return value


def window_of(head, size, width):
    start = jnp.minimum((head * size) // 128, width // 128 - 2) * 128
    start = pl.multiple_of(start, 128)
    lane = lax.broadcasted_iota(jnp.int32, (1, 256), 1) + start
    return pl.ds(start, 256), (lane >= head * size) & (lane < (head + 1) * size)


def forward_kernel(share, shards_ref, down_ref, act_ref, ada_ref, tokens_ref, cot_ref, seg_col_ref,
                   seg_row_ref, bins_ref,
                   weights_ref, down_part_ref, slope_ref, hidden_ref, query_ref, sides_ref, total_ref,
                   context_ref, attended_ref, middle_ref, hidden_two_ref, mlp_ref, out_ref, table_ref,
                   conds_ref, level_ref,
                   full, stage, part, part_recv, band, band_diag, band_x, band_y, band_z, halves_of,
                   seg_all, bias, work, active, grad_mlp, slope, *sems):
    (
        group_send, group_recv, z_send, z_recv, x_send, x_recv, y_send, y_recv,
        dx_send, dx_recv, dy_send, dy_recv, c_send, c_recv,
        cond_send, cond_recv, pc_send, pc_recv, pd_send, pd_recv, px_send, px_recv, py_send, py_recv,
        pz_send, pz_recv, pm_send, pm_recv, seg_send, seg_recv, kv_send, kv_recv,
        save_sem, grad_sem, slope_sem,
    ) = sems
    z, y, x, c = position()
    me = z * 4 + y * 2 + x
    group = x * 2 + c
    zy = z * 2 + y
    rows = 4 * share
    count, width = tokens_ref.shape
    halves = (pl.ds(0, CUT), pl.ds(CUT, rows - CUT))
    x_peer, y_peer, c_peer = device(z, y, 1 - x, c), device(z, 1 - y, x, c), device(z, y, x, 1 - c)
    partners = [(x, 1 - c), (1 - x, c), (1 - x, 1 - c)]
    greet(
        [((me + k) % CHIPS, c) for k in range(1, CHIPS)] + [c_peer, device(z, y, 1 - x, 1 - c)]
    )
    sends = {a: [] for a in (0, 1, 2, "other")}

    def send(a, *args):
        copy = remote(*args)
        copy.start()
        sends[a].append(copy)

    def finish_sends(a):
        for copy in sends[a]:
            copy.wait_send()
        sends[a] = []

    def place(a, k, other_y, other_x, core=None):
        zz = (z - k + 4) % 4
        yy = 1 - y if other_y else y
        xx = 1 - x if other_x else x
        cc = c if core is None else core
        block, row = block_of(a, zz * 2 + yy, xx * 2 + cc)
        return full.at[a, block, pl.ds(pl.multiple_of(row * rows, 16), rows)]

    def half(a, k, other_y, other_x, h):
        zz = (z - k + 4) % 4
        yy = 1 - y if other_y else y
        xx = 1 - x if other_x else x
        block, row = block_of(a, zz * 2 + yy, xx * 2 + c)
        start = row * rows + (CUT if h else 0)
        return full.at[a, block, pl.ds(pl.multiple_of(start, 16), rows - CUT if h else CUT)]

    for a in range(2):
        for j, (px, pc) in enumerate(partners):
            send(
                "other",
                shards_ref.at[a, px * 2 + pc],
                stage.at[a, pl.ds(pl.multiple_of(group * PAD, 16), PAD)],
                group_send.at[a, j],
                group_recv.at[a, j],
                device(z, y, px, pc),
            )
    for k in range(1, CHIPS):
        to = (me + k) % CHIPS
        send("other", act_ref.at[to], conds_ref.at[me], cond_send.at[k - 1], cond_recv.at[k - 1], (to, c))
    seg_all[c] = seg_row_ref[...]
    send("other", seg_row_ref, seg_all.at[c], seg_send, seg_recv, c_peer)
    conds_ref[me] = act_ref[me]
    for a in range(2):
        stage[a, pl.ds(pl.multiple_of(group * PAD, 16), PAD), :] = shards_ref[a, group]

    def own(a):
        block, row = block_of(a, zy, group)
        here = pl.ds(pl.multiple_of(row * rows, 16), rows)
        if a < 2:
            for j, (px, pc) in enumerate(partners):
                arrive(
                    stage.at[a, pl.ds(pl.multiple_of((px * 2 + pc) * PAD, 16), PAD)],
                    group_recv.at[a, j],
                    device(z, y, px, pc),
                )
            full[a, block, here, :] = product(row_selector(rows, share), stage[a]).astype(jnp.bfloat16)
        else:
            full[a, block, here, :] = down_ref[...]
        mine = place(a, 0, 0, 0)
        for k in (1, 2, 3):
            send(a, mine, mine, z_send.at[a, k - 1], z_recv.at[a, k - 1], device((z + k) % 4, y, x, c))

    def to_core(a, k, pos):
        piece = place(a, k, *PLACES[pos])
        send(a, piece, piece, c_send.at[a, k, pos], c_recv.at[a, k, pos], c_peer)

    def spread(a, k):
        if k:
            arrive(place(a, k, 0, 0), z_recv.at[a, k - 1], device((z - k + 4) % 4, y, x, c))
        for h in (0, 1):
            one, two = half(a, k, 0, 0, h), half(a, k, 0, 0, 1 - h)
            send(a, one, one, x_send.at[a, k, h], x_recv.at[a, k, h], x_peer)
            send(a, two, two, y_send.at[a, k, 1 - h], y_recv.at[a, k, 1 - h], y_peer)
        to_core(a, k, 0)

    def forward(a, k):
        top, low = half(a, k, 0, 1, 0), half(a, k, 1, 0, 1)
        arrive(top, x_recv.at[a, k, 0], x_peer)
        send(a, top, top, dy_send.at[a, k], dy_recv.at[a, k], y_peer)
        arrive(low, y_recv.at[a, k, 1], y_peer)
        send(a, low, low, dx_send.at[a, k], dx_recv.at[a, k], x_peer)
        arrive(half(a, k, 0, 1, 1), x_recv.at[a, k, 1], x_peer)
        to_core(a, k, 1)
        arrive(half(a, k, 1, 0, 0), y_recv.at[a, k, 0], y_peer)
        to_core(a, k, 2)

    def finish(a, k):
        arrive(half(a, k, 1, 1, 0), dy_recv.at[a, k], y_peer)
        arrive(half(a, k, 1, 1, 1), dx_recv.at[a, k], x_peer)
        to_core(a, k, 3)

    saves = []

    def complete(a):
        for k in range(4):
            for pos, (oy, ox) in enumerate(PLACES):
                arrive(place(a, k, oy, ox, 1 - c), c_recv.at[a, k, pos], c_peer)
        copy = pltpu.make_async_copy(full.at[a], weights_ref.at[a], save_sem.at[a])
        copy.start()
        saves.append(copy)

    def mod_start():
        for k in range(1, CHIPS):
            source = (me - k + CHIPS) % CHIPS
            arrive(conds_ref.at[source], cond_recv.at[k - 1], (source, c))
        acts = conds_ref[:, :8, :].astype(jnp.float32).reshape(CHIPS * 8, 128)
        row = lax.broadcasted_iota(jnp.int32, acts.shape, 0) % 8
        upper = jnp.where(row < CROPS, acts, 0.0).astype(jnp.bfloat16)
        lower = pltpu.roll(jnp.where(row < CROPS, acts, 0.0), CROPS, 0).astype(jnp.bfloat16)
        side = ada_ref.shape[1] // 2
        part[...] = product(upper, ada_ref[:, :side]) + product(lower, ada_ref[:, side:])
        far = pl.ds(pl.multiple_of((1 - c) * (side - BAND), 128), BAND)
        send("other", part.at[:, far], part_recv, pc_send, pc_recv, c_peer)

    def block8(zz, yy, xx):
        return pl.ds(pl.multiple_of((zz * 4 + yy * 2 + xx) * 8, 8), 8)

    def mod_cores():
        arrive(part_recv, pc_recv, c_peer)
        side = ada_ref.shape[1] // 2
        near = pl.ds(pl.multiple_of(c * (side - BAND), 128), BAND)
        band[...] = part[:, near] + part_recv[...]
        for k in range(4):
            zz = (z + k) % 4
            src = band.at[block8(zz, 1 - y, 1 - x)]
            send("other", src, band_diag.at[k], pd_send.at[k], pd_recv.at[k], x_peer if k % 2 else y_peer)

    def mod_plane():
        for k in range(4):
            zz = (z + k) % 4
            to_x, to_y = block8(zz, y, 1 - x), block8(zz, 1 - y, x)
            arrive(band_diag.at[k], pd_recv.at[k], x_peer if k % 2 else y_peer)
            fold = to_y if k % 2 else to_x
            band[fold, :] = band[fold, :] + band_diag[k]
            send("other", band.at[to_x], band_x.at[k], px_send.at[k], px_recv.at[k], x_peer)
            send("other", band.at[to_y], band_y.at[k], py_send.at[k], py_recv.at[k], y_peer)

    def mod_line():
        for k in (1, 2, 3, 0):
            zz = (z + k) % 4
            mine = block8(zz, y, x)
            arrive(band_x.at[k], px_recv.at[k], x_peer)
            arrive(band_y.at[k], py_recv.at[k], y_peer)
            band[mine, :] = band[mine, :] + band_x[k] + band_y[k]
            if k:
                send("other", band.at[mine], band_z.at[k - 1], pz_send.at[k - 1], pz_recv.at[k - 1], device(zz, y, x, c))

    def mod_last():
        for k in (1, 2, 3):
            arrive(band_z.at[k - 1], pz_recv.at[k - 1], device((z - k + 4) % 4, y, x, c))
        halves_of[c] = band[block8(z, y, x), :] + band_z[0] + band_z[1] + band_z[2]
        send("other", halves_of.at[c], halves_of.at[c], pm_send, pm_recv, c_peer)

    def mod_end():
        arrive(halves_of.at[1 - c], pm_recv, c_peer)
        side = ada_ref.shape[1] // 2
        table_ref[:, :BAND] = halves_of[0]
        table_ref[:, BAND:] = halves_of[1][:, 2 * BAND - side :]
        counts = jnp.sum(conds_ref[:, :, :].astype(jnp.float32)[:, CROPS : CROPS + 1, :], axis=0)
        lane = lax.broadcasted_iota(jnp.int32, counts.shape, 1)
        weight = jnp.where(lane < NBINS, 40.0 * CHIPS / jnp.where(lane < NBINS, counts, 1.0), 0.0)
        level_ref[...] = jnp.broadcast_to(
            jnp.sum(bins_ref[...] * weight, axis=-1, keepdims=True), level_ref.shape
        )

    def first_norm():
        def body(at):
            segments = seg_col_ref[at, :1]
            value, _ = normed(tokens_ref[at, :].astype(jnp.float32))
            value = value * (1.0 + pick(segments, table_ref, 0, 1, width))
            hidden_ref[at, :] = (value + pick(segments, table_ref, 0, 0, width)).astype(jnp.bfloat16)

        chunks(count, body)
        arrive(seg_all.at[1 - c], seg_recv, c_peer)
        for h in (0, 1):
            same = seg_col_ref[:, :1] == seg_all[h][:1, :]
            bias[:, h * count : (h + 1) * count] = jnp.where(same, 0.0, LARGE_NEGATIVE)

    def project():
        here = pl.ds(pl.multiple_of(c * count, 256), count)
        for q in (1, 2):
            sides_ref[q - 1, here, :] = product(hidden_ref[...], full[0, q]).astype(jnp.bfloat16)
            send("other", sides_ref.at[q - 1, here], sides_ref.at[q - 1, here], kv_send.at[q - 1], kv_recv.at[q - 1], c_peer)
        query_ref[...] = product(hidden_ref[...], full[0, 0]).astype(jnp.bfloat16)
        total_ref[...] = jnp.zeros_like(total_ref)
        work[...] = jnp.zeros_like(work)

    def attend(first, last):
        if first == 0:
            there = pl.ds(pl.multiple_of((1 - c) * count, 256), count)
            for q in (0, 1):
                arrive(sides_ref.at[q, there], kv_recv.at[q], c_peer)
        size = width // HEADS
        scale = 1.0 / math.sqrt(size)

        def body(head, carry):
            columns, inside = window_of(head, size, width)
            query = query_ref[:, columns]
            query = jnp.where(inside, query, jnp.zeros_like(query))
            scores = product_by_columns(query, sides_ref[0, :, columns]) * scale + bias[...]
            top = jnp.max(scores, axis=-1, keepdims=True)
            raised = jnp.exp(scores - top)
            total = jnp.sum(raised, axis=-1, keepdims=True)
            chance = (raised * (1.0 / total)).astype(jnp.bfloat16)
            context = product(chance, sides_ref[1, :, columns])
            work[:, columns] = jnp.where(inside, context, work[:, columns])
            lane = lax.broadcasted_iota(jnp.int32, (1, 128), 1)
            total_ref[...] = jnp.where(lane == head, top + jnp.log(total), total_ref[...])
            return carry

        lax.fori_loop(first, last, body, 0)

    def mix():
        context_ref[...] = work[...].astype(jnp.bfloat16)
        attended_ref[...] = product(context_ref[...], full[0, 3])

        def body(at):
            segments = seg_col_ref[at, :1]
            gate = pick(segments, table_ref, 0, 2, width)
            middle = tokens_ref[at, :].astype(jnp.float32) + gate * attended_ref[at, :]
            middle_ref[at, :] = middle
            value, _ = normed(middle)
            value = value * (1.0 + pick(segments, table_ref, 4, 1, width))
            hidden_two_ref[at, :] = (value + pick(segments, table_ref, 4, 0, width)).astype(jnp.bfloat16)
            level = level_ref[3:4, :1]
            for crop in (2, 1, 0):
                level = jnp.where(segments == crop, level_ref[crop : crop + 1, :1], level)
            grad = cot_ref[at, :].astype(jnp.float32) * level
            grad_mlp[at, :] = (grad * pick(segments, table_ref, 4, 2, width)).astype(jnp.bfloat16)

        chunks(count, body)

    slope_copies = {}

    def expand(q):
        work[...] = product(hidden_two_ref[...], full[1, q])
        if q >= 2:
            slope_copies[q - 2].wait()

        def body(at):
            u = work[at, :]
            square = u * u
            bend = jnp.tanh(GELU_SCALE * (u + GELU_CUBE * (square * u)))
            active[q, at, :] = (0.5 * u * (1.0 + bend)).astype(jnp.bfloat16)
            inner = GELU_SCALE * (1.0 + 3.0 * GELU_CUBE * square)
            slope[q % 2, at, :] = 0.5 * (1.0 + bend) + 0.5 * u * (1.0 - bend * bend) * inner

        chunks(count, body)
        copy = pltpu.make_async_copy(slope.at[q % 2], slope_ref.at[q], slope_sem.at[q % 2])
        copy.start()
        slope_copies[q] = copy

    def down_grad(q):
        if q == 0:
            finish_sends(0)
            saves[0].wait()
        full[0, q] = product_by_rows(active[q], grad_mlp[...]).astype(jnp.bfloat16)
        copy = pltpu.make_async_copy(full.at[0, q], down_part_ref.at[q], grad_sem.at[q])
        copy.start()
        saves.append(copy)

    def contract():
        work[...] = product(active[0], full[2, 0])
        for q in (1, 2, 3):
            work[...] += product(active[q], full[2, q])

        def body(at):
            mlp = work[at, :]
            mlp_ref[at, :] = mlp
            gate = pick(seg_col_ref[at, :1], table_ref, 4, 2, width)
            out_ref[at, :] = (middle_ref[at, :] + gate * mlp).astype(jnp.bfloat16)

        chunks(count, body)

    extra = {
        1: [mod_start],
        2: [mod_cores],
        3: [mod_plane],
        4: [mod_line],
        5: [mod_last],
        6: [mod_end, first_norm, partial(complete, 0), project],
        7: [partial(attend, 0, 8)],
        8: [partial(attend, 8, 16)],
        9: [mix],
        10: [partial(complete, 1), partial(expand, 0), partial(expand, 1)],
        11: [partial(expand, 2), partial(expand, 3)],
        12: [partial(down_grad, 0), partial(down_grad, 1)],
        13: [partial(down_grad, 2), partial(down_grad, 3)],
        14: [partial(complete, 2), contract],
    }
    order = [(a, k) for a in range(3) for k in range(4)]
    own(0)
    for i in range(len(order) + 3):
        if i < len(order):
            a, k = order[i]
            if k == 1 and a < 2:
                own(a + 1)
            spread(a, k)
        if 2 <= i < len(order) + 2:
            forward(*order[i - 2])
        if 3 <= i:
            finish(*order[i - 3])
        for step in extra.get(i, ()):
            step()
    for copy in saves[1:]:
        copy.wait()
    for q in (2, 3):
        slope_copies[q].wait()
    for a in (1, 2, "other"):
        finish_sends(a)


def run_forward(shards, down, acts, ada, tokens, cot, seg_col, seg_row, bins, share):
    count, width = tokens.shape
    dma = pltpu.SemaphoreType.DMA
    low, wide = jnp.bfloat16, jnp.float32
    side = ada.shape[1] // 2
    vmem, any_ = pl.BlockSpec(memory_space=pltpu.VMEM), pl.BlockSpec(memory_space=pl.ANY)
    out = jax.ShapeDtypeStruct
    return pl.pallas_call(
        partial(forward_kernel, share),
        out_shape=(
            out((3, 4, width, width), low),
            out((4, width, width), low),
            out((4, count, width), wide),
            out((count, width), low),
            out((count, width), low),
            out((2, 2 * count, width), low),
            out((count, 128), wide),
            out((count, width), low),
            out((count, width), wide),
            out((count, width), wide),
            out((count, width), low),
            out((count, width), wide),
            out((count, width), low),
            out((8, side), wide),
            out((CHIPS, 16, 128), low),
            out((8, 128), wide),
        ),
        in_specs=[vmem] * 9,
        out_specs=[any_] * 3 + [vmem] * 13,
        scratch_shapes=[
            pltpu.VMEM((3, 4, width, width), low),
            pltpu.VMEM((2, 4 * PAD, width), low),
            pltpu.VMEM((CHIPS * 8, side), wide),
            pltpu.VMEM((CHIPS * 8, BAND), wide),
            pltpu.VMEM((CHIPS * 8, BAND), wide),
            pltpu.VMEM((4, 8, BAND), wide),
            pltpu.VMEM((4, 8, BAND), wide),
            pltpu.VMEM((4, 8, BAND), wide),
            pltpu.VMEM((3, 8, BAND), wide),
            pltpu.VMEM((2, 8, BAND), wide),
            pltpu.VMEM((2, 8, count), jnp.int32),
            pltpu.VMEM((count, 2 * count), wide),
            pltpu.VMEM((count, width), wide),
            pltpu.VMEM((4, count, width), low),
            pltpu.VMEM((count, width), low),
            pltpu.VMEM((2, count, width), wide),
            dma((2, 3)), dma((2, 3)), dma((3, 3)), dma((3, 3)),
            dma((3, 4, 2)), dma((3, 4, 2)), dma((3, 4, 2)), dma((3, 4, 2)),
            dma((3, 4)), dma((3, 4)), dma((3, 4)), dma((3, 4)),
            dma((3, 4, 4)), dma((3, 4, 4)),
            dma((CHIPS - 1,)), dma((CHIPS - 1,)), dma, dma, dma((4,)), dma((4,)),
            dma((4,)), dma((4,)), dma((4,)), dma((4,)), dma((3,)), dma((3,)), dma, dma, dma, dma,
            dma((2,)), dma((2,)), dma((3,)), dma((4,)), dma((2,)),
        ],
        compiler_params=pltpu.CompilerParams(
            collective_id=0, has_side_effects=True, vmem_limit_bytes=63 * 2**20
        ),
        name="forward",
    )(shards, down, acts, ada, tokens, cot, seg_col, seg_row, bins)
def slot_of(kind, zy, group):
    return zy * 4 + group if kind == 2 else group * 8 + zy


def add_rows(dst, sources, start, rows):
    def body(i, carry):
        where = pl.ds(pl.multiple_of(start + i * 16, 16), 16)
        total = dst[where, :].astype(jnp.float32)
        for source in sources:
            total = total + source[where, :].astype(jnp.float32)
        dst[where, :] = total.astype(dst.dtype)
        return carry

    lax.fori_loop(0, rows // 16, body, 0)


def scatter_kernel(share, g1_ref, g2_ref, g3_ref, rows_ref, down_ref, held, from_core, diag,
                   from_x, from_y, from_z, spare, *sems):
    (
        load_sem, c_send, c_recv, dx_send, dx_recv, dy_send, dy_recv, x_send, x_recv,
        y_send, y_recv, z_send, z_recv, group_send, group_recv,
    ) = sems
    z, y, x, c = position()
    group = x * 2 + c
    rows = 4 * share
    x_peer, y_peer, c_peer = device(z, y, 1 - x, c), device(z, 1 - y, x, c), device(z, y, x, 1 - c)
    halves = (pl.ds(0, CUT), pl.ds(CUT, rows - CUT))
    given = (g1_ref, g2_ref, g3_ref)
    greet(
        [device((z + k) % 4, y, x, c) for k in (1, 2, 3)]
        + [x_peer, y_peer, c_peer, device(z, y, 1 - x, 1 - c)]
    )
    sends = []

    def send(*args):
        copy = remote(*args)
        copy.start()
        sends.append(copy)

    places = ((0, 0), (0, 1), (1, 0), (1, 1))
    loads = {}

    def begin(a, k):
        zz = (z + k) % 4
        for pos, (oy, ox) in enumerate(places):
            yy = 1 - y if oy else y
            xx = 1 - x if ox else x
            send(
                given[a].at[slot_of(a, zz * 2 + yy, xx * 2 + 1 - c)],
                from_core.at[a, k, pos],
                c_send.at[a, k, pos],
                c_recv.at[a, k, pos],
                c_peer,
            )
            loads[a, k, pos] = pltpu.make_async_copy(
                given[a].at[slot_of(a, zz * 2 + yy, xx * 2 + c)],
                held.at[a, k, pos],
                load_sem.at[a, k, pos],
            )
            loads[a, k, pos].start()

    def pair(a, k):
        for pos in (3, 1, 2, 0):
            loads[a, k, pos].wait()
            arrive(from_core.at[a, k, pos], c_recv.at[a, k, pos], c_peer)
            add_rows(held.at[a, k, pos], [from_core.at[a, k, pos]], 0, rows)
            if pos == 3:
                top, low = held.at[a, k, 3, halves[0]], held.at[a, k, 3, halves[1]]
                send(top, diag.at[a, k, halves[0]], dy_send.at[a, k], dy_recv.at[a, k], y_peer)
                send(low, diag.at[a, k, halves[1]], dx_send.at[a, k], dx_recv.at[a, k], x_peer)
            if pos == 1:
                send(held.at[a, k, 1, halves[1]], from_x.at[a, k, halves[1]], x_send.at[a, k, 1], x_recv.at[a, k, 1], x_peer)
            if pos == 2:
                send(held.at[a, k, 2, halves[0]], from_y.at[a, k, halves[0]], y_send.at[a, k, 0], y_recv.at[a, k, 0], y_peer)

    def relay(a, k):
        arrive(diag.at[a, k, halves[0]], dy_recv.at[a, k], y_peer)
        add_rows(held.at[a, k, 1], [diag.at[a, k]], 0, CUT)
        send(held.at[a, k, 1, halves[0]], from_x.at[a, k, halves[0]], x_send.at[a, k, 0], x_recv.at[a, k, 0], x_peer)
        arrive(diag.at[a, k, halves[1]], dx_recv.at[a, k], x_peer)
        add_rows(held.at[a, k, 2], [diag.at[a, k]], CUT, rows - CUT)
        send(held.at[a, k, 2, halves[1]], from_y.at[a, k, halves[1]], y_send.at[a, k, 1], y_recv.at[a, k, 1], y_peer)

    def plane(a, k):
        for h in (0, 1):
            arrive(from_x.at[a, k, halves[h]], x_recv.at[a, k, h], x_peer)
            arrive(from_y.at[a, k, halves[h]], y_recv.at[a, k, h], y_peer)
        if k:
            add_rows(held.at[a, k, 0], [from_x.at[a, k], from_y.at[a, k]], 0, rows)
            send(held.at[a, k, 0], from_z.at[a, k - 1], z_send.at[a, k - 1], z_recv.at[a, k - 1], device((z + k) % 4, y, x, c))
            return
        for j in (1, 2, 3):
            arrive(from_z.at[a, j - 1], z_recv.at[a, j - 1], device((z - j + 4) % 4, y, x, c))

        def body(i, carry):
            where = pl.ds(pl.multiple_of(i * 16, 16), 16)
            total = held[a, 0, 0, where, :].astype(jnp.float32)
            total = total + from_x[a, 0, where, :].astype(jnp.float32)
            total = total + from_y[a, 0, where, :].astype(jnp.float32)
            for j in range(3):
                total = total + from_z[a, j, where, :].astype(jnp.float32)
            if a == 2:
                down_ref[where, :] = total
            else:
                held[a, 0, 0, where, :] = total.astype(jnp.bfloat16)
            return carry

        lax.fori_loop(0, rows // 16, body, 0)
        if a == 2:
            return
        picked = row_selector(rows, share)
        spare[a] = lax.dot_general(
            picked, held[a, 0, 0], (((0,), (0,)), ((), ())), preferred_element_type=jnp.float32
        ).astype(jnp.bfloat16)
        for j, (px, pc) in enumerate(partners):
            send(
                spare.at[a, pl.ds(pl.multiple_of((px * 2 + pc) * PAD, 16), PAD)],
                rows_ref.at[a, group],
                group_send.at[a, j],
                group_recv.at[a, j],
                device(z, y, px, pc),
            )
        rows_ref[a, group] = spare[a, pl.ds(pl.multiple_of(group * PAD, 16), PAD), :]

    partners = [(x, 1 - c), (1 - x, c), (1 - x, 1 - c)]
    order = [(a, k) for a in (2, 1, 0) for k in (1, 2, 3, 0)]
    for i in range(3):
        begin(*order[i])
    for i in range(len(order) + 2):
        if i + 3 < len(order):
            begin(*order[i + 3])
        if i < len(order):
            pair(*order[i])
        if 1 <= i < len(order) + 1:
            relay(*order[i - 1])
        if 2 <= i:
            plane(*order[i - 2])
    for a in range(2):
        for j, (px, pc) in enumerate(partners):
            arrive(rows_ref.at[a, px * 2 + pc], group_recv.at[a, j], device(z, y, px, pc))
    for copy in sends:
        copy.wait_send()


def scatter_grads(first, second, third, share):
    rows, width = third.shape[-2:]
    dma = pltpu.SemaphoreType.DMA
    low = jnp.bfloat16
    return pl.pallas_call(
        partial(scatter_kernel, share),
        out_shape=(
            jax.ShapeDtypeStruct((2, 4, PAD, width), low),
            jax.ShapeDtypeStruct((rows, width), jnp.float32),
        ),
        in_specs=[pl.BlockSpec(memory_space=pl.ANY)] * 3,
        out_specs=[pl.BlockSpec(memory_space=pltpu.VMEM)] * 2,
        scratch_shapes=[
            pltpu.VMEM((3, 4, 4, rows, width), low),
            pltpu.VMEM((3, 4, 4, rows, width), low),
            pltpu.VMEM((3, 4, rows, width), low),
            pltpu.VMEM((3, 4, rows, width), low),
            pltpu.VMEM((3, 4, rows, width), low),
            pltpu.VMEM((3, 3, rows, width), low),
            pltpu.VMEM((2, 4 * PAD, width), low),
            dma((3, 4, 4)), dma((3, 4, 4)), dma((3, 4, 4)),
            dma((3, 4)), dma((3, 4)), dma((3, 4)), dma((3, 4)),
            dma((3, 4, 2)), dma((3, 4, 2)), dma((3, 4, 2)), dma((3, 4, 2)),
            dma((3, 3)), dma((3, 3)), dma((2, 3)), dma((2, 3)),
        ],
        compiler_params=pltpu.CompilerParams(
            collective_id=1, has_side_effects=True, vmem_limit_bytes=58 * 2**20
        ),
        name="scatter_grads",
    )(first, second, third)


def layer_norm(values):
    center = values - jnp.mean(values, axis=-1, keepdims=True)
    inverse = lax.rsqrt(jnp.mean(center * center, axis=-1, keepdims=True) + EPSILON)
    return (center * inverse, inverse)


def norm_back(grad_normed, normed, inverse):
    return inverse * (
        grad_normed
        - jnp.mean(grad_normed, axis=-1, keepdims=True)
        - normed * jnp.mean(grad_normed * normed, axis=-1, keepdims=True)
    )


def to_heads(array):
    return array.reshape(array.shape[0], HEADS, array.shape[1] // HEADS)


def dots(spec, left, right):
    return jnp.einsum(spec, left, right, preferred_element_type=jnp.float32)


def masked_scores(query_heads, key_heads, same_crop):
    scale_factor = 1.0 / math.sqrt(query_heads.shape[-1])
    scores = dots("qhd,khd->hqk", query_heads, key_heads) * scale_factor
    return jnp.where(same_crop[None], scores, LARGE_NEGATIVE)


def attend(query_seq, key_seq, value_seq, same_crop):
    scores = masked_scores(to_heads(query_seq), to_heads(key_seq), same_crop)
    row_max = jnp.max(scores, axis=-1, keepdims=True)
    raised = jnp.exp(scores - row_max)
    row_total = jnp.sum(raised, axis=-1, keepdims=True)
    probability = (raised / row_total).astype(jnp.bfloat16)
    context = dots("hqk,khd->qhd", probability, to_heads(value_seq))
    return (context.reshape(query_seq.shape[0], -1), (row_max + jnp.log(row_total))[..., 0])


def attend_back(query_seq, key_seq, value_seq, same_crop, log_total, grad_seq):
    query_heads = to_heads(query_seq)
    key_heads = to_heads(key_seq)
    value_heads = to_heads(value_seq)
    grad_heads = to_heads(grad_seq)
    scale_factor = 1.0 / math.sqrt(query_heads.shape[-1])
    scores = masked_scores(query_heads, key_heads, same_crop)
    probability = jnp.exp(scores - log_total[..., None])
    grad_prob = dots("qhd,khd->hqk", grad_heads, value_heads)
    inner = jnp.sum(probability * grad_prob, axis=-1, keepdims=True)
    grad_scores = (probability * (grad_prob - inner)).astype(jnp.bfloat16)
    grad_query = dots("hqk,khd->qhd", grad_scores, key_heads) * scale_factor
    grad_key = dots("hqk,qhd->khd", grad_scores, query_heads) * scale_factor
    grad_value = dots("hqk,qhd->khd", probability.astype(jnp.bfloat16), grad_heads)
    rows_here = query_seq.shape[0]
    rows_whole = key_seq.shape[0]
    return (
        grad_query.reshape(rows_here, -1),
        grad_key.reshape(rows_whole, -1),
        grad_value.reshape(rows_whole, -1),
    )


def kernel_inputs(segments, conditions, noise_bins, bin_counts, ada_weight, first, up_weight):
    share, width = first.shape[0], first.shape[1] // 4
    cores = lax.axis_size("sp")
    shards = jnp.stack([first, up_weight]).reshape(2, share, 4, width)
    shards = jnp.pad(shards.transpose(0, 2, 1, 3), ((0, 0), (0, 0), (0, PAD - share), (0, 0)))
    acts = jax.nn.silu(conditions.astype(jnp.float32)).astype(jnp.bfloat16)
    acts = acts.reshape(CROPS, CHIPS, cores, share)
    acts = lax.dynamic_index_in_dim(acts, lax.axis_index("sp"), 2, keepdims=False)
    acts = jnp.pad(acts.transpose(1, 0, 2), ((0, 0), (0, 0), (0, 128 - share)))
    counts = jnp.pad(bin_counts.astype(jnp.bfloat16), (0, 128 - NBINS))
    counts = jnp.broadcast_to(counts, (CHIPS, 1, 128))
    acts = jnp.pad(jnp.concatenate([acts, counts], axis=1), ((0, 0), (0, 11), (0, 0)))
    ada = jnp.pad(ada_weight, ((0, 128 - share), (0, 0)))
    count = segments.shape[0]
    seg_col = jnp.broadcast_to(segments[:, None], (count, 128))
    seg_row = jnp.broadcast_to(segments[None, :], (8, count))
    bins = jnp.pad(noise_bins, (0, 4), constant_values=-1)
    bins = (bins[:, None] == jnp.arange(128, dtype=jnp.int32)).astype(jnp.float32)
    return shards, acts, ada, seg_col, seg_row, bins


def forward_plain(tokens_float, segments, conditions, noise_bins, bin_counts, ada_weight, first, up_weight,
                  down_weight):
    groups, cores = lax.axis_size("dp"), lax.axis_size("sp")
    share, width = first.shape[0], tokens_float.shape[1]
    index = lax.axis_index("dp") * cores + lax.axis_index("sp")
    mixers = lax.all_gather(first, ("dp", "sp"), axis=0, tiled=True)
    uppers = lax.all_gather(up_weight, ("dp", "sp"), axis=0, tiled=True)
    downers = lax.all_gather(down_weight, ("dp", "sp"), axis=0, tiled=True)
    mixers = mixers.reshape(width, 4, width).transpose(1, 0, 2)
    uppers = uppers.reshape(width, 4, width).transpose(1, 0, 2)
    downers = downers.reshape(4, width, width)
    bin_total = lax.psum(bin_counts, "dp")
    bin_weight = 40.0 * groups / bin_total.astype(jnp.float32)
    crop_weight = jnp.sum(
        jnp.where(noise_bins[:, None] == jnp.arange(NBINS, dtype=jnp.int32), bin_weight, 0.0),
        axis=-1,
    )
    cond_all = lax.all_gather(conditions, "dp", axis=0, tiled=True)
    cond_here = lax.dynamic_slice_in_dim(cond_all, index * share, share, axis=1)
    cond_act = jax.nn.silu(cond_here.astype(jnp.float32)).astype(jnp.bfloat16)
    modulation_part = dots("sd,df->sf", cond_act, ada_weight).reshape(groups, CROPS, -1)
    modulation = lax.psum(lax.psum_scatter(modulation_part, "dp", scatter_dimension=0), "sp")
    selector = (segments[:, None] == jnp.arange(CROPS, dtype=jnp.int32)).astype(jnp.float32)
    per_token = jnp.einsum("tc,cf->tf", selector, modulation, precision=lax.Precision.HIGHEST)
    shift_one, scale_one, gate_one, shift_two, scale_two, _ = jnp.split(per_token, 6, axis=-1)
    normed_one, _ = layer_norm(tokens_float)
    hidden_one = (normed_one * (1.0 + scale_one) + shift_one).astype(jnp.bfloat16)
    projected = dots("td,qdf->qtf", hidden_one, mixers[:3]).astype(jnp.bfloat16)
    sides = lax.all_gather(projected[1:], "sp", axis=1, tiled=True)
    all_segments = lax.all_gather(segments, "sp", axis=0, tiled=True)
    same_crop = segments[:, None] == all_segments[None, :]
    context, log_total = attend(projected[0], sides[0], sides[1], same_crop)
    context_low = context.astype(jnp.bfloat16)
    attended = dots("td,df->tf", context_low, mixers[3])
    middle = tokens_float + gate_one * attended
    normed_two, _ = layer_norm(middle)
    hidden_two = (normed_two * (1.0 + scale_two) + shift_two).astype(jnp.bfloat16)
    upper_in = dots("td,qdf->qtf", hidden_two, uppers)
    activated = jax.nn.gelu(upper_in, approximate=True).astype(jnp.bfloat16)
    slope = jax.vjp(partial(jax.nn.gelu, approximate=True), upper_in)[1](jnp.ones_like(upper_in))[0]
    mlp_out = dots("qtf,qfd->td", activated, downers)
    return (
        (mixers, uppers, downers), activated, slope, hidden_one, projected[0], sides, log_total,
        context_low, attended, middle, hidden_two, mlp_out, modulation, cond_act, crop_weight, same_crop,
    )


def on_device(
    chips,
    tokens_in,
    segment_ids,
    conditions,
    noise_bins,
    bin_counts,
    cotangent,
    ada_weight,
    qkv_weight,
    out_weight,
    up_weight,
    down_weight,
):
    tokens_float = tokens_in[0].astype(jnp.float32)
    segments = segment_ids[0]
    width = tokens_float.shape[1]
    share = qkv_weight.shape[0]
    kernels = chips and 4 * share == down_weight.shape[0]
    first = jnp.concatenate([qkv_weight, out_weight], axis=1)
    if kernels:
        shards, acts, ada, seg_col, seg_row, bins = kernel_inputs(
            segments, conditions[0], noise_bins[0], bin_counts[0], ada_weight, first, up_weight
        )
        (
            weights, down_part, slope, hidden_one, queries, sides, log_total, context_low, attended,
            middle, hidden_two, mlp_out, tokens_out, table, conds, level,
        ) = run_forward(
            shards, down_weight, acts, ada, tokens_in[0], cotangent[0], seg_col, seg_row, bins, share
        )
        mixers, uppers, downers = weights[0], weights[1], weights[2]
        modulation = jnp.concatenate([table[:CROPS], table[CROPS:]], axis=1)
        cond_act = conds[:, :CROPS, :share].reshape(-1, share)
        crop_weight = level[:CROPS, 0]
        log_total = log_total[:, :HEADS].T
        all_segments = lax.all_gather(segments, "sp", axis=0, tiled=True)
        same_crop = segments[:, None] == all_segments[None, :]
    else:
        (
            (mixers, uppers, downers), activated, slope, hidden_one, queries, sides, log_total,
            context_low, attended, middle, hidden_two, mlp_out, modulation, cond_act, crop_weight, same_crop,
        ) = forward_plain(
            tokens_float, segments, conditions[0], noise_bins[0], bin_counts[0], ada_weight, first,
            up_weight, down_weight,
        )
    selector = (segments[:, None] == jnp.arange(CROPS, dtype=jnp.int32)).astype(jnp.float32)
    per_token = jnp.einsum("tc,cf->tf", selector, modulation, precision=lax.Precision.HIGHEST)
    _, scale_one, gate_one, _, scale_two, gate_two = jnp.split(per_token, 6, axis=-1)
    normed_one, inverse_one = layer_norm(tokens_float)
    normed_two, inverse_two = layer_norm(middle)

    token_weight = jnp.sum(selector * crop_weight[None, :], axis=-1)
    grad_out = cotangent[0].astype(jnp.float32) * token_weight[:, None]
    grad_mlp = (grad_out * gate_two).astype(jnp.bfloat16)
    if not kernels:
        tokens_out = (middle + gate_two * mlp_out).astype(jnp.bfloat16)
        down_part = dots("qtf,td->qfd", activated, grad_mlp).astype(jnp.bfloat16)
    grad_act = dots("td,qfd->qtf", grad_mlp, downers)
    grad_upper = (grad_act * slope).astype(jnp.bfloat16)
    up_part = dots("td,qtf->qdf", hidden_two, grad_upper).astype(jnp.bfloat16)
    grad_hidden_two = dots("qtf,qdf->td", grad_upper, uppers)
    grad_middle = grad_out + norm_back(grad_hidden_two * (1.0 + scale_two), normed_two, inverse_two)
    grad_attended = (grad_middle * gate_one).astype(jnp.bfloat16)
    grad_context = dots("tf,df->td", grad_attended, mixers[3]).astype(jnp.bfloat16)
    grad_query, grad_key, grad_value = attend_back(
        queries, sides[0], sides[1], same_crop, log_total, grad_context
    )
    grad_sides = lax.psum_scatter(
        jnp.stack([grad_key, grad_value]).astype(jnp.bfloat16),
        "sp",
        scatter_dimension=1,
        tiled=True,
    )
    grad_projected = jnp.concatenate([grad_query.astype(jnp.bfloat16)[None], grad_sides])
    out_part = dots("td,tf->df", context_low, grad_attended).astype(jnp.bfloat16)
    qkv_part = dots("td,qtf->qdf", hidden_one, grad_projected).astype(jnp.bfloat16)
    first_part = jnp.concatenate([qkv_part, out_part[None]])
    grad_hidden_one = dots("qtf,qdf->td", grad_projected, mixers[:3])
    tokens_grad = grad_middle + norm_back(
        grad_hidden_one * (1.0 + scale_one), normed_one, inverse_one
    )

    if kernels:
        pieces = (32, 4 * share, width)
        rows, down_grad = scatter_grads(
            first_part.reshape(pieces), up_part.reshape(pieces), down_part.reshape(pieces), share
        )
        rows = rows[:, :, :share].astype(jnp.float32).transpose(0, 2, 1, 3).reshape(2, share, 4 * width)
        first_grad, up_grad = rows[0], rows[1]
    else:
        joined = jnp.stack([first_part, up_part]).transpose(2, 0, 1, 3).reshape(width, 8 * width)
        rows = lax.psum_scatter(joined, ("dp", "sp"), scatter_dimension=0, tiled=True)
        rows = rows.astype(jnp.float32)
        first_grad, up_grad = rows[:, : 4 * width], rows[:, 4 * width :]
        down_grad = lax.psum_scatter(
            down_part.reshape(4 * width, width), ("dp", "sp"), scatter_dimension=0, tiled=True
        ).astype(jnp.float32)

    grad_per_token = jnp.concatenate(
        [
            grad_hidden_one,
            grad_hidden_one * normed_one,
            grad_middle * attended,
            grad_hidden_two,
            grad_hidden_two * normed_two,
            grad_out * mlp_out,
        ],
        axis=-1,
    )
    grad_modulation = lax.psum(
        jnp.einsum("tc,tf->cf", selector, grad_per_token, precision=lax.Precision.HIGHEST), "sp"
    )
    grad_rows = lax.all_gather(grad_modulation, "dp", axis=0, tiled=True)
    ada_grad = jnp.einsum(
        "sd,sf->df", cond_act.astype(jnp.float32), grad_rows, precision=lax.Precision.HIGHEST
    )
    silu_part = jnp.einsum(
        "sf,df->sd", grad_rows, ada_weight.astype(jnp.float32), precision=lax.Precision.HIGHEST
    )
    silu_all = lax.all_gather(silu_part, ("dp", "sp"), axis=0)
    silu_here = lax.dynamic_slice_in_dim(silu_all, lax.axis_index("dp") * CROPS, CROPS, axis=1)
    grad_silu = silu_here.transpose(1, 0, 2).reshape(CROPS, width)
    silu_pull = jax.vjp(jax.nn.silu, conditions[0].astype(jnp.float32))[1]
    cond_grad = silu_pull(grad_silu)[0]
    return (
        tokens_out[None],
        tokens_grad[None],
        cond_grad[None],
        ada_grad,
        first_grad[:, : 3 * width],
        first_grad[:, 3 * width :],
        up_grad,
        down_grad,
    )


def solution(mesh):
    placed = (
        P("dp", "sp", None),
        P("dp", "sp"),
        P("dp", None, None),
        P("dp", None),
        P("dp", None),
        P("dp", "sp", None),
        P(("dp", "sp"), None),
        P(("dp", "sp"), None),
        P(("dp", "sp"), None),
        P(("dp", "sp"), None),
        P(("dp", "sp"), None),
    )
    return jax.shard_map(
        partial(on_device, mesh.shape["dp"] == 16 and mesh.shape["sp"] == 2),
        mesh=mesh,
        in_specs=placed,
        out_specs=(
            P("dp", "sp", None),
            P("dp", "sp", None),
            P("dp", None, None),
            P(("dp", "sp"), None),
            P(("dp", "sp"), None),
            P(("dp", "sp"), None),
            P(("dp", "sp"), None),
            P(("dp", "sp"), None),
        ),
        check_vma=False,
    )
```

```python
from functools import partial
import math

import jax
import jax.numpy as jnp
from jax import lax
from jax.experimental import pallas as pl
from jax.experimental.pallas import tpu as pltpu
from jax.sharding import PartitionSpec as P

HEADS = 16
CROPS = 4
NBINS = 8
EPSILON = 1e-06
LARGE_NEGATIVE = -1e30
GELU_SCALE = math.sqrt(2.0 / math.pi)
GELU_CUBE = 0.044715

MESH = pl.DeviceIdType.MESH
PAD = 48
CUT = 80
CHIPS = 16
BAND = 1792
PLACES = ((0, 0), (0, 1), (1, 0), (1, 1))


def position():
    d = lax.axis_index("dp")
    c = lax.axis_index("sp")
    return d // 4, (d // 2) % 2, d % 2, c


def device(z, y, x, c):
    return (z * 4 + y * 2 + x, c)


def block_of(kind, zy, group):
    if kind == 2:
        return zy // 2, (zy % 2) * 4 + group
    return group, zy


def greet(peers):
    barrier = pltpu.get_barrier_semaphore()
    for peer in peers:
        pl.semaphore_signal(barrier, inc=1, device_id=peer, device_id_type=MESH)
    pl.semaphore_wait(barrier, len(peers))


def remote(src, dst, send, recv, target):
    return pltpu.make_async_remote_copy(
        src_ref=src,
        dst_ref=dst,
        send_sem=send,
        recv_sem=recv,
        device_id=target,
        device_id_type=MESH,
    )


def arrive(ref, sem, target):
    remote(ref, ref, sem, sem, target).wait_recv()


def row_selector(rows, share):
    shape = (rows, 4 * PAD)
    row = lax.broadcasted_iota(jnp.int32, shape, 0)
    column = lax.broadcasted_iota(jnp.int32, shape, 1)
    picked = jnp.zeros(shape, jnp.bool_)
    for k in range(4):
        inside = (row >= k * share) & (row < (k + 1) * share)
        picked = picked | (inside & (column == row - k * share + k * PAD))
    return picked.astype(jnp.float32).astype(jnp.bfloat16)


def product(left, right):
    return jnp.dot(left, right, preferred_element_type=jnp.float32)


def product_by_rows(left, right):
    return lax.dot_general(left, right, (((0,), (0,)), ((), ())), preferred_element_type=jnp.float32)


def product_by_columns(left, right):
    return lax.dot_general(left, right, (((1,), (1,)), ((), ())), preferred_element_type=jnp.float32)


def chunks(rows, body, step=16):
    def run(i, carry):
        body(pl.ds(pl.multiple_of(i * step, step), step))
        return carry

    lax.fori_loop(0, rows // step, run, 0)


def normed(values):
    center = values - jnp.mean(values, axis=-1, keepdims=True)
    inverse = lax.rsqrt(jnp.mean(center * center, axis=-1, keepdims=True) + EPSILON)
    return center * inverse, inverse


def pick(segments, table, first, column, width):
    columns = slice(column * width, (column + 1) * width)
    value = table[first + 3 : first + 4, columns]
    for crop in (2, 1, 0):
        value = jnp.where(segments == crop, table[first + crop : first + crop + 1, columns], value)
    return value


def window_of(head, size, width):
    start = jnp.minimum((head * size) // 128, width // 128 - 2) * 128
    start = pl.multiple_of(start, 128)
    lane = lax.broadcasted_iota(jnp.int32, (1, 256), 1) + start
    return pl.ds(start, 256), (lane >= head * size) & (lane < (head + 1) * size)


def forward_kernel(share, shards_ref, down_ref, act_ref, ada_ref, tokens_ref, cot_ref, seg_col_ref,
                   seg_row_ref, bins_ref,
                   weights_ref, down_part_ref, slope_ref, hidden_ref, query_ref, sides_ref, total_ref,
                   context_ref, attended_ref, middle_ref, hidden_two_ref, mlp_ref, out_ref, table_ref,
                   conds_ref, level_ref, grad_mlp, seg_all,
                   full, stage, part, part_recv, band, band_diag, band_x, band_y, band_z, halves_of,
                   bias, work, active, slope, *sems):
    (
        group_send, group_recv, z_send, z_recv, x_send, x_recv, y_send, y_recv,
        dx_send, dx_recv, dy_send, dy_recv, c_send, c_recv,
        cond_send, cond_recv, pc_send, pc_recv, pd_send, pd_recv, px_send, px_recv, py_send, py_recv,
        pz_send, pz_recv, pm_send, pm_recv, seg_send, seg_recv, kv_send, kv_recv,
        save_sem, grad_sem, slope_sem,
    ) = sems
    z, y, x, c = position()
    me = z * 4 + y * 2 + x
    group = x * 2 + c
    zy = z * 2 + y
    rows = 4 * share
    count, width = tokens_ref.shape
    halves = (pl.ds(0, CUT), pl.ds(CUT, rows - CUT))
    x_peer, y_peer, c_peer = device(z, y, 1 - x, c), device(z, 1 - y, x, c), device(z, y, x, 1 - c)
    partners = [(x, 1 - c), (1 - x, c), (1 - x, 1 - c)]
    greet(
        [((me + k) % CHIPS, c) for k in range(1, CHIPS)] + [c_peer, device(z, y, 1 - x, 1 - c)]
    )
    sends = {a: [] for a in (0, 1, 2, "other")}

    def send(a, *args):
        copy = remote(*args)
        copy.start()
        sends[a].append(copy)

    def finish_sends(a):
        for copy in sends[a]:
            copy.wait_send()
        sends[a] = []

    def place(a, k, other_y, other_x, core=None):
        zz = (z - k + 4) % 4
        yy = 1 - y if other_y else y
        xx = 1 - x if other_x else x
        cc = c if core is None else core
        block, row = block_of(a, zz * 2 + yy, xx * 2 + cc)
        return full.at[a, block, pl.ds(pl.multiple_of(row * rows, 16), rows)]

    def half(a, k, other_y, other_x, h):
        zz = (z - k + 4) % 4
        yy = 1 - y if other_y else y
        xx = 1 - x if other_x else x
        block, row = block_of(a, zz * 2 + yy, xx * 2 + c)
        start = row * rows + (CUT if h else 0)
        return full.at[a, block, pl.ds(pl.multiple_of(start, 16), rows - CUT if h else CUT)]

    for a in range(2):
        for j, (px, pc) in enumerate(partners):
            send(
                "other",
                shards_ref.at[a, px * 2 + pc],
                stage.at[a, pl.ds(pl.multiple_of(group * PAD, 16), PAD)],
                group_send.at[a, j],
                group_recv.at[a, j],
                device(z, y, px, pc),
            )
    for k in range(1, CHIPS):
        to = (me + k) % CHIPS
        send("other", act_ref.at[to], conds_ref.at[me], cond_send.at[k - 1], cond_recv.at[k - 1], (to, c))
    seg_all[c] = seg_row_ref[...]
    send("other", seg_row_ref, seg_all.at[c], seg_send, seg_recv, c_peer)
    conds_ref[me] = act_ref[me]
    for a in range(2):
        stage[a, pl.ds(pl.multiple_of(group * PAD, 16), PAD), :] = shards_ref[a, group]

    def own(a):
        block, row = block_of(a, zy, group)
        here = pl.ds(pl.multiple_of(row * rows, 16), rows)
        if a < 2:
            for j, (px, pc) in enumerate(partners):
                arrive(
                    stage.at[a, pl.ds(pl.multiple_of((px * 2 + pc) * PAD, 16), PAD)],
                    group_recv.at[a, j],
                    device(z, y, px, pc),
                )
            full[a, block, here, :] = product(row_selector(rows, share), stage[a]).astype(jnp.bfloat16)
        else:
            full[a, block, here, :] = down_ref[...]
        mine = place(a, 0, 0, 0)
        for k in (1, 2, 3):
            send(a, mine, mine, z_send.at[a, k - 1], z_recv.at[a, k - 1], device((z + k) % 4, y, x, c))

    def to_core(a, k, pos):
        piece = place(a, k, *PLACES[pos])
        send(a, piece, piece, c_send.at[a, k, pos], c_recv.at[a, k, pos], c_peer)

    def spread(a, k):
        if k:
            arrive(place(a, k, 0, 0), z_recv.at[a, k - 1], device((z - k + 4) % 4, y, x, c))
        for h in (0, 1):
            one, two = half(a, k, 0, 0, h), half(a, k, 0, 0, 1 - h)
            send(a, one, one, x_send.at[a, k, h], x_recv.at[a, k, h], x_peer)
            send(a, two, two, y_send.at[a, k, 1 - h], y_recv.at[a, k, 1 - h], y_peer)
        to_core(a, k, 0)

    def forward(a, k):
        top, low = half(a, k, 0, 1, 0), half(a, k, 1, 0, 1)
        arrive(top, x_recv.at[a, k, 0], x_peer)
        send(a, top, top, dy_send.at[a, k], dy_recv.at[a, k], y_peer)
        arrive(low, y_recv.at[a, k, 1], y_peer)
        send(a, low, low, dx_send.at[a, k], dx_recv.at[a, k], x_peer)
        arrive(half(a, k, 0, 1, 1), x_recv.at[a, k, 1], x_peer)
        to_core(a, k, 1)
        arrive(half(a, k, 1, 0, 0), y_recv.at[a, k, 0], y_peer)
        to_core(a, k, 2)

    def finish(a, k):
        arrive(half(a, k, 1, 1, 0), dy_recv.at[a, k], y_peer)
        arrive(half(a, k, 1, 1, 1), dx_recv.at[a, k], x_peer)
        to_core(a, k, 3)

    saves = []

    def complete(a):
        for k in range(4):
            for pos, (oy, ox) in enumerate(PLACES):
                arrive(place(a, k, oy, ox, 1 - c), c_recv.at[a, k, pos], c_peer)
        copy = pltpu.make_async_copy(full.at[a], weights_ref.at[a], save_sem.at[a])
        copy.start()
        saves.append(copy)

    def mod_start():
        for k in range(1, CHIPS):
            source = (me - k + CHIPS) % CHIPS
            arrive(conds_ref.at[source], cond_recv.at[k - 1], (source, c))
        acts = conds_ref[:, :8, :].astype(jnp.float32).reshape(CHIPS * 8, 128)
        row = lax.broadcasted_iota(jnp.int32, acts.shape, 0) % 8
        upper = jnp.where(row < CROPS, acts, 0.0).astype(jnp.bfloat16)
        lower = pltpu.roll(jnp.where(row < CROPS, acts, 0.0), CROPS, 0).astype(jnp.bfloat16)
        side = ada_ref.shape[1] // 2
        part[...] = product(upper, ada_ref[:, :side]) + product(lower, ada_ref[:, side:])
        far = pl.ds(pl.multiple_of((1 - c) * (side - BAND), 128), BAND)
        send("other", part.at[:, far], part_recv, pc_send, pc_recv, c_peer)

    def block8(zz, yy, xx):
        return pl.ds(pl.multiple_of((zz * 4 + yy * 2 + xx) * 8, 8), 8)

    def mod_cores():
        arrive(part_recv, pc_recv, c_peer)
        side = ada_ref.shape[1] // 2
        near = pl.ds(pl.multiple_of(c * (side - BAND), 128), BAND)
        band[...] = part[:, near] + part_recv[...]
        for k in range(4):
            zz = (z + k) % 4
            src = band.at[block8(zz, 1 - y, 1 - x)]
            send("other", src, band_diag.at[k], pd_send.at[k], pd_recv.at[k], x_peer if k % 2 else y_peer)

    def mod_plane():
        for k in range(4):
            zz = (z + k) % 4
            to_x, to_y = block8(zz, y, 1 - x), block8(zz, 1 - y, x)
            arrive(band_diag.at[k], pd_recv.at[k], x_peer if k % 2 else y_peer)
            fold = to_y if k % 2 else to_x
            band[fold, :] = band[fold, :] + band_diag[k]
            send("other", band.at[to_x], band_x.at[k], px_send.at[k], px_recv.at[k], x_peer)
            send("other", band.at[to_y], band_y.at[k], py_send.at[k], py_recv.at[k], y_peer)

    def mod_line():
        for k in (1, 2, 3, 0):
            zz = (z + k) % 4
            mine = block8(zz, y, x)
            arrive(band_x.at[k], px_recv.at[k], x_peer)
            arrive(band_y.at[k], py_recv.at[k], y_peer)
            band[mine, :] = band[mine, :] + band_x[k] + band_y[k]
            if k:
                send("other", band.at[mine], band_z.at[k - 1], pz_send.at[k - 1], pz_recv.at[k - 1], device(zz, y, x, c))

    def mod_last():
        for k in (1, 2, 3):
            arrive(band_z.at[k - 1], pz_recv.at[k - 1], device((z - k + 4) % 4, y, x, c))
        halves_of[c] = band[block8(z, y, x), :] + band_z[0] + band_z[1] + band_z[2]
        send("other", halves_of.at[c], halves_of.at[c], pm_send, pm_recv, c_peer)

    def mod_end():
        arrive(halves_of.at[1 - c], pm_recv, c_peer)
        side = ada_ref.shape[1] // 2
        table_ref[:, :BAND] = halves_of[0]
        table_ref[:, BAND:] = halves_of[1][:, 2 * BAND - side :]
        counts = jnp.sum(conds_ref[:, :, :].astype(jnp.float32)[:, CROPS : CROPS + 1, :], axis=0)
        lane = lax.broadcasted_iota(jnp.int32, counts.shape, 1)
        weight = jnp.where(lane < NBINS, 40.0 * CHIPS / jnp.where(lane < NBINS, counts, 1.0), 0.0)
        level_ref[...] = jnp.broadcast_to(
            jnp.sum(bins_ref[...] * weight, axis=-1, keepdims=True), level_ref.shape
        )

    def first_norm():
        def body(at):
            segments = seg_col_ref[at, :1]
            value, _ = normed(tokens_ref[at, :].astype(jnp.float32))
            value = value * (1.0 + pick(segments, table_ref, 0, 1, width))
            hidden_ref[at, :] = (value + pick(segments, table_ref, 0, 0, width)).astype(jnp.bfloat16)

        chunks(count, body)
        arrive(seg_all.at[1 - c], seg_recv, c_peer)
        for h in (0, 1):
            same = seg_col_ref[:, :1] == seg_all[h][:1, :]
            bias[:, h * count : (h + 1) * count] = jnp.where(same, 0.0, LARGE_NEGATIVE)

    def project():
        here = pl.ds(pl.multiple_of(c * count, 256), count)
        for q in (1, 2):
            sides_ref[q - 1, here, :] = product(hidden_ref[...], full[0, q]).astype(jnp.bfloat16)
            send("other", sides_ref.at[q - 1, here], sides_ref.at[q - 1, here], kv_send.at[q - 1], kv_recv.at[q - 1], c_peer)
        query_ref[...] = product(hidden_ref[...], full[0, 0]).astype(jnp.bfloat16)
        total_ref[...] = jnp.zeros_like(total_ref)
        work[...] = jnp.zeros_like(work)

    def attend(first, last):
        if first == 0:
            there = pl.ds(pl.multiple_of((1 - c) * count, 256), count)
            for q in (0, 1):
                arrive(sides_ref.at[q, there], kv_recv.at[q], c_peer)
        size = width // HEADS
        scale = 1.0 / math.sqrt(size)

        def body(head, carry):
            columns, inside = window_of(head, size, width)
            query = query_ref[:, columns]
            query = jnp.where(inside, query, jnp.zeros_like(query))
            scores = product_by_columns(query, sides_ref[0, :, columns]) * scale + bias[...]
            top = jnp.max(scores, axis=-1, keepdims=True)
            raised = jnp.exp(scores - top)
            total = jnp.sum(raised, axis=-1, keepdims=True)
            chance = (raised * (1.0 / total)).astype(jnp.bfloat16)
            context = product(chance, sides_ref[1, :, columns])
            work[:, columns] = jnp.where(inside, context, work[:, columns])
            lane = lax.broadcasted_iota(jnp.int32, (1, 128), 1)
            total_ref[...] = jnp.where(lane == head, top + jnp.log(total), total_ref[...])
            return carry

        lax.fori_loop(first, last, body, 0)

    def mix():
        context_ref[...] = work[...].astype(jnp.bfloat16)
        attended_ref[...] = product(context_ref[...], full[0, 3])

        def body(at):
            segments = seg_col_ref[at, :1]
            gate = pick(segments, table_ref, 0, 2, width)
            middle = tokens_ref[at, :].astype(jnp.float32) + gate * attended_ref[at, :]
            middle_ref[at, :] = middle
            value, _ = normed(middle)
            value = value * (1.0 + pick(segments, table_ref, 4, 1, width))
            hidden_two_ref[at, :] = (value + pick(segments, table_ref, 4, 0, width)).astype(jnp.bfloat16)
            level = level_ref[3:4, :1]
            for crop in (2, 1, 0):
                level = jnp.where(segments == crop, level_ref[crop : crop + 1, :1], level)
            grad = cot_ref[at, :].astype(jnp.float32) * level
            grad_mlp[at, :] = (grad * pick(segments, table_ref, 4, 2, width)).astype(jnp.bfloat16)

        chunks(count, body)

    slope_copies = {}

    def expand(q):
        work[...] = product(hidden_two_ref[...], full[1, q])
        if q >= 2:
            slope_copies[q - 2].wait()

        def body(at):
            u = work[at, :]
            square = u * u
            bend = jnp.tanh(GELU_SCALE * (u + GELU_CUBE * (square * u)))
            active[q, at, :] = (0.5 * u * (1.0 + bend)).astype(jnp.bfloat16)
            inner = GELU_SCALE * (1.0 + 3.0 * GELU_CUBE * square)
            slope[q % 2, at, :] = 0.5 * (1.0 + bend) + 0.5 * u * (1.0 - bend * bend) * inner

        chunks(count, body)
        copy = pltpu.make_async_copy(slope.at[q % 2], slope_ref.at[q], slope_sem.at[q % 2])
        copy.start()
        slope_copies[q] = copy

    def down_grad(q):
        if q == 0:
            finish_sends(0)
            saves[0].wait()
        full[0, q] = product_by_rows(active[q], grad_mlp[...]).astype(jnp.bfloat16)
        copy = pltpu.make_async_copy(full.at[0, q], down_part_ref.at[q], grad_sem.at[q])
        copy.start()
        saves.append(copy)

    def contract():
        work[...] = product(active[0], full[2, 0])
        for q in (1, 2, 3):
            work[...] += product(active[q], full[2, q])

        def body(at):
            mlp = work[at, :]
            mlp_ref[at, :] = mlp
            gate = pick(seg_col_ref[at, :1], table_ref, 4, 2, width)
            out_ref[at, :] = (middle_ref[at, :] + gate * mlp).astype(jnp.bfloat16)

        chunks(count, body)

    extra = {
        1: [mod_start],
        2: [mod_cores],
        3: [mod_plane],
        4: [mod_line],
        5: [mod_last],
        6: [mod_end, first_norm, partial(complete, 0), project],
        7: [partial(attend, 0, 8)],
        8: [partial(attend, 8, 16)],
        9: [mix],
        10: [partial(complete, 1), partial(expand, 0), partial(expand, 1)],
        11: [partial(expand, 2), partial(expand, 3)],
        12: [partial(down_grad, 0), partial(down_grad, 1)],
        13: [partial(down_grad, 2), partial(down_grad, 3)],
        14: [partial(complete, 2), contract],
    }
    order = [(a, k) for a in range(3) for k in range(4)]
    own(0)
    for i in range(len(order) + 3):
        if i < len(order):
            a, k = order[i]
            if k == 1 and a < 2:
                own(a + 1)
            spread(a, k)
        if 2 <= i < len(order) + 2:
            forward(*order[i - 2])
        if 3 <= i:
            finish(*order[i - 3])
        for step in extra.get(i, ()):
            step()
    for copy in saves[1:]:
        copy.wait()
    for q in (2, 3):
        slope_copies[q].wait()
    for a in (1, 2, "other"):
        finish_sends(a)


def run_forward(shards, down, acts, ada, tokens, cot, seg_col, seg_row, bins, share):
    count, width = tokens.shape
    dma = pltpu.SemaphoreType.DMA
    low, wide = jnp.bfloat16, jnp.float32
    side = ada.shape[1] // 2
    vmem, any_ = pl.BlockSpec(memory_space=pltpu.VMEM), pl.BlockSpec(memory_space=pl.ANY)
    out = jax.ShapeDtypeStruct
    return pl.pallas_call(
        partial(forward_kernel, share),
        out_shape=(
            out((3, 4, width, width), low),
            out((4, width, width), low),
            out((4, count, width), wide),
            out((count, width), low),
            out((count, width), low),
            out((2, 2 * count, width), low),
            out((count, 128), wide),
            out((count, width), low),
            out((count, width), wide),
            out((count, width), wide),
            out((count, width), low),
            out((count, width), wide),
            out((count, width), low),
            out((8, side), wide),
            out((CHIPS, 16, 128), low),
            out((8, 128), wide),
            out((count, width), low),
            out((2, 8, count), jnp.int32),
        ),
        in_specs=[vmem] * 9,
        out_specs=[any_] * 3 + [vmem] * 15,
        scratch_shapes=[
            pltpu.VMEM((3, 4, width, width), low),
            pltpu.VMEM((2, 4 * PAD, width), low),
            pltpu.VMEM((CHIPS * 8, side), wide),
            pltpu.VMEM((CHIPS * 8, BAND), wide),
            pltpu.VMEM((CHIPS * 8, BAND), wide),
            pltpu.VMEM((4, 8, BAND), wide),
            pltpu.VMEM((4, 8, BAND), wide),
            pltpu.VMEM((4, 8, BAND), wide),
            pltpu.VMEM((3, 8, BAND), wide),
            pltpu.VMEM((2, 8, BAND), wide),
            pltpu.VMEM((count, 2 * count), wide),
            pltpu.VMEM((count, width), wide),
            pltpu.VMEM((4, count, width), low),
            pltpu.VMEM((2, count, width), wide),
            dma((2, 3)), dma((2, 3)), dma((3, 3)), dma((3, 3)),
            dma((3, 4, 2)), dma((3, 4, 2)), dma((3, 4, 2)), dma((3, 4, 2)),
            dma((3, 4)), dma((3, 4)), dma((3, 4)), dma((3, 4)),
            dma((3, 4, 4)), dma((3, 4, 4)),
            dma((CHIPS - 1,)), dma((CHIPS - 1,)), dma, dma, dma((4,)), dma((4,)),
            dma((4,)), dma((4,)), dma((4,)), dma((4,)), dma((3,)), dma((3,)), dma, dma, dma, dma,
            dma((2,)), dma((2,)), dma((3,)), dma((4,)), dma((2,)),
        ],
        compiler_params=pltpu.CompilerParams(
            collective_id=0, has_side_effects=True, vmem_limit_bytes=63 * 2**20
        ),
        name="forward",
    )(shards, down, acts, ada, tokens, cot, seg_col, seg_row, bins)


def add_rows(dst, sources, start, rows):
    def body(i, carry):
        where = pl.ds(pl.multiple_of(start + i * 16, 16), 16)
        total = dst[where, :].astype(jnp.float32)
        for source in sources:
            total = total + source[where, :].astype(jnp.float32)
        dst[where, :] = total.astype(dst.dtype)
        return carry

    lax.fori_loop(0, rows // 16, body, 0)


def split_low(values):
    high = values.astype(jnp.bfloat16)
    return high, (values - high.astype(jnp.float32)).astype(jnp.bfloat16)


def backward_kernel(share, weights_ref, down_part_ref, slope_ref, middle_ref, attended_ref, mlp_ref,
                    hidden_ref, query_ref, sides_ref, total_ref, context_ref, hidden_two_ref,
                    grad_mlp_ref, table_ref, conds_ref, level_ref, seg_all_ref, seg_col_ref, tokens_ref,
                    cot_ref, ada_ref,
                    mixer_part_ref, up_part_ref, rows_ref, down_ref, tokens_grad_ref, ada_grad_ref, silu_ref,
                    held, from_core, diag, from_x, from_y, from_z, spare, block, part, quad, lows,
                    work, grad_middle, grad_context, leave, enter, bias, sums, sums_row, sums_core, band, silu_part,
                    *sems):
    (
        load_sem, c_send, c_recv, dx_send, dx_recv, dy_send, dy_recv, x_send, x_recv,
        y_send, y_recv, z_send, z_recv, group_send, group_recv, block_sem, part_sem, quad_sem,
        side_send, side_recv, m_send, m_recv, mz_send, mz_recv, mx_send, mx_recv, my_send, my_recv,
        md_send, md_recv, mc_send, mc_recv, s_send, s_recv, sc_send, sc_recv,
    ) = sems
    z, y, x, c = position()
    me = z * 4 + y * 2 + x
    group = x * 2 + c
    rows = 4 * share
    count, width = tokens_ref.shape
    halves = (pl.ds(0, CUT), pl.ds(CUT, rows - CUT))
    x_peer, y_peer, c_peer = device(z, y, 1 - x, c), device(z, 1 - y, x, c), device(z, y, x, 1 - c)
    partners = [(x, 1 - c), (1 - x, c), (1 - x, 1 - c)]
    greet(
        [((me + k) % CHIPS, c) for k in range(1, CHIPS)] + [c_peer, device(z, y, 1 - x, 1 - c)]
    )
    sends = {}

    def send(owner, *args):
        copy = remote(*args)
        copy.start()
        sends.setdefault(owner, []).append(copy)

    def finish_sends(owner):
        for copy in sends.pop(owner, []):
            copy.wait_send()

    order = [(a, k) for a in (2, 1, 0) for k in (1, 2, 3, 0)]
    given = (mixer_part_ref, up_part_ref, down_part_ref)
    loads = {}

    def begin(i):
        a, k = order[i]
        finish_sends(("held", i - 5))
        zz = (z + k) % 4
        for pos, (oy, ox) in enumerate(PLACES):
            yy = 1 - y if oy else y
            xx = 1 - x if ox else x
            for core in (0, 1):
                cc = 1 - c if core else c
                where, row = block_of(a, zz * 2 + yy, xx * 2 + cc)
                src = given[a].at[where, pl.ds(pl.multiple_of(row * rows, 16), rows)]
                if core:
                    send("core", src, from_core.at[i % 4, pos], c_send.at[i, pos], c_recv.at[i, pos], c_peer)
                else:
                    loads[i, pos] = pltpu.make_async_copy(src, held.at[i % 5, pos], load_sem.at[i, pos])
                    loads[i, pos].start()

    def pair(i):
        for pos in (3, 1, 2, 0):
            loads[i, pos].wait()
            arrive(from_core.at[i % 4, pos], c_recv.at[i, pos], c_peer)
            add_rows(held.at[i % 5, pos], [from_core.at[i % 4, pos]], 0, rows)
            mine = held.at[i % 5, pos]
            top, low = mine.at[halves[0]], mine.at[halves[1]]
            if pos == 3:
                send(("held", i), top, diag.at[i % 4, halves[0]], dy_send.at[i], dy_recv.at[i], y_peer)
                send(("held", i), low, diag.at[i % 4, halves[1]], dx_send.at[i], dx_recv.at[i], x_peer)
            if pos == 1:
                send(("held", i), low, from_x.at[i % 5, halves[1]], x_send.at[i, 1], x_recv.at[i, 1], x_peer)
            if pos == 2:
                send(("held", i), top, from_y.at[i % 5, halves[0]], y_send.at[i, 0], y_recv.at[i, 0], y_peer)

    def relay(i):
        far = diag.at[i % 4]
        arrive(far.at[halves[0]], dy_recv.at[i], y_peer)
        add_rows(held.at[i % 5, 1], [far], 0, CUT)
        top = held.at[i % 5, 1, halves[0]]
        send(("held", i), top, from_x.at[i % 5, halves[0]], x_send.at[i, 0], x_recv.at[i, 0], x_peer)
        arrive(far.at[halves[1]], dx_recv.at[i], x_peer)
        add_rows(held.at[i % 5, 2], [far], CUT, rows - CUT)
        low = held.at[i % 5, 2, halves[1]]
        send(("held", i), low, from_y.at[i % 5, halves[1]], y_send.at[i, 1], y_recv.at[i, 1], y_peer)

    def plane(i):
        a, k = order[i]
        for h in (0, 1):
            arrive(from_x.at[i % 5, halves[h]], x_recv.at[i, h], x_peer)
            arrive(from_y.at[i % 5, halves[h]], y_recv.at[i, h], y_peer)
        mine = held.at[i % 5, 0]
        if k:
            add_rows(mine, [from_x.at[i % 5], from_y.at[i % 5]], 0, rows)
            send(("held", i), mine, from_z.at[a, k - 1], z_send.at[a, k - 1], z_recv.at[a, k - 1], device((z + k) % 4, y, x, c))
            return
        for j in (1, 2, 3):
            arrive(from_z.at[a, j - 1], z_recv.at[a, j - 1], device((z - j + 4) % 4, y, x, c))

        def body(at):
            total = mine[at, :].astype(jnp.float32)
            total = total + from_x[i % 5, at, :].astype(jnp.float32)
            total = total + from_y[i % 5, at, :].astype(jnp.float32)
            for j in range(3):
                total = total + from_z[a, j, at, :].astype(jnp.float32)
            if a == 2:
                down_ref[at, :] = total
            else:
                mine[at, :] = total.astype(jnp.bfloat16)

        chunks(rows, body)
        if a == 2:
            return
        spare[a] = product_by_rows(row_selector(rows, share), mine[...]).astype(jnp.bfloat16)
        for j, (px, pc) in enumerate(partners):
            send(
                "end",
                spare.at[a, pl.ds(pl.multiple_of((px * 2 + pc) * PAD, 16), PAD)],
                rows_ref.at[a, group],
                group_send.at[a, j],
                group_recv.at[a, j],
                device(z, y, px, pc),
            )
        rows_ref[a, group] = spare[a, pl.ds(pl.multiple_of(group * PAD, 16), PAD), :]

    uses = [(2, q) for q in range(4)] + [(1, q) for q in range(4)] + [(0, 3), (0, 0), (0, 1), (0, 2)]
    coming = {}

    def fetch(n):
        if n < len(uses):
            copy = pltpu.make_async_copy(weights_ref.at[uses[n]], block.at[n % 2], block_sem.at[n % 2])
            copy.start()
            coming[n] = copy

    def take(n):
        coming[n].wait()
        return block[n % 2]

    going = {}

    def put(n, left, right, target):
        if n - 2 in going:
            going.pop(n - 2).wait()

        def body(i, carry):
            columns = pl.ds(pl.multiple_of(i * 384, 128), 384)
            part[n % 2, columns, :] = product_by_rows(left[:, columns], right[...]).astype(jnp.bfloat16)
            return carry

        lax.fori_loop(0, width // 384, body, 0)
        going[n] = pltpu.make_async_copy(part.at[n % 2], target, part_sem.at[n % 2])
        going[n].start()

    quads = {}

    def slopes(q):
        quads[q] = pltpu.make_async_copy(slope_ref.at[q], quad.at[q], quad_sem.at[q])
        quads[q].start()

    def through_down(q):
        work[...] = product_by_columns(grad_mlp_ref[...], take(q))
        fetch(q + 2)
        quads[q].wait()

        def body(at):
            lows[q, at, :] = (work[at, :] * quad[q, at, :]).astype(jnp.bfloat16)

        chunks(count, body)
        if q < 3:
            source = (middle_ref, attended_ref, mlp_ref)[q]
            quads[q] = pltpu.make_async_copy(source, quad.at[q], quad_sem.at[q])
            quads[q].start()

    def up_grad(q):
        put(q, hidden_two_ref, lows.at[q], up_part_ref.at[q])

    def through_up(q):
        value = product_by_columns(lows[q], take(4 + q))
        work[...] = work[...] + value if q else value
        fetch(6 + q)

    def norm_pull(grad, value, inverse):
        return inverse * (
            grad
            - jnp.mean(grad, axis=-1, keepdims=True)
            - value * jnp.mean(grad * value, axis=-1, keepdims=True)
        )

    def add_sums(segments, which, value):
        for crop in range(CROPS):
            kept = jnp.where(segments == crop, value, 0.0)
            sums[which, crop] = sums[which, crop] + kept[:8] + kept[8:]

    def second_norm():
        for q in range(3):
            quads[q].wait()
        sums[...] = jnp.zeros_like(sums)

        def body(at):
            segments = seg_col_ref[at, :1]
            grad = work[at, :]
            value, inverse = normed(quad[0, at, :])
            level = level_ref[3:4, :1]
            for crop in (2, 1, 0):
                level = jnp.where(segments == crop, level_ref[crop : crop + 1, :1], level)
            grad_out = cot_ref[at, :].astype(jnp.float32) * level
            add_sums(segments, 3, grad)
            add_sums(segments, 4, grad * value)
            add_sums(segments, 5, grad_out * quad[2, at, :])
            scaled = grad * (1.0 + pick(segments, table_ref, 4, 1, width))
            total = grad_out + norm_pull(scaled, value, inverse)
            grad_middle[at, :] = total
            add_sums(segments, 2, total * quad[1, at, :])
            lows[3, at, :] = (total * pick(segments, table_ref, 0, 2, width)).astype(jnp.bfloat16)

        chunks(count, body)

    def through_out():
        grad_context[...] = product_by_columns(lows[3], take(8)).astype(jnp.bfloat16)
        fetch(10)
        put(4, context_ref, lows.at[3], mixer_part_ref.at[3])
        for h in (0, 1):
            same = seg_col_ref[:, :1] == seg_all_ref[h][:1, :]
            bias[:, h * count : (h + 1) * count] = jnp.where(same, 0.0, LARGE_NEGATIVE)

    def attend_back(first, last):
        size = width // HEADS
        scale = 1.0 / math.sqrt(size)

        def body(head, carry):
            columns, inside = window_of(head, size, width)
            query, keys = query_ref[:, columns], sides_ref[0, :, columns]
            grad = grad_context[:, columns]
            scores = product_by_columns(jnp.where(inside, query, jnp.zeros_like(query)), keys)
            lane = lax.broadcasted_iota(jnp.int32, (1, 128), 1)
            total = jnp.sum(jnp.where(lane == head, total_ref[...], 0.0), axis=-1, keepdims=True)
            chance = jnp.exp(scores * scale + bias[...] - total)
            pulled = product_by_columns(
                jnp.where(inside, grad, jnp.zeros_like(grad)), sides_ref[1, :, columns]
            )
            inner = jnp.sum(chance * pulled, axis=-1, keepdims=True)
            grad_scores = (chance * (pulled - inner)).astype(jnp.bfloat16)
            grad_query = (product(grad_scores, keys) * scale).astype(jnp.bfloat16)
            lows[0, :, columns] = jnp.where(inside, grad_query, lows[0, :, columns])
            grad_key = product_by_rows(grad_scores, query) * scale
            grad_value = product_by_rows(chance.astype(jnp.bfloat16), grad)
            for h in (0, 1):
                here = slice(h * count, (h + 1) * count)
                quad[h, :, columns] = jnp.where(inside, grad_key[here], quad[h, :, columns])
                quad[2 + h, :, columns] = jnp.where(inside, grad_value[here], quad[2 + h, :, columns])
            return carry

        lax.fori_loop(first, last, body, 0)

    def swap_sides():
        for j in (0, 1):
            leave[j] = quad[2 * j + 1 - c].astype(jnp.bfloat16)
            send("end", leave.at[j], enter.at[j], side_send.at[j], side_recv.at[j], c_peer)

    def query_grad():
        put(5, hidden_ref, lows.at[0], mixer_part_ref.at[0])

    def sides_grad():
        for j in (0, 1):
            arrive(enter.at[j], side_recv.at[j], c_peer)

            def body(at):
                total = quad[2 * j + c, at, :] + enter[j, at, :].astype(jnp.float32)
                lows[1 + j, at, :] = total.astype(jnp.bfloat16)

            chunks(count, body)
            put(6 + j, hidden_ref, lows.at[1 + j], mixer_part_ref.at[1 + j])

    def through_qkv():
        for q in range(3):
            value = product_by_columns(lows[q], take(9 + q))
            work[...] = work[...] + value if q else value
            fetch(11 + q)

    def first_norm():
        def body(at):
            segments = seg_col_ref[at, :1]
            grad = work[at, :]
            value, inverse = normed(tokens_ref[at, :].astype(jnp.float32))
            add_sums(segments, 0, grad)
            add_sums(segments, 1, grad * value)
            scaled = grad * (1.0 + pick(segments, table_ref, 0, 1, width))
            tokens_grad_ref[at, :] = grad_middle[at, :] + norm_pull(scaled, value, inverse)

        chunks(count, body)
        for which in range(6):
            for crop in range(CROPS):
                row = which // 3 * CROPS + crop
                columns = slice(which % 3 * width, (which % 3 + 1) * width)
                sums_row[row : row + 1, columns] = jnp.sum(sums[which, crop], axis=0, keepdims=True)
        send("end", sums_row, sums_core, m_send, m_recv, c_peer)

    side = sums_row.shape[1]

    def place(k, other_y, other_x):
        zz = (z - k + 4) % 4
        yy = 1 - y if other_y else y
        xx = 1 - x if other_x else x
        return band.at[c, pl.ds(pl.multiple_of((zz * 4 + yy * 2 + xx) * 8, 8), 8)]

    def sums_start():
        arrive(sums_core, m_recv, c_peer)
        near = pl.ds(pl.multiple_of(c * (side - BAND), 128), BAND)
        band[c, pl.ds(pl.multiple_of(me * 8, 8), 8), :] = sums_row[:, near] + sums_core[:, near]
        mine = place(0, 0, 0)
        for k in (1, 2, 3):
            send("end", mine, mine, mz_send.at[k - 1], mz_recv.at[k - 1], device((z + k) % 4, y, x, c))
        send("end", mine, mine, mx_send.at[0], mx_recv.at[0], x_peer)
        send("end", mine, mine, my_send.at[0], my_recv.at[0], y_peer)

    def sums_line():
        for k in (1, 2, 3):
            piece = place(k, 0, 0)
            arrive(piece, mz_recv.at[k - 1], device((z - k + 4) % 4, y, x, c))
            send("end", piece, piece, mx_send.at[k], mx_recv.at[k], x_peer)
            send("end", piece, piece, my_send.at[k], my_recv.at[k], y_peer)

    def sums_plane():
        for k in range(4):
            from_side, from_up = place(k, 0, 1), place(k, 1, 0)
            arrive(from_side, mx_recv.at[k], x_peer)
            arrive(from_up, my_recv.at[k], y_peer)
            if k % 2:
                send("end", from_side, from_side, md_send.at[k], md_recv.at[k], y_peer)
            else:
                send("end", from_up, from_up, md_send.at[k], md_recv.at[k], x_peer)

    def sums_cores():
        for k in range(4):
            arrive(place(k, 1, 1), md_recv.at[k], y_peer if k % 2 else x_peer)
        send("end", band.at[c], band.at[c], mc_send, mc_recv, c_peer)

    def condition():
        arrive(band.at[1 - c], mc_recv, c_peer)
        acts = conds_ref[:, :8, :].astype(jnp.float32).reshape(CHIPS * 8, 128)
        row = lax.broadcasted_iota(jnp.int32, acts.shape, 0) % 8
        acts = jnp.where(row < CROPS, acts, 0.0)
        upper = acts.astype(jnp.bfloat16)
        lower = pltpu.roll(acts, CROPS, 0).astype(jnp.bfloat16)
        sides = [jnp.zeros((CHIPS * 8, 128), jnp.float32)] * 2
        for at, source, skip, size in ((0, 0, 0, BAND), (BAND, 1, 2 * BAND - side, side - BAND)):
            terms = split_low(band[source, :, skip : skip + size])
            for which, act in enumerate((upper, lower)):
                columns = slice(which * side + at, which * side + at + size)
                value = product_by_rows(act, terms[0]) + product_by_rows(act, terms[1])
                ada_grad_ref[:, columns] = value[:share]
                for term in terms:
                    sides[which] = sides[which] + product_by_columns(term, ada_ref[:, columns])
        silu_part[...] = sides[0] + pltpu.roll(sides[1], CHIPS * 8 - CROPS, 0)
        silu_ref[c, me] = silu_part[pl.ds(pl.multiple_of(me * 8, 8), 8), :]
        for k in range(1, CHIPS):
            to = (me + k) % CHIPS
            src = silu_part.at[pl.ds(pl.multiple_of(to * 8, 8), 8)]
            send("end", src, silu_ref.at[c, me], s_send.at[k - 1], s_recv.at[k - 1], (to, c))

    def condition_cores():
        for k in range(1, CHIPS):
            source = (me - k + CHIPS) % CHIPS
            arrive(silu_ref.at[c, source], s_recv.at[k - 1], (source, c))
        send("end", silu_ref.at[c], silu_ref.at[c], sc_send, sc_recv, c_peer)

    extra = {
        0: [partial(through_down, 0), partial(through_down, 1)],
        1: [partial(through_down, 2), partial(through_down, 3), partial(up_grad, 0)],
        2: [partial(up_grad, 1), partial(up_grad, 2), partial(up_grad, 3)],
        3: [partial(through_up, q) for q in range(4)] + [second_norm],
        4: [through_out, partial(attend_back, 0, 4)],
        5: [partial(attend_back, 4, 12)],
        6: [partial(attend_back, 12, 16), swap_sides, query_grad, sides_grad],
        7: [through_qkv, first_norm],
        8: [sums_start],
        9: [sums_line],
        10: [sums_plane],
        11: [sums_cores],
        12: [condition],
        13: [condition_cores],
    }
    begin(0)
    for q in range(4):
        slopes(q)
    fetch(0)
    fetch(1)
    for i in range(len(order) + 2):
        if i + 1 < len(order):
            if (i + 1) % 4 == 0:
                for n in sorted(going):
                    going.pop(n).wait()
            begin(i + 1)
        if i < len(order):
            pair(i)
        if 1 <= i < len(order) + 1:
            relay(i - 1)
        if 2 <= i:
            plane(i - 2)
        for step in extra.get(i, ()):
            step()
    for a in range(2):
        for j, (px, pc) in enumerate(partners):
            arrive(rows_ref.at[a, px * 2 + pc], group_recv.at[a, j], device(z, y, px, pc))
    arrive(silu_ref.at[1 - c], sc_recv, c_peer)
    for owner in list(sends):
        finish_sends(owner)


def run_backward(given, share):
    (weights, down_part, slope, middle, attended, mlp, hidden, query, sides, total, context, hidden_two,
     grad_mlp, table, conds, level, seg_all, seg_col, tokens, cot, ada) = given
    count, width = tokens.shape
    rows, side = 4 * share, ada.shape[1] // 2
    dma = pltpu.SemaphoreType.DMA
    low, wide = jnp.bfloat16, jnp.float32
    vmem, any_ = pl.BlockSpec(memory_space=pltpu.VMEM), pl.BlockSpec(memory_space=pl.ANY)
    out, buffer = jax.ShapeDtypeStruct, pltpu.VMEM
    slots = 12
    return pl.pallas_call(
        partial(backward_kernel, share),
        out_shape=(
            out((4, width, width), low),
            out((4, width, width), low),
            out((2, 4, PAD, width), low),
            out((rows, width), wide),
            out((count, width), wide),
            out((share, ada.shape[1]), wide),
            out((2, CHIPS, 8, 128), wide),
        ),
        in_specs=[any_] * 6 + [vmem] * 15,
        out_specs=[any_] * 2 + [vmem] * 5,
        scratch_shapes=[
            buffer((5, 4, rows, width), low),
            buffer((4, 4, rows, width), low),
            buffer((4, rows, width), low),
            buffer((5, rows, width), low),
            buffer((5, rows, width), low),
            buffer((3, 3, rows, width), low),
            buffer((2, 4 * PAD, width), low),
            buffer((2, width, width), low),
            buffer((2, width, width), low),
            buffer((4, count, width), wide),
            buffer((4, count, width), low),
            buffer((count, width), wide),
            buffer((count, width), wide),
            buffer((count, width), low),
            buffer((2, count, width), low),
            buffer((2, count, width), low),
            buffer((count, 2 * count), wide),
            buffer((6, CROPS, 8, width), wide),
            buffer((8, side), wide),
            buffer((8, side), wide),
            buffer((2, CHIPS * 8, BAND), wide),
            buffer((CHIPS * 8, 128), wide),
            dma((slots, 4)), dma((slots, 4)), dma((slots, 4)),
            dma((slots,)), dma((slots,)), dma((slots,)), dma((slots,)),
            dma((slots, 2)), dma((slots, 2)), dma((slots, 2)), dma((slots, 2)),
            dma((3, 3)), dma((3, 3)), dma((2, 3)), dma((2, 3)), dma((2,)), dma((2,)), dma((4,)),
            dma((2,)), dma((2,)), dma, dma, dma((3,)), dma((3,)), dma((4,)), dma((4,)), dma((4,)), dma((4,)),
            dma((4,)), dma((4,)), dma, dma, dma((CHIPS - 1,)), dma((CHIPS - 1,)), dma, dma,
        ],
        compiler_params=pltpu.CompilerParams(
            collective_id=1, has_side_effects=True, vmem_limit_bytes=63 * 2**20
        ),
        name="backward",
    )(*given)


def layer_norm(values):
    center = values - jnp.mean(values, axis=-1, keepdims=True)
    inverse = lax.rsqrt(jnp.mean(center * center, axis=-1, keepdims=True) + EPSILON)
    return (center * inverse, inverse)


def norm_back(grad_normed, normed, inverse):
    return inverse * (
        grad_normed
        - jnp.mean(grad_normed, axis=-1, keepdims=True)
        - normed * jnp.mean(grad_normed * normed, axis=-1, keepdims=True)
    )


def to_heads(array):
    return array.reshape(array.shape[0], HEADS, array.shape[1] // HEADS)


def dots(spec, left, right):
    return jnp.einsum(spec, left, right, preferred_element_type=jnp.float32)


def masked_scores(query_heads, key_heads, same_crop):
    scale_factor = 1.0 / math.sqrt(query_heads.shape[-1])
    scores = dots("qhd,khd->hqk", query_heads, key_heads) * scale_factor
    return jnp.where(same_crop[None], scores, LARGE_NEGATIVE)


def attend(query_seq, key_seq, value_seq, same_crop):
    scores = masked_scores(to_heads(query_seq), to_heads(key_seq), same_crop)
    row_max = jnp.max(scores, axis=-1, keepdims=True)
    raised = jnp.exp(scores - row_max)
    row_total = jnp.sum(raised, axis=-1, keepdims=True)
    probability = (raised / row_total).astype(jnp.bfloat16)
    context = dots("hqk,khd->qhd", probability, to_heads(value_seq))
    return (context.reshape(query_seq.shape[0], -1), (row_max + jnp.log(row_total))[..., 0])


def attend_back(query_seq, key_seq, value_seq, same_crop, log_total, grad_seq):
    query_heads = to_heads(query_seq)
    key_heads = to_heads(key_seq)
    value_heads = to_heads(value_seq)
    grad_heads = to_heads(grad_seq)
    scale_factor = 1.0 / math.sqrt(query_heads.shape[-1])
    scores = masked_scores(query_heads, key_heads, same_crop)
    probability = jnp.exp(scores - log_total[..., None])
    grad_prob = dots("qhd,khd->hqk", grad_heads, value_heads)
    inner = jnp.sum(probability * grad_prob, axis=-1, keepdims=True)
    grad_scores = (probability * (grad_prob - inner)).astype(jnp.bfloat16)
    grad_query = dots("hqk,khd->qhd", grad_scores, key_heads) * scale_factor
    grad_key = dots("hqk,qhd->khd", grad_scores, query_heads) * scale_factor
    grad_value = dots("hqk,qhd->khd", probability.astype(jnp.bfloat16), grad_heads)
    rows_here = query_seq.shape[0]
    rows_whole = key_seq.shape[0]
    return (
        grad_query.reshape(rows_here, -1),
        grad_key.reshape(rows_whole, -1),
        grad_value.reshape(rows_whole, -1),
    )


def kernel_inputs(segments, conditions, noise_bins, bin_counts, ada_weight, first, up_weight):
    share, width = first.shape[0], first.shape[1] // 4
    cores = lax.axis_size("sp")
    shards = jnp.stack([first, up_weight]).reshape(2, share, 4, width)
    shards = jnp.pad(shards.transpose(0, 2, 1, 3), ((0, 0), (0, 0), (0, PAD - share), (0, 0)))
    acts = jax.nn.silu(conditions.astype(jnp.float32)).astype(jnp.bfloat16)
    acts = acts.reshape(CROPS, CHIPS, cores, share)
    acts = lax.dynamic_index_in_dim(acts, lax.axis_index("sp"), 2, keepdims=False)
    acts = jnp.pad(acts.transpose(1, 0, 2), ((0, 0), (0, 0), (0, 128 - share)))
    counts = jnp.pad(bin_counts.astype(jnp.bfloat16), (0, 128 - NBINS))
    counts = jnp.broadcast_to(counts, (CHIPS, 1, 128))
    acts = jnp.pad(jnp.concatenate([acts, counts], axis=1), ((0, 0), (0, 11), (0, 0)))
    ada = jnp.pad(ada_weight, ((0, 128 - share), (0, 0)))
    count = segments.shape[0]
    seg_col = jnp.broadcast_to(segments[:, None], (count, 128))
    seg_row = jnp.broadcast_to(segments[None, :], (8, count))
    bins = jnp.pad(noise_bins, (0, 4), constant_values=-1)
    bins = (bins[:, None] == jnp.arange(128, dtype=jnp.int32)).astype(jnp.float32)
    return shards, acts, ada, seg_col, seg_row, bins


def forward_plain(tokens_float, segments, conditions, noise_bins, bin_counts, ada_weight, first, up_weight,
                  down_weight):
    groups, cores = lax.axis_size("dp"), lax.axis_size("sp")
    share, width = first.shape[0], tokens_float.shape[1]
    index = lax.axis_index("dp") * cores + lax.axis_index("sp")
    mixers = lax.all_gather(first, ("dp", "sp"), axis=0, tiled=True)
    uppers = lax.all_gather(up_weight, ("dp", "sp"), axis=0, tiled=True)
    downers = lax.all_gather(down_weight, ("dp", "sp"), axis=0, tiled=True)
    mixers = mixers.reshape(width, 4, width).transpose(1, 0, 2)
    uppers = uppers.reshape(width, 4, width).transpose(1, 0, 2)
    downers = downers.reshape(4, width, width)
    bin_total = lax.psum(bin_counts, "dp")
    bin_weight = 40.0 * groups / bin_total.astype(jnp.float32)
    crop_weight = jnp.sum(
        jnp.where(noise_bins[:, None] == jnp.arange(NBINS, dtype=jnp.int32), bin_weight, 0.0),
        axis=-1,
    )
    cond_all = lax.all_gather(conditions, "dp", axis=0, tiled=True)
    cond_here = lax.dynamic_slice_in_dim(cond_all, index * share, share, axis=1)
    cond_act = jax.nn.silu(cond_here.astype(jnp.float32)).astype(jnp.bfloat16)
    modulation_part = dots("sd,df->sf", cond_act, ada_weight).reshape(groups, CROPS, -1)
    modulation = lax.psum(lax.psum_scatter(modulation_part, "dp", scatter_dimension=0), "sp")
    selector = (segments[:, None] == jnp.arange(CROPS, dtype=jnp.int32)).astype(jnp.float32)
    per_token = jnp.einsum("tc,cf->tf", selector, modulation, precision=lax.Precision.HIGHEST)
    shift_one, scale_one, gate_one, shift_two, scale_two, _ = jnp.split(per_token, 6, axis=-1)
    normed_one, _ = layer_norm(tokens_float)
    hidden_one = (normed_one * (1.0 + scale_one) + shift_one).astype(jnp.bfloat16)
    projected = dots("td,qdf->qtf", hidden_one, mixers[:3]).astype(jnp.bfloat16)
    sides = lax.all_gather(projected[1:], "sp", axis=1, tiled=True)
    all_segments = lax.all_gather(segments, "sp", axis=0, tiled=True)
    same_crop = segments[:, None] == all_segments[None, :]
    context, log_total = attend(projected[0], sides[0], sides[1], same_crop)
    context_low = context.astype(jnp.bfloat16)
    attended = dots("td,df->tf", context_low, mixers[3])
    middle = tokens_float + gate_one * attended
    normed_two, _ = layer_norm(middle)
    hidden_two = (normed_two * (1.0 + scale_two) + shift_two).astype(jnp.bfloat16)
    upper_in = dots("td,qdf->qtf", hidden_two, uppers)
    activated = jax.nn.gelu(upper_in, approximate=True).astype(jnp.bfloat16)
    slope = jax.vjp(partial(jax.nn.gelu, approximate=True), upper_in)[1](jnp.ones_like(upper_in))[0]
    mlp_out = dots("qtf,qfd->td", activated, downers)
    return (
        (mixers, uppers, downers), activated, slope, hidden_one, projected[0], sides, log_total,
        context_low, attended, middle, hidden_two, mlp_out, modulation, cond_act, crop_weight, same_crop,
    )


def layer_plain(tokens_float, segments, conditions, noise_bins, bin_counts, cotangent, ada_weight, first,
                up_weight, down_weight):
    width = tokens_float.shape[1]
    (
        (mixers, uppers, downers), activated, slope, hidden_one, queries, sides, log_total,
        context_low, attended, middle, hidden_two, mlp_out, modulation, cond_act, crop_weight, same_crop,
    ) = forward_plain(
        tokens_float, segments, conditions, noise_bins, bin_counts, ada_weight, first, up_weight,
        down_weight,
    )
    selector = (segments[:, None] == jnp.arange(CROPS, dtype=jnp.int32)).astype(jnp.float32)
    per_token = jnp.einsum("tc,cf->tf", selector, modulation, precision=lax.Precision.HIGHEST)
    _, scale_one, gate_one, _, scale_two, gate_two = jnp.split(per_token, 6, axis=-1)
    normed_one, inverse_one = layer_norm(tokens_float)
    normed_two, inverse_two = layer_norm(middle)

    token_weight = jnp.sum(selector * crop_weight[None, :], axis=-1)
    grad_out = cotangent.astype(jnp.float32) * token_weight[:, None]
    grad_mlp = (grad_out * gate_two).astype(jnp.bfloat16)
    tokens_out = (middle + gate_two * mlp_out).astype(jnp.bfloat16)
    down_part = dots("qtf,td->qfd", activated, grad_mlp).astype(jnp.bfloat16)
    grad_act = dots("td,qfd->qtf", grad_mlp, downers)
    grad_upper = (grad_act * slope).astype(jnp.bfloat16)
    up_part = dots("td,qtf->qdf", hidden_two, grad_upper).astype(jnp.bfloat16)
    grad_hidden_two = dots("qtf,qdf->td", grad_upper, uppers)
    grad_middle = grad_out + norm_back(grad_hidden_two * (1.0 + scale_two), normed_two, inverse_two)
    grad_attended = (grad_middle * gate_one).astype(jnp.bfloat16)
    grad_context = dots("tf,df->td", grad_attended, mixers[3]).astype(jnp.bfloat16)
    grad_query, grad_key, grad_value = attend_back(
        queries, sides[0], sides[1], same_crop, log_total, grad_context
    )
    grad_sides = lax.psum_scatter(
        jnp.stack([grad_key, grad_value]).astype(jnp.bfloat16),
        "sp",
        scatter_dimension=1,
        tiled=True,
    )
    grad_projected = jnp.concatenate([grad_query.astype(jnp.bfloat16)[None], grad_sides])
    out_part = dots("td,tf->df", context_low, grad_attended).astype(jnp.bfloat16)
    qkv_part = dots("td,qtf->qdf", hidden_one, grad_projected).astype(jnp.bfloat16)
    first_part = jnp.concatenate([qkv_part, out_part[None]])
    grad_hidden_one = dots("qtf,qdf->td", grad_projected, mixers[:3])
    tokens_grad = grad_middle + norm_back(
        grad_hidden_one * (1.0 + scale_one), normed_one, inverse_one
    )

    joined = jnp.stack([first_part, up_part]).transpose(2, 0, 1, 3).reshape(width, 8 * width)
    rows = lax.psum_scatter(joined, ("dp", "sp"), scatter_dimension=0, tiled=True)
    rows = rows.astype(jnp.float32)
    first_grad, up_grad = rows[:, : 4 * width], rows[:, 4 * width :]
    down_grad = lax.psum_scatter(
        down_part.reshape(4 * width, width), ("dp", "sp"), scatter_dimension=0, tiled=True
    ).astype(jnp.float32)

    grad_per_token = jnp.concatenate(
        [
            grad_hidden_one,
            grad_hidden_one * normed_one,
            grad_middle * attended,
            grad_hidden_two,
            grad_hidden_two * normed_two,
            grad_out * mlp_out,
        ],
        axis=-1,
    )
    grad_modulation = lax.psum(
        jnp.einsum("tc,tf->cf", selector, grad_per_token, precision=lax.Precision.HIGHEST), "sp"
    )
    grad_rows = lax.all_gather(grad_modulation, "dp", axis=0, tiled=True)
    ada_grad = jnp.einsum(
        "sd,sf->df", cond_act.astype(jnp.float32), grad_rows, precision=lax.Precision.HIGHEST
    )
    silu_part = jnp.einsum(
        "sf,df->sd", grad_rows, ada_weight.astype(jnp.float32), precision=lax.Precision.HIGHEST
    )
    silu_all = lax.all_gather(silu_part, ("dp", "sp"), axis=0)
    silu_here = lax.dynamic_slice_in_dim(silu_all, lax.axis_index("dp") * CROPS, CROPS, axis=1)
    grad_silu = silu_here.transpose(1, 0, 2).reshape(CROPS, width)
    return tokens_out, tokens_grad, grad_silu, ada_grad, first_grad, up_grad, down_grad


def on_device(
    chips,
    tokens_in,
    segment_ids,
    conditions,
    noise_bins,
    bin_counts,
    cotangent,
    ada_weight,
    qkv_weight,
    out_weight,
    up_weight,
    down_weight,
):
    tokens_float = tokens_in[0].astype(jnp.float32)
    segments = segment_ids[0]
    width = tokens_float.shape[1]
    share = qkv_weight.shape[0]
    kernels = chips and 4 * share == down_weight.shape[0]
    first = jnp.concatenate([qkv_weight, out_weight], axis=1)
    if kernels:
        shards, acts, ada, seg_col, seg_row, bins = kernel_inputs(
            segments, conditions[0], noise_bins[0], bin_counts[0], ada_weight, first, up_weight
        )
        (
            weights, down_part, slope, hidden_one, queries, sides, log_total, context_low, attended,
            middle, hidden_two, mlp_out, tokens_out, table, conds, level, grad_mlp, seg_all,
        ) = run_forward(
            shards, down_weight, acts, ada, tokens_in[0], cotangent[0], seg_col, seg_row, bins, share
        )
        given = (
            weights, down_part, slope, middle, attended, mlp_out, hidden_one, queries, sides, log_total,
            context_low, hidden_two, grad_mlp, table, conds, level, seg_all, seg_col, tokens_in[0],
            cotangent[0], ada,
        )
        _, _, rows, down_grad, tokens_grad, ada_grad, silu_part = run_backward(given, share)
        rows = rows[:, :, :share].astype(jnp.float32).transpose(0, 2, 1, 3).reshape(2, share, 4 * width)
        first_grad, up_grad = rows[0], rows[1]
        grad_silu = silu_part[:, :, :CROPS, :share].transpose(2, 1, 0, 3).reshape(CROPS, width)
    else:
        tokens_out, tokens_grad, grad_silu, ada_grad, first_grad, up_grad, down_grad = layer_plain(
            tokens_float, segments, conditions[0], noise_bins[0], bin_counts[0], cotangent[0],
            ada_weight, first, up_weight, down_weight,
        )
    silu_pull = jax.vjp(jax.nn.silu, conditions[0].astype(jnp.float32))[1]
    cond_grad = silu_pull(grad_silu)[0]
    return (
        tokens_out[None],
        tokens_grad[None],
        cond_grad[None],
        ada_grad,
        first_grad[:, : 3 * width],
        first_grad[:, 3 * width :],
        up_grad,
        down_grad,
    )


def solution(mesh):
    placed = (
        P("dp", "sp", None),
        P("dp", "sp"),
        P("dp", None, None),
        P("dp", None),
        P("dp", None),
        P("dp", "sp", None),
        P(("dp", "sp"), None),
        P(("dp", "sp"), None),
        P(("dp", "sp"), None),
        P(("dp", "sp"), None),
        P(("dp", "sp"), None),
    )
    return jax.shard_map(
        partial(on_device, mesh.shape["dp"] == 16 and mesh.shape["sp"] == 2),
        mesh=mesh,
        in_specs=placed,
        out_specs=(
            P("dp", "sp", None),
            P("dp", "sp", None),
            P("dp", None, None),
            P(("dp", "sp"), None),
            P(("dp", "sp"), None),
            P(("dp", "sp"), None),
            P(("dp", "sp"), None),
            P(("dp", "sp"), None),
        ),
        check_vma=False,
    )
```

```python
from functools import partial
import math

import jax
import jax.numpy as jnp
from jax import lax
from jax.experimental import pallas as pl
from jax.experimental.pallas import tpu as pltpu
from jax.sharding import PartitionSpec as P

HEADS = 16
CROPS = 4
NBINS = 8
EPSILON = 1e-06
LARGE_NEGATIVE = -1e30
GELU_SCALE = math.sqrt(2.0 / math.pi)
GELU_CUBE = 0.044715

MESH = pl.DeviceIdType.MESH
PAD = 48
NEAR = (80, 64)
FAR = (32, 32)
CHIPS = 16
BAND = 1792
PLACES = ((0, 0), (0, 1), (1, 0), (1, 1))


def position():
    d = lax.axis_index("dp")
    c = lax.axis_index("sp")
    return d // 4, (d // 2) % 2, d % 2, c


def device(z, y, x, c):
    return (z * 4 + y * 2 + x, c)


def block_of(kind, zy, group):
    if kind == 2:
        return zy // 2, (zy % 2) * 4 + group
    return group, zy


def greet(peers):
    barrier = pltpu.get_barrier_semaphore()
    for peer in peers:
        pl.semaphore_signal(barrier, inc=1, device_id=peer, device_id_type=MESH)
    pl.semaphore_wait(barrier, len(peers))


def remote(src, dst, send, recv, target):
    return pltpu.make_async_remote_copy(
        src_ref=src,
        dst_ref=dst,
        send_sem=send,
        recv_sem=recv,
        device_id=target,
        device_id_type=MESH,
    )


def arrive(ref, sem, target):
    remote(ref, ref, sem, sem, target).wait_recv()


def row_selector(rows, share):
    shape = (rows, 4 * PAD)
    row = lax.broadcasted_iota(jnp.int32, shape, 0)
    column = lax.broadcasted_iota(jnp.int32, shape, 1)
    picked = jnp.zeros(shape, jnp.bool_)
    for k in range(4):
        inside = (row >= k * share) & (row < (k + 1) * share)
        picked = picked | (inside & (column == row - k * share + k * PAD))
    return picked.astype(jnp.float32).astype(jnp.bfloat16)


def product(left, right):
    return jnp.dot(left, right, preferred_element_type=jnp.float32)


def product_by_rows(left, right):
    return lax.dot_general(left, right, (((0,), (0,)), ((), ())), preferred_element_type=jnp.float32)


def product_by_columns(left, right):
    return lax.dot_general(left, right, (((1,), (1,)), ((), ())), preferred_element_type=jnp.float32)


def chunks(rows, body, step=16):
    def run(i, carry):
        body(pl.ds(pl.multiple_of(i * step, step), step))
        return carry

    lax.fori_loop(0, rows // step, run, 0)


def normed(values):
    center = values - jnp.mean(values, axis=-1, keepdims=True)
    inverse = lax.rsqrt(jnp.mean(center * center, axis=-1, keepdims=True) + EPSILON)
    return center * inverse, inverse


def pick(segments, table, first, column, width):
    columns = slice(column * width, (column + 1) * width)
    value = table[first + 3 : first + 4, columns]
    for crop in (2, 1, 0):
        value = jnp.where(segments == crop, table[first + crop : first + crop + 1, columns], value)
    return value


def window_of(head, size, width):
    start = jnp.minimum((head * size) // 128, width // 128 - 2) * 128
    start = pl.multiple_of(start, 128)
    lane = lax.broadcasted_iota(jnp.int32, (1, 256), 1) + start
    return pl.ds(start, 256), (lane >= head * size) & (lane < (head + 1) * size)


def forward_kernel(share, shards_ref, down_ref, act_ref, ada_ref, tokens_ref, cot_ref, seg_col_ref,
                   seg_row_ref, bins_ref,
                   weights_ref, down_part_ref, slope_ref, hidden_ref, query_ref, sides_ref, total_ref,
                   context_ref, attended_ref, middle_ref, hidden_two_ref, mlp_ref, out_ref, table_ref,
                   conds_ref, level_ref, grad_mlp, seg_all,
                   full, stage, part, part_recv, band, band_diag, band_x, band_y, band_z, halves_of,
                   bias, work, active, slope, *sems):
    (
        group_send, group_recv, z_send, z_recv, zd_send, zd_recv, x_send, x_recv, y_send, y_recv,
        dx_send, dx_recv, dy_send, dy_recv, c_send, c_recv,
        cond_send, cond_recv, pc_send, pc_recv, pd_send, pd_recv, px_send, px_recv, py_send, py_recv,
        pz_send, pz_recv, pm_send, pm_recv, seg_send, seg_recv, kv_send, kv_recv,
        save_sem, grad_sem, slope_sem,
    ) = sems
    z, y, x, c = position()
    me = z * 4 + y * 2 + x
    group = x * 2 + c
    zy = z * 2 + y
    rows = 4 * share
    count, width = tokens_ref.shape
    x_peer, y_peer, c_peer = device(z, y, 1 - x, c), device(z, 1 - y, x, c), device(z, y, x, 1 - c)
    partners = [(x, 1 - c), (1 - x, c), (1 - x, 1 - c)]
    greet(
        [((me + k) % CHIPS, c) for k in range(1, CHIPS)] + [c_peer, device(z, y, 1 - x, 1 - c)]
    )
    sends = {a: [] for a in (0, 1, 2, "other")}

    def send(a, *args):
        copy = remote(*args)
        copy.start()
        sends[a].append((None, copy))

    def finish_sends(a):
        for go, copy in sends[a]:
            if go is None:
                copy.wait_send()
            else:
                pl.when(go)(copy.wait_send)
        sends[a] = []

    def level(k):
        if k == 0:
            return z
        upper = z // 2
        inner = z * (1 - upper) + (3 - z) * upper
        step = k - inner if k == 1 else k
        return step * (1 - upper) + (3 - step) * upper

    def place(a, k, other_y, other_x, core=None, first=0, last=None):
        yy = 1 - y if other_y else y
        xx = 1 - x if other_x else x
        cc = c if core is None else core
        block, row = block_of(a, level(k) * 2 + yy, xx * 2 + cc)
        count = (rows if last is None else last) - first
        return full.at[a, block, pl.ds(pl.multiple_of(row * rows + first, 16), count)]

    def cuts(k):
        top, low = FAR if k else NEAR
        return top, rows - low

    def along(a, k, ref, send_sem, recv_sem):
        source = level(k)
        for way, step in ((0, 1), (1, -1)):
            to = z + step
            go = (to >= 0) & (to < 4)
            if k:
                go = go & ((source < z) if step == 1 else (source > z))
            copy = remote(ref, ref, send_sem.at[a, k, way], recv_sem.at[a, source], device(jnp.clip(to, 0, 3), y, x, c))
            pl.when(go)(copy.start)
            sends[a].append((go, copy))

    def from_line(a, k, ref, recv_sem):
        source = level(k)
        arrive(ref, recv_sem.at[a, source], device((z + 1) % 4, y, x, c))

    for a in range(2):
        for j, (px, pc) in enumerate(partners):
            send(
                "other",
                shards_ref.at[a, px * 2 + pc],
                stage.at[a, pl.ds(pl.multiple_of(group * PAD, 16), PAD)],
                group_send.at[a, j],
                group_recv.at[a, j],
                device(z, y, px, pc),
            )
    for k in range(1, CHIPS):
        to = (me + k) % CHIPS
        send("other", act_ref.at[to], conds_ref.at[me], cond_send.at[k - 1], cond_recv.at[k - 1], (to, c))
    seg_all[c] = seg_row_ref[...]
    send("other", seg_row_ref, seg_all.at[c], seg_send, seg_recv, c_peer)
    conds_ref[me] = act_ref[me]
    for a in range(2):
        stage[a, pl.ds(pl.multiple_of(group * PAD, 16), PAD), :] = shards_ref[a, group]

    def own(a):
        block, row = block_of(a, zy, group)
        here = pl.ds(pl.multiple_of(row * rows, 16), rows)
        if a < 2:
            for j, (px, pc) in enumerate(partners):
                arrive(
                    stage.at[a, pl.ds(pl.multiple_of((px * 2 + pc) * PAD, 16), PAD)],
                    group_recv.at[a, j],
                    device(z, y, px, pc),
                )
            full[a, block, here, :] = product(row_selector(rows, share), stage[a]).astype(jnp.bfloat16)
        else:
            full[a, block, here, :] = down_ref[...]
        along(a, 0, place(a, 0, 0, 0), z_send, z_recv)

    def to_core(a, k, pos):
        piece = place(a, k, *PLACES[pos])
        send(a, piece, piece, c_send.at[a, k, pos], c_recv.at[a, k, pos], c_peer)

    def spread(a, k):
        if k:
            from_line(a, k, place(a, k, 0, 0), z_recv)
            along(a, k, place(a, k, 0, 0), z_send, z_recv)
        top, low = cuts(k)
        for h, first, last in ((0, 0, top), (1, top, rows)):
            part = place(a, k, 0, 0, None, first, last)
            send(a, part, part, x_send.at[a, k, h], x_recv.at[a, k, h], x_peer)
        for h, first, last in ((1, low, rows), (0, 0, low)):
            part = place(a, k, 0, 0, None, first, last)
            send(a, part, part, y_send.at[a, k, h], y_recv.at[a, k, h], y_peer)
        to_core(a, k, 0)

    def forward(a, k):
        top, low = cuts(k)
        part = place(a, k, 0, 1, None, 0, top)
        arrive(part, x_recv.at[a, k, 0], x_peer)
        send(a, part, part, dy_send.at[a, k], dy_recv.at[a, k], y_peer)
        part = place(a, k, 1, 0, None, low, rows)
        arrive(part, y_recv.at[a, k, 1], y_peer)
        send(a, part, part, dx_send.at[a, k], dx_recv.at[a, k], x_peer)
        arrive(place(a, k, 0, 1, None, top, rows), x_recv.at[a, k, 1], x_peer)
        to_core(a, k, 1)
        arrive(place(a, k, 1, 0, None, 0, low), y_recv.at[a, k, 0], y_peer)
        to_core(a, k, 2)

    def finish(a, k):
        top, low = cuts(k)
        arrive(place(a, k, 1, 1, None, 0, top), dy_recv.at[a, k], y_peer)
        arrive(place(a, k, 1, 1, None, low, rows), dx_recv.at[a, k], x_peer)
        middle = place(a, k, 1, 1, None, FAR[0], rows - FAR[1])
        if k:
            from_line(a, k, middle, zd_recv)
        along(a, k, middle, zd_send, zd_recv)
        to_core(a, k, 3)

    saves = []

    def complete(a):
        for k in range(4):
            for pos, (oy, ox) in enumerate(PLACES):
                arrive(place(a, k, oy, ox, 1 - c), c_recv.at[a, k, pos], c_peer)
        copy = pltpu.make_async_copy(full.at[a], weights_ref.at[a], save_sem.at[a])
        copy.start()
        saves.append(copy)

    def mod_start():
        for k in range(1, CHIPS):
            source = (me - k + CHIPS) % CHIPS
            arrive(conds_ref.at[source], cond_recv.at[k - 1], (source, c))
        acts = conds_ref[:, :8, :].astype(jnp.float32).reshape(CHIPS * 8, 128)
        row = lax.broadcasted_iota(jnp.int32, acts.shape, 0) % 8
        upper = jnp.where(row < CROPS, acts, 0.0).astype(jnp.bfloat16)
        lower = pltpu.roll(jnp.where(row < CROPS, acts, 0.0), CROPS, 0).astype(jnp.bfloat16)
        side = ada_ref.shape[1] // 2
        part[...] = product(upper, ada_ref[:, :side]) + product(lower, ada_ref[:, side:])
        far = pl.ds(pl.multiple_of((1 - c) * (side - BAND), 128), BAND)
        send("other", part.at[:, far], part_recv, pc_send, pc_recv, c_peer)

    def block8(zz, yy, xx):
        return pl.ds(pl.multiple_of((zz * 4 + yy * 2 + xx) * 8, 8), 8)

    def mod_cores():
        arrive(part_recv, pc_recv, c_peer)
        side = ada_ref.shape[1] // 2
        near = pl.ds(pl.multiple_of(c * (side - BAND), 128), BAND)
        band[...] = part[:, near] + part_recv[...]
        for k in range(4):
            zz = (z + k) % 4
            src = band.at[block8(zz, 1 - y, 1 - x)]
            send("other", src, band_diag.at[k], pd_send.at[k], pd_recv.at[k], x_peer if k % 2 else y_peer)

    def mod_plane():
        for k in range(4):
            zz = (z + k) % 4
            to_x, to_y = block8(zz, y, 1 - x), block8(zz, 1 - y, x)
            arrive(band_diag.at[k], pd_recv.at[k], x_peer if k % 2 else y_peer)
            fold = to_y if k % 2 else to_x
            band[fold, :] = band[fold, :] + band_diag[k]
            send("other", band.at[to_x], band_x.at[k], px_send.at[k], px_recv.at[k], x_peer)
            send("other", band.at[to_y], band_y.at[k], py_send.at[k], py_recv.at[k], y_peer)

    def mod_line():
        for k in (1, 2, 3, 0):
            zz = (z + k) % 4
            mine = block8(zz, y, x)
            arrive(band_x.at[k], px_recv.at[k], x_peer)
            arrive(band_y.at[k], py_recv.at[k], y_peer)
            band[mine, :] = band[mine, :] + band_x[k] + band_y[k]
            if k:
                send("other", band.at[mine], band_z.at[k - 1], pz_send.at[k - 1], pz_recv.at[k - 1], device(zz, y, x, c))

    def mod_last():
        for k in (1, 2, 3):
            arrive(band_z.at[k - 1], pz_recv.at[k - 1], device((z - k + 4) % 4, y, x, c))
        halves_of[c] = band[block8(z, y, x), :] + band_z[0] + band_z[1] + band_z[2]
        send("other", halves_of.at[c], halves_of.at[c], pm_send, pm_recv, c_peer)

    def mod_end():
        arrive(halves_of.at[1 - c], pm_recv, c_peer)
        side = ada_ref.shape[1] // 2
        table_ref[:, :BAND] = halves_of[0]
        table_ref[:, BAND:] = halves_of[1][:, 2 * BAND - side :]
        counts = jnp.sum(conds_ref[:, :, :].astype(jnp.float32)[:, CROPS : CROPS + 1, :], axis=0)
        lane = lax.broadcasted_iota(jnp.int32, counts.shape, 1)
        weight = jnp.where(lane < NBINS, 40.0 * CHIPS / jnp.where(lane < NBINS, counts, 1.0), 0.0)
        level_ref[...] = jnp.broadcast_to(
            jnp.sum(bins_ref[...] * weight, axis=-1, keepdims=True), level_ref.shape
        )

    def first_norm():
        def body(at):
            segments = seg_col_ref[at, :1]
            value, _ = normed(tokens_ref[at, :].astype(jnp.float32))
            value = value * (1.0 + pick(segments, table_ref, 0, 1, width))
            hidden_ref[at, :] = (value + pick(segments, table_ref, 0, 0, width)).astype(jnp.bfloat16)

        chunks(count, body)
        arrive(seg_all.at[1 - c], seg_recv, c_peer)
        for h in (0, 1):
            same = seg_col_ref[:, :1] == seg_all[h][:1, :]
            bias[:, h * count : (h + 1) * count] = jnp.where(same, 0.0, LARGE_NEGATIVE)

    def project():
        here = pl.ds(pl.multiple_of(c * count, 256), count)
        for q in (1, 2):
            sides_ref[q - 1, here, :] = product(hidden_ref[...], full[0, q]).astype(jnp.bfloat16)
            send("other", sides_ref.at[q - 1, here], sides_ref.at[q - 1, here], kv_send.at[q - 1], kv_recv.at[q - 1], c_peer)
        query_ref[...] = product(hidden_ref[...], full[0, 0]).astype(jnp.bfloat16)
        total_ref[...] = jnp.zeros_like(total_ref)
        work[...] = jnp.zeros_like(work)

    def attend(first, last):
        if first == 0:
            there = pl.ds(pl.multiple_of((1 - c) * count, 256), count)
            for q in (0, 1):
                arrive(sides_ref.at[q, there], kv_recv.at[q], c_peer)
        size = width // HEADS
        scale = 1.0 / math.sqrt(size)

        def body(head, carry):
            columns, inside = window_of(head, size, width)
            query = query_ref[:, columns]
            query = jnp.where(inside, query, jnp.zeros_like(query))
            scores = product_by_columns(query, sides_ref[0, :, columns]) * scale + bias[...]
            top = jnp.max(scores, axis=-1, keepdims=True)
            raised = jnp.exp(scores - top)
            total = jnp.sum(raised, axis=-1, keepdims=True)
            chance = (raised * (1.0 / total)).astype(jnp.bfloat16)
            context = product(chance, sides_ref[1, :, columns])
            work[:, columns] = jnp.where(inside, context, work[:, columns])
            lane = lax.broadcasted_iota(jnp.int32, (1, 128), 1)
            total_ref[...] = jnp.where(lane == head, top + jnp.log(total), total_ref[...])
            return carry

        lax.fori_loop(first, last, body, 0)

    def mix():
        context_ref[...] = work[...].astype(jnp.bfloat16)
        attended_ref[...] = product(context_ref[...], full[0, 3])

        def body(at):
            segments = seg_col_ref[at, :1]
            gate = pick(segments, table_ref, 0, 2, width)
            middle = tokens_ref[at, :].astype(jnp.float32) + gate * attended_ref[at, :]
            middle_ref[at, :] = middle
            value, _ = normed(middle)
            value = value * (1.0 + pick(segments, table_ref, 4, 1, width))
            hidden_two_ref[at, :] = (value + pick(segments, table_ref, 4, 0, width)).astype(jnp.bfloat16)
            level = level_ref[3:4, :1]
            for crop in (2, 1, 0):
                level = jnp.where(segments == crop, level_ref[crop : crop + 1, :1], level)
            grad = cot_ref[at, :].astype(jnp.float32) * level
            grad_mlp[at, :] = (grad * pick(segments, table_ref, 4, 2, width)).astype(jnp.bfloat16)

        chunks(count, body)

    slope_copies = {}

    def expand(q):
        work[...] = product(hidden_two_ref[...], full[1, q])
        if q >= 2:
            slope_copies[q - 2].wait()

        def body(at):
            u = work[at, :]
            square = u * u
            bend = jnp.tanh(GELU_SCALE * (u + GELU_CUBE * (square * u)))
            active[q, at, :] = (0.5 * u * (1.0 + bend)).astype(jnp.bfloat16)
            inner = GELU_SCALE * (1.0 + 3.0 * GELU_CUBE * square)
            slope[q % 2, at, :] = 0.5 * (1.0 + bend) + 0.5 * u * (1.0 - bend * bend) * inner

        chunks(count, body)
        copy = pltpu.make_async_copy(slope.at[q % 2], slope_ref.at[q], slope_sem.at[q % 2])
        copy.start()
        slope_copies[q] = copy

    def down_grad(q):
        if q == 0:
            finish_sends(0)
            saves[0].wait()
        full[0, q] = product_by_rows(active[q], grad_mlp[...]).astype(jnp.bfloat16)
        copy = pltpu.make_async_copy(full.at[0, q], down_part_ref.at[q], grad_sem.at[q])
        copy.start()
        saves.append(copy)

    def contract():
        work[...] = product(active[0], full[2, 0])
        for q in (1, 2, 3):
            work[...] += product(active[q], full[2, q])

        def body(at):
            mlp = work[at, :]
            mlp_ref[at, :] = mlp
            gate = pick(seg_col_ref[at, :1], table_ref, 4, 2, width)
            out_ref[at, :] = (middle_ref[at, :] + gate * mlp).astype(jnp.bfloat16)

        chunks(count, body)

    extra = {
        0: [mod_start],
        1: [mod_cores],
        2: [mod_plane],
        3: [mod_line],
        4: [mod_last],
        5: [mod_end, first_norm, partial(complete, 0), project],
        6: [partial(attend, 0, 8)],
        7: [partial(attend, 8, 16)],
        8: [mix],
        9: [partial(complete, 1), partial(expand, 0), partial(expand, 1), partial(expand, 2)],
        10: [partial(expand, 3), partial(down_grad, 0), partial(down_grad, 1)],
        11: [partial(down_grad, 2), partial(down_grad, 3)],
        13: [partial(complete, 2), contract],
    }
    order = [(a, k) for a in range(3) for k in range(4)]
    for i in range(len(order) + 2):
        if i < len(order):
            if order[i][1] == 0:
                own(order[i][0])
            spread(*order[i])
        if 1 <= i < len(order) + 1:
            forward(*order[i - 1])
        if 2 <= i:
            finish(*order[i - 2])
        for step in extra.get(i, ()):
            step()
    for copy in saves[1:]:
        copy.wait()
    for q in (2, 3):
        slope_copies[q].wait()
    for a in (1, 2, "other"):
        finish_sends(a)


def run_forward(shards, down, acts, ada, tokens, cot, seg_col, seg_row, bins, share):
    count, width = tokens.shape
    dma = pltpu.SemaphoreType.DMA
    low, wide = jnp.bfloat16, jnp.float32
    side = ada.shape[1] // 2
    vmem, any_ = pl.BlockSpec(memory_space=pltpu.VMEM), pl.BlockSpec(memory_space=pl.ANY)
    out = jax.ShapeDtypeStruct
    return pl.pallas_call(
        partial(forward_kernel, share),
        out_shape=(
            out((3, 4, width, width), low),
            out((4, width, width), low),
            out((4, count, width), wide),
            out((count, width), low),
            out((count, width), low),
            out((2, 2 * count, width), low),
            out((count, 128), wide),
            out((count, width), low),
            out((count, width), wide),
            out((count, width), wide),
            out((count, width), low),
            out((count, width), wide),
            out((count, width), low),
            out((8, side), wide),
            out((CHIPS, 16, 128), low),
            out((8, 128), wide),
            out((count, width), low),
            out((2, 8, count), jnp.int32),
        ),
        in_specs=[vmem] * 9,
        out_specs=[any_] * 3 + [vmem] * 15,
        scratch_shapes=[
            pltpu.VMEM((3, 4, width, width), low),
            pltpu.VMEM((2, 4 * PAD, width), low),
            pltpu.VMEM((CHIPS * 8, side), wide),
            pltpu.VMEM((CHIPS * 8, BAND), wide),
            pltpu.VMEM((CHIPS * 8, BAND), wide),
            pltpu.VMEM((4, 8, BAND), wide),
            pltpu.VMEM((4, 8, BAND), wide),
            pltpu.VMEM((4, 8, BAND), wide),
            pltpu.VMEM((3, 8, BAND), wide),
            pltpu.VMEM((2, 8, BAND), wide),
            pltpu.VMEM((count, 2 * count), wide),
            pltpu.VMEM((count, width), wide),
            pltpu.VMEM((4, count, width), low),
            pltpu.VMEM((2, count, width), wide),
            dma((2, 3)), dma((2, 3)), dma((3, 4, 2)), dma((3, 4)), dma((3, 4, 2)), dma((3, 4)),
            dma((3, 4, 2)), dma((3, 4, 2)), dma((3, 4, 2)), dma((3, 4, 2)),
            dma((3, 4)), dma((3, 4)), dma((3, 4)), dma((3, 4)),
            dma((3, 4, 4)), dma((3, 4, 4)),
            dma((CHIPS - 1,)), dma((CHIPS - 1,)), dma, dma, dma((4,)), dma((4,)),
            dma((4,)), dma((4,)), dma((4,)), dma((4,)), dma((3,)), dma((3,)), dma, dma, dma, dma,
            dma((2,)), dma((2,)), dma((3,)), dma((4,)), dma((2,)),
        ],
        compiler_params=pltpu.CompilerParams(
            collective_id=0, has_side_effects=True, vmem_limit_bytes=63 * 2**20
        ),
        name="forward",
    )(shards, down, acts, ada, tokens, cot, seg_col, seg_row, bins)


def add_rows(dst, sources, start, rows):
    def body(i, carry):
        where = pl.ds(pl.multiple_of(start + i * 16, 16), 16)
        total = dst[where, :].astype(jnp.float32)
        for source in sources:
            total = total + source[where, :].astype(jnp.float32)
        dst[where, :] = total.astype(dst.dtype)
        return carry

    lax.fori_loop(0, rows // 16, body, 0)


def split_low(values):
    high = values.astype(jnp.bfloat16)
    return high, (values - high.astype(jnp.float32)).astype(jnp.bfloat16)


def backward_kernel(share, weights_ref, down_part_ref, slope_ref, middle_ref, attended_ref, mlp_ref,
                    hidden_ref, query_ref, sides_ref, total_ref, context_ref, hidden_two_ref,
                    grad_mlp_ref, table_ref, conds_ref, level_ref, seg_all_ref, seg_col_ref, tokens_ref,
                    cot_ref, ada_ref,
                    mixer_part_ref, up_part_ref, rows_ref, down_ref, tokens_grad_ref, ada_grad_ref, silu_ref,
                    held, from_core, diag, from_x, from_y, from_z, spare, block, part, quad, lows,
                    work, grad_middle, grad_context, leave, enter, bias, sums, sums_row, sums_core, band, silu_part,
                    *sems):
    (
        load_sem, c_send, c_recv, dx_send, dx_recv, dy_send, dy_recv, x_send, x_recv,
        y_send, y_recv, z_send, z_recv, group_send, group_recv, block_sem, part_sem, quad_sem,
        side_send, side_recv, m_send, m_recv, mz_send, mz_recv, mx_send, mx_recv, my_send, my_recv,
        md_send, md_recv, mc_send, mc_recv, s_send, s_recv, sc_send, sc_recv,
    ) = sems
    z, y, x, c = position()
    me = z * 4 + y * 2 + x
    group = x * 2 + c
    rows = 4 * share
    count, width = tokens_ref.shape
    halves = (pl.ds(0, NEAR[0]), pl.ds(NEAR[0], rows - NEAR[0]))
    x_peer, y_peer, c_peer = device(z, y, 1 - x, c), device(z, 1 - y, x, c), device(z, y, x, 1 - c)
    partners = [(x, 1 - c), (1 - x, c), (1 - x, 1 - c)]
    greet(
        [((me + k) % CHIPS, c) for k in range(1, CHIPS)] + [c_peer, device(z, y, 1 - x, 1 - c)]
    )
    sends = {}

    def send(owner, *args):
        copy = remote(*args)
        copy.start()
        sends.setdefault(owner, []).append(copy)

    def finish_sends(owner):
        for copy in sends.pop(owner, []):
            copy.wait_send()

    order = [(a, k) for a in (2, 1, 0) for k in (1, 2, 3, 0)]
    given = (mixer_part_ref, up_part_ref, down_part_ref)
    loads = {}

    def begin(i):
        a, k = order[i]
        finish_sends(("held", i - 5))
        zz = (z + k) % 4
        for pos, (oy, ox) in enumerate(PLACES):
            yy = 1 - y if oy else y
            xx = 1 - x if ox else x
            for core in (0, 1):
                cc = 1 - c if core else c
                where, row = block_of(a, zz * 2 + yy, xx * 2 + cc)
                src = given[a].at[where, pl.ds(pl.multiple_of(row * rows, 16), rows)]
                if core:
                    send("core", src, from_core.at[i % 4, pos], c_send.at[i, pos], c_recv.at[i, pos], c_peer)
                else:
                    loads[i, pos] = pltpu.make_async_copy(src, held.at[i % 5, pos], load_sem.at[i, pos])
                    loads[i, pos].start()

    def pair(i):
        for pos in (3, 1, 2, 0):
            loads[i, pos].wait()
            arrive(from_core.at[i % 4, pos], c_recv.at[i, pos], c_peer)
            add_rows(held.at[i % 5, pos], [from_core.at[i % 4, pos]], 0, rows)
            mine = held.at[i % 5, pos]
            top, low = mine.at[halves[0]], mine.at[halves[1]]
            if pos == 3:
                send(("held", i), top, diag.at[i % 4, halves[0]], dy_send.at[i], dy_recv.at[i], y_peer)
                send(("held", i), low, diag.at[i % 4, halves[1]], dx_send.at[i], dx_recv.at[i], x_peer)
            if pos == 1:
                send(("held", i), low, from_x.at[i % 5, halves[1]], x_send.at[i, 1], x_recv.at[i, 1], x_peer)
            if pos == 2:
                send(("held", i), top, from_y.at[i % 5, halves[0]], y_send.at[i, 0], y_recv.at[i, 0], y_peer)

    def relay(i):
        far = diag.at[i % 4]
        arrive(far.at[halves[0]], dy_recv.at[i], y_peer)
        add_rows(held.at[i % 5, 1], [far], 0, NEAR[0])
        top = held.at[i % 5, 1, halves[0]]
        send(("held", i), top, from_x.at[i % 5, halves[0]], x_send.at[i, 0], x_recv.at[i, 0], x_peer)
        arrive(far.at[halves[1]], dx_recv.at[i], x_peer)
        add_rows(held.at[i % 5, 2], [far], NEAR[0], rows - NEAR[0])
        low = held.at[i % 5, 2, halves[1]]
        send(("held", i), low, from_y.at[i % 5, halves[1]], y_send.at[i, 1], y_recv.at[i, 1], y_peer)

    def plane(i):
        a, k = order[i]
        for h in (0, 1):
            arrive(from_x.at[i % 5, halves[h]], x_recv.at[i, h], x_peer)
            arrive(from_y.at[i % 5, halves[h]], y_recv.at[i, h], y_peer)
        mine = held.at[i % 5, 0]
        if k:
            add_rows(mine, [from_x.at[i % 5], from_y.at[i % 5]], 0, rows)
            send(("held", i), mine, from_z.at[a, k - 1], z_send.at[a, k - 1], z_recv.at[a, k - 1], device((z + k) % 4, y, x, c))
            return
        for j in (1, 2, 3):
            arrive(from_z.at[a, j - 1], z_recv.at[a, j - 1], device((z - j + 4) % 4, y, x, c))

        def body(at):
            total = mine[at, :].astype(jnp.float32)
            total = total + from_x[i % 5, at, :].astype(jnp.float32)
            total = total + from_y[i % 5, at, :].astype(jnp.float32)
            for j in range(3):
                total = total + from_z[a, j, at, :].astype(jnp.float32)
            if a == 2:
                down_ref[at, :] = total
            else:
                mine[at, :] = total.astype(jnp.bfloat16)

        chunks(rows, body)
        if a == 2:
            return
        spare[a] = product_by_rows(row_selector(rows, share), mine[...]).astype(jnp.bfloat16)
        for j, (px, pc) in enumerate(partners):
            send(
                "end",
                spare.at[a, pl.ds(pl.multiple_of((px * 2 + pc) * PAD, 16), PAD)],
                rows_ref.at[a, group],
                group_send.at[a, j],
                group_recv.at[a, j],
                device(z, y, px, pc),
            )
        rows_ref[a, group] = spare[a, pl.ds(pl.multiple_of(group * PAD, 16), PAD), :]

    uses = [(2, q) for q in range(4)] + [(1, q) for q in range(4)] + [(0, 3), (0, 0), (0, 1), (0, 2)]
    coming = {}

    def fetch(n):
        if n < len(uses):
            copy = pltpu.make_async_copy(weights_ref.at[uses[n]], block.at[n % 2], block_sem.at[n % 2])
            copy.start()
            coming[n] = copy

    def take(n):
        coming[n].wait()
        return block[n % 2]

    going = {}

    def put(n, left, right, target):
        if n - 2 in going:
            going.pop(n - 2).wait()

        def body(i, carry):
            columns = pl.ds(pl.multiple_of(i * 384, 128), 384)
            part[n % 2, columns, :] = product_by_rows(left[:, columns], right[...]).astype(jnp.bfloat16)
            return carry

        lax.fori_loop(0, width // 384, body, 0)
        going[n] = pltpu.make_async_copy(part.at[n % 2], target, part_sem.at[n % 2])
        going[n].start()

    quads = {}

    def slopes(q):
        quads[q] = pltpu.make_async_copy(slope_ref.at[q], quad.at[q], quad_sem.at[q])
        quads[q].start()

    def through_down(q):
        work[...] = product_by_columns(grad_mlp_ref[...], take(q))
        fetch(q + 2)
        quads[q].wait()

        def body(at):
            lows[q, at, :] = (work[at, :] * quad[q, at, :]).astype(jnp.bfloat16)

        chunks(count, body)
        if q < 3:
            source = (middle_ref, attended_ref, mlp_ref)[q]
            quads[q] = pltpu.make_async_copy(source, quad.at[q], quad_sem.at[q])
            quads[q].start()

    def up_grad(q):
        put(q, hidden_two_ref, lows.at[q], up_part_ref.at[q])

    def through_up(q):
        value = product_by_columns(lows[q], take(4 + q))
        work[...] = work[...] + value if q else value
        fetch(6 + q)

    def norm_pull(grad, value, inverse):
        return inverse * (
            grad
            - jnp.mean(grad, axis=-1, keepdims=True)
            - value * jnp.mean(grad * value, axis=-1, keepdims=True)
        )

    def add_sums(segments, which, value):
        for crop in range(CROPS):
            kept = jnp.where(segments == crop, value, 0.0)
            sums[which, crop] = sums[which, crop] + kept[:8] + kept[8:]

    def second_norm():
        for q in range(3):
            quads[q].wait()
        sums[...] = jnp.zeros_like(sums)

        def body(at):
            segments = seg_col_ref[at, :1]
            grad = work[at, :]
            value, inverse = normed(quad[0, at, :])
            level = level_ref[3:4, :1]
            for crop in (2, 1, 0):
                level = jnp.where(segments == crop, level_ref[crop : crop + 1, :1], level)
            grad_out = cot_ref[at, :].astype(jnp.float32) * level
            add_sums(segments, 3, grad)
            add_sums(segments, 4, grad * value)
            add_sums(segments, 5, grad_out * quad[2, at, :])
            scaled = grad * (1.0 + pick(segments, table_ref, 4, 1, width))
            total = grad_out + norm_pull(scaled, value, inverse)
            grad_middle[at, :] = total
            add_sums(segments, 2, total * quad[1, at, :])
            lows[3, at, :] = (total * pick(segments, table_ref, 0, 2, width)).astype(jnp.bfloat16)

        chunks(count, body)

    def through_out():
        grad_context[...] = product_by_columns(lows[3], take(8)).astype(jnp.bfloat16)
        fetch(10)
        put(4, context_ref, lows.at[3], mixer_part_ref.at[3])
        for h in (0, 1):
            same = seg_col_ref[:, :1] == seg_all_ref[h][:1, :]
            bias[:, h * count : (h + 1) * count] = jnp.where(same, 0.0, LARGE_NEGATIVE)

    def attend_back(first, last):
        size = width // HEADS
        scale = 1.0 / math.sqrt(size)

        def body(head, carry):
            columns, inside = window_of(head, size, width)
            query, keys = query_ref[:, columns], sides_ref[0, :, columns]
            grad = grad_context[:, columns]
            scores = product_by_columns(jnp.where(inside, query, jnp.zeros_like(query)), keys)
            lane = lax.broadcasted_iota(jnp.int32, (1, 128), 1)
            total = jnp.sum(jnp.where(lane == head, total_ref[...], 0.0), axis=-1, keepdims=True)
            chance = jnp.exp(scores * scale + bias[...] - total)
            pulled = product_by_columns(
                jnp.where(inside, grad, jnp.zeros_like(grad)), sides_ref[1, :, columns]
            )
            inner = jnp.sum(chance * pulled, axis=-1, keepdims=True)
            grad_scores = (chance * (pulled - inner)).astype(jnp.bfloat16)
            grad_query = (product(grad_scores, keys) * scale).astype(jnp.bfloat16)
            lows[0, :, columns] = jnp.where(inside, grad_query, lows[0, :, columns])
            grad_key = product_by_rows(grad_scores, query) * scale
            grad_value = product_by_rows(chance.astype(jnp.bfloat16), grad)
            for h in (0, 1):
                here = slice(h * count, (h + 1) * count)
                quad[h, :, columns] = jnp.where(inside, grad_key[here], quad[h, :, columns])
                quad[2 + h, :, columns] = jnp.where(inside, grad_value[here], quad[2 + h, :, columns])
            return carry

        lax.fori_loop(first, last, body, 0)

    def swap_sides():
        for j in (0, 1):
            leave[j] = quad[2 * j + 1 - c].astype(jnp.bfloat16)
            send("end", leave.at[j], enter.at[j], side_send.at[j], side_recv.at[j], c_peer)

    def query_grad():
        put(5, hidden_ref, lows.at[0], mixer_part_ref.at[0])

    def sides_grad():
        for j in (0, 1):
            arrive(enter.at[j], side_recv.at[j], c_peer)

            def body(at):
                total = quad[2 * j + c, at, :] + enter[j, at, :].astype(jnp.float32)
                lows[1 + j, at, :] = total.astype(jnp.bfloat16)

            chunks(count, body)
            put(6 + j, hidden_ref, lows.at[1 + j], mixer_part_ref.at[1 + j])

    def through_qkv():
        for q in range(3):
            value = product_by_columns(lows[q], take(9 + q))
            work[...] = work[...] + value if q else value
            fetch(11 + q)

    def first_norm():
        def body(at):
            segments = seg_col_ref[at, :1]
            grad = work[at, :]
            value, inverse = normed(tokens_ref[at, :].astype(jnp.float32))
            add_sums(segments, 0, grad)
            add_sums(segments, 1, grad * value)
            scaled = grad * (1.0 + pick(segments, table_ref, 0, 1, width))
            tokens_grad_ref[at, :] = grad_middle[at, :] + norm_pull(scaled, value, inverse)

        chunks(count, body)
        for which in range(6):
            for crop in range(CROPS):
                row = which // 3 * CROPS + crop
                columns = slice(which % 3 * width, (which % 3 + 1) * width)
                sums_row[row : row + 1, columns] = jnp.sum(sums[which, crop], axis=0, keepdims=True)
        send("end", sums_row, sums_core, m_send, m_recv, c_peer)

    side = sums_row.shape[1]

    def place(k, other_y, other_x):
        zz = (z - k + 4) % 4
        yy = 1 - y if other_y else y
        xx = 1 - x if other_x else x
        return band.at[c, pl.ds(pl.multiple_of((zz * 4 + yy * 2 + xx) * 8, 8), 8)]

    def sums_start():
        arrive(sums_core, m_recv, c_peer)
        near = pl.ds(pl.multiple_of(c * (side - BAND), 128), BAND)
        band[c, pl.ds(pl.multiple_of(me * 8, 8), 8), :] = sums_row[:, near] + sums_core[:, near]
        mine = place(0, 0, 0)
        for k in (1, 2, 3):
            send("end", mine, mine, mz_send.at[k - 1], mz_recv.at[k - 1], device((z + k) % 4, y, x, c))
        send("end", mine, mine, mx_send.at[0], mx_recv.at[0], x_peer)
        send("end", mine, mine, my_send.at[0], my_recv.at[0], y_peer)

    def sums_line():
        for k in (1, 2, 3):
            piece = place(k, 0, 0)
            arrive(piece, mz_recv.at[k - 1], device((z - k + 4) % 4, y, x, c))
            send("end", piece, piece, mx_send.at[k], mx_recv.at[k], x_peer)
            send("end", piece, piece, my_send.at[k], my_recv.at[k], y_peer)

    def sums_plane():
        for k in range(4):
            from_side, from_up = place(k, 0, 1), place(k, 1, 0)
            arrive(from_side, mx_recv.at[k], x_peer)
            arrive(from_up, my_recv.at[k], y_peer)
            if k % 2:
                send("end", from_side, from_side, md_send.at[k], md_recv.at[k], y_peer)
            else:
                send("end", from_up, from_up, md_send.at[k], md_recv.at[k], x_peer)

    def sums_cores():
        for k in range(4):
            arrive(place(k, 1, 1), md_recv.at[k], y_peer if k % 2 else x_peer)
        send("end", band.at[c], band.at[c], mc_send, mc_recv, c_peer)

    def condition():
        arrive(band.at[1 - c], mc_recv, c_peer)
        acts = conds_ref[:, :8, :].astype(jnp.float32).reshape(CHIPS * 8, 128)
        row = lax.broadcasted_iota(jnp.int32, acts.shape, 0) % 8
        acts = jnp.where(row < CROPS, acts, 0.0)
        upper = acts.astype(jnp.bfloat16)
        lower = pltpu.roll(acts, CROPS, 0).astype(jnp.bfloat16)
        sides = [jnp.zeros((CHIPS * 8, 128), jnp.float32)] * 2
        for at, source, skip, size in ((0, 0, 0, BAND), (BAND, 1, 2 * BAND - side, side - BAND)):
            terms = split_low(band[source, :, skip : skip + size])
            for which, act in enumerate((upper, lower)):
                columns = slice(which * side + at, which * side + at + size)
                value = product_by_rows(act, terms[0]) + product_by_rows(act, terms[1])
                ada_grad_ref[:, columns] = value[: ada_grad_ref.shape[0]]
                for term in terms:
                    sides[which] = sides[which] + product_by_columns(term, ada_ref[:, columns])
        silu_part[...] = sides[0] + pltpu.roll(sides[1], CHIPS * 8 - CROPS, 0)
        silu_ref[c, me] = silu_part[pl.ds(pl.multiple_of(me * 8, 8), 8), :]
        for k in range(1, CHIPS):
            to = (me + k) % CHIPS
            src = silu_part.at[pl.ds(pl.multiple_of(to * 8, 8), 8)]
            send("end", src, silu_ref.at[c, me], s_send.at[k - 1], s_recv.at[k - 1], (to, c))

    def condition_cores():
        for k in range(1, CHIPS):
            source = (me - k + CHIPS) % CHIPS
            arrive(silu_ref.at[c, source], s_recv.at[k - 1], (source, c))
        send("end", silu_ref.at[c], silu_ref.at[c], sc_send, sc_recv, c_peer)

    extra = {
        0: [partial(through_down, 0), partial(through_down, 1)],
        1: [partial(through_down, 2), partial(through_down, 3), partial(up_grad, 0)],
        2: [partial(up_grad, 1), partial(up_grad, 2), partial(up_grad, 3)],
        3: [partial(through_up, q) for q in range(4)] + [second_norm],
        4: [through_out, partial(attend_back, 0, 4)],
        5: [partial(attend_back, 4, 12)],
        6: [partial(attend_back, 12, 16), swap_sides, query_grad, sides_grad],
        7: [through_qkv, first_norm],
        8: [sums_start],
        9: [sums_line],
        10: [sums_plane],
        11: [sums_cores],
        12: [condition],
        13: [condition_cores],
    }
    begin(0)
    for q in range(4):
        slopes(q)
    fetch(0)
    fetch(1)
    for i in range(len(order) + 2):
        if i + 1 < len(order):
            if (i + 1) % 4 == 0:
                for n in sorted(going):
                    going.pop(n).wait()
            begin(i + 1)
        if i < len(order):
            pair(i)
        if 1 <= i < len(order) + 1:
            relay(i - 1)
        if 2 <= i:
            plane(i - 2)
        for step in extra.get(i, ()):
            step()
    for a in range(2):
        for j, (px, pc) in enumerate(partners):
            arrive(rows_ref.at[a, px * 2 + pc], group_recv.at[a, j], device(z, y, px, pc))
    arrive(silu_ref.at[1 - c], sc_recv, c_peer)
    for owner in list(sends):
        finish_sends(owner)


def run_backward(given, share):
    (weights, down_part, slope, middle, attended, mlp, hidden, query, sides, total, context, hidden_two,
     grad_mlp, table, conds, level, seg_all, seg_col, tokens, cot, ada) = given
    count, width = tokens.shape
    rows, side = 4 * share, ada.shape[1] // 2
    dma = pltpu.SemaphoreType.DMA
    low, wide = jnp.bfloat16, jnp.float32
    vmem, any_ = pl.BlockSpec(memory_space=pltpu.VMEM), pl.BlockSpec(memory_space=pl.ANY)
    out, buffer = jax.ShapeDtypeStruct, pltpu.VMEM
    slots = 12
    return pl.pallas_call(
        partial(backward_kernel, share),
        out_shape=(
            out((4, width, width), low),
            out((4, width, width), low),
            out((2, 4, PAD, width), low),
            out((rows, width), wide),
            out((count, width), wide),
            out((-(-share // 8) * 8, ada.shape[1]), wide),
            out((2, CHIPS, 8, 128), wide),
        ),
        in_specs=[any_] * 6 + [vmem] * 15,
        out_specs=[any_] * 2 + [vmem] * 5,
        scratch_shapes=[
            buffer((5, 4, rows, width), low),
            buffer((4, 4, rows, width), low),
            buffer((4, rows, width), low),
            buffer((5, rows, width), low),
            buffer((5, rows, width), low),
            buffer((3, 3, rows, width), low),
            buffer((2, 4 * PAD, width), low),
            buffer((2, width, width), low),
            buffer((2, width, width), low),
            buffer((4, count, width), wide),
            buffer((4, count, width), low),
            buffer((count, width), wide),
            buffer((count, width), wide),
            buffer((count, width), low),
            buffer((2, count, width), low),
            buffer((2, count, width), low),
            buffer((count, 2 * count), wide),
            buffer((6, CROPS, 8, width), wide),
            buffer((8, side), wide),
            buffer((8, side), wide),
            buffer((2, CHIPS * 8, BAND), wide),
            buffer((CHIPS * 8, 128), wide),
            dma((slots, 4)), dma((slots, 4)), dma((slots, 4)),
            dma((slots,)), dma((slots,)), dma((slots,)), dma((slots,)),
            dma((slots, 2)), dma((slots, 2)), dma((slots, 2)), dma((slots, 2)),
            dma((3, 3)), dma((3, 3)), dma((2, 3)), dma((2, 3)), dma((2,)), dma((2,)), dma((4,)),
            dma((2,)), dma((2,)), dma, dma, dma((3,)), dma((3,)), dma((4,)), dma((4,)), dma((4,)), dma((4,)),
            dma((4,)), dma((4,)), dma, dma, dma((CHIPS - 1,)), dma((CHIPS - 1,)), dma, dma,
        ],
        compiler_params=pltpu.CompilerParams(
            collective_id=1, has_side_effects=True, vmem_limit_bytes=63 * 2**20
        ),
        name="backward",
    )(*given)


def layer_norm(values):
    center = values - jnp.mean(values, axis=-1, keepdims=True)
    inverse = lax.rsqrt(jnp.mean(center * center, axis=-1, keepdims=True) + EPSILON)
    return (center * inverse, inverse)


def norm_back(grad_normed, normed, inverse):
    return inverse * (
        grad_normed
        - jnp.mean(grad_normed, axis=-1, keepdims=True)
        - normed * jnp.mean(grad_normed * normed, axis=-1, keepdims=True)
    )


def to_heads(array):
    return array.reshape(array.shape[0], HEADS, array.shape[1] // HEADS)


def dots(spec, left, right):
    return jnp.einsum(spec, left, right, preferred_element_type=jnp.float32)


def masked_scores(query_heads, key_heads, same_crop):
    scale_factor = 1.0 / math.sqrt(query_heads.shape[-1])
    scores = dots("qhd,khd->hqk", query_heads, key_heads) * scale_factor
    return jnp.where(same_crop[None], scores, LARGE_NEGATIVE)


def attend(query_seq, key_seq, value_seq, same_crop):
    scores = masked_scores(to_heads(query_seq), to_heads(key_seq), same_crop)
    row_max = jnp.max(scores, axis=-1, keepdims=True)
    raised = jnp.exp(scores - row_max)
    row_total = jnp.sum(raised, axis=-1, keepdims=True)
    probability = (raised / row_total).astype(jnp.bfloat16)
    context = dots("hqk,khd->qhd", probability, to_heads(value_seq))
    return (context.reshape(query_seq.shape[0], -1), (row_max + jnp.log(row_total))[..., 0])


def attend_back(query_seq, key_seq, value_seq, same_crop, log_total, grad_seq):
    query_heads = to_heads(query_seq)
    key_heads = to_heads(key_seq)
    value_heads = to_heads(value_seq)
    grad_heads = to_heads(grad_seq)
    scale_factor = 1.0 / math.sqrt(query_heads.shape[-1])
    scores = masked_scores(query_heads, key_heads, same_crop)
    probability = jnp.exp(scores - log_total[..., None])
    grad_prob = dots("qhd,khd->hqk", grad_heads, value_heads)
    inner = jnp.sum(probability * grad_prob, axis=-1, keepdims=True)
    grad_scores = (probability * (grad_prob - inner)).astype(jnp.bfloat16)
    grad_query = dots("hqk,khd->qhd", grad_scores, key_heads) * scale_factor
    grad_key = dots("hqk,qhd->khd", grad_scores, query_heads) * scale_factor
    grad_value = dots("hqk,qhd->khd", probability.astype(jnp.bfloat16), grad_heads)
    rows_here = query_seq.shape[0]
    rows_whole = key_seq.shape[0]
    return (
        grad_query.reshape(rows_here, -1),
        grad_key.reshape(rows_whole, -1),
        grad_value.reshape(rows_whole, -1),
    )


def kernel_inputs(segments, conditions, noise_bins, bin_counts, ada_weight, first, up_weight):
    share, width = first.shape[0], first.shape[1] // 4
    cores = lax.axis_size("sp")
    shards = jnp.stack([first, up_weight]).reshape(2, share, 4, width)
    shards = jnp.pad(shards.transpose(0, 2, 1, 3), ((0, 0), (0, 0), (0, PAD - share), (0, 0)))
    acts = jax.nn.silu(conditions.astype(jnp.float32)).astype(jnp.bfloat16)
    acts = acts.reshape(CROPS, CHIPS, cores, share)
    acts = lax.dynamic_index_in_dim(acts, lax.axis_index("sp"), 2, keepdims=False)
    acts = jnp.pad(acts.transpose(1, 0, 2), ((0, 0), (0, 0), (0, 128 - share)))
    counts = jnp.pad(bin_counts.astype(jnp.bfloat16), (0, 128 - NBINS))
    counts = jnp.broadcast_to(counts, (CHIPS, 1, 128))
    acts = jnp.pad(jnp.concatenate([acts, counts], axis=1), ((0, 0), (0, 11), (0, 0)))
    ada = jnp.pad(ada_weight, ((0, 128 - share), (0, 0)))
    count = segments.shape[0]
    seg_col = jnp.broadcast_to(segments[:, None], (count, 128))
    seg_row = jnp.broadcast_to(segments[None, :], (8, count))
    bins = jnp.pad(noise_bins, (0, 4), constant_values=-1)
    bins = (bins[:, None] == jnp.arange(128, dtype=jnp.int32)).astype(jnp.float32)
    return shards, acts, ada, seg_col, seg_row, bins


def forward_plain(tokens_float, segments, conditions, noise_bins, bin_counts, ada_weight, first, up_weight,
                  down_weight):
    groups, cores = lax.axis_size("dp"), lax.axis_size("sp")
    share, width = first.shape[0], tokens_float.shape[1]
    index = lax.axis_index("dp") * cores + lax.axis_index("sp")
    mixers = lax.all_gather(first, ("dp", "sp"), axis=0, tiled=True)
    uppers = lax.all_gather(up_weight, ("dp", "sp"), axis=0, tiled=True)
    downers = lax.all_gather(down_weight, ("dp", "sp"), axis=0, tiled=True)
    mixers = mixers.reshape(width, 4, width).transpose(1, 0, 2)
    uppers = uppers.reshape(width, 4, width).transpose(1, 0, 2)
    downers = downers.reshape(4, width, width)
    bin_total = lax.psum(bin_counts, "dp")
    bin_weight = 40.0 * groups / bin_total.astype(jnp.float32)
    crop_weight = jnp.sum(
        jnp.where(noise_bins[:, None] == jnp.arange(NBINS, dtype=jnp.int32), bin_weight, 0.0),
        axis=-1,
    )
    cond_all = lax.all_gather(conditions, "dp", axis=0, tiled=True)
    cond_here = lax.dynamic_slice_in_dim(cond_all, index * share, share, axis=1)
    cond_act = jax.nn.silu(cond_here.astype(jnp.float32)).astype(jnp.bfloat16)
    modulation_part = dots("sd,df->sf", cond_act, ada_weight).reshape(groups, CROPS, -1)
    modulation = lax.psum(lax.psum_scatter(modulation_part, "dp", scatter_dimension=0), "sp")
    selector = (segments[:, None] == jnp.arange(CROPS, dtype=jnp.int32)).astype(jnp.float32)
    per_token = jnp.einsum("tc,cf->tf", selector, modulation, precision=lax.Precision.HIGHEST)
    shift_one, scale_one, gate_one, shift_two, scale_two, _ = jnp.split(per_token, 6, axis=-1)
    normed_one, _ = layer_norm(tokens_float)
    hidden_one = (normed_one * (1.0 + scale_one) + shift_one).astype(jnp.bfloat16)
    projected = dots("td,qdf->qtf", hidden_one, mixers[:3]).astype(jnp.bfloat16)
    sides = lax.all_gather(projected[1:], "sp", axis=1, tiled=True)
    all_segments = lax.all_gather(segments, "sp", axis=0, tiled=True)
    same_crop = segments[:, None] == all_segments[None, :]
    context, log_total = attend(projected[0], sides[0], sides[1], same_crop)
    context_low = context.astype(jnp.bfloat16)
    attended = dots("td,df->tf", context_low, mixers[3])
    middle = tokens_float + gate_one * attended
    normed_two, _ = layer_norm(middle)
    hidden_two = (normed_two * (1.0 + scale_two) + shift_two).astype(jnp.bfloat16)
    upper_in = dots("td,qdf->qtf", hidden_two, uppers)
    activated = jax.nn.gelu(upper_in, approximate=True).astype(jnp.bfloat16)
    slope = jax.vjp(partial(jax.nn.gelu, approximate=True), upper_in)[1](jnp.ones_like(upper_in))[0]
    mlp_out = dots("qtf,qfd->td", activated, downers)
    return (
        (mixers, uppers, downers), activated, slope, hidden_one, projected[0], sides, log_total,
        context_low, attended, middle, hidden_two, mlp_out, modulation, cond_act, crop_weight, same_crop,
    )


def layer_plain(tokens_float, segments, conditions, noise_bins, bin_counts, cotangent, ada_weight, first,
                up_weight, down_weight):
    width = tokens_float.shape[1]
    (
        (mixers, uppers, downers), activated, slope, hidden_one, queries, sides, log_total,
        context_low, attended, middle, hidden_two, mlp_out, modulation, cond_act, crop_weight, same_crop,
    ) = forward_plain(
        tokens_float, segments, conditions, noise_bins, bin_counts, ada_weight, first, up_weight,
        down_weight,
    )
    selector = (segments[:, None] == jnp.arange(CROPS, dtype=jnp.int32)).astype(jnp.float32)
    per_token = jnp.einsum("tc,cf->tf", selector, modulation, precision=lax.Precision.HIGHEST)
    _, scale_one, gate_one, _, scale_two, gate_two = jnp.split(per_token, 6, axis=-1)
    normed_one, inverse_one = layer_norm(tokens_float)
    normed_two, inverse_two = layer_norm(middle)

    token_weight = jnp.sum(selector * crop_weight[None, :], axis=-1)
    grad_out = cotangent.astype(jnp.float32) * token_weight[:, None]
    grad_mlp = (grad_out * gate_two).astype(jnp.bfloat16)
    tokens_out = (middle + gate_two * mlp_out).astype(jnp.bfloat16)
    down_part = dots("qtf,td->qfd", activated, grad_mlp).astype(jnp.bfloat16)
    grad_act = dots("td,qfd->qtf", grad_mlp, downers)
    grad_upper = (grad_act * slope).astype(jnp.bfloat16)
    up_part = dots("td,qtf->qdf", hidden_two, grad_upper).astype(jnp.bfloat16)
    grad_hidden_two = dots("qtf,qdf->td", grad_upper, uppers)
    grad_middle = grad_out + norm_back(grad_hidden_two * (1.0 + scale_two), normed_two, inverse_two)
    grad_attended = (grad_middle * gate_one).astype(jnp.bfloat16)
    grad_context = dots("tf,df->td", grad_attended, mixers[3]).astype(jnp.bfloat16)
    grad_query, grad_key, grad_value = attend_back(
        queries, sides[0], sides[1], same_crop, log_total, grad_context
    )
    grad_sides = lax.psum_scatter(
        jnp.stack([grad_key, grad_value]).astype(jnp.bfloat16),
        "sp",
        scatter_dimension=1,
        tiled=True,
    )
    grad_projected = jnp.concatenate([grad_query.astype(jnp.bfloat16)[None], grad_sides])
    out_part = dots("td,tf->df", context_low, grad_attended).astype(jnp.bfloat16)
    qkv_part = dots("td,qtf->qdf", hidden_one, grad_projected).astype(jnp.bfloat16)
    first_part = jnp.concatenate([qkv_part, out_part[None]])
    grad_hidden_one = dots("qtf,qdf->td", grad_projected, mixers[:3])
    tokens_grad = grad_middle + norm_back(
        grad_hidden_one * (1.0 + scale_one), normed_one, inverse_one
    )

    joined = jnp.stack([first_part, up_part]).transpose(2, 0, 1, 3).reshape(width, 8 * width)
    rows = lax.psum_scatter(joined, ("dp", "sp"), scatter_dimension=0, tiled=True)
    rows = rows.astype(jnp.float32)
    first_grad, up_grad = rows[:, : 4 * width], rows[:, 4 * width :]
    down_grad = lax.psum_scatter(
        down_part.reshape(4 * width, width), ("dp", "sp"), scatter_dimension=0, tiled=True
    ).astype(jnp.float32)

    grad_per_token = jnp.concatenate(
        [
            grad_hidden_one,
            grad_hidden_one * normed_one,
            grad_middle * attended,
            grad_hidden_two,
            grad_hidden_two * normed_two,
            grad_out * mlp_out,
        ],
        axis=-1,
    )
    grad_modulation = lax.psum(
        jnp.einsum("tc,tf->cf", selector, grad_per_token, precision=lax.Precision.HIGHEST), "sp"
    )
    grad_rows = lax.all_gather(grad_modulation, "dp", axis=0, tiled=True)
    ada_grad = jnp.einsum(
        "sd,sf->df", cond_act.astype(jnp.float32), grad_rows, precision=lax.Precision.HIGHEST
    )
    silu_part = jnp.einsum(
        "sf,df->sd", grad_rows, ada_weight.astype(jnp.float32), precision=lax.Precision.HIGHEST
    )
    silu_all = lax.all_gather(silu_part, ("dp", "sp"), axis=0)
    silu_here = lax.dynamic_slice_in_dim(silu_all, lax.axis_index("dp") * CROPS, CROPS, axis=1)
    grad_silu = silu_here.transpose(1, 0, 2).reshape(CROPS, width)
    return tokens_out, tokens_grad, grad_silu, ada_grad, first_grad, up_grad, down_grad


def on_device(
    chips,
    tokens_in,
    segment_ids,
    conditions,
    noise_bins,
    bin_counts,
    cotangent,
    ada_weight,
    qkv_weight,
    out_weight,
    up_weight,
    down_weight,
):
    tokens_float = tokens_in[0].astype(jnp.float32)
    segments = segment_ids[0]
    width = tokens_float.shape[1]
    share = qkv_weight.shape[0]
    kernels = chips and 4 * share == down_weight.shape[0]
    first = jnp.concatenate([qkv_weight, out_weight], axis=1)
    if kernels:
        shards, acts, ada, seg_col, seg_row, bins = kernel_inputs(
            segments, conditions[0], noise_bins[0], bin_counts[0], ada_weight, first, up_weight
        )
        (
            weights, down_part, slope, hidden_one, queries, sides, log_total, context_low, attended,
            middle, hidden_two, mlp_out, tokens_out, table, conds, level, grad_mlp, seg_all,
        ) = run_forward(
            shards, down_weight, acts, ada, tokens_in[0], cotangent[0], seg_col, seg_row, bins, share
        )
        given = (
            weights, down_part, slope, middle, attended, mlp_out, hidden_one, queries, sides, log_total,
            context_low, hidden_two, grad_mlp, table, conds, level, seg_all, seg_col, tokens_in[0],
            cotangent[0], ada,
        )
        _, _, rows, down_grad, tokens_grad, ada_grad, silu_part = run_backward(given, share)
        rows = rows[:, :, :share].astype(jnp.float32).transpose(0, 2, 1, 3).reshape(2, share, 4 * width)
        first_grad, up_grad, ada_grad = rows[0], rows[1], ada_grad[:share]
        grad_silu = silu_part[:, :, :CROPS, :share].transpose(2, 1, 0, 3).reshape(CROPS, width)
    else:
        tokens_out, tokens_grad, grad_silu, ada_grad, first_grad, up_grad, down_grad = layer_plain(
            tokens_float, segments, conditions[0], noise_bins[0], bin_counts[0], cotangent[0],
            ada_weight, first, up_weight, down_weight,
        )
    silu_pull = jax.vjp(jax.nn.silu, conditions[0].astype(jnp.float32))[1]
    cond_grad = silu_pull(grad_silu)[0]
    return (
        tokens_out[None],
        tokens_grad[None],
        cond_grad[None],
        ada_grad,
        first_grad[:, : 3 * width],
        first_grad[:, 3 * width :],
        up_grad,
        down_grad,
    )


def solution(mesh):
    placed = (
        P("dp", "sp", None),
        P("dp", "sp"),
        P("dp", None, None),
        P("dp", None),
        P("dp", None),
        P("dp", "sp", None),
        P(("dp", "sp"), None),
        P(("dp", "sp"), None),
        P(("dp", "sp"), None),
        P(("dp", "sp"), None),
        P(("dp", "sp"), None),
    )
    return jax.shard_map(
        partial(on_device, mesh.shape["dp"] == 16 and mesh.shape["sp"] == 2),
        mesh=mesh,
        in_specs=placed,
        out_specs=(
            P("dp", "sp", None),
            P("dp", "sp", None),
            P("dp", None, None),
            P(("dp", "sp"), None),
            P(("dp", "sp"), None),
            P(("dp", "sp"), None),
            P(("dp", "sp"), None),
            P(("dp", "sp"), None),
        ),
        check_vma=False,
    )
```

```python
from functools import partial
import math

import jax
import jax.numpy as jnp
from jax import lax
from jax.experimental import pallas as pl
from jax.experimental.pallas import tpu as pltpu
from jax.sharding import PartitionSpec as P

HEADS = 16
CROPS = 4
NBINS = 8
EPSILON = 1e-06
LARGE_NEGATIVE = -1e30
GELU_SCALE = math.sqrt(2.0 / math.pi)
GELU_CUBE = 0.044715

MESH = pl.DeviceIdType.MESH
PAD = 48
NEAR = (80, 64)
FAR = (32, 32)
HELD = 6
BACKWARD_AFTER = (1, 4, 10, 17, 17, 19, 19, 19, 19, 20, 21, 23, 27, 31, 33, 35, 36, 36, 40, 42, 43, 49, 51, 51, 52, 53, 53, 55, 59, 60, 62, 69, 69, 69, 71, 78, 83, 91, 97, 102, 105)
CHIPS = 16
BAND = 1792
PLACES = ((0, 0), (0, 1), (1, 0), (1, 1))


def position():
    d = lax.axis_index("dp")
    c = lax.axis_index("sp")
    return d // 4, (d // 2) % 2, d % 2, c


def device(z, y, x, c):
    return (z * 4 + y * 2 + x, c)


def block_of(kind, zy, group):
    if kind == 2:
        return zy // 2, (zy % 2) * 4 + group
    return group, zy


def level_of(z, k):
    if k == 0:
        return z
    upper = z // 2
    inner = z * (1 - upper) + (3 - z) * upper
    step = k - inner if k == 1 else k
    return step * (1 - upper) + (3 - step) * upper


def greet(peers):
    barrier = pltpu.get_barrier_semaphore()
    for peer in peers:
        pl.semaphore_signal(barrier, inc=1, device_id=peer, device_id_type=MESH)
    pl.semaphore_wait(barrier, len(peers))


def remote(src, dst, send, recv, target):
    return pltpu.make_async_remote_copy(
        src_ref=src,
        dst_ref=dst,
        send_sem=send,
        recv_sem=recv,
        device_id=target,
        device_id_type=MESH,
    )


def arrive(ref, sem, target):
    remote(ref, ref, sem, sem, target).wait_recv()


def row_selector(rows, share):
    shape = (rows, 4 * PAD)
    row = lax.broadcasted_iota(jnp.int32, shape, 0)
    column = lax.broadcasted_iota(jnp.int32, shape, 1)
    picked = jnp.zeros(shape, jnp.bool_)
    for k in range(4):
        inside = (row >= k * share) & (row < (k + 1) * share)
        picked = picked | (inside & (column == row - k * share + k * PAD))
    return picked.astype(jnp.float32).astype(jnp.bfloat16)


def product(left, right):
    return jnp.dot(left, right, preferred_element_type=jnp.float32)


def product_by_rows(left, right):
    return lax.dot_general(left, right, (((0,), (0,)), ((), ())), preferred_element_type=jnp.float32)


def product_by_columns(left, right):
    return lax.dot_general(left, right, (((1,), (1,)), ((), ())), preferred_element_type=jnp.float32)


def chunks(rows, body, first=0, step=16):
    def run(i, carry):
        body(pl.ds(pl.multiple_of(first + i * step, step), step))
        return carry

    lax.fori_loop(0, rows // step, run, 0)


def normed(values):
    center = values - jnp.mean(values, axis=-1, keepdims=True)
    inverse = lax.rsqrt(jnp.mean(center * center, axis=-1, keepdims=True) + EPSILON)
    return center * inverse, inverse


def pick(segments, table, first, column, width):
    columns = slice(column * width, (column + 1) * width)
    value = table[first + 3 : first + 4, columns]
    for crop in (2, 1, 0):
        value = jnp.where(segments == crop, table[first + crop : first + crop + 1, columns], value)
    return value


def window_of(head, size, width):
    start = jnp.minimum((head * size) // 128, width // 128 - 2) * 128
    start = pl.multiple_of(start, 128)
    lane = lax.broadcasted_iota(jnp.int32, (1, 256), 1) + start
    return pl.ds(start, 256), (lane >= head * size) & (lane < (head + 1) * size)


def forward_kernel(share, shards_ref, down_ref, act_ref, ada_ref, tokens_ref, cot_ref, seg_col_ref,
                   seg_row_ref, bins_ref,
                   weights_ref, down_part_ref, slope_ref, hidden_ref, query_ref, sides_ref, total_ref,
                   context_ref, attended_ref, middle_ref, hidden_two_ref, mlp_ref, out_ref, table_ref,
                   conds_ref, level_ref, grad_mlp, seg_all,
                   full, stage, part, part_recv, band, band_diag, band_x, band_y, band_z, halves_of,
                   bias, work, active, slope, *sems):
    (
        group_send, group_recv, z_send, z_recv, zd_send, zd_recv, x_send, x_recv, y_send, y_recv,
        dx_send, dx_recv, dy_send, dy_recv, c_send, c_recv,
        cond_send, cond_recv, pc_send, pc_recv, pd_send, pd_recv, px_send, px_recv, py_send, py_recv,
        pz_send, pz_recv, pm_send, pm_recv, seg_send, seg_recv, kv_send, kv_recv,
        save_sem, grad_sem, slope_sem,
    ) = sems
    z, y, x, c = position()
    me = z * 4 + y * 2 + x
    group = x * 2 + c
    zy = z * 2 + y
    rows = 4 * share
    count, width = tokens_ref.shape
    x_peer, y_peer, c_peer = device(z, y, 1 - x, c), device(z, 1 - y, x, c), device(z, y, x, 1 - c)
    partners = [(x, 1 - c), (1 - x, c), (1 - x, 1 - c)]
    greet(
        [((me + k) % CHIPS, c) for k in range(1, CHIPS)] + [c_peer, device(z, y, 1 - x, 1 - c)]
    )
    sends = {a: [] for a in (0, 1, 2, "other")}

    def send(a, *args):
        copy = remote(*args)
        copy.start()
        sends[a].append((None, copy))

    def finish_sends(a):
        for go, copy in sends[a]:
            if go is None:
                copy.wait_send()
            else:
                pl.when(go)(copy.wait_send)
        sends[a] = []

    level = partial(level_of, z)

    def place(a, k, other_y, other_x, core=None, first=0, last=None):
        yy = 1 - y if other_y else y
        xx = 1 - x if other_x else x
        cc = c if core is None else core
        block, row = block_of(a, level(k) * 2 + yy, xx * 2 + cc)
        count = (rows if last is None else last) - first
        return full.at[a, block, pl.ds(pl.multiple_of(row * rows + first, 16), count)]

    def cuts(k):
        top, low = FAR if k else NEAR
        return top, rows - low

    def along(a, k, ref, send_sem, recv_sem):
        source = level(k)
        for way, step in ((0, 1), (1, -1)):
            to = z + step
            go = (to >= 0) & (to < 4)
            if k:
                go = go & ((source < z) if step == 1 else (source > z))
            copy = remote(ref, ref, send_sem.at[a, k, way], recv_sem.at[a, source], device(jnp.clip(to, 0, 3), y, x, c))
            pl.when(go)(copy.start)
            sends[a].append((go, copy))

    def from_line(a, k, ref, recv_sem):
        source = level(k)
        arrive(ref, recv_sem.at[a, source], device((z + 1) % 4, y, x, c))

    for a in range(2):
        for j, (px, pc) in enumerate(partners):
            send(
                "other",
                shards_ref.at[a, px * 2 + pc],
                stage.at[a, pl.ds(pl.multiple_of(group * PAD, 16), PAD)],
                group_send.at[a, j],
                group_recv.at[a, j],
                device(z, y, px, pc),
            )
    for k in range(1, CHIPS):
        to = (me + k) % CHIPS
        send("other", act_ref.at[to], conds_ref.at[me], cond_send.at[k - 1], cond_recv.at[k - 1], (to, c))
    seg_all[c] = seg_row_ref[...]
    send("other", seg_row_ref, seg_all.at[c], seg_send, seg_recv, c_peer)
    conds_ref[me] = act_ref[me]
    for a in range(2):
        stage[a, pl.ds(pl.multiple_of(group * PAD, 16), PAD), :] = shards_ref[a, group]

    def own(a):
        block, row = block_of(a, zy, group)
        here = pl.ds(pl.multiple_of(row * rows, 16), rows)
        if a < 2:
            for j, (px, pc) in enumerate(partners):
                arrive(
                    stage.at[a, pl.ds(pl.multiple_of((px * 2 + pc) * PAD, 16), PAD)],
                    group_recv.at[a, j],
                    device(z, y, px, pc),
                )
            full[a, block, here, :] = product(row_selector(rows, share), stage[a]).astype(jnp.bfloat16)
        else:
            full[a, block, here, :] = down_ref[...]
        along(a, 0, place(a, 0, 0, 0), z_send, z_recv)

    def to_core(a, k, pos):
        piece = place(a, k, *PLACES[pos])
        send(a, piece, piece, c_send.at[a, k, pos], c_recv.at[a, k, pos], c_peer)

    def spread(a, k):
        if k:
            from_line(a, k, place(a, k, 0, 0), z_recv)
            along(a, k, place(a, k, 0, 0), z_send, z_recv)
        top, low = cuts(k)
        for h, first, last in ((0, 0, top), (1, top, rows)):
            part = place(a, k, 0, 0, None, first, last)
            send(a, part, part, x_send.at[a, k, h], x_recv.at[a, k, h], x_peer)
        for h, first, last in ((1, low, rows), (0, 0, low)):
            part = place(a, k, 0, 0, None, first, last)
            send(a, part, part, y_send.at[a, k, h], y_recv.at[a, k, h], y_peer)
        to_core(a, k, 0)

    def forward(a, k):
        top, low = cuts(k)
        part = place(a, k, 0, 1, None, 0, top)
        arrive(part, x_recv.at[a, k, 0], x_peer)
        send(a, part, part, dy_send.at[a, k], dy_recv.at[a, k], y_peer)
        part = place(a, k, 1, 0, None, low, rows)
        arrive(part, y_recv.at[a, k, 1], y_peer)
        send(a, part, part, dx_send.at[a, k], dx_recv.at[a, k], x_peer)
        arrive(place(a, k, 0, 1, None, top, rows), x_recv.at[a, k, 1], x_peer)
        to_core(a, k, 1)
        arrive(place(a, k, 1, 0, None, 0, low), y_recv.at[a, k, 0], y_peer)
        to_core(a, k, 2)

    def finish(a, k):
        top, low = cuts(k)
        arrive(place(a, k, 1, 1, None, 0, top), dy_recv.at[a, k], y_peer)
        arrive(place(a, k, 1, 1, None, low, rows), dx_recv.at[a, k], x_peer)
        middle = place(a, k, 1, 1, None, FAR[0], rows - FAR[1])
        if k:
            from_line(a, k, middle, zd_recv)
        along(a, k, middle, zd_send, zd_recv)
        to_core(a, k, 3)

    saves = []

    def complete(a):
        for k in range(4):
            for pos, (oy, ox) in enumerate(PLACES):
                arrive(place(a, k, oy, ox, 1 - c), c_recv.at[a, k, pos], c_peer)
        copy = pltpu.make_async_copy(full.at[a], weights_ref.at[a], save_sem.at[a])
        copy.start()
        saves.append(copy)

    def mod_start():
        for k in range(1, CHIPS):
            source = (me - k + CHIPS) % CHIPS
            arrive(conds_ref.at[source], cond_recv.at[k - 1], (source, c))
        acts = conds_ref[:, :8, :].astype(jnp.float32).reshape(CHIPS * 8, 128)
        row = lax.broadcasted_iota(jnp.int32, acts.shape, 0) % 8
        upper = jnp.where(row < CROPS, acts, 0.0).astype(jnp.bfloat16)
        lower = pltpu.roll(jnp.where(row < CROPS, acts, 0.0), CROPS, 0).astype(jnp.bfloat16)
        side = ada_ref.shape[1] // 2
        part[...] = product(upper[:, :PAD], ada_ref[:, :side]) + product(lower[:, :PAD], ada_ref[:, side:])
        far = pl.ds(pl.multiple_of((1 - c) * (side - BAND), 128), BAND)
        send("other", part.at[:, far], part_recv, pc_send, pc_recv, c_peer)

    def block8(zz, yy, xx):
        return pl.ds(pl.multiple_of((zz * 4 + yy * 2 + xx) * 8, 8), 8)

    def mod_cores():
        arrive(part_recv, pc_recv, c_peer)
        side = ada_ref.shape[1] // 2
        near = pl.ds(pl.multiple_of(c * (side - BAND), 128), BAND)
        band[...] = part[:, near] + part_recv[...]
        for k in range(4):
            zz = (z + k) % 4
            src = band.at[block8(zz, 1 - y, 1 - x)]
            send("other", src, band_diag.at[k], pd_send.at[k], pd_recv.at[k], x_peer if k % 2 else y_peer)

    def mod_plane():
        for k in range(4):
            zz = (z + k) % 4
            to_x, to_y = block8(zz, y, 1 - x), block8(zz, 1 - y, x)
            arrive(band_diag.at[k], pd_recv.at[k], x_peer if k % 2 else y_peer)
            fold = to_y if k % 2 else to_x
            band[fold, :] = band[fold, :] + band_diag[k]
            send("other", band.at[to_x], band_x.at[k], px_send.at[k], px_recv.at[k], x_peer)
            send("other", band.at[to_y], band_y.at[k], py_send.at[k], py_recv.at[k], y_peer)

    def mod_line():
        for k in (1, 2, 3, 0):
            zz = (z + k) % 4
            mine = block8(zz, y, x)
            arrive(band_x.at[k], px_recv.at[k], x_peer)
            arrive(band_y.at[k], py_recv.at[k], y_peer)
            band[mine, :] = band[mine, :] + band_x[k] + band_y[k]
            if k:
                send("other", band.at[mine], band_z.at[k - 1], pz_send.at[k - 1], pz_recv.at[k - 1], device(zz, y, x, c))

    def mod_last():
        for k in (1, 2, 3):
            arrive(band_z.at[k - 1], pz_recv.at[k - 1], device((z - k + 4) % 4, y, x, c))
        halves_of[c] = band[block8(z, y, x), :] + band_z[0] + band_z[1] + band_z[2]
        send("other", halves_of.at[c], halves_of.at[c], pm_send, pm_recv, c_peer)

    def mod_end():
        arrive(halves_of.at[1 - c], pm_recv, c_peer)
        side = ada_ref.shape[1] // 2
        table_ref[:, :BAND] = halves_of[0]
        table_ref[:, BAND:] = halves_of[1][:, 2 * BAND - side :]
        counts = jnp.sum(conds_ref[:, :, :].astype(jnp.float32)[:, CROPS : CROPS + 1, :], axis=0)
        lane = lax.broadcasted_iota(jnp.int32, counts.shape, 1)
        weight = jnp.where(lane < NBINS, 40.0 * CHIPS / jnp.where(lane < NBINS, counts, 1.0), 0.0)
        level_ref[...] = jnp.broadcast_to(
            jnp.sum(bins_ref[...] * weight, axis=-1, keepdims=True), level_ref.shape
        )

    def first_norm():
        def body(at):
            segments = seg_col_ref[at, :1]
            value, _ = normed(tokens_ref[at, :].astype(jnp.float32))
            value = value * (1.0 + pick(segments, table_ref, 0, 1, width))
            hidden_ref[at, :] = (value + pick(segments, table_ref, 0, 0, width)).astype(jnp.bfloat16)

        chunks(count, body)
        arrive(seg_all.at[1 - c], seg_recv, c_peer)
        for h in (0, 1):
            same = seg_col_ref[:, :1] == seg_all[h][:1, :]
            bias[:, h * count : (h + 1) * count] = jnp.where(same, 0.0, LARGE_NEGATIVE)

    def project():
        here = pl.ds(pl.multiple_of(c * count, 256), count)
        for q in (1, 2):
            sides_ref[q - 1, here, :] = product(hidden_ref[...], full[0, q]).astype(jnp.bfloat16)
            send("other", sides_ref.at[q - 1, here], sides_ref.at[q - 1, here], kv_send.at[q - 1], kv_recv.at[q - 1], c_peer)
        query_ref[...] = product(hidden_ref[...], full[0, 0]).astype(jnp.bfloat16)
        total_ref[...] = jnp.zeros_like(total_ref)
        work[...] = jnp.zeros_like(work)

    def attend(first, last):
        if first == 0:
            there = pl.ds(pl.multiple_of((1 - c) * count, 256), count)
            for q in (0, 1):
                arrive(sides_ref.at[q, there], kv_recv.at[q], c_peer)
        size = width // HEADS
        scale = 1.0 / math.sqrt(size)

        def body(head, carry):
            columns, inside = window_of(head, size, width)
            query = query_ref[:, columns]
            query = jnp.where(inside, query, jnp.zeros_like(query))
            scores = product_by_columns(query, sides_ref[0, :, columns]) * scale + bias[...]
            top = jnp.max(scores, axis=-1, keepdims=True)
            raised = jnp.exp(scores - top)
            total = jnp.sum(raised, axis=-1, keepdims=True)
            chance = (raised * (1.0 / total)).astype(jnp.bfloat16)
            context = product(chance, sides_ref[1, :, columns])
            work[:, columns] = jnp.where(inside, context, work[:, columns])
            lane = lax.broadcasted_iota(jnp.int32, (1, 128), 1)
            total_ref[...] = jnp.where(lane == head, top + jnp.log(total), total_ref[...])
            return carry

        lax.fori_loop(first, last, body, 0)

    def mix():
        context_ref[...] = work[...].astype(jnp.bfloat16)
        attended_ref[...] = product(context_ref[...], full[0, 3])

        def body(at):
            segments = seg_col_ref[at, :1]
            gate = pick(segments, table_ref, 0, 2, width)
            middle = tokens_ref[at, :].astype(jnp.float32) + gate * attended_ref[at, :]
            middle_ref[at, :] = middle
            value, _ = normed(middle)
            value = value * (1.0 + pick(segments, table_ref, 4, 1, width))
            hidden_two_ref[at, :] = (value + pick(segments, table_ref, 4, 0, width)).astype(jnp.bfloat16)
            level = level_ref[3:4, :1]
            for crop in (2, 1, 0):
                level = jnp.where(segments == crop, level_ref[crop : crop + 1, :1], level)
            grad = cot_ref[at, :].astype(jnp.float32) * level
            grad_mlp[at, :] = (grad * pick(segments, table_ref, 4, 2, width)).astype(jnp.bfloat16)

        chunks(count, body)

    slope_copies = {}

    def expand(q):
        work[...] = product(hidden_two_ref[...], full[1, q])
        if q >= 2:
            slope_copies[q - 2].wait()

        def body(at):
            u = work[at, :]
            square = u * u
            bend = jnp.tanh(GELU_SCALE * (u + GELU_CUBE * (square * u)))
            active[q, at, :] = (0.5 * u * (1.0 + bend)).astype(jnp.bfloat16)
            inner = GELU_SCALE * (1.0 + 3.0 * GELU_CUBE * square)
            slope[q % 2, at, :] = 0.5 * (1.0 + bend) + 0.5 * u * (1.0 - bend * bend) * inner

        chunks(count, body)
        copy = pltpu.make_async_copy(slope.at[q % 2], slope_ref.at[q], slope_sem.at[q % 2])
        copy.start()
        slope_copies[q] = copy

    def down_grad(q):
        if q == 0:
            finish_sends(0)
            saves[0].wait()
        full[0, q] = product_by_rows(active[q], grad_mlp[...]).astype(jnp.bfloat16)
        copy = pltpu.make_async_copy(full.at[0, q], down_part_ref.at[q], grad_sem.at[q])
        copy.start()
        saves.append(copy)

    def contract():
        work[...] = product(active[0], full[2, 0])
        for q in (1, 2, 3):
            work[...] += product(active[q], full[2, q])

        def body(at):
            mlp = work[at, :]
            mlp_ref[at, :] = mlp
            gate = pick(seg_col_ref[at, :1], table_ref, 4, 2, width)
            out_ref[at, :] = (middle_ref[at, :] + gate * mlp).astype(jnp.bfloat16)

        chunks(count, body)

    extra = {
        0: [mod_start],
        1: [mod_cores],
        2: [mod_plane],
        3: [mod_line],
        4: [mod_last],
        5: [mod_end, first_norm, partial(complete, 0), project],
        6: [partial(attend, 0, 8)],
        7: [partial(attend, 8, 16)],
        8: [mix],
        9: [partial(complete, 1), partial(expand, 0), partial(expand, 1), partial(expand, 2)],
        10: [partial(expand, 3), partial(down_grad, 0), partial(down_grad, 1)],
        11: [partial(down_grad, 2), partial(down_grad, 3)],
        13: [partial(complete, 2), contract],
    }
    order = [(a, k) for a in range(3) for k in range(4)]
    for i in range(len(order) + 2):
        if i < len(order):
            if order[i][1] == 0:
                own(order[i][0])
            spread(*order[i])
        if 1 <= i < len(order) + 1:
            forward(*order[i - 1])
        if 2 <= i:
            finish(*order[i - 2])
        for step in extra.get(i, ()):
            step()
    for copy in saves[1:]:
        copy.wait()
    for q in (2, 3):
        slope_copies[q].wait()
    for a in (1, 2, "other"):
        finish_sends(a)


def run_forward(shards, down, acts, ada, tokens, cot, seg_col, seg_row, bins, share):
    count, width = tokens.shape
    dma = pltpu.SemaphoreType.DMA
    low, wide = jnp.bfloat16, jnp.float32
    side = ada.shape[1] // 2
    vmem, any_ = pl.BlockSpec(memory_space=pltpu.VMEM), pl.BlockSpec(memory_space=pl.ANY)
    out = jax.ShapeDtypeStruct
    return pl.pallas_call(
        partial(forward_kernel, share),
        out_shape=(
            out((3, 4, width, width), low),
            out((4, width, width), low),
            out((4, count, width), wide),
            out((count, width), low),
            out((count, width), low),
            out((2, 2 * count, width), low),
            out((count, 128), wide),
            out((count, width), low),
            out((count, width), wide),
            out((count, width), wide),
            out((count, width), low),
            out((count, width), wide),
            out((count, width), low),
            out((8, side), wide),
            out((CHIPS, 16, 128), low),
            out((8, 128), wide),
            out((count, width), low),
            out((2, 8, count), jnp.int32),
        ),
        in_specs=[vmem] * 9,
        out_specs=[any_] * 3 + [vmem] * 15,
        scratch_shapes=[
            pltpu.VMEM((3, 4, width, width), low),
            pltpu.VMEM((2, 4 * PAD, width), low),
            pltpu.VMEM((CHIPS * 8, side), wide),
            pltpu.VMEM((CHIPS * 8, BAND), wide),
            pltpu.VMEM((CHIPS * 8, BAND), wide),
            pltpu.VMEM((4, 8, BAND), wide),
            pltpu.VMEM((4, 8, BAND), wide),
            pltpu.VMEM((4, 8, BAND), wide),
            pltpu.VMEM((3, 8, BAND), wide),
            pltpu.VMEM((2, 8, BAND), wide),
            pltpu.VMEM((count, 2 * count), wide),
            pltpu.VMEM((count, width), wide),
            pltpu.VMEM((4, count, width), low),
            pltpu.VMEM((2, count, width), wide),
            dma((2, 3)), dma((2, 3)), dma((3, 4, 2)), dma((3, 4)), dma((3, 4, 2)), dma((3, 4)),
            dma((3, 4, 2)), dma((3, 4, 2)), dma((3, 4, 2)), dma((3, 4, 2)),
            dma((3, 4)), dma((3, 4)), dma((3, 4)), dma((3, 4)),
            dma((3, 4, 4)), dma((3, 4, 4)),
            dma((CHIPS - 1,)), dma((CHIPS - 1,)), dma, dma, dma((4,)), dma((4,)),
            dma((4,)), dma((4,)), dma((4,)), dma((4,)), dma((3,)), dma((3,)), dma, dma, dma, dma,
            dma((2,)), dma((2,)), dma((3,)), dma((4,)), dma((2,)),
        ],
        compiler_params=pltpu.CompilerParams(
            collective_id=0, has_side_effects=True, vmem_limit_bytes=63 * 2**20
        ),
        name="forward",
    )(shards, down, acts, ada, tokens, cot, seg_col, seg_row, bins)


def add_rows(dst, sources, start, rows):
    def body(i, carry):
        where = pl.ds(pl.multiple_of(start + i * 16, 16), 16)
        total = dst[where, :].astype(jnp.float32)
        for source in sources:
            total = total + source[where, :].astype(jnp.float32)
        dst[where, :] = total.astype(dst.dtype)
        return carry

    lax.fori_loop(0, rows // 16, body, 0)


def interleave(steps, layer, after):
    done = 0
    for count, step in enumerate(steps):
        while done < len(layer) and after[done] <= count:
            layer[done]()
            done += 1
        step()
    for step in layer[done:]:
        step()


def split_low(values):
    high = values.astype(jnp.bfloat16)
    return high, (values - high.astype(jnp.float32)).astype(jnp.bfloat16)


def backward_kernel(share, weights_ref, down_part_ref, slope_ref, middle_ref, attended_ref, mlp_ref,
                    hidden_ref, query_ref, sides_ref, total_ref, context_ref, hidden_two_ref,
                    grad_mlp_ref, table_ref, conds_ref, level_ref, seg_all_ref, seg_col_ref, tokens_ref,
                    cot_ref, ada_ref,
                    mixer_part_ref, up_part_ref, rows_ref, down_ref, tokens_grad_ref, ada_grad_ref, silu_ref,
                    held, from_core, diag, from_x, from_y, piece_line, diag_line, spare, block, part, quad, lows,
                    work, grad_middle, grad_context, leave, enter, bias, sums, sums_row, sums_core, band, silu_part, silu_side,
                    *sems):
    (
        load_sem, c_send, c_recv, dx_send, dx_recv, dy_send, dy_recv, x_send, x_recv,
        y_send, y_recv, zo_send, zo_recv, zd_send, zd_recv, group_send, group_recv, block_sem, part_sem, quad_sem,
        side_send, side_recv, m_send, m_recv, mz_send, mz_recv, mx_send, mx_recv, my_send, my_recv,
        md_send, md_recv, mc_send, mc_recv, s_send, s_recv, sc_send, sc_recv,
    ) = sems
    z, y, x, c = position()
    me = z * 4 + y * 2 + x
    group = x * 2 + c
    rows = 4 * share
    count, width = tokens_ref.shape
    x_peer, y_peer, c_peer = device(z, y, 1 - x, c), device(z, 1 - y, x, c), device(z, y, x, 1 - c)
    partners = [(x, 1 - c), (1 - x, c), (1 - x, 1 - c)]
    greet(
        [((me + k) % CHIPS, c) for k in range(1, CHIPS)] + [c_peer, device(z, y, 1 - x, 1 - c)]
    )
    sends = {}

    def send(owner, *args):
        copy = remote(*args)
        copy.start()
        sends.setdefault(owner, []).append(copy)

    def finish_sends(owner):
        for copy in sends.pop(owner, []):
            copy.wait_send()

    order = [(a, k) for a in (2, 1, 0) for k in (3, 2, 1, 0)]
    given = (mixer_part_ref, up_part_ref, down_part_ref)
    loads = {}
    inner_rows = slice(FAR[0], rows - FAR[1])

    def cuts(i):
        top, low = FAR if order[i][1] else NEAR
        return top, rows - low

    def line(k):
        to = level_of(z, k)
        step = jnp.where(z < to, 1, -1)
        behind = z - step
        return to, z + step, (behind >= 0) & (behind < 4)

    def along(i, ref, lines, send_sem, recv_sem):
        a, k = order[i]
        to, after, _ = line(k)
        spot = jnp.where((after == to) & (z > to), 4, to)
        copy = remote(ref, lines.at[a % 2, spot], send_sem.at[a, k], recv_sem.at[a, spot], device(after, y, x, c))
        copy.start()
        return copy

    def from_line(i, lines, recv_sem, spot):
        a = order[i][0]
        arrive(lines.at[a % 2, spot], recv_sem.at[a, spot], device((z + 1) % 4, y, x, c))

    def hold(i, ref, lines, send_sem, recv_sem):
        sends.setdefault(("held", i), []).append(
            remote(ref, lines.at[0, 0], send_sem.at[order[i]], recv_sem.at[order[i][0], 0], x_peer)
        )

    def begin(i):
        a, k = order[i]
        if i % 4 == 0:
            for n in sorted(going):
                going.pop(n).wait()
        finish_sends(("held", i - HELD))
        zz = level_of(z, k)
        for pos in (3, 1, 2, 0):
            yy = 1 - y if PLACES[pos][0] else y
            xx = 1 - x if PLACES[pos][1] else x
            for cc in (1 - c, c):
                where, row = block_of(a, zz * 2 + yy, xx * 2 + cc)
                src = given[a].at[where, pl.ds(pl.multiple_of(row * rows, 16), rows)]
                if cc is c:
                    loads[i, pos] = pltpu.make_async_copy(src, held.at[i % HELD, pos], load_sem.at[i, pos])
                    loads[i, pos].start()
                else:
                    send("core", src, from_core.at[i % 4, pos], c_send.at[i, pos], c_recv.at[i, pos], c_peer)

    def pair(i, pos):
        k = order[i][1]
        top, low = cuts(i)
        mine = held.at[i % HELD, pos]
        loads[i, pos].wait()
        arrive(from_core.at[i % 4, pos], c_recv.at[i, pos], c_peer)
        add_rows(mine, [from_core.at[i % 4, pos]], 0, rows)
        if pos == 3 and k:
            diagonal(i)
            part = mine.at[inner_rows]
            hold(i, part, diag_line, zd_send, zd_recv)
            _, _, fed = line(k)

            @pl.when(jnp.logical_not(fed))
            def _():
                along(i, part, diag_line, zd_send, zd_recv)

        if pos == 1:
            part = mine.at[top:rows]
            send(("held", i), part, from_x.at[i % 6, top:rows], x_send.at[i, 1], x_recv.at[i, 1], x_peer)
        if pos == 2:
            part = mine.at[0:low]
            send(("held", i), part, from_y.at[i % 6, 0:low], y_send.at[i, 0], y_recv.at[i, 0], y_peer)

    def diagonal(i):
        top, low = cuts(i)
        mine, far = held.at[i % HELD, 3], diag.at[i % 5]
        send(("held", i), mine.at[0:top], far.at[0:top], dy_send.at[i], dy_recv.at[i], y_peer)
        send(("held", i), mine.at[low:rows], far.at[low:rows], dx_send.at[i], dx_recv.at[i], x_peer)

    def diag_along(i):
        k = order[i][1]
        mine = held.at[i % HELD, 3, inner_rows]
        size = rows - FAR[0] - FAR[1]
        if k:
            to, _, fed = line(k)

            @pl.when(fed)
            def _():
                from_line(i, diag_line, zd_recv, to)
                add_rows(mine, [diag_line.at[order[i][0] % 2, to]], 0, size)
                along(i, mine, diag_line, zd_send, zd_recv)

        else:
            for spot, here in ((z, z > 0), (4, z < 3)):

                @pl.when(here)
                def _():
                    from_line(i, diag_line, zd_recv, spot)
                    add_rows(mine, [diag_line.at[order[i][0] % 2, spot]], 0, size)

            diagonal(i)

    def relay(i):
        top, low = cuts(i)
        far = diag.at[i % 5]
        arrive(far.at[0:top], dy_recv.at[i], y_peer)
        add_rows(held.at[i % HELD, 1], [far], 0, top)
        part = held.at[i % HELD, 1, 0:top]
        send(("held", i), part, from_x.at[i % 6, 0:top], x_send.at[i, 0], x_recv.at[i, 0], x_peer)
        arrive(far.at[low:rows], dx_recv.at[i], x_peer)
        add_rows(held.at[i % HELD, 2], [far], low, rows - low)
        part = held.at[i % HELD, 2, low:rows]
        send(("held", i), part, from_y.at[i % 6, low:rows], y_send.at[i, 1], y_recv.at[i, 1], y_peer)

    def plane(i):
        k = order[i][1]
        top, low = cuts(i)
        mine = held.at[i % HELD, 0]
        arrive(from_x.at[i % 6, 0:top], x_recv.at[i, 0], x_peer)
        arrive(from_x.at[i % 6, top:rows], x_recv.at[i, 1], x_peer)
        arrive(from_y.at[i % 6, 0:low], y_recv.at[i, 0], y_peer)
        arrive(from_y.at[i % 6, low:rows], y_recv.at[i, 1], y_peer)
        add_rows(mine, [from_x.at[i % 6], from_y.at[i % 6]], 0, rows)
        if k:
            hold(i, mine, piece_line, zo_send, zo_recv)
            _, _, fed = line(k)

            @pl.when(jnp.logical_not(fed))
            def _():
                along(i, mine, piece_line, zo_send, zo_recv)

    def piece_along(i):
        a, k = order[i]
        mine = held.at[i % HELD, 0]
        if k:
            to, _, fed = line(k)

            @pl.when(fed)
            def _():
                from_line(i, piece_line, zo_recv, to)
                add_rows(mine, [piece_line.at[a % 2, to]], 0, rows)
                along(i, mine, piece_line, zo_send, zo_recv)

            return
        for spot, here in ((z, z > 0), (4, z < 3)):

            @pl.when(here)
            def _():
                from_line(i, piece_line, zo_recv, spot)
                add_rows(mine, [piece_line.at[a % 2, spot]], 0, rows)

        if a == 2:
            down_ref[...] = mine[...].astype(jnp.float32)
            return
        spare[a] = product_by_rows(row_selector(rows, share), mine[...]).astype(jnp.bfloat16)
        for j, (px, pc) in enumerate(partners):
            send(
                "end",
                spare.at[a, pl.ds(pl.multiple_of((px * 2 + pc) * PAD, 16), PAD)],
                rows_ref.at[a, group],
                group_send.at[a, j],
                group_recv.at[a, j],
                device(z, y, px, pc),
            )
        rows_ref[a, group] = spare[a, pl.ds(pl.multiple_of(group * PAD, 16), PAD), :]

    uses = [(2, q) for q in range(4)] + [(1, q) for q in range(4)] + [(0, 3), (0, 0), (0, 1), (0, 2)]
    coming = {}

    def fetch(n):
        if n < len(uses):
            copy = pltpu.make_async_copy(weights_ref.at[uses[n]], block.at[n % 2], block_sem.at[n % 2])
            copy.start()
            coming[n] = copy

    def take(n):
        coming[n].wait()
        return block[n % 2]

    going = {}

    def put(n, left, right, target):
        if n - 2 in going:
            going.pop(n - 2).wait()

        def body(i, carry):
            columns = pl.ds(pl.multiple_of(i * 384, 128), 384)
            part[n % 2, columns, :] = product_by_rows(left[:, columns], right[...]).astype(jnp.bfloat16)
            return carry

        lax.fori_loop(0, width // 384, body, 0)
        going[n] = pltpu.make_async_copy(part.at[n % 2], target, part_sem.at[n % 2])
        going[n].start()

    quads = {}

    def slopes(q):
        quads[q] = pltpu.make_async_copy(slope_ref.at[q], quad.at[q], quad_sem.at[q])
        quads[q].start()

    def through_down(q):
        work[...] = product_by_columns(grad_mlp_ref[...], take(q))
        fetch(q + 2)
        quads[q].wait()

        def body(at):
            lows[q, at, :] = (work[at, :] * quad[q, at, :]).astype(jnp.bfloat16)

        chunks(count, body)
        if q < 3:
            source = (middle_ref, attended_ref, mlp_ref)[q]
            quads[q] = pltpu.make_async_copy(source, quad.at[q], quad_sem.at[q])
            quads[q].start()

    def up_grad(q):
        put(q, hidden_two_ref, lows.at[q], up_part_ref.at[q])

    def through_up(q):
        value = product_by_columns(lows[q], take(4 + q))
        work[...] = work[...] + value if q else value
        fetch(6 + q)

    def norm_pull(grad, value, inverse):
        return inverse * (
            grad
            - jnp.mean(grad, axis=-1, keepdims=True)
            - value * jnp.mean(grad * value, axis=-1, keepdims=True)
        )

    def add_sums(segments, which, value):
        for crop in range(CROPS):
            kept = jnp.where(segments == crop, value, 0.0)
            sums[which, crop] = sums[which, crop] + kept[:8] + kept[8:]

    def second_norm(half):
        if half == 0:
            for q in range(3):
                quads[q].wait()
            sums[...] = jnp.zeros_like(sums)

        def body(at):
            segments = seg_col_ref[at, :1]
            grad = work[at, :]
            value, inverse = normed(quad[0, at, :])
            level = level_ref[3:4, :1]
            for crop in (2, 1, 0):
                level = jnp.where(segments == crop, level_ref[crop : crop + 1, :1], level)
            grad_out = cot_ref[at, :].astype(jnp.float32) * level
            add_sums(segments, 3, grad)
            add_sums(segments, 4, grad * value)
            add_sums(segments, 5, grad_out * quad[2, at, :])
            scaled = grad * (1.0 + pick(segments, table_ref, 4, 1, width))
            total = grad_out + norm_pull(scaled, value, inverse)
            grad_middle[at, :] = total
            add_sums(segments, 2, total * quad[1, at, :])
            lows[3, at, :] = (total * pick(segments, table_ref, 0, 2, width)).astype(jnp.bfloat16)

        chunks(count // 2, body, half * (count // 2))

    def context_grad():
        grad_context[...] = product_by_columns(lows[3], take(8)).astype(jnp.bfloat16)
        fetch(10)

    def out_grad():
        put(4, context_ref, lows.at[3], mixer_part_ref.at[3])
        for h in (0, 1):
            same = seg_col_ref[:, :1] == seg_all_ref[h][:1, :]
            bias[:, h * count : (h + 1) * count] = jnp.where(same, 0.0, LARGE_NEGATIVE)

    def attend_back(first, last):
        size = width // HEADS
        scale = 1.0 / math.sqrt(size)

        def body(head, carry):
            columns, inside = window_of(head, size, width)
            query, keys = query_ref[:, columns], sides_ref[0, :, columns]
            grad = grad_context[:, columns]
            scores = product_by_columns(jnp.where(inside, query, jnp.zeros_like(query)), keys)
            lane = lax.broadcasted_iota(jnp.int32, (1, 128), 1)
            total = jnp.sum(jnp.where(lane == head, total_ref[...], 0.0), axis=-1, keepdims=True)
            chance = jnp.exp(scores * scale + bias[...] - total)
            pulled = product_by_columns(
                jnp.where(inside, grad, jnp.zeros_like(grad)), sides_ref[1, :, columns]
            )
            inner = jnp.sum(chance * pulled, axis=-1, keepdims=True)
            grad_scores = (chance * (pulled - inner)).astype(jnp.bfloat16)
            grad_query = (product(grad_scores, keys) * scale).astype(jnp.bfloat16)
            lows[0, :, columns] = jnp.where(inside, grad_query, lows[0, :, columns])
            grad_key = product_by_rows(grad_scores, query) * scale
            grad_value = product_by_rows(chance.astype(jnp.bfloat16), grad)
            for h in (0, 1):
                here = slice(h * count, (h + 1) * count)
                quad[h, :, columns] = jnp.where(inside, grad_key[here], quad[h, :, columns])
                quad[2 + h, :, columns] = jnp.where(inside, grad_value[here], quad[2 + h, :, columns])
            return carry

        lax.fori_loop(first, last, body, 0)

    def swap_sides():
        for j in (0, 1):
            leave[j] = quad[2 * j + 1 - c].astype(jnp.bfloat16)
            send("end", leave.at[j], enter.at[j], side_send.at[j], side_recv.at[j], c_peer)

    def query_grad():
        put(5, hidden_ref, lows.at[0], mixer_part_ref.at[0])

    def side_grad(j):
        arrive(enter.at[j], side_recv.at[j], c_peer)

        def body(at):
            total = quad[2 * j + c, at, :] + enter[j, at, :].astype(jnp.float32)
            lows[1 + j, at, :] = total.astype(jnp.bfloat16)

        chunks(count, body)
        put(6 + j, hidden_ref, lows.at[1 + j], mixer_part_ref.at[1 + j])

    def through_qkv(q):
        value = product_by_columns(lows[q], take(9 + q))
        work[...] = work[...] + value if q else value
        fetch(11 + q)

    def first_norm(half):
        def body(at):
            segments = seg_col_ref[at, :1]
            grad = work[at, :]
            value, inverse = normed(tokens_ref[at, :].astype(jnp.float32))
            add_sums(segments, 0, grad)
            add_sums(segments, 1, grad * value)
            scaled = grad * (1.0 + pick(segments, table_ref, 0, 1, width))
            tokens_grad_ref[at, :] = grad_middle[at, :] + norm_pull(scaled, value, inverse)

        chunks(count // 2, body, half * (count // 2))

    def sums_leave():
        for which in range(6):
            for crop in range(CROPS):
                row = which // 3 * CROPS + crop
                columns = slice(which % 3 * width, (which % 3 + 1) * width)
                sums_row[row : row + 1, columns] = jnp.sum(sums[which, crop], axis=0, keepdims=True)
        send("end", sums_row, sums_core, m_send, m_recv, c_peer)

    side = sums_row.shape[1]

    def place(k, other_y, other_x):
        zz = (z - k + 4) % 4
        yy = 1 - y if other_y else y
        xx = 1 - x if other_x else x
        return band.at[c, pl.ds(pl.multiple_of((zz * 4 + yy * 2 + xx) * 8, 8), 8)]

    def sums_start():
        arrive(sums_core, m_recv, c_peer)
        near = pl.ds(pl.multiple_of(c * (side - BAND), 128), BAND)
        band[c, pl.ds(pl.multiple_of(me * 8, 8), 8), :] = sums_row[:, near] + sums_core[:, near]
        mine = place(0, 0, 0)
        for k in (1, 2, 3):
            send("end", mine, mine, mz_send.at[k - 1], mz_recv.at[k - 1], device((z + k) % 4, y, x, c))
        send("end", mine, mine, mx_send.at[0], mx_recv.at[0], x_peer)
        send("end", mine, mine, my_send.at[0], my_recv.at[0], y_peer)

    def sums_line():
        for k in (1, 2, 3):
            piece = place(k, 0, 0)
            arrive(piece, mz_recv.at[k - 1], device((z - k + 4) % 4, y, x, c))
            send("end", piece, piece, mx_send.at[k], mx_recv.at[k], x_peer)
            send("end", piece, piece, my_send.at[k], my_recv.at[k], y_peer)

    def sums_plane():
        for k in range(4):
            from_side, from_up = place(k, 0, 1), place(k, 1, 0)
            arrive(from_side, mx_recv.at[k], x_peer)
            arrive(from_up, my_recv.at[k], y_peer)
            if k % 2:
                send("end", from_side, from_side, md_send.at[k], md_recv.at[k], y_peer)
            else:
                send("end", from_up, from_up, md_send.at[k], md_recv.at[k], x_peer)

    def sums_cores():
        for k in range(4):
            arrive(place(k, 1, 1), md_recv.at[k], y_peer if k % 2 else x_peer)
        send("end", band.at[c], band.at[c], mc_send, mc_recv, c_peer)

    def condition(source):
        if source == 0:
            arrive(band.at[1 - c], mc_recv, c_peer)
            silu_side[...] = jnp.zeros_like(silu_side)
        acts = conds_ref[:, :8, :].astype(jnp.float32).reshape(CHIPS * 8, 128)
        row = lax.broadcasted_iota(jnp.int32, acts.shape, 0) % 8
        acts = jnp.where(row < CROPS, acts, 0.0)
        upper = acts.astype(jnp.bfloat16)
        lower = pltpu.roll(acts, CROPS, 0).astype(jnp.bfloat16)
        first, skip, size = ((0, 0, BAND), (BAND, 2 * BAND - side, side - BAND))[source]
        terms = split_low(band[source, :, skip : skip + size])
        for which, act in enumerate((upper, lower)):
            columns = slice(which * side + first, which * side + first + size)
            value = product_by_rows(act, terms[0]) + product_by_rows(act, terms[1])
            ada_grad_ref[:, columns] = value[: ada_grad_ref.shape[0]]
            value = product_by_columns(terms[0], ada_ref[:, columns])
            value = value + product_by_columns(terms[1], ada_ref[:, columns])
            silu_side[which, :, :PAD] = silu_side[which, :, :PAD] + value
        if source == 0:
            return
        silu_part[...] = silu_side[0] + pltpu.roll(silu_side[1], CHIPS * 8 - CROPS, 0)
        silu_ref[c, me] = silu_part[pl.ds(pl.multiple_of(me * 8, 8), 8), :]
        for k in range(1, CHIPS):
            to = (me + k) % CHIPS
            src = silu_part.at[pl.ds(pl.multiple_of(to * 8, 8), 8)]
            send("end", src, silu_ref.at[c, me], s_send.at[k - 1], s_recv.at[k - 1], (to, c))

    def condition_cores():
        for k in range(1, CHIPS):
            source = (me - k + CHIPS) % CHIPS
            arrive(silu_ref.at[c, source], s_recv.at[k - 1], (source, c))
        send("end", silu_ref.at[c], silu_ref.at[c], sc_send, sc_recv, c_peer)

    steps = []
    for i in range(len(order) + 5):
        if i + 1 < len(order):
            steps.append(partial(begin, i + 1))
        if i < len(order):
            steps += [partial(pair, i, pos) for pos in (3, 1, 2, 0)]
        if 1 <= i <= len(order):
            steps.append(partial(diag_along, i - 1))
        for step, lag in ((relay, 1), (plane, 2), (piece_along, 3)):
            for j in (i - lag - 1, i - lag):
                if 0 <= j < len(order) and j + lag + (order[j][1] == 0) == i:
                    steps.append(partial(step, j))
    layer = [partial(through_down, q) for q in range(4)] + [partial(up_grad, q) for q in range(4)]
    layer += [partial(through_up, q) for q in range(4)] + [partial(second_norm, h) for h in (0, 1)]
    layer += [context_grad, out_grad] + [partial(attend_back, h, h + 2) for h in range(0, HEADS, 2)]
    layer += [swap_sides, query_grad, partial(side_grad, 0), partial(side_grad, 1)]
    layer += [partial(through_qkv, q) for q in range(3)] + [partial(first_norm, h) for h in (0, 1)]
    layer += [sums_leave, sums_start, sums_line, sums_plane, sums_cores]
    layer += [partial(condition, 0), partial(condition, 1), condition_cores]
    begin(0)
    for q in range(4):
        slopes(q)
    fetch(0)
    fetch(1)
    interleave(steps, layer, BACKWARD_AFTER)
    for a in range(2):
        for j, (px, pc) in enumerate(partners):
            arrive(rows_ref.at[a, px * 2 + pc], group_recv.at[a, j], device(z, y, px, pc))
    arrive(silu_ref.at[1 - c], sc_recv, c_peer)
    for owner in list(sends):
        finish_sends(owner)


def run_backward(given, share):
    (weights, down_part, slope, middle, attended, mlp, hidden, query, sides, total, context, hidden_two,
     grad_mlp, table, conds, level, seg_all, seg_col, tokens, cot, ada) = given
    count, width = tokens.shape
    rows, side = 4 * share, ada.shape[1] // 2
    dma = pltpu.SemaphoreType.DMA
    low, wide = jnp.bfloat16, jnp.float32
    vmem, any_ = pl.BlockSpec(memory_space=pltpu.VMEM), pl.BlockSpec(memory_space=pl.ANY)
    out, buffer = jax.ShapeDtypeStruct, pltpu.VMEM
    slots = 12
    return pl.pallas_call(
        partial(backward_kernel, share),
        out_shape=(
            out((4, width, width), low),
            out((4, width, width), low),
            out((2, 4, PAD, width), low),
            out((rows, width), wide),
            out((count, width), wide),
            out((-(-share // 8) * 8, ada.shape[1]), wide),
            out((2, CHIPS, 8, 128), wide),
        ),
        in_specs=[any_] * 6 + [vmem] * 15,
        out_specs=[any_] * 2 + [vmem] * 5,
        scratch_shapes=[
            buffer((HELD, 4, rows, width), low),
            buffer((4, 4, rows, width), low),
            buffer((5, rows, width), low),
            buffer((6, rows, width), low),
            buffer((6, rows, width), low),
            buffer((2, 5, rows, width), low),
            buffer((2, 5, rows - FAR[0] - FAR[1], width), low),
            buffer((2, 4 * PAD, width), low),
            buffer((2, width, width), low),
            buffer((2, width, width), low),
            buffer((4, count, width), wide),
            buffer((4, count, width), low),
            buffer((count, width), wide),
            buffer((count, width), wide),
            buffer((count, width), low),
            buffer((2, count, width), low),
            buffer((2, count, width), low),
            buffer((count, 2 * count), wide),
            buffer((6, CROPS, 8, width), wide),
            buffer((8, side), wide),
            buffer((8, side), wide),
            buffer((2, CHIPS * 8, BAND), wide),
            buffer((CHIPS * 8, 128), wide),
            buffer((2, CHIPS * 8, 128), wide),
            dma((slots, 4)), dma((slots, 4)), dma((slots, 4)),
            dma((slots,)), dma((slots,)), dma((slots,)), dma((slots,)),
            dma((slots, 2)), dma((slots, 2)), dma((slots, 2)), dma((slots, 2)),
            dma((3, 4)), dma((3, 5)), dma((3, 4)), dma((3, 5)),
            dma((2, 3)), dma((2, 3)), dma((2,)), dma((2,)), dma((4,)),
            dma((2,)), dma((2,)), dma, dma, dma((3,)), dma((3,)), dma((4,)), dma((4,)), dma((4,)), dma((4,)),
            dma((4,)), dma((4,)), dma, dma, dma((CHIPS - 1,)), dma((CHIPS - 1,)), dma, dma,
        ],
        compiler_params=pltpu.CompilerParams(
            collective_id=1, has_side_effects=True, vmem_limit_bytes=63 * 2**20
        ),
        name="backward",
    )(*given)


def layer_norm(values):
    center = values - jnp.mean(values, axis=-1, keepdims=True)
    inverse = lax.rsqrt(jnp.mean(center * center, axis=-1, keepdims=True) + EPSILON)
    return (center * inverse, inverse)


def norm_back(grad_normed, normed, inverse):
    return inverse * (
        grad_normed
        - jnp.mean(grad_normed, axis=-1, keepdims=True)
        - normed * jnp.mean(grad_normed * normed, axis=-1, keepdims=True)
    )


def to_heads(array):
    return array.reshape(array.shape[0], HEADS, array.shape[1] // HEADS)


def dots(spec, left, right):
    return jnp.einsum(spec, left, right, preferred_element_type=jnp.float32)


def masked_scores(query_heads, key_heads, same_crop):
    scale_factor = 1.0 / math.sqrt(query_heads.shape[-1])
    scores = dots("qhd,khd->hqk", query_heads, key_heads) * scale_factor
    return jnp.where(same_crop[None], scores, LARGE_NEGATIVE)


def attend(query_seq, key_seq, value_seq, same_crop):
    scores = masked_scores(to_heads(query_seq), to_heads(key_seq), same_crop)
    row_max = jnp.max(scores, axis=-1, keepdims=True)
    raised = jnp.exp(scores - row_max)
    row_total = jnp.sum(raised, axis=-1, keepdims=True)
    probability = (raised / row_total).astype(jnp.bfloat16)
    context = dots("hqk,khd->qhd", probability, to_heads(value_seq))
    return (context.reshape(query_seq.shape[0], -1), (row_max + jnp.log(row_total))[..., 0])


def attend_back(query_seq, key_seq, value_seq, same_crop, log_total, grad_seq):
    query_heads = to_heads(query_seq)
    key_heads = to_heads(key_seq)
    value_heads = to_heads(value_seq)
    grad_heads = to_heads(grad_seq)
    scale_factor = 1.0 / math.sqrt(query_heads.shape[-1])
    scores = masked_scores(query_heads, key_heads, same_crop)
    probability = jnp.exp(scores - log_total[..., None])
    grad_prob = dots("qhd,khd->hqk", grad_heads, value_heads)
    inner = jnp.sum(probability * grad_prob, axis=-1, keepdims=True)
    grad_scores = (probability * (grad_prob - inner)).astype(jnp.bfloat16)
    grad_query = dots("hqk,khd->qhd", grad_scores, key_heads) * scale_factor
    grad_key = dots("hqk,qhd->khd", grad_scores, query_heads) * scale_factor
    grad_value = dots("hqk,qhd->khd", probability.astype(jnp.bfloat16), grad_heads)
    rows_here = query_seq.shape[0]
    rows_whole = key_seq.shape[0]
    return (
        grad_query.reshape(rows_here, -1),
        grad_key.reshape(rows_whole, -1),
        grad_value.reshape(rows_whole, -1),
    )


def kernel_inputs(segments, conditions, noise_bins, bin_counts, ada_weight, first, up_weight):
    share, width = first.shape[0], first.shape[1] // 4
    cores = lax.axis_size("sp")
    shards = jnp.stack([first, up_weight]).reshape(2, share, 4, width)
    shards = jnp.pad(shards.transpose(0, 2, 1, 3), ((0, 0), (0, 0), (0, PAD - share), (0, 0)))
    acts = jax.nn.silu(conditions.astype(jnp.float32)).astype(jnp.bfloat16)
    acts = acts.reshape(CROPS, CHIPS, cores, share)
    acts = lax.dynamic_index_in_dim(acts, lax.axis_index("sp"), 2, keepdims=False)
    acts = jnp.pad(acts.transpose(1, 0, 2), ((0, 0), (0, 0), (0, 128 - share)))
    counts = jnp.pad(bin_counts.astype(jnp.bfloat16), (0, 128 - NBINS))
    counts = jnp.broadcast_to(counts, (CHIPS, 1, 128))
    acts = jnp.pad(jnp.concatenate([acts, counts], axis=1), ((0, 0), (0, 11), (0, 0)))
    ada = jnp.pad(ada_weight, ((0, PAD - share), (0, 0)))
    count = segments.shape[0]
    seg_col = jnp.broadcast_to(segments[:, None], (count, 128))
    seg_row = jnp.broadcast_to(segments[None, :], (8, count))
    bins = jnp.pad(noise_bins, (0, 4), constant_values=-1)
    bins = (bins[:, None] == jnp.arange(128, dtype=jnp.int32)).astype(jnp.float32)
    return shards, acts, ada, seg_col, seg_row, bins


def forward_plain(tokens_float, segments, conditions, noise_bins, bin_counts, ada_weight, first, up_weight,
                  down_weight):
    groups, cores = lax.axis_size("dp"), lax.axis_size("sp")
    share, width = first.shape[0], tokens_float.shape[1]
    index = lax.axis_index("dp") * cores + lax.axis_index("sp")
    mixers = lax.all_gather(first, ("dp", "sp"), axis=0, tiled=True)
    uppers = lax.all_gather(up_weight, ("dp", "sp"), axis=0, tiled=True)
    downers = lax.all_gather(down_weight, ("dp", "sp"), axis=0, tiled=True)
    mixers = mixers.reshape(width, 4, width).transpose(1, 0, 2)
    uppers = uppers.reshape(width, 4, width).transpose(1, 0, 2)
    downers = downers.reshape(4, width, width)
    bin_total = lax.psum(bin_counts, "dp")
    bin_weight = 40.0 * groups / bin_total.astype(jnp.float32)
    crop_weight = jnp.sum(
        jnp.where(noise_bins[:, None] == jnp.arange(NBINS, dtype=jnp.int32), bin_weight, 0.0),
        axis=-1,
    )
    cond_all = lax.all_gather(conditions, "dp", axis=0, tiled=True)
    cond_here = lax.dynamic_slice_in_dim(cond_all, index * share, share, axis=1)
    cond_act = jax.nn.silu(cond_here.astype(jnp.float32)).astype(jnp.bfloat16)
    modulation_part = dots("sd,df->sf", cond_act, ada_weight).reshape(groups, CROPS, -1)
    modulation = lax.psum(lax.psum_scatter(modulation_part, "dp", scatter_dimension=0), "sp")
    selector = (segments[:, None] == jnp.arange(CROPS, dtype=jnp.int32)).astype(jnp.float32)
    per_token = jnp.einsum("tc,cf->tf", selector, modulation, precision=lax.Precision.HIGHEST)
    shift_one, scale_one, gate_one, shift_two, scale_two, _ = jnp.split(per_token, 6, axis=-1)
    normed_one, _ = layer_norm(tokens_float)
    hidden_one = (normed_one * (1.0 + scale_one) + shift_one).astype(jnp.bfloat16)
    projected = dots("td,qdf->qtf", hidden_one, mixers[:3]).astype(jnp.bfloat16)
    sides = lax.all_gather(projected[1:], "sp", axis=1, tiled=True)
    all_segments = lax.all_gather(segments, "sp", axis=0, tiled=True)
    same_crop = segments[:, None] == all_segments[None, :]
    context, log_total = attend(projected[0], sides[0], sides[1], same_crop)
    context_low = context.astype(jnp.bfloat16)
    attended = dots("td,df->tf", context_low, mixers[3])
    middle = tokens_float + gate_one * attended
    normed_two, _ = layer_norm(middle)
    hidden_two = (normed_two * (1.0 + scale_two) + shift_two).astype(jnp.bfloat16)
    upper_in = dots("td,qdf->qtf", hidden_two, uppers)
    activated = jax.nn.gelu(upper_in, approximate=True).astype(jnp.bfloat16)
    slope = jax.vjp(partial(jax.nn.gelu, approximate=True), upper_in)[1](jnp.ones_like(upper_in))[0]
    mlp_out = dots("qtf,qfd->td", activated, downers)
    return (
        (mixers, uppers, downers), activated, slope, hidden_one, projected[0], sides, log_total,
        context_low, attended, middle, hidden_two, mlp_out, modulation, cond_act, crop_weight, same_crop,
    )


def layer_plain(tokens_float, segments, conditions, noise_bins, bin_counts, cotangent, ada_weight, first,
                up_weight, down_weight):
    width = tokens_float.shape[1]
    (
        (mixers, uppers, downers), activated, slope, hidden_one, queries, sides, log_total,
        context_low, attended, middle, hidden_two, mlp_out, modulation, cond_act, crop_weight, same_crop,
    ) = forward_plain(
        tokens_float, segments, conditions, noise_bins, bin_counts, ada_weight, first, up_weight,
        down_weight,
    )
    selector = (segments[:, None] == jnp.arange(CROPS, dtype=jnp.int32)).astype(jnp.float32)
    per_token = jnp.einsum("tc,cf->tf", selector, modulation, precision=lax.Precision.HIGHEST)
    _, scale_one, gate_one, _, scale_two, gate_two = jnp.split(per_token, 6, axis=-1)
    normed_one, inverse_one = layer_norm(tokens_float)
    normed_two, inverse_two = layer_norm(middle)

    token_weight = jnp.sum(selector * crop_weight[None, :], axis=-1)
    grad_out = cotangent.astype(jnp.float32) * token_weight[:, None]
    grad_mlp = (grad_out * gate_two).astype(jnp.bfloat16)
    tokens_out = (middle + gate_two * mlp_out).astype(jnp.bfloat16)
    down_part = dots("qtf,td->qfd", activated, grad_mlp).astype(jnp.bfloat16)
    grad_act = dots("td,qfd->qtf", grad_mlp, downers)
    grad_upper = (grad_act * slope).astype(jnp.bfloat16)
    up_part = dots("td,qtf->qdf", hidden_two, grad_upper).astype(jnp.bfloat16)
    grad_hidden_two = dots("qtf,qdf->td", grad_upper, uppers)
    grad_middle = grad_out + norm_back(grad_hidden_two * (1.0 + scale_two), normed_two, inverse_two)
    grad_attended = (grad_middle * gate_one).astype(jnp.bfloat16)
    grad_context = dots("tf,df->td", grad_attended, mixers[3]).astype(jnp.bfloat16)
    grad_query, grad_key, grad_value = attend_back(
        queries, sides[0], sides[1], same_crop, log_total, grad_context
    )
    grad_sides = lax.psum_scatter(
        jnp.stack([grad_key, grad_value]).astype(jnp.bfloat16),
        "sp",
        scatter_dimension=1,
        tiled=True,
    )
    grad_projected = jnp.concatenate([grad_query.astype(jnp.bfloat16)[None], grad_sides])
    out_part = dots("td,tf->df", context_low, grad_attended).astype(jnp.bfloat16)
    qkv_part = dots("td,qtf->qdf", hidden_one, grad_projected).astype(jnp.bfloat16)
    first_part = jnp.concatenate([qkv_part, out_part[None]])
    grad_hidden_one = dots("qtf,qdf->td", grad_projected, mixers[:3])
    tokens_grad = grad_middle + norm_back(
        grad_hidden_one * (1.0 + scale_one), normed_one, inverse_one
    )

    joined = jnp.stack([first_part, up_part]).transpose(2, 0, 1, 3).reshape(width, 8 * width)
    rows = lax.psum_scatter(joined, ("dp", "sp"), scatter_dimension=0, tiled=True)
    rows = rows.astype(jnp.float32)
    first_grad, up_grad = rows[:, : 4 * width], rows[:, 4 * width :]
    down_grad = lax.psum_scatter(
        down_part.reshape(4 * width, width), ("dp", "sp"), scatter_dimension=0, tiled=True
    ).astype(jnp.float32)

    grad_per_token = jnp.concatenate(
        [
            grad_hidden_one,
            grad_hidden_one * normed_one,
            grad_middle * attended,
            grad_hidden_two,
            grad_hidden_two * normed_two,
            grad_out * mlp_out,
        ],
        axis=-1,
    )
    grad_modulation = lax.psum(
        jnp.einsum("tc,tf->cf", selector, grad_per_token, precision=lax.Precision.HIGHEST), "sp"
    )
    grad_rows = lax.all_gather(grad_modulation, "dp", axis=0, tiled=True)
    ada_grad = jnp.einsum(
        "sd,sf->df", cond_act.astype(jnp.float32), grad_rows, precision=lax.Precision.HIGHEST
    )
    silu_part = jnp.einsum(
        "sf,df->sd", grad_rows, ada_weight.astype(jnp.float32), precision=lax.Precision.HIGHEST
    )
    silu_all = lax.all_gather(silu_part, ("dp", "sp"), axis=0)
    silu_here = lax.dynamic_slice_in_dim(silu_all, lax.axis_index("dp") * CROPS, CROPS, axis=1)
    grad_silu = silu_here.transpose(1, 0, 2).reshape(CROPS, width)
    return tokens_out, tokens_grad, grad_silu, ada_grad, first_grad, up_grad, down_grad


def on_device(
    chips,
    tokens_in,
    segment_ids,
    conditions,
    noise_bins,
    bin_counts,
    cotangent,
    ada_weight,
    qkv_weight,
    out_weight,
    up_weight,
    down_weight,
):
    tokens_float = tokens_in[0].astype(jnp.float32)
    segments = segment_ids[0]
    width = tokens_float.shape[1]
    share = qkv_weight.shape[0]
    kernels = chips and 4 * share == down_weight.shape[0]
    first = jnp.concatenate([qkv_weight, out_weight], axis=1)
    if kernels:
        shards, acts, ada, seg_col, seg_row, bins = kernel_inputs(
            segments, conditions[0], noise_bins[0], bin_counts[0], ada_weight, first, up_weight
        )
        (
            weights, down_part, slope, hidden_one, queries, sides, log_total, context_low, attended,
            middle, hidden_two, mlp_out, tokens_out, table, conds, level, grad_mlp, seg_all,
        ) = run_forward(
            shards, down_weight, acts, ada, tokens_in[0], cotangent[0], seg_col, seg_row, bins, share
        )
        given = (
            weights, down_part, slope, middle, attended, mlp_out, hidden_one, queries, sides, log_total,
            context_low, hidden_two, grad_mlp, table, conds, level, seg_all, seg_col, tokens_in[0],
            cotangent[0], ada,
        )
        _, _, rows, down_grad, tokens_grad, ada_grad, silu_part = run_backward(given, share)
        rows = rows[:, :, :share].astype(jnp.float32).transpose(0, 2, 1, 3).reshape(2, share, 4 * width)
        first_grad, up_grad, ada_grad = rows[0], rows[1], ada_grad[:share]
        grad_silu = silu_part[:, :, :CROPS, :share].transpose(2, 1, 0, 3).reshape(CROPS, width)
    else:
        tokens_out, tokens_grad, grad_silu, ada_grad, first_grad, up_grad, down_grad = layer_plain(
            tokens_float, segments, conditions[0], noise_bins[0], bin_counts[0], cotangent[0],
            ada_weight, first, up_weight, down_weight,
        )
    silu_pull = jax.vjp(jax.nn.silu, conditions[0].astype(jnp.float32))[1]
    cond_grad = silu_pull(grad_silu)[0]
    return (
        tokens_out[None],
        tokens_grad[None],
        cond_grad[None],
        ada_grad,
        first_grad[:, : 3 * width],
        first_grad[:, 3 * width :],
        up_grad,
        down_grad,
    )


def solution(mesh):
    placed = (
        P("dp", "sp", None),
        P("dp", "sp"),
        P("dp", None, None),
        P("dp", None),
        P("dp", None),
        P("dp", "sp", None),
        P(("dp", "sp"), None),
        P(("dp", "sp"), None),
        P(("dp", "sp"), None),
        P(("dp", "sp"), None),
        P(("dp", "sp"), None),
    )
    return jax.shard_map(
        partial(on_device, mesh.shape["dp"] == 16 and mesh.shape["sp"] == 2),
        mesh=mesh,
        in_specs=placed,
        out_specs=(
            P("dp", "sp", None),
            P("dp", "sp", None),
            P("dp", None, None),
            P(("dp", "sp"), None),
            P(("dp", "sp"), None),
            P(("dp", "sp"), None),
            P(("dp", "sp"), None),
            P(("dp", "sp"), None),
        ),
        check_vma=False,
    )
```

```python
from functools import partial
import math

import jax
import jax.numpy as jnp
from jax import lax
from jax.experimental import pallas as pl
from jax.experimental.pallas import tpu as pltpu
from jax.sharding import PartitionSpec as P

HEADS = 16
CROPS = 4
NBINS = 8
EPSILON = 1e-06
LARGE_NEGATIVE = -1e30
GELU_SCALE = math.sqrt(2.0 / math.pi)
GELU_CUBE = 0.044715

MESH = pl.DeviceIdType.MESH
PAD = 48
NEAR = (80, 64)
FAR = (32, 32)
HELD = 6
FORWARD_AFTER = (
    0, 2, 9, 18, 20, 22, 25, 26, 30, 30, 30, 32, 41, 41, 41, 41, 42, 43, 43, 43, 46, 47, 50, 50, 50, 51, 52, 53, 55, 56, 56, 56, 56, 62, 64, 66,
)
BACKWARD_AFTER = (
    1, 7, 8, 13, 17, 18, 19, 20, 21, 24, 24, 27, 32, 33, 36, 36, 41, 43, 43, 44, 46, 47, 48, 49, 50, 52, 55, 55, 65, 70, 71, 76, 76, 76, 77, 83, 84, 92, 93, 97, 105,
)
CHIPS = 16
BAND = 1792
PLACES = ((0, 0), (0, 1), (1, 0), (1, 1))


def position():
    d = lax.axis_index("dp")
    c = lax.axis_index("sp")
    return d // 4, (d // 2) % 2, d % 2, c


def device(z, y, x, c):
    return (z * 4 + y * 2 + x, c)


def block_of(kind, zy, group):
    if kind == 2:
        return zy // 2, (zy % 2) * 4 + group
    return group, zy


def level_of(z, k):
    if k == 0:
        return z
    upper = z // 2
    inner = z * (1 - upper) + (3 - z) * upper
    step = k - inner if k == 1 else k
    return step * (1 - upper) + (3 - step) * upper


def greet(peers, meanwhile=None):
    barrier = pltpu.get_barrier_semaphore()
    for peer in peers:
        pl.semaphore_signal(barrier, inc=1, device_id=peer, device_id_type=MESH)
    if meanwhile is not None:
        meanwhile()
    pl.semaphore_wait(barrier, len(peers))


def remote(src, dst, send, recv, target):
    return pltpu.make_async_remote_copy(
        src_ref=src,
        dst_ref=dst,
        send_sem=send,
        recv_sem=recv,
        device_id=target,
        device_id_type=MESH,
    )


def arrive(ref, sem, target):
    remote(ref, ref, sem, sem, target).wait_recv()


def row_selector(rows, share):
    shape = (rows, 4 * PAD)
    row = lax.broadcasted_iota(jnp.int32, shape, 0)
    column = lax.broadcasted_iota(jnp.int32, shape, 1)
    picked = jnp.zeros(shape, jnp.bool_)
    for k in range(4):
        inside = (row >= k * share) & (row < (k + 1) * share)
        picked = picked | (inside & (column == row - k * share + k * PAD))
    return picked.astype(jnp.float32).astype(jnp.bfloat16)


def product(left, right):
    return jnp.dot(left, right, preferred_element_type=jnp.float32)


def product_by_rows(left, right):
    return lax.dot_general(left, right, (((0,), (0,)), ((), ())), preferred_element_type=jnp.float32)


def product_by_columns(left, right):
    return lax.dot_general(left, right, (((1,), (1,)), ((), ())), preferred_element_type=jnp.float32)


def chunks(rows, body, first=0, step=16):
    def run(i, carry):
        body(pl.ds(pl.multiple_of(first + i * step, step), step))
        return carry

    lax.fori_loop(0, rows // step, run, 0)


def normed(values):
    center = values - jnp.mean(values, axis=-1, keepdims=True)
    inverse = lax.rsqrt(jnp.mean(center * center, axis=-1, keepdims=True) + EPSILON)
    return center * inverse, inverse


def pick(segments, table, first, column, width):
    columns = slice(column * width, (column + 1) * width)
    value = table[first + 3 : first + 4, columns]
    for crop in (2, 1, 0):
        value = jnp.where(segments == crop, table[first + crop : first + crop + 1, columns], value)
    return value


def window_of(head, size, width):
    start = jnp.minimum((head * size) // 128, width // 128 - 2) * 128
    start = pl.multiple_of(start, 128)
    lane = lax.broadcasted_iota(jnp.int32, (1, 256), 1) + start
    return pl.ds(start, 256), (lane >= head * size) & (lane < (head + 1) * size)


def share_window(device_number, share, width):
    column = device_number * share
    start = jnp.minimum(column // 128, width // 128 - 2) * 128
    return pl.multiple_of(start, 128), column - start


def forward_kernel(share, qkv_ref, out_weight_ref, up_ref, down_ref, cond_ref, noise_ref, counts_ref, given_ada_ref,
                   tokens_ref, cot_ref, seg_ref,
                   weights_ref, down_part_ref, slope_ref, active_ref, sides_out_ref, attended_out_ref, middle_out_ref,
                   hidden_ref, query_ref, total_ref, context_ref, hidden_two_ref, table_ref,
                   conds_ref, level_ref, grad_mlp, seg_all, seg_col_ref, ada_ref,
                   full, shards_ref, stage, acts, acts_low, windows, part, part_recv, band, band_diag, band_x, band_y,
                   band_z, halves_of, sides_ref, attended_ref, middle_ref, bias, work, active, slope, *sems):
    (
        group_send, group_recv, z_send, z_recv, zd_send, zd_recv, x_send, x_recv, y_send, y_recv,
        dx_send, dx_recv, dy_send, dy_recv, c_send, c_recv,
        cond_send, cond_recv, pc_send, pc_recv, pd_send, pd_recv, px_send, px_recv, py_send, py_recv,
        pz_send, pz_recv, pm_send, pm_recv, seg_send, seg_recv, kv_send, kv_recv,
        save_sem, grad_sem, slope_sem, block_sem, store_sem,
    ) = sems
    z, y, x, c = position()
    me = z * 4 + y * 2 + x
    group = x * 2 + c
    zy = z * 2 + y
    rows = 4 * share
    count, width = tokens_ref.shape
    x_peer, y_peer, c_peer = device(z, y, 1 - x, c), device(z, 1 - y, x, c), device(z, y, x, 1 - c)
    partners = [(x, 1 - c), (1 - x, c), (1 - x, 1 - c)]

    def prepare():
        tail = share // 16 * 16
        for a in range(2):
            for q in range(4):
                source, at = (up_ref, q) if a else ((out_weight_ref, 0) if q == 3 else (qkv_ref, q))
                shards_ref[a, q, tail:, :] = jnp.zeros((PAD - tail, width), jnp.bfloat16)
                shards_ref[a, q, :share, :] = source[:, at * width : (at + 1) * width]
        ada_ref[tail:, :] = jnp.zeros((PAD - tail, ada_ref.shape[1]), jnp.bfloat16)
        ada_ref[:share, :] = given_ada_ref[...]
        cond = cond_ref[...].astype(jnp.float32)
        acts[...] = jnp.zeros_like(acts)
        acts[:CROPS, :] = cond * (1.0 / (1.0 + jnp.exp(-cond)))
        counts = counts_ref[...].astype(jnp.float32)
        for tile in range(width // 128):
            acts[CROPS : CROPS + 1, tile * 128 : tile * 128 + NBINS] = counts
        acts_low[...] = acts[...].astype(jnp.bfloat16)
        seg_all[c] = jnp.broadcast_to(seg_ref[...], (8, count))
        seg_col_ref[...] = jnp.transpose(jnp.broadcast_to(seg_ref[...], (128, count)))
        for a in range(2):
            stage[a, pl.ds(pl.multiple_of(group * PAD, 16), PAD), :] = shards_ref[a, group]
        start, _ = share_window(2 * me + c, share, width)
        windows[me] = acts_low[:, pl.ds(start, 256)]

    greet(
        [((me + k) % CHIPS, c) for k in range(1, CHIPS)] + [c_peer, device(z, y, 1 - x, 1 - c)], prepare
    )
    sends = {a: [] for a in (0, 1, 2, "other")}

    def send(a, *args):
        copy = remote(*args)
        copy.start()
        sends[a].append((None, copy))

    def finish_sends(a):
        for go, copy in sends[a]:
            if go is None:
                copy.wait_send()
            else:
                pl.when(go)(copy.wait_send)
        sends[a] = []

    level = partial(level_of, z)

    def place(a, k, other_y, other_x, core=None, first=0, last=None):
        yy = 1 - y if other_y else y
        xx = 1 - x if other_x else x
        cc = c if core is None else core
        block, row = block_of(a, level(k) * 2 + yy, xx * 2 + cc)
        count = (rows if last is None else last) - first
        return full.at[a, block, pl.ds(pl.multiple_of(row * rows + first, 16), count)]

    def cuts(k):
        top, low = FAR if k else NEAR
        return top, rows - low

    def along(a, k, ref, send_sem, recv_sem):
        source = level(k)
        for way, step in ((0, 1), (1, -1)):
            to = z + step
            go = (to >= 0) & (to < 4)
            if k:
                go = go & ((source < z) if step == 1 else (source > z))
            copy = remote(ref, ref, send_sem.at[a, k, way], recv_sem.at[a, source], device(jnp.clip(to, 0, 3), y, x, c))
            pl.when(go)(copy.start)
            sends[a].append((go, copy))

    def from_line(a, k, ref, recv_sem):
        source = level(k)
        arrive(ref, recv_sem.at[a, source], device((z + 1) % 4, y, x, c))

    for a in range(2):
        for j, (px, pc) in enumerate(partners):
            send(
                "other",
                shards_ref.at[a, px * 2 + pc],
                stage.at[a, pl.ds(pl.multiple_of(group * PAD, 16), PAD)],
                group_send.at[a, j],
                group_recv.at[a, j],
                device(z, y, px, pc),
            )
    for k in range(1, CHIPS):
        to = (me + k) % CHIPS
        start, _ = share_window(2 * to + c, share, width)
        send("other", acts_low.at[:, pl.ds(start, 256)], windows.at[me], cond_send.at[k - 1], cond_recv.at[k - 1], (to, c))
    send("other", seg_all.at[c], seg_all.at[c], seg_send, seg_recv, c_peer)

    def own(a):
        block, row = block_of(a, zy, group)
        here = pl.ds(pl.multiple_of(row * rows, 16), rows)
        if a < 2:
            for j, (px, pc) in enumerate(partners):
                arrive(
                    stage.at[a, pl.ds(pl.multiple_of((px * 2 + pc) * PAD, 16), PAD)],
                    group_recv.at[a, j],
                    device(z, y, px, pc),
                )
            full[a, block, here, :] = product(row_selector(rows, share), stage[a]).astype(jnp.bfloat16)
        else:
            full[a, block, here, :] = down_ref[...]
        along(a, 0, place(a, 0, 0, 0), z_send, z_recv)

    def to_core(a, k, pos):
        piece = place(a, k, *PLACES[pos])
        send(a, piece, piece, c_send.at[a, k, pos], c_recv.at[a, k, pos], c_peer)

    def spread(a, k):
        if k:
            from_line(a, k, place(a, k, 0, 0), z_recv)
            along(a, k, place(a, k, 0, 0), z_send, z_recv)
        top, low = cuts(k)
        for h, first, last in ((0, 0, top), (1, top, rows)):
            part = place(a, k, 0, 0, None, first, last)
            send(a, part, part, x_send.at[a, k, h], x_recv.at[a, k, h], x_peer)
        for h, first, last in ((1, low, rows), (0, 0, low)):
            part = place(a, k, 0, 0, None, first, last)
            send(a, part, part, y_send.at[a, k, h], y_recv.at[a, k, h], y_peer)
        to_core(a, k, 0)

    def turn_y(a, k):
        part = place(a, k, 0, 1, None, 0, cuts(k)[0])
        arrive(part, x_recv.at[a, k, 0], x_peer)
        send(a, part, part, dy_send.at[a, k], dy_recv.at[a, k], y_peer)

    def turn_x(a, k):
        part = place(a, k, 1, 0, None, cuts(k)[1], rows)
        arrive(part, y_recv.at[a, k, 1], y_peer)
        send(a, part, part, dx_send.at[a, k], dx_recv.at[a, k], x_peer)

    def share_sides(a, k):
        top, low = cuts(k)
        arrive(place(a, k, 0, 1, None, top, rows), x_recv.at[a, k, 1], x_peer)
        to_core(a, k, 1)
        arrive(place(a, k, 1, 0, None, 0, low), y_recv.at[a, k, 0], y_peer)
        to_core(a, k, 2)

    def finish(a, k):
        top, low = cuts(k)
        arrive(place(a, k, 1, 1, None, 0, top), dy_recv.at[a, k], y_peer)
        arrive(place(a, k, 1, 1, None, low, rows), dx_recv.at[a, k], x_peer)
        middle = place(a, k, 1, 1, None, FAR[0], rows - FAR[1])
        if k:
            from_line(a, k, middle, zd_recv)
        along(a, k, middle, zd_send, zd_recv)
        to_core(a, k, 3)

    saves = []

    def keep(src, dst, sem):
        copy = pltpu.make_async_copy(src, dst, sem)
        copy.start()
        saves.append(copy)

    def arrive_cores(a, k):
        for pos, (oy, ox) in enumerate(PLACES):
            arrive(place(a, k, oy, ox, 1 - c), c_recv.at[a, k, pos], c_peer)

    def complete(a):
        for k in range(4):
            arrive_cores(a, k)
        keep(full.at[a], weights_ref.at[a], save_sem.at[a])

    def complete_level(k):
        arrive_cores(2, k)
        keep(full.at[2, level(k)], weights_ref.at[2, level(k)], block_sem.at[k])

    def mod_start():
        for k in range(1, CHIPS):
            source = (me - k + CHIPS) % CHIPS
            arrive(windows.at[source], cond_recv.at[k - 1], (source, c))
        _, offset = share_window(2 * me + c, share, width)
        lane = lax.broadcasted_iota(jnp.int32, (256, 128), 1)
        picked = (lax.broadcasted_iota(jnp.int32, (256, 128), 0) == lane + offset) & (lane < share)
        picked = picked.astype(jnp.float32).astype(jnp.bfloat16)
        mine = product(windows[...].reshape(CHIPS * 16, 256), picked)
        conds_ref[...] = mine.reshape(CHIPS, 16, 128).astype(jnp.bfloat16)
        here = mine.reshape(CHIPS, 16, 128)[:, :8, :].reshape(CHIPS * 8, 128)
        row = lax.broadcasted_iota(jnp.int32, here.shape, 0) % 8
        here = jnp.where(row < CROPS, here, 0.0)
        upper = here.astype(jnp.bfloat16)
        lower = pltpu.roll(here, CROPS, 0).astype(jnp.bfloat16)
        side = ada_ref.shape[1] // 2
        part[...] = product(upper[:, :PAD], ada_ref[:, :side]) + product(lower[:, :PAD], ada_ref[:, side:])
        far = pl.ds(pl.multiple_of((1 - c) * (side - BAND), 128), BAND)
        send("other", part.at[:, far], part_recv, pc_send, pc_recv, c_peer)

    def block8(zz, yy, xx):
        return pl.ds(pl.multiple_of((zz * 4 + yy * 2 + xx) * 8, 8), 8)

    def mod_cores():
        arrive(part_recv, pc_recv, c_peer)
        side = ada_ref.shape[1] // 2
        near = pl.ds(pl.multiple_of(c * (side - BAND), 128), BAND)
        band[...] = part[:, near] + part_recv[...]
        for k in range(4):
            zz = (z + k) % 4
            src = band.at[block8(zz, 1 - y, 1 - x)]
            send("other", src, band_diag.at[k], pd_send.at[k], pd_recv.at[k], x_peer if k % 2 else y_peer)

    def mod_plane():
        for k in range(4):
            zz = (z + k) % 4
            to_x, to_y = block8(zz, y, 1 - x), block8(zz, 1 - y, x)
            arrive(band_diag.at[k], pd_recv.at[k], x_peer if k % 2 else y_peer)
            fold = to_y if k % 2 else to_x
            band[fold, :] = band[fold, :] + band_diag[k]
            send("other", band.at[to_x], band_x.at[k], px_send.at[k], px_recv.at[k], x_peer)
            send("other", band.at[to_y], band_y.at[k], py_send.at[k], py_recv.at[k], y_peer)

    def mod_line():
        for k in (1, 2, 3, 0):
            zz = (z + k) % 4
            mine = block8(zz, y, x)
            arrive(band_x.at[k], px_recv.at[k], x_peer)
            arrive(band_y.at[k], py_recv.at[k], y_peer)
            band[mine, :] = band[mine, :] + band_x[k] + band_y[k]
            if k:
                send("other", band.at[mine], band_z.at[k - 1], pz_send.at[k - 1], pz_recv.at[k - 1], device(zz, y, x, c))

    def mod_last():
        for k in (1, 2, 3):
            arrive(band_z.at[k - 1], pz_recv.at[k - 1], device((z - k + 4) % 4, y, x, c))
        halves_of[c] = band[block8(z, y, x), :] + band_z[0] + band_z[1] + band_z[2]
        send("other", halves_of.at[c], halves_of.at[c], pm_send, pm_recv, c_peer)

    def mod_end():
        arrive(halves_of.at[1 - c], pm_recv, c_peer)
        side = ada_ref.shape[1] // 2
        table_ref[:, :BAND] = halves_of[0]
        table_ref[:, BAND:] = halves_of[1][:, 2 * BAND - side :]
        counts = jnp.sum(windows[:, :, :128].astype(jnp.float32)[:, CROPS : CROPS + 1, :], axis=0)
        lane = lax.broadcasted_iota(jnp.int32, counts.shape, 1)
        weight = jnp.where(lane < NBINS, 40.0 * CHIPS / jnp.where(lane < NBINS, counts, 1.0), 0.0)
        level_ref[...] = jnp.zeros_like(level_ref)
        for crop in range(CROPS):
            mine = jnp.where(lane == noise_ref[:, crop : crop + 1], weight, 0.0)
            level_ref[crop : crop + 1, :] = jnp.broadcast_to(jnp.sum(mine, axis=-1, keepdims=True), (1, 128))

    def first_norm(part_of):
        def body(at):
            segments = seg_col_ref[at, :1]
            value, _ = normed(tokens_ref[at, :].astype(jnp.float32))
            value = value * (1.0 + pick(segments, table_ref, 0, 1, width))
            hidden_ref[at, :] = (value + pick(segments, table_ref, 0, 0, width)).astype(jnp.bfloat16)

        chunks(count // 2, body, part_of * (count // 2))
        if part_of == 0:
            arrive(seg_all.at[1 - c], seg_recv, c_peer)
            return
        for h in (0, 1):
            same = seg_col_ref[:, :1] == seg_all[h][:1, :]
            bias[:, h * count : (h + 1) * count] = jnp.where(same, 0.0, LARGE_NEGATIVE)

    def project(q):
        value = product(hidden_ref[...], full[0, q]).astype(jnp.bfloat16)
        if q == 0:
            query_ref[...] = value
            total_ref[...] = jnp.zeros_like(total_ref)
            work[...] = jnp.zeros_like(work)
            return
        here = pl.ds(pl.multiple_of(c * count, 256), count)
        sides_ref[q - 1, here, :] = value
        send("other", sides_ref.at[q - 1, here], sides_ref.at[q - 1, here], kv_send.at[q - 1], kv_recv.at[q - 1], c_peer)

    def attend(first, last):
        if first == 0:
            there = pl.ds(pl.multiple_of((1 - c) * count, 256), count)
            for q in (0, 1):
                arrive(sides_ref.at[q, there], kv_recv.at[q], c_peer)
            keep(sides_ref, sides_out_ref, store_sem.at[0])
        size = width // HEADS
        scale = 1.0 / math.sqrt(size)

        def body(head, carry):
            columns, inside = window_of(head, size, width)
            query = query_ref[:, columns]
            query = jnp.where(inside, query, jnp.zeros_like(query))
            scores = product_by_columns(query, sides_ref[0, :, columns]) * scale + bias[...]
            top = jnp.max(scores, axis=-1, keepdims=True)
            raised = jnp.exp(scores - top)
            total = jnp.sum(raised, axis=-1, keepdims=True)
            chance = (raised * (1.0 / total)).astype(jnp.bfloat16)
            context = product(chance, sides_ref[1, :, columns])
            work[:, columns] = jnp.where(inside, context, work[:, columns])
            lane = lax.broadcasted_iota(jnp.int32, (1, 128), 1)
            total_ref[...] = jnp.where(lane == head, top + jnp.log(total), total_ref[...])
            return carry

        lax.fori_loop(first, last, body, 0)

    def mix():
        context_ref[...] = work[...].astype(jnp.bfloat16)
        attended_ref[...] = product(context_ref[...], full[0, 3])
        keep(attended_ref, attended_out_ref, store_sem.at[1])

    def second_norm(part_of):
        def body(at):
            segments = seg_col_ref[at, :1]
            gate = pick(segments, table_ref, 0, 2, width)
            middle = tokens_ref[at, :].astype(jnp.float32) + gate * attended_ref[at, :]
            middle_ref[at, :] = middle
            value, _ = normed(middle)
            value = value * (1.0 + pick(segments, table_ref, 4, 1, width))
            hidden_two_ref[at, :] = (value + pick(segments, table_ref, 4, 0, width)).astype(jnp.bfloat16)
            level = level_ref[3:4, :1]
            for crop in (2, 1, 0):
                level = jnp.where(segments == crop, level_ref[crop : crop + 1, :1], level)
            grad = cot_ref[at, :].astype(jnp.float32) * level
            grad_mlp[at, :] = (grad * pick(segments, table_ref, 4, 2, width)).astype(jnp.bfloat16)

        chunks(count // 2, body, part_of * (count // 2))
        if part_of:
            keep(middle_ref, middle_out_ref, store_sem.at[2])

    slope_copies = {}

    def expand(q):
        work[...] = product(hidden_two_ref[...], full[1, q])

    def bend(q):
        if q >= 2:
            slope_copies[q - 2].wait()

        def body(at):
            u = work[at, :]
            square = u * u
            curve = jnp.tanh(GELU_SCALE * (u + GELU_CUBE * (square * u)))
            active[q, at, :] = (0.5 * u * (1.0 + curve)).astype(jnp.bfloat16)
            inner = GELU_SCALE * (1.0 + 3.0 * GELU_CUBE * square)
            slope[q % 2, at, :] = 0.5 * (1.0 + curve) + 0.5 * u * (1.0 - curve * curve) * inner

        chunks(count, body)
        copy = pltpu.make_async_copy(slope.at[q % 2], slope_ref.at[q], slope_sem.at[q % 2])
        copy.start()
        slope_copies[q] = copy
        keep(active.at[q], active_ref.at[q], store_sem.at[3 + q])

    def down_grad(q):
        if q == 0:
            finish_sends(0)
            saves.pop(0).wait()
        full[0, q] = product_by_rows(active[q], grad_mlp[...]).astype(jnp.bfloat16)
        keep(full.at[0, q], down_part_ref.at[q], grad_sem.at[q])

    order = [(a, k) for a in range(3) for k in range(4)]
    steps = []
    for i in range(len(order) + 2):
        if i < len(order):
            if order[i][1] == 0:
                steps.append(partial(own, order[i][0]))
            steps.append(partial(spread, *order[i]))
        if 1 <= i <= len(order):
            steps += [partial(step, *order[i - 1]) for step in (turn_y, turn_x, share_sides)]
        if 2 <= i:
            steps.append(partial(finish, *order[i - 2]))
        if i > 10:
            steps.append(partial(complete_level, i - 11))
    layer = [mod_start, mod_cores, mod_plane, mod_line, mod_last, mod_end]
    layer += [partial(first_norm, h) for h in (0, 1)] + [partial(complete, 0)]
    layer += [partial(project, q) for q in (1, 2, 0)] + [partial(attend, h, h + 2) for h in range(0, HEADS, 2)]
    layer += [mix, partial(second_norm, 0), partial(second_norm, 1), partial(complete, 1)]
    for q in range(4):
        layer += [partial(expand, q), partial(bend, q)]
    layer += [partial(down_grad, q) for q in range(4)]
    interleave(steps, layer, FORWARD_AFTER)
    complete_level(3)
    for copy in saves:
        copy.wait()
    for q in (2, 3):
        slope_copies[q].wait()
    for a in (1, 2, "other"):
        finish_sends(a)


def run_forward(qkv, out_weight, up, down, cond, noise, counts, ada, tokens, cot, segments):
    count, width = tokens.shape
    share = qkv.shape[0]
    dma = pltpu.SemaphoreType.DMA
    low, wide, whole = jnp.bfloat16, jnp.float32, jnp.int32
    side = ada.shape[1] // 2
    vmem, any_ = pl.BlockSpec(memory_space=pltpu.VMEM), pl.BlockSpec(memory_space=pl.ANY)
    out, buffer = jax.ShapeDtypeStruct, pltpu.VMEM
    return pl.pallas_call(
        partial(forward_kernel, share),
        out_shape=(
            out((3, 4, width, width), low),
            out((4, width, width), low),
            out((4, count, width), wide),
            out((4, count, width), low),
            out((2, 2 * count, width), low),
            out((count, width), wide),
            out((count, width), wide),
            out((count, width), low),
            out((count, width), low),
            out((count, 128), wide),
            out((count, width), low),
            out((count, width), low),
            out((8, side), wide),
            out((CHIPS, 16, 128), low),
            out((8, 128), wide),
            out((count, width), low),
            out((2, 8, count), whole),
            out((count, 128), whole),
            out((PAD, 2 * side), low),
        ),
        in_specs=[vmem] * 11,
        out_specs=[any_] * 7 + [vmem] * 12,
        scratch_shapes=[
            buffer((3, 4, width, width), low),
            buffer((2, 4, PAD, width), low),
            buffer((2, 4 * PAD, width), low),
            buffer((16, width), wide),
            buffer((16, width), low),
            buffer((CHIPS, 16, 256), low),
            buffer((CHIPS * 8, side), wide),
            buffer((CHIPS * 8, BAND), wide),
            buffer((CHIPS * 8, BAND), wide),
            buffer((4, 8, BAND), wide),
            buffer((4, 8, BAND), wide),
            buffer((4, 8, BAND), wide),
            buffer((3, 8, BAND), wide),
            buffer((2, 8, BAND), wide),
            buffer((2, 2 * count, width), low),
            buffer((count, width), wide),
            buffer((count, width), wide),
            buffer((count, 2 * count), wide),
            buffer((count, width), wide),
            buffer((4, count, width), low),
            buffer((2, count, width), wide),
            dma((2, 3)), dma((2, 3)), dma((3, 4, 2)), dma((3, 4)), dma((3, 4, 2)), dma((3, 4)),
            dma((3, 4, 2)), dma((3, 4, 2)), dma((3, 4, 2)), dma((3, 4, 2)),
            dma((3, 4)), dma((3, 4)), dma((3, 4)), dma((3, 4)),
            dma((3, 4, 4)), dma((3, 4, 4)),
            dma((CHIPS - 1,)), dma((CHIPS - 1,)), dma, dma, dma((4,)), dma((4,)),
            dma((4,)), dma((4,)), dma((4,)), dma((4,)), dma((3,)), dma((3,)), dma, dma, dma, dma,
            dma((2,)), dma((2,)), dma((2,)), dma((4,)), dma((2,)), dma((4,)), dma((7,)),
        ],
        compiler_params=pltpu.CompilerParams(
            collective_id=0, has_side_effects=True, vmem_limit_bytes=63 * 2**20
        ),
        name="forward",
    )(qkv, out_weight, up, down, cond, noise, counts, ada, tokens, cot, segments)


def interleave(steps, layer, after):
    done = 0
    for count, step in enumerate(steps):
        while done < len(layer) and after[done] <= count:
            layer[done]()
            done += 1
        step()
    for step in layer[done:]:
        step()


def add_rows(dst, sources, start, rows):
    def body(i, carry):
        where = pl.ds(pl.multiple_of(start + i * 16, 16), 16)
        total = dst[where, :].astype(jnp.float32)
        for source in sources:
            total = total + source[where, :].astype(jnp.float32)
        dst[where, :] = total.astype(dst.dtype)
        return carry

    lax.fori_loop(0, rows // 16, body, 0)


def split_low(values):
    high = values.astype(jnp.bfloat16)
    return high, (values - high.astype(jnp.float32)).astype(jnp.bfloat16)


def backward_kernel(share, weights_ref, down_part_ref, slope_ref, middle_ref, attended_ref, active_ref,
                    hidden_ref, query_ref, sides_ref, total_ref, context_ref, hidden_two_ref,
                    grad_mlp_ref, table_ref, conds_ref, level_ref, seg_all_ref, seg_col_ref, tokens_ref,
                    cot_ref, ada_ref,
                    mixer_part_ref, up_part_ref, rows_ref, down_ref, tokens_grad_ref, ada_grad_ref, silu_ref,
                    out_ref,
                    held, from_core, diag, from_x, from_y, piece_line, diag_line, spare, block, part, quad, lows,
                    work, grad_middle, grad_context, leave, enter, bias, sums, sums_row, sums_core, band, silu_part, silu_side,
                    *sems):
    (
        load_sem, c_send, c_recv, dx_send, dx_recv, dy_send, dy_recv, x_send, x_recv,
        y_send, y_recv, zo_send, zo_recv, zd_send, zd_recv, group_send, group_recv, block_sem, part_sem, quad_sem, low_sem, out_sem,
        side_send, side_recv, m_send, m_recv, mz_send, mz_recv, mx_send, mx_recv, my_send, my_recv,
        md_send, md_recv, mc_send, mc_recv, s_send, s_recv, sc_send, sc_recv,
    ) = sems
    z, y, x, c = position()
    me = z * 4 + y * 2 + x
    group = x * 2 + c
    rows = 4 * share
    count, width = tokens_ref.shape
    x_peer, y_peer, c_peer = device(z, y, 1 - x, c), device(z, 1 - y, x, c), device(z, y, x, 1 - c)
    partners = [(x, 1 - c), (1 - x, c), (1 - x, 1 - c)]
    greet(
        [((me + k) % CHIPS, c) for k in range(1, CHIPS)] + [c_peer, device(z, y, 1 - x, 1 - c)]
    )
    sends = {}

    def send(owner, *args):
        copy = remote(*args)
        copy.start()
        sends.setdefault(owner, []).append(copy)

    def finish_sends(owner):
        for copy in sends.pop(owner, []):
            copy.wait_send()

    order = [(a, k) for a in (2, 1, 0) for k in (3, 2, 1, 0)]
    given = (mixer_part_ref, up_part_ref, down_part_ref)
    loads = {}
    inner_rows = slice(FAR[0], rows - FAR[1])

    def cuts(i):
        top, low = FAR if order[i][1] else NEAR
        return top, rows - low

    def line(k):
        to = level_of(z, k)
        step = jnp.where(z < to, 1, -1)
        behind = z - step
        return to, z + step, (behind >= 0) & (behind < 4)

    def along(i, ref, lines, send_sem, recv_sem):
        a, k = order[i]
        to, after, _ = line(k)
        spot = jnp.where((after == to) & (z > to), 4, to)
        copy = remote(ref, lines.at[a % 2, spot], send_sem.at[a, k], recv_sem.at[a, spot], device(after, y, x, c))
        copy.start()
        return copy

    def from_line(i, lines, recv_sem, spot):
        a = order[i][0]
        arrive(lines.at[a % 2, spot], recv_sem.at[a, spot], device((z + 1) % 4, y, x, c))

    def hold(i, ref, lines, send_sem, recv_sem):
        sends.setdefault(("held", i), []).append(
            remote(ref, lines.at[0, 0], send_sem.at[order[i]], recv_sem.at[order[i][0], 0], x_peer)
        )

    def begin(i):
        a, k = order[i]
        if i % 4 == 0:
            for n in sorted(going):
                going.pop(n).wait()
        finish_sends(("held", i - HELD))
        zz = level_of(z, k)
        for pos in (3, 1, 2, 0):
            yy = 1 - y if PLACES[pos][0] else y
            xx = 1 - x if PLACES[pos][1] else x
            for cc in (1 - c, c):
                where, row = block_of(a, zz * 2 + yy, xx * 2 + cc)
                src = given[a].at[where, pl.ds(pl.multiple_of(row * rows, 16), rows)]
                if cc is c:
                    loads[i, pos] = pltpu.make_async_copy(src, held.at[i % HELD, pos], load_sem.at[i, pos])
                    loads[i, pos].start()
                else:
                    send("core", src, from_core.at[i % 4, pos], c_send.at[i, pos], c_recv.at[i, pos], c_peer)

    def pair(i, pos):
        k = order[i][1]
        top, low = cuts(i)
        mine = held.at[i % HELD, pos]
        loads[i, pos].wait()
        arrive(from_core.at[i % 4, pos], c_recv.at[i, pos], c_peer)
        add_rows(mine, [from_core.at[i % 4, pos]], 0, rows)
        if pos == 3 and k:
            diagonal(i)
            part = mine.at[inner_rows]
            hold(i, part, diag_line, zd_send, zd_recv)
            _, _, fed = line(k)

            @pl.when(jnp.logical_not(fed))
            def _():
                along(i, part, diag_line, zd_send, zd_recv)

        if pos == 1:
            part = mine.at[top:rows]
            send(("held", i), part, from_x.at[i % 6, top:rows], x_send.at[i, 1], x_recv.at[i, 1], x_peer)
        if pos == 2:
            part = mine.at[0:low]
            send(("held", i), part, from_y.at[i % 6, 0:low], y_send.at[i, 0], y_recv.at[i, 0], y_peer)

    def diagonal(i):
        top, low = cuts(i)
        mine, far = held.at[i % HELD, 3], diag.at[i % 5]
        send(("held", i), mine.at[0:top], far.at[0:top], dy_send.at[i], dy_recv.at[i], y_peer)
        send(("held", i), mine.at[low:rows], far.at[low:rows], dx_send.at[i], dx_recv.at[i], x_peer)

    def diag_along(i):
        k = order[i][1]
        mine = held.at[i % HELD, 3, inner_rows]
        size = rows - FAR[0] - FAR[1]
        if k:
            to, _, fed = line(k)

            @pl.when(fed)
            def _():
                from_line(i, diag_line, zd_recv, to)
                add_rows(mine, [diag_line.at[order[i][0] % 2, to]], 0, size)
                along(i, mine, diag_line, zd_send, zd_recv)

        else:
            for spot, here in ((z, z > 0), (4, z < 3)):

                @pl.when(here)
                def _():
                    from_line(i, diag_line, zd_recv, spot)
                    add_rows(mine, [diag_line.at[order[i][0] % 2, spot]], 0, size)

            diagonal(i)

    def relay(i):
        top, low = cuts(i)
        far = diag.at[i % 5]
        arrive(far.at[0:top], dy_recv.at[i], y_peer)
        add_rows(held.at[i % HELD, 1], [far], 0, top)
        part = held.at[i % HELD, 1, 0:top]
        send(("held", i), part, from_x.at[i % 6, 0:top], x_send.at[i, 0], x_recv.at[i, 0], x_peer)
        arrive(far.at[low:rows], dx_recv.at[i], x_peer)
        add_rows(held.at[i % HELD, 2], [far], low, rows - low)
        part = held.at[i % HELD, 2, low:rows]
        send(("held", i), part, from_y.at[i % 6, low:rows], y_send.at[i, 1], y_recv.at[i, 1], y_peer)

    def plane(i):
        k = order[i][1]
        top, low = cuts(i)
        mine = held.at[i % HELD, 0]
        arrive(from_x.at[i % 6, 0:top], x_recv.at[i, 0], x_peer)
        arrive(from_x.at[i % 6, top:rows], x_recv.at[i, 1], x_peer)
        arrive(from_y.at[i % 6, 0:low], y_recv.at[i, 0], y_peer)
        arrive(from_y.at[i % 6, low:rows], y_recv.at[i, 1], y_peer)
        add_rows(mine, [from_x.at[i % 6], from_y.at[i % 6]], 0, rows)
        if k:
            hold(i, mine, piece_line, zo_send, zo_recv)
            _, _, fed = line(k)

            @pl.when(jnp.logical_not(fed))
            def _():
                along(i, mine, piece_line, zo_send, zo_recv)

    def piece_along(i):
        a, k = order[i]
        mine = held.at[i % HELD, 0]
        if k:
            to, _, fed = line(k)

            @pl.when(fed)
            def _():
                from_line(i, piece_line, zo_recv, to)
                add_rows(mine, [piece_line.at[a % 2, to]], 0, rows)
                along(i, mine, piece_line, zo_send, zo_recv)

            return
        for spot, here in ((z, z > 0), (4, z < 3)):

            @pl.when(here)
            def _():
                from_line(i, piece_line, zo_recv, spot)
                add_rows(mine, [piece_line.at[a % 2, spot]], 0, rows)

        if a == 2:
            down_ref[...] = mine[...].astype(jnp.float32)
            return
        spare[a] = product_by_rows(row_selector(rows, share), mine[...]).astype(jnp.bfloat16)
        for j, (px, pc) in enumerate(partners):
            send(
                "end",
                spare.at[a, pl.ds(pl.multiple_of((px * 2 + pc) * PAD, 16), PAD)],
                rows_ref.at[a, group],
                group_send.at[a, j],
                group_recv.at[a, j],
                device(z, y, px, pc),
            )
        rows_ref[a, group] = spare[a, pl.ds(pl.multiple_of(group * PAD, 16), PAD), :]

    uses = [(2, q) for q in range(4)] + [(1, q) for q in range(4)] + [(0, 3), (0, 0), (0, 1), (0, 2)]
    coming = {}

    def fetch(n):
        if n < len(uses):
            copy = pltpu.make_async_copy(weights_ref.at[uses[n]], block.at[n % 2], block_sem.at[n % 2])
            copy.start()
            coming[n] = copy

    def take(n):
        coming[n].wait()
        return block[n % 2]

    going = {}

    def put(n, left, right, target):
        if n - 2 in going:
            going.pop(n - 2).wait()

        def body(i, carry):
            columns = pl.ds(pl.multiple_of(i * 384, 128), 384)
            part[n % 2, columns, :] = product_by_rows(left[:, columns], right[...]).astype(jnp.bfloat16)
            return carry

        lax.fori_loop(0, width // 384, body, 0)
        going[n] = pltpu.make_async_copy(part.at[n % 2], target, part_sem.at[n % 2])
        going[n].start()

    quads = {}

    def slopes(q):
        quads[q] = pltpu.make_async_copy(slope_ref.at[q], quad.at[q], quad_sem.at[q])
        quads[q].start()
        quads["active", q] = pltpu.make_async_copy(active_ref.at[q], lows.at[q], low_sem.at[q])
        quads["active", q].start()

    def through_down(q):
        quads.pop(("active", q)).wait()
        value = product(lows[q], take(q))
        grad_middle[...] = grad_middle[...] + value if q else value
        work[...] = product_by_columns(grad_mlp_ref[...], block[q % 2])
        fetch(q + 2)
        quads[q].wait()

        def body(at):
            lows[q, at, :] = (work[at, :] * quad[q, at, :]).astype(jnp.bfloat16)

        chunks(count, body)
        if q < 2:
            source = (middle_ref, attended_ref)[q]
            quads[q] = pltpu.make_async_copy(source, quad.at[q], quad_sem.at[q])
            quads[q].start()

    def up_grad(q):
        put(q, hidden_two_ref, lows.at[q], up_part_ref.at[q])

    def through_up(q):
        value = product_by_columns(lows[q], take(4 + q))
        work[...] = work[...] + value if q else value
        fetch(6 + q)

    def norm_pull(grad, value, inverse):
        return inverse * (
            grad
            - jnp.mean(grad, axis=-1, keepdims=True)
            - value * jnp.mean(grad * value, axis=-1, keepdims=True)
        )

    def add_sums(segments, which, value):
        for crop in range(CROPS):
            kept = jnp.where(segments == crop, value, 0.0)
            sums[which, crop] = sums[which, crop] + kept[:8] + kept[8:]

    def second_norm(half):
        if half == 0:
            for q in range(2):
                quads[q].wait()
            sums[...] = jnp.zeros_like(sums)

        def body(at):
            segments = seg_col_ref[at, :1]
            grad = work[at, :]
            middle, mlp = quad[0, at, :], grad_middle[at, :]
            value, inverse = normed(middle)
            gate = pick(segments, table_ref, 4, 2, width)
            leave[0, at, :] = (middle + gate * mlp).astype(jnp.bfloat16)
            level = level_ref[3:4, :1]
            for crop in (2, 1, 0):
                level = jnp.where(segments == crop, level_ref[crop : crop + 1, :1], level)
            grad_out = cot_ref[at, :].astype(jnp.float32) * level
            add_sums(segments, 3, grad)
            add_sums(segments, 4, grad * value)
            add_sums(segments, 5, grad_out * mlp)
            scaled = grad * (1.0 + pick(segments, table_ref, 4, 1, width))
            total = grad_out + norm_pull(scaled, value, inverse)
            grad_middle[at, :] = total
            add_sums(segments, 2, total * quad[1, at, :])
            lows[3, at, :] = (total * pick(segments, table_ref, 0, 2, width)).astype(jnp.bfloat16)

        chunks(count // 2, body, half * (count // 2))
        if half:
            quads["out"] = pltpu.make_async_copy(leave.at[0], out_ref, out_sem)
            quads["out"].start()

    def context_grad():
        grad_context[...] = product_by_columns(lows[3], take(8)).astype(jnp.bfloat16)
        fetch(10)

    def out_grad():
        put(4, context_ref, lows.at[3], mixer_part_ref.at[3])
        for h in (0, 1):
            same = seg_col_ref[:, :1] == seg_all_ref[h][:1, :]
            bias[:, h * count : (h + 1) * count] = jnp.where(same, 0.0, LARGE_NEGATIVE)

    def attend_back(first, last):
        size = width // HEADS
        scale = 1.0 / math.sqrt(size)

        def body(head, carry):
            columns, inside = window_of(head, size, width)
            query, keys = query_ref[:, columns], sides_ref[0, :, columns]
            grad = grad_context[:, columns]
            scores = product_by_columns(jnp.where(inside, query, jnp.zeros_like(query)), keys)
            lane = lax.broadcasted_iota(jnp.int32, (1, 128), 1)
            total = jnp.sum(jnp.where(lane == head, total_ref[...], 0.0), axis=-1, keepdims=True)
            chance = jnp.exp(scores * scale + bias[...] - total)
            pulled = product_by_columns(
                jnp.where(inside, grad, jnp.zeros_like(grad)), sides_ref[1, :, columns]
            )
            inner = jnp.sum(chance * pulled, axis=-1, keepdims=True)
            grad_scores = (chance * (pulled - inner)).astype(jnp.bfloat16)
            grad_query = (product(grad_scores, keys) * scale).astype(jnp.bfloat16)
            lows[0, :, columns] = jnp.where(inside, grad_query, lows[0, :, columns])
            grad_key = product_by_rows(grad_scores, query) * scale
            grad_value = product_by_rows(chance.astype(jnp.bfloat16), grad)
            for h in (0, 1):
                here = slice(h * count, (h + 1) * count)
                quad[h, :, columns] = jnp.where(inside, grad_key[here], quad[h, :, columns])
                quad[2 + h, :, columns] = jnp.where(inside, grad_value[here], quad[2 + h, :, columns])
            return carry

        lax.fori_loop(first, last, body, 0)

    def swap_sides():
        quads["out"].wait()
        for j in (0, 1):
            leave[j] = quad[2 * j + 1 - c].astype(jnp.bfloat16)
            send("end", leave.at[j], enter.at[j], side_send.at[j], side_recv.at[j], c_peer)

    def query_grad():
        put(5, hidden_ref, lows.at[0], mixer_part_ref.at[0])

    def side_grad(j):
        arrive(enter.at[j], side_recv.at[j], c_peer)

        def body(at):
            total = quad[2 * j + c, at, :] + enter[j, at, :].astype(jnp.float32)
            lows[1 + j, at, :] = total.astype(jnp.bfloat16)

        chunks(count, body)
        put(6 + j, hidden_ref, lows.at[1 + j], mixer_part_ref.at[1 + j])

    def through_qkv(q):
        value = product_by_columns(lows[q], take(9 + q))
        work[...] = work[...] + value if q else value
        fetch(11 + q)

    def first_norm(half):
        def body(at):
            segments = seg_col_ref[at, :1]
            grad = work[at, :]
            value, inverse = normed(tokens_ref[at, :].astype(jnp.float32))
            add_sums(segments, 0, grad)
            add_sums(segments, 1, grad * value)
            scaled = grad * (1.0 + pick(segments, table_ref, 0, 1, width))
            tokens_grad_ref[at, :] = grad_middle[at, :] + norm_pull(scaled, value, inverse)

        chunks(count // 2, body, half * (count // 2))

    def sums_leave():
        for which in range(6):
            for crop in range(CROPS):
                row = which // 3 * CROPS + crop
                columns = slice(which % 3 * width, (which % 3 + 1) * width)
                sums_row[row : row + 1, columns] = jnp.sum(sums[which, crop], axis=0, keepdims=True)
        send("end", sums_row, sums_core, m_send, m_recv, c_peer)

    side = sums_row.shape[1]

    def place(k, other_y, other_x):
        zz = (z - k + 4) % 4
        yy = 1 - y if other_y else y
        xx = 1 - x if other_x else x
        return band.at[c, pl.ds(pl.multiple_of((zz * 4 + yy * 2 + xx) * 8, 8), 8)]

    def sums_start():
        arrive(sums_core, m_recv, c_peer)
        near = pl.ds(pl.multiple_of(c * (side - BAND), 128), BAND)
        band[c, pl.ds(pl.multiple_of(me * 8, 8), 8), :] = sums_row[:, near] + sums_core[:, near]
        mine = place(0, 0, 0)
        for k in (1, 2, 3):
            send("end", mine, mine, mz_send.at[k - 1], mz_recv.at[k - 1], device((z + k) % 4, y, x, c))
        send("end", mine, mine, mx_send.at[0], mx_recv.at[0], x_peer)
        send("end", mine, mine, my_send.at[0], my_recv.at[0], y_peer)

    def sums_line():
        for k in (1, 2, 3):
            piece = place(k, 0, 0)
            arrive(piece, mz_recv.at[k - 1], device((z - k + 4) % 4, y, x, c))
            send("end", piece, piece, mx_send.at[k], mx_recv.at[k], x_peer)
            send("end", piece, piece, my_send.at[k], my_recv.at[k], y_peer)

    def sums_plane():
        for k in range(4):
            from_side, from_up = place(k, 0, 1), place(k, 1, 0)
            arrive(from_side, mx_recv.at[k], x_peer)
            arrive(from_up, my_recv.at[k], y_peer)
            if k % 2:
                send("end", from_side, from_side, md_send.at[k], md_recv.at[k], y_peer)
            else:
                send("end", from_up, from_up, md_send.at[k], md_recv.at[k], x_peer)

    def sums_cores():
        for k in range(4):
            arrive(place(k, 1, 1), md_recv.at[k], y_peer if k % 2 else x_peer)
        send("end", band.at[c], band.at[c], mc_send, mc_recv, c_peer)

    def condition(source):
        if source == 0:
            arrive(band.at[1 - c], mc_recv, c_peer)
            silu_side[...] = jnp.zeros_like(silu_side)
        acts = conds_ref[:, :8, :].astype(jnp.float32).reshape(CHIPS * 8, 128)
        row = lax.broadcasted_iota(jnp.int32, acts.shape, 0) % 8
        acts = jnp.where(row < CROPS, acts, 0.0)
        upper = acts.astype(jnp.bfloat16)
        lower = pltpu.roll(acts, CROPS, 0).astype(jnp.bfloat16)
        first, skip, size = ((0, 0, BAND), (BAND, 2 * BAND - side, side - BAND))[source]
        terms = split_low(band[source, :, skip : skip + size])
        for which, act in enumerate((upper, lower)):
            columns = slice(which * side + first, which * side + first + size)
            value = product_by_rows(act, terms[0]) + product_by_rows(act, terms[1])
            ada_grad_ref[:, columns] = value[: ada_grad_ref.shape[0]]
            value = product_by_columns(terms[0], ada_ref[:, columns])
            value = value + product_by_columns(terms[1], ada_ref[:, columns])
            silu_side[which, :, :PAD] = silu_side[which, :, :PAD] + value
        if source == 0:
            return
        silu_part[...] = silu_side[0] + pltpu.roll(silu_side[1], CHIPS * 8 - CROPS, 0)
        silu_ref[c, me] = silu_part[pl.ds(pl.multiple_of(me * 8, 8), 8), :]
        for k in range(1, CHIPS):
            to = (me + k) % CHIPS
            src = silu_part.at[pl.ds(pl.multiple_of(to * 8, 8), 8)]
            send("end", src, silu_ref.at[c, me], s_send.at[k - 1], s_recv.at[k - 1], (to, c))

    def condition_cores():
        for k in range(1, CHIPS):
            source = (me - k + CHIPS) % CHIPS
            arrive(silu_ref.at[c, source], s_recv.at[k - 1], (source, c))
        send("end", silu_ref.at[c], silu_ref.at[c], sc_send, sc_recv, c_peer)

    steps = []
    for i in range(len(order) + 5):
        if i + 1 < len(order):
            steps.append(partial(begin, i + 1))
        if i < len(order):
            steps += [partial(pair, i, pos) for pos in (3, 1, 2, 0)]
        if 1 <= i <= len(order):
            steps.append(partial(diag_along, i - 1))
        for step, lag in ((relay, 1), (plane, 2), (piece_along, 3)):
            for j in (i - lag - 1, i - lag):
                if 0 <= j < len(order) and j + lag + (order[j][1] == 0) == i:
                    steps.append(partial(step, j))
    layer = [partial(through_down, q) for q in range(4)] + [partial(up_grad, q) for q in range(4)]
    layer += [partial(through_up, q) for q in range(4)] + [partial(second_norm, h) for h in (0, 1)]
    layer += [context_grad, out_grad] + [partial(attend_back, h, h + 2) for h in range(0, HEADS, 2)]
    layer += [swap_sides, query_grad, partial(side_grad, 0), partial(side_grad, 1)]
    layer += [partial(through_qkv, q) for q in range(3)] + [partial(first_norm, h) for h in (0, 1)]
    layer += [sums_leave, sums_start, sums_line, sums_plane, sums_cores]
    layer += [partial(condition, 0), partial(condition, 1), condition_cores]
    begin(0)
    for q in range(4):
        slopes(q)
    fetch(0)
    fetch(1)
    interleave(steps, layer, BACKWARD_AFTER)
    for a in range(2):
        for j, (px, pc) in enumerate(partners):
            arrive(rows_ref.at[a, px * 2 + pc], group_recv.at[a, j], device(z, y, px, pc))
    arrive(silu_ref.at[1 - c], sc_recv, c_peer)
    for owner in list(sends):
        finish_sends(owner)


def run_backward(given, share):
    (weights, down_part, slope, middle, attended, active, hidden, query, sides, total, context, hidden_two,
     grad_mlp, table, conds, level, seg_all, seg_col, tokens, cot, ada) = given
    count, width = tokens.shape
    rows, side = 4 * share, ada.shape[1] // 2
    dma = pltpu.SemaphoreType.DMA
    low, wide = jnp.bfloat16, jnp.float32
    vmem, any_ = pl.BlockSpec(memory_space=pltpu.VMEM), pl.BlockSpec(memory_space=pl.ANY)
    out, buffer = jax.ShapeDtypeStruct, pltpu.VMEM
    slots = 12
    return pl.pallas_call(
        partial(backward_kernel, share),
        out_shape=(
            out((4, width, width), low),
            out((4, width, width), low),
            out((2, 4, PAD, width), low),
            out((rows, width), wide),
            out((count, width), wide),
            out((-(-share // 8) * 8, ada.shape[1]), wide),
            out((2, CHIPS, 8, 128), wide),
            out((count, width), low),
        ),
        in_specs=[any_] * 6 + [vmem] * 15,
        out_specs=[any_] * 2 + [vmem] * 5 + [any_],
        scratch_shapes=[
            buffer((HELD, 4, rows, width), low),
            buffer((4, 4, rows, width), low),
            buffer((5, rows, width), low),
            buffer((6, rows, width), low),
            buffer((6, rows, width), low),
            buffer((2, 5, rows, width), low),
            buffer((2, 5, rows - FAR[0] - FAR[1], width), low),
            buffer((2, 4 * PAD, width), low),
            buffer((2, width, width), low),
            buffer((2, width, width), low),
            buffer((4, count, width), wide),
            buffer((4, count, width), low),
            buffer((count, width), wide),
            buffer((count, width), wide),
            buffer((count, width), low),
            buffer((2, count, width), low),
            buffer((2, count, width), low),
            buffer((count, 2 * count), wide),
            buffer((6, CROPS, 8, width), wide),
            buffer((8, side), wide),
            buffer((8, side), wide),
            buffer((2, CHIPS * 8, BAND), wide),
            buffer((CHIPS * 8, 128), wide),
            buffer((2, CHIPS * 8, 128), wide),
            dma((slots, 4)), dma((slots, 4)), dma((slots, 4)),
            dma((slots,)), dma((slots,)), dma((slots,)), dma((slots,)),
            dma((slots, 2)), dma((slots, 2)), dma((slots, 2)), dma((slots, 2)),
            dma((3, 4)), dma((3, 5)), dma((3, 4)), dma((3, 5)),
            dma((2, 3)), dma((2, 3)), dma((2,)), dma((2,)), dma((4,)), dma((4,)), dma,
            dma((2,)), dma((2,)), dma, dma, dma((3,)), dma((3,)), dma((4,)), dma((4,)), dma((4,)), dma((4,)),
            dma((4,)), dma((4,)), dma, dma, dma((CHIPS - 1,)), dma((CHIPS - 1,)), dma, dma,
        ],
        compiler_params=pltpu.CompilerParams(
            collective_id=1, has_side_effects=True, vmem_limit_bytes=63 * 2**20 + 2**19
        ),
        name="backward",
    )(*given)


def finish_kernel(share, rows_ref, ada_given_ref, silu_ref, cond_ref, down_given, tokens_grad_given, out_given,
                  qkv_ref, out_grad_ref, up_ref, ada_ref, cond_grad_ref, down_ref, tokens_grad_ref, out_ref):
    for given, ref in ((down_given, down_ref), (tokens_grad_given, tokens_grad_ref), (out_given, out_ref)):

        def body(at):
            ref[at, :] = given[at, :]

        chunks(ref.shape[0], body)
    width = rows_ref.shape[-1]
    for q in range(4):
        value = rows_ref[0, q].astype(jnp.float32)[:share]
        if q == 3:
            out_grad_ref[...] = value
        else:
            qkv_ref[:, q * width : (q + 1) * width] = value
        up_ref[:, q * width : (q + 1) * width] = rows_ref[1, q].astype(jnp.float32)[:share]
    ada_ref[...] = ada_given_ref[...][:share]
    lane = lax.broadcasted_iota(jnp.int32, (8, 128), 1)
    tiles = [jnp.zeros((8, 128), jnp.float32)] * (width // 128)
    for number in range(2 * CHIPS):
        tile, offset = divmod(number * share, 128)
        value = jnp.where(lane < share, silu_ref[number % 2, number // 2], 0.0)
        if offset:
            value = pltpu.roll(value, offset, 1)
        tiles[tile] = tiles[tile] + jnp.where(lane >= offset, value, 0.0)
        if offset + share > 128:
            tiles[tile + 1] = tiles[tile + 1] + jnp.where(lane < offset, value, 0.0)
    grad = jnp.concatenate(tiles, axis=1)[:CROPS]
    cond = cond_ref[...].astype(jnp.float32)
    chance = 1.0 / (1.0 + jnp.exp(-cond))
    cond_grad_ref[...] = grad * (chance * (1.0 + cond * (1.0 - chance)))


def run_finish(rows, ada_grad, silu_part, cond, down_grad, tokens_grad, tokens_out, share):
    width = rows.shape[-1]
    wide = jnp.float32
    vmem, out = pl.BlockSpec(memory_space=pltpu.VMEM), jax.ShapeDtypeStruct
    return pl.pallas_call(
        partial(finish_kernel, share),
        out_shape=(
            out((share, 3 * width), wide),
            out((share, width), wide),
            out((share, 4 * width), wide),
            out((share, ada_grad.shape[1]), wide),
            out(cond.shape, wide),
            out(down_grad.shape, wide),
            out(tokens_grad.shape, wide),
            out(tokens_out.shape, tokens_out.dtype),
        ),
        in_specs=[vmem] * 7,
        out_specs=[vmem] * 8,
        compiler_params=pltpu.CompilerParams(vmem_limit_bytes=32 * 2**20),
        name="finish",
    )(rows, ada_grad, silu_part, cond, down_grad, tokens_grad, tokens_out)


def layer_norm(values):
    center = values - jnp.mean(values, axis=-1, keepdims=True)
    inverse = lax.rsqrt(jnp.mean(center * center, axis=-1, keepdims=True) + EPSILON)
    return (center * inverse, inverse)


def norm_back(grad_normed, normed, inverse):
    return inverse * (
        grad_normed
        - jnp.mean(grad_normed, axis=-1, keepdims=True)
        - normed * jnp.mean(grad_normed * normed, axis=-1, keepdims=True)
    )


def to_heads(array):
    return array.reshape(array.shape[0], HEADS, array.shape[1] // HEADS)


def dots(spec, left, right):
    return jnp.einsum(spec, left, right, preferred_element_type=jnp.float32)


def masked_scores(query_heads, key_heads, same_crop):
    scale_factor = 1.0 / math.sqrt(query_heads.shape[-1])
    scores = dots("qhd,khd->hqk", query_heads, key_heads) * scale_factor
    return jnp.where(same_crop[None], scores, LARGE_NEGATIVE)


def attend(query_seq, key_seq, value_seq, same_crop):
    scores = masked_scores(to_heads(query_seq), to_heads(key_seq), same_crop)
    row_max = jnp.max(scores, axis=-1, keepdims=True)
    raised = jnp.exp(scores - row_max)
    row_total = jnp.sum(raised, axis=-1, keepdims=True)
    probability = (raised / row_total).astype(jnp.bfloat16)
    context = dots("hqk,khd->qhd", probability, to_heads(value_seq))
    return (context.reshape(query_seq.shape[0], -1), (row_max + jnp.log(row_total))[..., 0])


def attend_back(query_seq, key_seq, value_seq, same_crop, log_total, grad_seq):
    query_heads = to_heads(query_seq)
    key_heads = to_heads(key_seq)
    value_heads = to_heads(value_seq)
    grad_heads = to_heads(grad_seq)
    scale_factor = 1.0 / math.sqrt(query_heads.shape[-1])
    scores = masked_scores(query_heads, key_heads, same_crop)
    probability = jnp.exp(scores - log_total[..., None])
    grad_prob = dots("qhd,khd->hqk", grad_heads, value_heads)
    inner = jnp.sum(probability * grad_prob, axis=-1, keepdims=True)
    grad_scores = (probability * (grad_prob - inner)).astype(jnp.bfloat16)
    grad_query = dots("hqk,khd->qhd", grad_scores, key_heads) * scale_factor
    grad_key = dots("hqk,qhd->khd", grad_scores, query_heads) * scale_factor
    grad_value = dots("hqk,qhd->khd", probability.astype(jnp.bfloat16), grad_heads)
    rows_here = query_seq.shape[0]
    rows_whole = key_seq.shape[0]
    return (
        grad_query.reshape(rows_here, -1),
        grad_key.reshape(rows_whole, -1),
        grad_value.reshape(rows_whole, -1),
    )


def forward_plain(tokens_float, segments, conditions, noise_bins, bin_counts, ada_weight, first, up_weight,
                  down_weight):
    groups, cores = lax.axis_size("dp"), lax.axis_size("sp")
    share, width = first.shape[0], tokens_float.shape[1]
    index = lax.axis_index("dp") * cores + lax.axis_index("sp")
    mixers = lax.all_gather(first, ("dp", "sp"), axis=0, tiled=True)
    uppers = lax.all_gather(up_weight, ("dp", "sp"), axis=0, tiled=True)
    downers = lax.all_gather(down_weight, ("dp", "sp"), axis=0, tiled=True)
    mixers = mixers.reshape(width, 4, width).transpose(1, 0, 2)
    uppers = uppers.reshape(width, 4, width).transpose(1, 0, 2)
    downers = downers.reshape(4, width, width)
    bin_total = lax.psum(bin_counts, "dp")
    bin_weight = 40.0 * groups / bin_total.astype(jnp.float32)
    crop_weight = jnp.sum(
        jnp.where(noise_bins[:, None] == jnp.arange(NBINS, dtype=jnp.int32), bin_weight, 0.0),
        axis=-1,
    )
    cond_all = lax.all_gather(conditions, "dp", axis=0, tiled=True)
    cond_here = lax.dynamic_slice_in_dim(cond_all, index * share, share, axis=1)
    cond_act = jax.nn.silu(cond_here.astype(jnp.float32)).astype(jnp.bfloat16)
    modulation_part = dots("sd,df->sf", cond_act, ada_weight).reshape(groups, CROPS, -1)
    modulation = lax.psum(lax.psum_scatter(modulation_part, "dp", scatter_dimension=0), "sp")
    selector = (segments[:, None] == jnp.arange(CROPS, dtype=jnp.int32)).astype(jnp.float32)
    per_token = jnp.einsum("tc,cf->tf", selector, modulation, precision=lax.Precision.HIGHEST)
    shift_one, scale_one, gate_one, shift_two, scale_two, _ = jnp.split(per_token, 6, axis=-1)
    normed_one, _ = layer_norm(tokens_float)
    hidden_one = (normed_one * (1.0 + scale_one) + shift_one).astype(jnp.bfloat16)
    projected = dots("td,qdf->qtf", hidden_one, mixers[:3]).astype(jnp.bfloat16)
    sides = lax.all_gather(projected[1:], "sp", axis=1, tiled=True)
    all_segments = lax.all_gather(segments, "sp", axis=0, tiled=True)
    same_crop = segments[:, None] == all_segments[None, :]
    context, log_total = attend(projected[0], sides[0], sides[1], same_crop)
    context_low = context.astype(jnp.bfloat16)
    attended = dots("td,df->tf", context_low, mixers[3])
    middle = tokens_float + gate_one * attended
    normed_two, _ = layer_norm(middle)
    hidden_two = (normed_two * (1.0 + scale_two) + shift_two).astype(jnp.bfloat16)
    upper_in = dots("td,qdf->qtf", hidden_two, uppers)
    activated = jax.nn.gelu(upper_in, approximate=True).astype(jnp.bfloat16)
    slope = jax.vjp(partial(jax.nn.gelu, approximate=True), upper_in)[1](jnp.ones_like(upper_in))[0]
    mlp_out = dots("qtf,qfd->td", activated, downers)
    return (
        (mixers, uppers, downers), activated, slope, hidden_one, projected[0], sides, log_total,
        context_low, attended, middle, hidden_two, mlp_out, modulation, cond_act, crop_weight, same_crop,
    )


def layer_plain(tokens_float, segments, conditions, noise_bins, bin_counts, cotangent, ada_weight, first,
                up_weight, down_weight):
    width = tokens_float.shape[1]
    (
        (mixers, uppers, downers), activated, slope, hidden_one, queries, sides, log_total,
        context_low, attended, middle, hidden_two, mlp_out, modulation, cond_act, crop_weight, same_crop,
    ) = forward_plain(
        tokens_float, segments, conditions, noise_bins, bin_counts, ada_weight, first, up_weight,
        down_weight,
    )
    selector = (segments[:, None] == jnp.arange(CROPS, dtype=jnp.int32)).astype(jnp.float32)
    per_token = jnp.einsum("tc,cf->tf", selector, modulation, precision=lax.Precision.HIGHEST)
    _, scale_one, gate_one, _, scale_two, gate_two = jnp.split(per_token, 6, axis=-1)
    normed_one, inverse_one = layer_norm(tokens_float)
    normed_two, inverse_two = layer_norm(middle)

    token_weight = jnp.sum(selector * crop_weight[None, :], axis=-1)
    grad_out = cotangent.astype(jnp.float32) * token_weight[:, None]
    grad_mlp = (grad_out * gate_two).astype(jnp.bfloat16)
    tokens_out = (middle + gate_two * mlp_out).astype(jnp.bfloat16)
    down_part = dots("qtf,td->qfd", activated, grad_mlp).astype(jnp.bfloat16)
    grad_act = dots("td,qfd->qtf", grad_mlp, downers)
    grad_upper = (grad_act * slope).astype(jnp.bfloat16)
    up_part = dots("td,qtf->qdf", hidden_two, grad_upper).astype(jnp.bfloat16)
    grad_hidden_two = dots("qtf,qdf->td", grad_upper, uppers)
    grad_middle = grad_out + norm_back(grad_hidden_two * (1.0 + scale_two), normed_two, inverse_two)
    grad_attended = (grad_middle * gate_one).astype(jnp.bfloat16)
    grad_context = dots("tf,df->td", grad_attended, mixers[3]).astype(jnp.bfloat16)
    grad_query, grad_key, grad_value = attend_back(
        queries, sides[0], sides[1], same_crop, log_total, grad_context
    )
    grad_sides = lax.psum_scatter(
        jnp.stack([grad_key, grad_value]).astype(jnp.bfloat16),
        "sp",
        scatter_dimension=1,
        tiled=True,
    )
    grad_projected = jnp.concatenate([grad_query.astype(jnp.bfloat16)[None], grad_sides])
    out_part = dots("td,tf->df", context_low, grad_attended).astype(jnp.bfloat16)
    qkv_part = dots("td,qtf->qdf", hidden_one, grad_projected).astype(jnp.bfloat16)
    first_part = jnp.concatenate([qkv_part, out_part[None]])
    grad_hidden_one = dots("qtf,qdf->td", grad_projected, mixers[:3])
    tokens_grad = grad_middle + norm_back(
        grad_hidden_one * (1.0 + scale_one), normed_one, inverse_one
    )

    joined = jnp.stack([first_part, up_part]).transpose(2, 0, 1, 3).reshape(width, 8 * width)
    rows = lax.psum_scatter(joined, ("dp", "sp"), scatter_dimension=0, tiled=True)
    rows = rows.astype(jnp.float32)
    first_grad, up_grad = rows[:, : 4 * width], rows[:, 4 * width :]
    down_grad = lax.psum_scatter(
        down_part.reshape(4 * width, width), ("dp", "sp"), scatter_dimension=0, tiled=True
    ).astype(jnp.float32)

    grad_per_token = jnp.concatenate(
        [
            grad_hidden_one,
            grad_hidden_one * normed_one,
            grad_middle * attended,
            grad_hidden_two,
            grad_hidden_two * normed_two,
            grad_out * mlp_out,
        ],
        axis=-1,
    )
    grad_modulation = lax.psum(
        jnp.einsum("tc,tf->cf", selector, grad_per_token, precision=lax.Precision.HIGHEST), "sp"
    )
    grad_rows = lax.all_gather(grad_modulation, "dp", axis=0, tiled=True)
    ada_grad = jnp.einsum(
        "sd,sf->df", cond_act.astype(jnp.float32), grad_rows, precision=lax.Precision.HIGHEST
    )
    silu_part = jnp.einsum(
        "sf,df->sd", grad_rows, ada_weight.astype(jnp.float32), precision=lax.Precision.HIGHEST
    )
    silu_all = lax.all_gather(silu_part, ("dp", "sp"), axis=0)
    silu_here = lax.dynamic_slice_in_dim(silu_all, lax.axis_index("dp") * CROPS, CROPS, axis=1)
    grad_silu = silu_here.transpose(1, 0, 2).reshape(CROPS, width)
    return tokens_out, tokens_grad, grad_silu, ada_grad, first_grad, up_grad, down_grad


def on_device(
    chips,
    tokens_in,
    segment_ids,
    conditions,
    noise_bins,
    bin_counts,
    cotangent,
    ada_weight,
    qkv_weight,
    out_weight,
    up_weight,
    down_weight,
):
    share = qkv_weight.shape[0]
    if chips and 4 * share == down_weight.shape[0]:
        (
            weights, down_part, slope, active, sides, attended, middle, hidden_one, queries, log_total,
            context_low, hidden_two, table, conds, level, grad_mlp, seg_all, seg_col, ada,
        ) = run_forward(
            qkv_weight, out_weight, up_weight, down_weight, conditions[0], noise_bins, bin_counts,
            ada_weight, tokens_in[0], cotangent[0], segment_ids,
        )
        given = (
            weights, down_part, slope, middle, attended, active, hidden_one, queries, sides, log_total,
            context_low, hidden_two, grad_mlp, table, conds, level, seg_all, seg_col, tokens_in[0],
            cotangent[0], ada,
        )
        _, _, rows, down_grad, tokens_grad, ada_grad, silu_part, tokens_out = run_backward(given, share)
        qkv_grad, out_grad, up_grad, ada_grad, cond_grad, down_grad, tokens_grad, tokens_out = run_finish(
            rows, ada_grad, silu_part, conditions[0], down_grad, tokens_grad, tokens_out, share
        )
    else:
        first = jnp.concatenate([qkv_weight, out_weight], axis=1)
        width = out_weight.shape[1]
        tokens_out, tokens_grad, grad_silu, ada_grad, first_grad, up_grad, down_grad = layer_plain(
            tokens_in[0].astype(jnp.float32), segment_ids[0], conditions[0], noise_bins[0], bin_counts[0],
            cotangent[0], ada_weight, first, up_weight, down_weight,
        )
        qkv_grad, out_grad = first_grad[:, : 3 * width], first_grad[:, 3 * width :]
        cond_grad = jax.vjp(jax.nn.silu, conditions[0].astype(jnp.float32))[1](grad_silu)[0]
    return (
        tokens_out[None],
        tokens_grad[None],
        cond_grad[None],
        ada_grad,
        qkv_grad,
        out_grad,
        up_grad,
        down_grad,
    )


def solution(mesh):
    placed = (
        P("dp", "sp", None),
        P("dp", "sp"),
        P("dp", None, None),
        P("dp", None),
        P("dp", None),
        P("dp", "sp", None),
        P(("dp", "sp"), None),
        P(("dp", "sp"), None),
        P(("dp", "sp"), None),
        P(("dp", "sp"), None),
        P(("dp", "sp"), None),
    )
    return jax.shard_map(
        partial(on_device, mesh.shape["dp"] == 16 and mesh.shape["sp"] == 2),
        mesh=mesh,
        in_specs=placed,
        out_specs=(
            P("dp", "sp", None),
            P("dp", "sp", None),
            P("dp", None, None),
            P(("dp", "sp"), None),
            P(("dp", "sp"), None),
            P(("dp", "sp"), None),
            P(("dp", "sp"), None),
            P(("dp", "sp"), None),
        ),
        check_vma=False,
    )
```

```python
from functools import partial
import math

import jax
import jax.numpy as jnp
from jax import lax
from jax.experimental import pallas as pl
from jax.experimental.pallas import tpu as pltpu
from jax.sharding import PartitionSpec as P

HEADS = 16
CROPS = 4
NBINS = 8
EPSILON = 1e-06
LARGE_NEGATIVE = -1e30
GELU_SCALE = math.sqrt(2.0 / math.pi)
GELU_CUBE = 0.044715

MESH = pl.DeviceIdType.MESH
PAD = 48
NEAR = (80, 64)
FAR = (32, 32)
HELD = 6
FORWARD_STEPS = (
    0, 2, 11, 12, 21, 3, 4, 22, 13, 5, 14, 31, 32, 7, 23, 24, 100, 15, 102, 33,
    16, 34, 26, 25, 111, 27, 121, 17, 103, 104, 35, 36, 112, 122, 37, 113, 114, 105, 107, 131,
    115, 132, 200, 123, 124, 116, 202, 133, 134, 126, 125, 211, 135, 212, 203, 117, 204, 221, 127, 136,
    137, 205, 222, 213, 214, 215, 207, 231, 232, 223, 224, 225, 216, 217, 233, 234, 226, 235, 236, 227,
    237,
)
BACKWARD_STEPS = (
    10, 4, 1, 3, 20, 12, 2, 30, 14, 6, 13, 22, 7, 5, 16, 11, 23, 34, 17, 32,
    8, 24, 40, 21, 33, 15, 18, 25, 44, 42, 26, 43, 27, 35, 9, 50, 47, 31, 46, 41,
    54, 60, 53, 52, 19, 28, 45, 36, 51, 62, 37, 64, 55, 61, 57, 70, 29, 63, 38, 56,
    48, 72, 65, 73, 66, 80, 67, 58, 39, 49, 74, 71, 90, 82, 100, 75, 84, 92, 81, 94,
    83, 59, 110, 91, 68, 76, 69, 86, 77, 85, 111, 87, 104, 102, 95, 96, 93, 101, 97, 103,
    78, 79, 105, 88, 114, 89, 107, 106, 115, 113, 112, 98, 116, 99, 108, 109, 117, 118, 119,
)
FORWARD_AFTER = (
    0, 2, 8, 20, 24, 26, 34, 35, 37, 39, 43, 47, 47, 47, 47, 49, 49, 51, 51, 54,
    59, 59, 62, 63, 64, 64, 65, 65, 67, 67, 70, 71, 77, 77, 78, 81,
)
BACKWARD_AFTER = (
    1, 9, 13, 14, 16, 18, 22, 22, 23, 24, 30, 31, 32, 40, 44, 45, 45, 46, 52, 54,
    54, 56, 57, 57, 57, 63, 65, 65, 81, 81, 85, 86, 88, 90, 98, 109, 116, 119, 119, 119,
    119,
)
CHIPS = 16
BAND = 1792
PLACES = ((0, 0), (0, 1), (1, 0), (1, 1))


def position():
    d = lax.axis_index("dp")
    c = lax.axis_index("sp")
    return d // 4, (d // 2) % 2, d % 2, c


def device(z, y, x, c):
    return (z * 4 + y * 2 + x, c)


def block_of(kind, zy, group):
    if kind == 2:
        return zy // 2, (zy % 2) * 4 + group
    return group, zy


def level_of(z, k):
    if k == 0:
        return z
    upper = z // 2
    inner = z * (1 - upper) + (3 - z) * upper
    step = k - inner if k == 1 else k
    return step * (1 - upper) + (3 - step) * upper


def greet(peers, meanwhile=None):
    barrier = pltpu.get_barrier_semaphore()
    for peer in peers:
        pl.semaphore_signal(barrier, inc=1, device_id=peer, device_id_type=MESH)
    if meanwhile is not None:
        meanwhile()
    pl.semaphore_wait(barrier, len(peers))


def remote(src, dst, send, recv, target):
    return pltpu.make_async_remote_copy(
        src_ref=src,
        dst_ref=dst,
        send_sem=send,
        recv_sem=recv,
        device_id=target,
        device_id_type=MESH,
    )


def arrive(ref, sem, target):
    remote(ref, ref, sem, sem, target).wait_recv()


def row_selector(rows, share):
    shape = (rows, 4 * PAD)
    row = lax.broadcasted_iota(jnp.int32, shape, 0)
    column = lax.broadcasted_iota(jnp.int32, shape, 1)
    picked = jnp.zeros(shape, jnp.bool_)
    for k in range(4):
        inside = (row >= k * share) & (row < (k + 1) * share)
        picked = picked | (inside & (column == row - k * share + k * PAD))
    return picked.astype(jnp.float32).astype(jnp.bfloat16)


def product(left, right):
    return jnp.dot(left, right, preferred_element_type=jnp.float32)


def product_by_rows(left, right):
    return lax.dot_general(left, right, (((0,), (0,)), ((), ())), preferred_element_type=jnp.float32)


def product_by_columns(left, right):
    return lax.dot_general(left, right, (((1,), (1,)), ((), ())), preferred_element_type=jnp.float32)


def chunks(rows, body, first=0, step=16):
    def run(i, carry):
        body(pl.ds(pl.multiple_of(first + i * step, step), step))
        return carry

    lax.fori_loop(0, rows // step, run, 0)


def normed(values):
    center = values - jnp.mean(values, axis=-1, keepdims=True)
    inverse = lax.rsqrt(jnp.mean(center * center, axis=-1, keepdims=True) + EPSILON)
    return center * inverse, inverse


def pick(segments, table, first, column, width):
    columns = slice(column * width, (column + 1) * width)
    value = table[first + 3 : first + 4, columns]
    for crop in (2, 1, 0):
        value = jnp.where(segments == crop, table[first + crop : first + crop + 1, columns], value)
    return value


def window_of(head, size, width):
    start = jnp.minimum((head * size) // 128, width // 128 - 2) * 128
    start = pl.multiple_of(start, 128)
    lane = lax.broadcasted_iota(jnp.int32, (1, 256), 1) + start
    return pl.ds(start, 256), (lane >= head * size) & (lane < (head + 1) * size)


def share_window(device_number, share, width):
    column = device_number * share
    start = jnp.minimum(column // 128, width // 128 - 2) * 128
    return pl.multiple_of(start, 128), column - start


def forward_kernel(share, qkv_ref, out_weight_ref, up_ref, down_ref, cond_ref, noise_ref, counts_ref, given_ada_ref,
                   tokens_ref, cot_ref, seg_ref,
                   weights_ref, down_part_ref, slope_ref, active_ref, sides_out_ref, attended_out_ref, middle_out_ref,
                   hidden_ref, query_ref, total_ref, context_ref, hidden_two_ref, table_ref,
                   conds_ref, level_ref, grad_mlp, seg_all, seg_col_ref, ada_ref,
                   full, shards_ref, stage, acts, acts_low, windows, part, part_recv, band, band_diag, band_x, band_y,
                   band_z, halves_of, sides_ref, attended_ref, middle_ref, bias, work, active, slope, *sems):
    (
        group_send, group_recv, z_send, z_recv, zd_send, zd_recv, x_send, x_recv, y_send, y_recv,
        dx_send, dx_recv, dy_send, dy_recv, c_send, c_recv,
        cond_send, cond_recv, pc_send, pc_recv, pd_send, pd_recv, px_send, px_recv, py_send, py_recv,
        pz_send, pz_recv, pm_send, pm_recv, seg_send, seg_recv, kv_send, kv_recv,
        save_sem, grad_sem, slope_sem, block_sem, store_sem,
    ) = sems
    z, y, x, c = position()
    me = z * 4 + y * 2 + x
    group = x * 2 + c
    zy = z * 2 + y
    rows = 4 * share
    count, width = tokens_ref.shape
    x_peer, y_peer, c_peer = device(z, y, 1 - x, c), device(z, 1 - y, x, c), device(z, y, x, 1 - c)
    partners = [(x, 1 - c), (1 - x, c), (1 - x, 1 - c)]

    def prepare():
        tail = share // 16 * 16
        for a in range(2):
            for q in range(4):
                source, at = (up_ref, q) if a else ((out_weight_ref, 0) if q == 3 else (qkv_ref, q))
                shards_ref[a, q, tail:, :] = jnp.zeros((PAD - tail, width), jnp.bfloat16)
                shards_ref[a, q, :share, :] = source[:, at * width : (at + 1) * width]
        ada_ref[tail:, :] = jnp.zeros((PAD - tail, ada_ref.shape[1]), jnp.bfloat16)
        ada_ref[:share, :] = given_ada_ref[...]
        cond = cond_ref[...].astype(jnp.float32)
        acts[...] = jnp.zeros_like(acts)
        acts[:CROPS, :] = cond * (1.0 / (1.0 + jnp.exp(-cond)))
        counts = counts_ref[...].astype(jnp.float32)
        for tile in range(width // 128):
            acts[CROPS : CROPS + 1, tile * 128 : tile * 128 + NBINS] = counts
        acts_low[...] = acts[...].astype(jnp.bfloat16)
        seg_all[c] = jnp.broadcast_to(seg_ref[...], (8, count))
        seg_col_ref[...] = jnp.transpose(jnp.broadcast_to(seg_ref[...], (128, count)))
        for a in range(2):
            stage[a, pl.ds(pl.multiple_of(group * PAD, 16), PAD), :] = shards_ref[a, group]
        start, _ = share_window(2 * me + c, share, width)
        windows[me] = acts_low[:, pl.ds(start, 256)]

    greet(
        [((me + k) % CHIPS, c) for k in range(1, CHIPS)] + [c_peer, device(z, y, 1 - x, 1 - c)], prepare
    )
    sends = {a: [] for a in (0, 1, 2, "other")}

    def send(a, *args):
        copy = remote(*args)
        copy.start()
        sends[a].append((None, copy))

    def finish_sends(a):
        for go, copy in sends[a]:
            if go is None:
                copy.wait_send()
            else:
                pl.when(go)(copy.wait_send)
        sends[a] = []

    level = partial(level_of, z)

    def place(a, k, other_y, other_x, core=None, first=0, last=None):
        yy = 1 - y if other_y else y
        xx = 1 - x if other_x else x
        cc = c if core is None else core
        block, row = block_of(a, level(k) * 2 + yy, xx * 2 + cc)
        count = (rows if last is None else last) - first
        return full.at[a, block, pl.ds(pl.multiple_of(row * rows + first, 16), count)]

    def cuts(k):
        top, low = FAR if k else NEAR
        return top, rows - low

    def along(a, k, ref, send_sem, recv_sem):
        source = level(k)
        for way, step in ((0, 1), (1, -1)):
            to = z + step
            go = (to >= 0) & (to < 4)
            if k:
                go = go & ((source < z) if step == 1 else (source > z))
            copy = remote(ref, ref, send_sem.at[a, k, way], recv_sem.at[a, source], device(jnp.clip(to, 0, 3), y, x, c))
            pl.when(go)(copy.start)
            sends[a].append((go, copy))

    def from_line(a, k, ref, recv_sem):
        source = level(k)
        arrive(ref, recv_sem.at[a, source], device((z + 1) % 4, y, x, c))

    for a in range(2):
        for j, (px, pc) in enumerate(partners):
            send(
                "other",
                shards_ref.at[a, px * 2 + pc],
                stage.at[a, pl.ds(pl.multiple_of(group * PAD, 16), PAD)],
                group_send.at[a, j],
                group_recv.at[a, j],
                device(z, y, px, pc),
            )
    for k in range(1, CHIPS):
        to = (me + k) % CHIPS
        start, _ = share_window(2 * to + c, share, width)
        send("other", acts_low.at[:, pl.ds(start, 256)], windows.at[me], cond_send.at[k - 1], cond_recv.at[k - 1], (to, c))
    send("other", seg_all.at[c], seg_all.at[c], seg_send, seg_recv, c_peer)

    def own(a):
        block, row = block_of(a, zy, group)
        here = pl.ds(pl.multiple_of(row * rows, 16), rows)
        if a < 2:
            for j, (px, pc) in enumerate(partners):
                arrive(
                    stage.at[a, pl.ds(pl.multiple_of((px * 2 + pc) * PAD, 16), PAD)],
                    group_recv.at[a, j],
                    device(z, y, px, pc),
                )
            full[a, block, here, :] = product(row_selector(rows, share), stage[a]).astype(jnp.bfloat16)
        else:
            full[a, block, here, :] = down_ref[...]
        along(a, 0, place(a, 0, 0, 0), z_send, z_recv)

    def to_core(a, k, pos):
        piece = place(a, k, *PLACES[pos])
        send(a, piece, piece, c_send.at[a, k, pos], c_recv.at[a, k, pos], c_peer)

    def pass_piece(a, k):
        from_line(a, k, place(a, k, 0, 0), z_recv)
        along(a, k, place(a, k, 0, 0), z_send, z_recv)

    def spread(a, k):
        top, low = cuts(k)
        for x_half, x_rows, y_half, y_rows in ((0, (0, top), 1, (low, rows)), (1, (top, rows), 0, (0, low))):
            part = place(a, k, 0, 0, None, *x_rows)
            send(a, part, part, x_send.at[a, k, x_half], x_recv.at[a, k, x_half], x_peer)
            part = place(a, k, 0, 0, None, *y_rows)
            send(a, part, part, y_send.at[a, k, y_half], y_recv.at[a, k, y_half], y_peer)
        to_core(a, k, 0)

    def turn_y(a, k):
        part = place(a, k, 0, 1, None, 0, cuts(k)[0])
        arrive(part, x_recv.at[a, k, 0], x_peer)
        send(a, part, part, dy_send.at[a, k], dy_recv.at[a, k], y_peer)

    def turn_x(a, k):
        part = place(a, k, 1, 0, None, cuts(k)[1], rows)
        arrive(part, y_recv.at[a, k, 1], y_peer)
        send(a, part, part, dx_send.at[a, k], dx_recv.at[a, k], x_peer)

    def share_sides(a, k):
        top, low = cuts(k)
        arrive(place(a, k, 0, 1, None, top, rows), x_recv.at[a, k, 1], x_peer)
        to_core(a, k, 1)
        arrive(place(a, k, 1, 0, None, 0, low), y_recv.at[a, k, 0], y_peer)
        to_core(a, k, 2)

    def middle(a, k):
        return place(a, k, 1, 1, None, FAR[0], rows - FAR[1])

    def pass_diagonal(a, k):
        from_line(a, k, middle(a, k), zd_recv)
        along(a, k, middle(a, k), zd_send, zd_recv)

    pending = []

    def finish(a, k):
        top, low = cuts(k)
        arrive(place(a, k, 1, 1, None, 0, top), dy_recv.at[a, k], y_peer)
        arrive(place(a, k, 1, 1, None, low, rows), dx_recv.at[a, k], x_peer)
        if k == 0:
            along(a, k, middle(a, k), zd_send, zd_recv)
        to_core(a, k, 3)
        if a == 2:
            while pending:
                complete_level(pending.pop())
            pending.append(k)

    saves = []

    def keep(src, dst, sem):
        copy = pltpu.make_async_copy(src, dst, sem)
        copy.start()
        saves.append(copy)

    def arrive_cores(a, k):
        for pos, (oy, ox) in enumerate(PLACES):
            arrive(place(a, k, oy, ox, 1 - c), c_recv.at[a, k, pos], c_peer)

    def complete(a):
        for k in range(4):
            arrive_cores(a, k)
        keep(full.at[a], weights_ref.at[a], save_sem.at[a])

    def complete_level(k):
        arrive_cores(2, k)
        keep(full.at[2, level(k)], weights_ref.at[2, level(k)], block_sem.at[k])

    def mod_start():
        for k in range(1, CHIPS):
            source = (me - k + CHIPS) % CHIPS
            arrive(windows.at[source], cond_recv.at[k - 1], (source, c))
        _, offset = share_window(2 * me + c, share, width)
        lane = lax.broadcasted_iota(jnp.int32, (256, 128), 1)
        picked = (lax.broadcasted_iota(jnp.int32, (256, 128), 0) == lane + offset) & (lane < share)
        picked = picked.astype(jnp.float32).astype(jnp.bfloat16)
        mine = product(windows[...].reshape(CHIPS * 16, 256), picked)
        conds_ref[...] = mine.reshape(CHIPS, 16, 128).astype(jnp.bfloat16)
        here = mine.reshape(CHIPS, 16, 128)[:, :8, :].reshape(CHIPS * 8, 128)
        row = lax.broadcasted_iota(jnp.int32, here.shape, 0) % 8
        here = jnp.where(row < CROPS, here, 0.0)
        upper = here.astype(jnp.bfloat16)
        lower = pltpu.roll(here, CROPS, 0).astype(jnp.bfloat16)
        side = ada_ref.shape[1] // 2
        part[...] = product(upper[:, :PAD], ada_ref[:, :side]) + product(lower[:, :PAD], ada_ref[:, side:])
        far = pl.ds(pl.multiple_of((1 - c) * (side - BAND), 128), BAND)
        send("other", part.at[:, far], part_recv, pc_send, pc_recv, c_peer)

    def block8(zz, yy, xx):
        return pl.ds(pl.multiple_of((zz * 4 + yy * 2 + xx) * 8, 8), 8)

    def mod_cores():
        arrive(part_recv, pc_recv, c_peer)
        side = ada_ref.shape[1] // 2
        near = pl.ds(pl.multiple_of(c * (side - BAND), 128), BAND)
        band[...] = part[:, near] + part_recv[...]
        for k in range(4):
            zz = (z + k) % 4
            src = band.at[block8(zz, 1 - y, 1 - x)]
            send("other", src, band_diag.at[k], pd_send.at[k], pd_recv.at[k], x_peer if k % 2 else y_peer)

    def mod_plane():
        for k in range(4):
            zz = (z + k) % 4
            to_x, to_y = block8(zz, y, 1 - x), block8(zz, 1 - y, x)
            arrive(band_diag.at[k], pd_recv.at[k], x_peer if k % 2 else y_peer)
            fold = to_y if k % 2 else to_x
            band[fold, :] = band[fold, :] + band_diag[k]
            send("other", band.at[to_x], band_x.at[k], px_send.at[k], px_recv.at[k], x_peer)
            send("other", band.at[to_y], band_y.at[k], py_send.at[k], py_recv.at[k], y_peer)

    def mod_line():
        for k in (1, 2, 3, 0):
            zz = (z + k) % 4
            mine = block8(zz, y, x)
            arrive(band_x.at[k], px_recv.at[k], x_peer)
            arrive(band_y.at[k], py_recv.at[k], y_peer)
            band[mine, :] = band[mine, :] + band_x[k] + band_y[k]
            if k:
                send("other", band.at[mine], band_z.at[k - 1], pz_send.at[k - 1], pz_recv.at[k - 1], device(zz, y, x, c))

    def mod_last():
        for k in (1, 2, 3):
            arrive(band_z.at[k - 1], pz_recv.at[k - 1], device((z - k + 4) % 4, y, x, c))
        halves_of[c] = band[block8(z, y, x), :] + band_z[0] + band_z[1] + band_z[2]
        send("other", halves_of.at[c], halves_of.at[c], pm_send, pm_recv, c_peer)

    def mod_end():
        arrive(halves_of.at[1 - c], pm_recv, c_peer)
        side = ada_ref.shape[1] // 2
        table_ref[:, :BAND] = halves_of[0]
        table_ref[:, BAND:] = halves_of[1][:, 2 * BAND - side :]
        counts = jnp.sum(windows[:, :, :128].astype(jnp.float32)[:, CROPS : CROPS + 1, :], axis=0)
        lane = lax.broadcasted_iota(jnp.int32, counts.shape, 1)
        weight = jnp.where(lane < NBINS, 40.0 * CHIPS / jnp.where(lane < NBINS, counts, 1.0), 0.0)
        level_ref[...] = jnp.zeros_like(level_ref)
        for crop in range(CROPS):
            mine = jnp.where(lane == noise_ref[:, crop : crop + 1], weight, 0.0)
            level_ref[crop : crop + 1, :] = jnp.broadcast_to(jnp.sum(mine, axis=-1, keepdims=True), (1, 128))

    def first_norm(part_of):
        def body(at):
            segments = seg_col_ref[at, :1]
            value, _ = normed(tokens_ref[at, :].astype(jnp.float32))
            value = value * (1.0 + pick(segments, table_ref, 0, 1, width))
            hidden_ref[at, :] = (value + pick(segments, table_ref, 0, 0, width)).astype(jnp.bfloat16)

        chunks(count // 2, body, part_of * (count // 2))
        if part_of == 0:
            arrive(seg_all.at[1 - c], seg_recv, c_peer)
            return
        for h in (0, 1):
            same = seg_col_ref[:, :1] == seg_all[h][:1, :]
            bias[:, h * count : (h + 1) * count] = jnp.where(same, 0.0, LARGE_NEGATIVE)

    def project(q):
        value = product(hidden_ref[...], full[0, q]).astype(jnp.bfloat16)
        if q == 0:
            query_ref[...] = value
            total_ref[...] = jnp.zeros_like(total_ref)
            work[...] = jnp.zeros_like(work)
            return
        here = pl.ds(pl.multiple_of(c * count, 256), count)
        sides_ref[q - 1, here, :] = value
        send("other", sides_ref.at[q - 1, here], sides_ref.at[q - 1, here], kv_send.at[q - 1], kv_recv.at[q - 1], c_peer)

    def attend(first, last):
        if first == 0:
            there = pl.ds(pl.multiple_of((1 - c) * count, 256), count)
            for q in (0, 1):
                arrive(sides_ref.at[q, there], kv_recv.at[q], c_peer)
            keep(sides_ref, sides_out_ref, store_sem.at[0])
        size = width // HEADS
        scale = 1.0 / math.sqrt(size)

        def body(head, carry):
            columns, inside = window_of(head, size, width)
            query = query_ref[:, columns]
            query = jnp.where(inside, query, jnp.zeros_like(query))
            scores = product_by_columns(query, sides_ref[0, :, columns]) * scale + bias[...]
            top = jnp.max(scores, axis=-1, keepdims=True)
            raised = jnp.exp(scores - top)
            total = jnp.sum(raised, axis=-1, keepdims=True)
            chance = (raised * (1.0 / total)).astype(jnp.bfloat16)
            context = product(chance, sides_ref[1, :, columns])
            work[:, columns] = jnp.where(inside, context, work[:, columns])
            lane = lax.broadcasted_iota(jnp.int32, (1, 128), 1)
            total_ref[...] = jnp.where(lane == head, top + jnp.log(total), total_ref[...])
            return carry

        lax.fori_loop(first, last, body, 0)

    def mix():
        context_ref[...] = work[...].astype(jnp.bfloat16)
        attended_ref[...] = product(context_ref[...], full[0, 3])
        keep(attended_ref, attended_out_ref, store_sem.at[1])

    def second_norm(part_of):
        def body(at):
            segments = seg_col_ref[at, :1]
            gate = pick(segments, table_ref, 0, 2, width)
            middle = tokens_ref[at, :].astype(jnp.float32) + gate * attended_ref[at, :]
            middle_ref[at, :] = middle
            value, _ = normed(middle)
            value = value * (1.0 + pick(segments, table_ref, 4, 1, width))
            hidden_two_ref[at, :] = (value + pick(segments, table_ref, 4, 0, width)).astype(jnp.bfloat16)
            level = level_ref[3:4, :1]
            for crop in (2, 1, 0):
                level = jnp.where(segments == crop, level_ref[crop : crop + 1, :1], level)
            grad = cot_ref[at, :].astype(jnp.float32) * level
            grad_mlp[at, :] = (grad * pick(segments, table_ref, 4, 2, width)).astype(jnp.bfloat16)

        chunks(count // 2, body, part_of * (count // 2))
        if part_of:
            keep(middle_ref, middle_out_ref, store_sem.at[2])

    slope_copies = {}

    def expand(q):
        work[...] = product(hidden_two_ref[...], full[1, q])

    def bend(q):
        if q >= 2:
            slope_copies[q - 2].wait()

        def body(at):
            u = work[at, :]
            square = u * u
            curve = jnp.tanh(GELU_SCALE * (u + GELU_CUBE * (square * u)))
            active[q, at, :] = (0.5 * u * (1.0 + curve)).astype(jnp.bfloat16)
            inner = GELU_SCALE * (1.0 + 3.0 * GELU_CUBE * square)
            slope[q % 2, at, :] = 0.5 * (1.0 + curve) + 0.5 * u * (1.0 - curve * curve) * inner

        chunks(count, body)
        copy = pltpu.make_async_copy(slope.at[q % 2], slope_ref.at[q], slope_sem.at[q % 2])
        copy.start()
        slope_copies[q] = copy
        keep(active.at[q], active_ref.at[q], store_sem.at[3 + q])

    def down_grad(q):
        if q == 0:
            finish_sends(0)
            saves.pop(0).wait()
        full[0, q] = product_by_rows(active[q], grad_mlp[...]).astype(jnp.bfloat16)
        keep(full.at[0, q], down_part_ref.at[q], grad_sem.at[q])

    kinds = (lambda a, k: own(a), pass_piece, spread, turn_y, turn_x, share_sides, pass_diagonal, finish)
    steps = [partial(kinds[n % 10], n // 100, n // 10 % 10) for n in FORWARD_STEPS]
    layer = [mod_start, mod_cores, mod_plane, mod_line, mod_last, mod_end]
    layer += [partial(first_norm, h) for h in (0, 1)] + [partial(complete, 0)]
    layer += [partial(project, q) for q in (1, 2, 0)] + [partial(attend, h, h + 2) for h in range(0, HEADS, 2)]
    layer += [mix, partial(second_norm, 0), partial(second_norm, 1), partial(complete, 1)]
    for q in range(4):
        layer += [partial(expand, q), partial(bend, q)]
    layer += [partial(down_grad, q) for q in range(4)]
    interleave(steps, layer, FORWARD_AFTER)
    complete_level(pending.pop())
    for copy in saves:
        copy.wait()
    for q in (2, 3):
        slope_copies[q].wait()
    for a in (1, 2, "other"):
        finish_sends(a)


def run_forward(qkv, out_weight, up, down, cond, noise, counts, ada, tokens, cot, segments):
    count, width = tokens.shape
    share = qkv.shape[0]
    dma = pltpu.SemaphoreType.DMA
    low, wide, whole = jnp.bfloat16, jnp.float32, jnp.int32
    side = ada.shape[1] // 2
    vmem, any_ = pl.BlockSpec(memory_space=pltpu.VMEM), pl.BlockSpec(memory_space=pl.ANY)
    out, buffer = jax.ShapeDtypeStruct, pltpu.VMEM
    return pl.pallas_call(
        partial(forward_kernel, share),
        out_shape=(
            out((3, 4, width, width), low),
            out((4, width, width), low),
            out((4, count, width), wide),
            out((4, count, width), low),
            out((2, 2 * count, width), low),
            out((count, width), wide),
            out((count, width), wide),
            out((count, width), low),
            out((count, width), low),
            out((count, 128), wide),
            out((count, width), low),
            out((count, width), low),
            out((8, side), wide),
            out((CHIPS, 16, 128), low),
            out((8, 128), wide),
            out((count, width), low),
            out((2, 8, count), whole),
            out((count, 128), whole),
            out((PAD, 2 * side), low),
        ),
        in_specs=[vmem] * 11,
        out_specs=[any_] * 7 + [vmem] * 12,
        scratch_shapes=[
            buffer((3, 4, width, width), low),
            buffer((2, 4, PAD, width), low),
            buffer((2, 4 * PAD, width), low),
            buffer((16, width), wide),
            buffer((16, width), low),
            buffer((CHIPS, 16, 256), low),
            buffer((CHIPS * 8, side), wide),
            buffer((CHIPS * 8, BAND), wide),
            buffer((CHIPS * 8, BAND), wide),
            buffer((4, 8, BAND), wide),
            buffer((4, 8, BAND), wide),
            buffer((4, 8, BAND), wide),
            buffer((3, 8, BAND), wide),
            buffer((2, 8, BAND), wide),
            buffer((2, 2 * count, width), low),
            buffer((count, width), wide),
            buffer((count, width), wide),
            buffer((count, 2 * count), wide),
            buffer((count, width), wide),
            buffer((4, count, width), low),
            buffer((2, count, width), wide),
            dma((2, 3)), dma((2, 3)), dma((3, 4, 2)), dma((3, 4)), dma((3, 4, 2)), dma((3, 4)),
            dma((3, 4, 2)), dma((3, 4, 2)), dma((3, 4, 2)), dma((3, 4, 2)),
            dma((3, 4)), dma((3, 4)), dma((3, 4)), dma((3, 4)),
            dma((3, 4, 4)), dma((3, 4, 4)),
            dma((CHIPS - 1,)), dma((CHIPS - 1,)), dma, dma, dma((4,)), dma((4,)),
            dma((4,)), dma((4,)), dma((4,)), dma((4,)), dma((3,)), dma((3,)), dma, dma, dma, dma,
            dma((2,)), dma((2,)), dma((2,)), dma((4,)), dma((2,)), dma((4,)), dma((7,)),
        ],
        compiler_params=pltpu.CompilerParams(
            collective_id=0, has_side_effects=True, vmem_limit_bytes=63 * 2**20
        ),
        name="forward",
    )(qkv, out_weight, up, down, cond, noise, counts, ada, tokens, cot, segments)


def interleave(steps, layer, after):
    done = 0
    for count, step in enumerate(steps):
        while done < len(layer) and after[done] <= count:
            layer[done]()
            done += 1
        step()
    for step in layer[done:]:
        step()


def add_rows(dst, sources, start, rows):
    def body(i, carry):
        where = pl.ds(pl.multiple_of(start + i * 16, 16), 16)
        total = dst[where, :].astype(jnp.float32)
        for source in sources:
            total = total + source[where, :].astype(jnp.float32)
        dst[where, :] = total.astype(dst.dtype)
        return carry

    lax.fori_loop(0, rows // 16, body, 0)


def backward_kernel(share, weights_ref, down_part_ref, slope_ref, middle_ref, attended_ref, active_ref,
                    hidden_ref, query_ref, sides_ref, total_ref, context_ref, hidden_two_ref,
                    grad_mlp_ref, table_ref, conds_ref, level_ref, seg_all_ref, seg_col_ref, tokens_ref,
                    cot_ref, ada_ref,
                    mixer_part_ref, up_part_ref, rows_ref, down_ref, tokens_grad_ref, ada_grad_ref, silu_ref,
                    out_ref,
                    held, from_core, diag, from_x, from_y, piece_line, diag_line, spare, block, part, quad, lows,
                    work, grad_middle, grad_context, leave, enter, bias, sums, sums_row, sums_core, band, silu_part, silu_side,
                    *sems):
    (
        load_sem, c_send, c_recv, dx_send, dx_recv, dy_send, dy_recv, x_send, x_recv,
        y_send, y_recv, zo_send, zo_recv, zd_send, zd_recv, group_send, group_recv, block_sem, part_sem, quad_sem, low_sem, out_sem,
        side_send, side_recv, m_send, m_recv, mz_send, mz_recv, mx_send, mx_recv, my_send, my_recv,
        md_send, md_recv, mc_send, mc_recv, s_send, s_recv, sc_send, sc_recv,
    ) = sems
    z, y, x, c = position()
    me = z * 4 + y * 2 + x
    group = x * 2 + c
    rows = 4 * share
    count, width = tokens_ref.shape
    x_peer, y_peer, c_peer = device(z, y, 1 - x, c), device(z, 1 - y, x, c), device(z, y, x, 1 - c)
    partners = [(x, 1 - c), (1 - x, c), (1 - x, 1 - c)]
    greet(
        [((me + k) % CHIPS, c) for k in range(1, CHIPS)] + [c_peer, device(z, y, 1 - x, 1 - c)]
    )
    sends = {}

    def send(owner, *args):
        copy = remote(*args)
        copy.start()
        sends.setdefault(owner, []).append(copy)

    def finish_sends(owner):
        for copy in sends.pop(owner, []):
            copy.wait_send()

    order = [(a, k) for a in (2, 1, 0) for k in (3, 2, 1, 0)]
    given = (mixer_part_ref, up_part_ref, down_part_ref)
    loads = {}
    inner_rows = slice(FAR[0], rows - FAR[1])

    def cuts(i):
        top, low = FAR if order[i][1] else NEAR
        return top, rows - low

    def line(k):
        to = level_of(z, k)
        step = jnp.where(z < to, 1, -1)
        behind = z - step
        return to, z + step, (behind >= 0) & (behind < 4)

    def along(i, ref, lines, send_sem, recv_sem):
        a, k = order[i]
        to, after, _ = line(k)
        spot = jnp.where((after == to) & (z > to), 4, to)
        copy = remote(ref, lines.at[a % 2, spot], send_sem.at[a, k], recv_sem.at[a, spot], device(after, y, x, c))
        copy.start()
        return copy

    def from_line(i, lines, recv_sem, spot):
        a = order[i][0]
        arrive(lines.at[a % 2, spot], recv_sem.at[a, spot], device((z + 1) % 4, y, x, c))

    def hold(i, ref, lines, send_sem, recv_sem):
        sends.setdefault(("held", i), []).append(
            remote(ref, lines.at[0, 0], send_sem.at[order[i]], recv_sem.at[order[i][0], 0], x_peer)
        )

    def begin(i):
        a, k = order[i]
        if i % 4 == 0:
            for n in sorted(going):
                going.pop(n).wait()
        finish_sends(("held", i - HELD))
        zz = level_of(z, k)
        for pos in (3, 1, 2, 0):
            yy = 1 - y if PLACES[pos][0] else y
            xx = 1 - x if PLACES[pos][1] else x
            for cc in (1 - c, c):
                where, row = block_of(a, zz * 2 + yy, xx * 2 + cc)
                src = given[a].at[where, pl.ds(pl.multiple_of(row * rows, 16), rows)]
                if cc is c:
                    loads[i, pos] = pltpu.make_async_copy(src, held.at[i % HELD, pos], load_sem.at[i, pos])
                    loads[i, pos].start()
                else:
                    send("core", src, from_core.at[i % 4, pos], c_send.at[i, pos], c_recv.at[i, pos], c_peer)

    def pair(i, pos):
        k = order[i][1]
        top, low = cuts(i)
        mine = held.at[i % HELD, pos]
        loads[i, pos].wait()
        arrive(from_core.at[i % 4, pos], c_recv.at[i, pos], c_peer)
        add_rows(mine, [from_core.at[i % 4, pos]], 0, rows)
        if pos == 3 and k:
            diagonal(i)
            part = mine.at[inner_rows]
            hold(i, part, diag_line, zd_send, zd_recv)
            _, _, fed = line(k)

            @pl.when(jnp.logical_not(fed))
            def _():
                along(i, part, diag_line, zd_send, zd_recv)

        if pos == 1:
            part = mine.at[top:rows]
            send(("held", i), part, from_x.at[i % 6, top:rows], x_send.at[i, 1], x_recv.at[i, 1], x_peer)
        if pos == 2:
            part = mine.at[0:low]
            send(("held", i), part, from_y.at[i % 6, 0:low], y_send.at[i, 0], y_recv.at[i, 0], y_peer)

    def diagonal(i):
        top, low = cuts(i)
        mine, far = held.at[i % HELD, 3], diag.at[i % 5]
        send(("held", i), mine.at[0:top], far.at[0:top], dy_send.at[i], dy_recv.at[i], y_peer)
        send(("held", i), mine.at[low:rows], far.at[low:rows], dx_send.at[i], dx_recv.at[i], x_peer)

    def diag_along(i):
        k = order[i][1]
        mine = held.at[i % HELD, 3, inner_rows]
        size = rows - FAR[0] - FAR[1]
        if k:
            to, _, fed = line(k)

            @pl.when(fed)
            def _():
                from_line(i, diag_line, zd_recv, to)
                add_rows(mine, [diag_line.at[order[i][0] % 2, to]], 0, size)
                along(i, mine, diag_line, zd_send, zd_recv)

        else:
            for spot, here in ((z, z > 0), (4, z < 3)):

                @pl.when(here)
                def _():
                    from_line(i, diag_line, zd_recv, spot)
                    add_rows(mine, [diag_line.at[order[i][0] % 2, spot]], 0, size)

            diagonal(i)

    def relay_x(i):
        top, _ = cuts(i)
        far, mine = diag.at[i % 5], held.at[i % HELD, 1]
        arrive(far.at[0:top], dy_recv.at[i], y_peer)
        add_rows(mine, [far], 0, top)
        send(("held", i), mine.at[0:top], from_x.at[i % 6, 0:top], x_send.at[i, 0], x_recv.at[i, 0], x_peer)

    def relay_y(i):
        _, low = cuts(i)
        far, mine = diag.at[i % 5], held.at[i % HELD, 2]
        arrive(far.at[low:rows], dx_recv.at[i], x_peer)
        add_rows(mine, [far], low, rows - low)
        send(("held", i), mine.at[low:rows], from_y.at[i % 6, low:rows], y_send.at[i, 1], y_recv.at[i, 1], y_peer)

    def plane(i):
        k = order[i][1]
        top, low = cuts(i)
        mine = held.at[i % HELD, 0]
        arrive(from_x.at[i % 6, 0:top], x_recv.at[i, 0], x_peer)
        arrive(from_x.at[i % 6, top:rows], x_recv.at[i, 1], x_peer)
        arrive(from_y.at[i % 6, 0:low], y_recv.at[i, 0], y_peer)
        arrive(from_y.at[i % 6, low:rows], y_recv.at[i, 1], y_peer)
        add_rows(mine, [from_x.at[i % 6], from_y.at[i % 6]], 0, rows)
        if k:
            hold(i, mine, piece_line, zo_send, zo_recv)
            _, _, fed = line(k)

            @pl.when(jnp.logical_not(fed))
            def _():
                along(i, mine, piece_line, zo_send, zo_recv)

    def piece_along(i):
        a, k = order[i]
        mine = held.at[i % HELD, 0]
        if k:
            to, _, fed = line(k)

            @pl.when(fed)
            def _():
                from_line(i, piece_line, zo_recv, to)
                add_rows(mine, [piece_line.at[a % 2, to]], 0, rows)
                along(i, mine, piece_line, zo_send, zo_recv)

            return
        for spot, here in ((z, z > 0), (4, z < 3)):

            @pl.when(here)
            def _():
                from_line(i, piece_line, zo_recv, spot)
                add_rows(mine, [piece_line.at[a % 2, spot]], 0, rows)

        if a == 2:
            down_ref[...] = mine[...].astype(jnp.float32)
            return
        spare[a] = product_by_rows(row_selector(rows, share), mine[...]).astype(jnp.bfloat16)
        for j, (px, pc) in enumerate(partners):
            send(
                "end",
                spare.at[a, pl.ds(pl.multiple_of((px * 2 + pc) * PAD, 16), PAD)],
                rows_ref.at[a, group],
                group_send.at[a, j],
                group_recv.at[a, j],
                device(z, y, px, pc),
            )
        rows_ref[a, group] = spare[a, pl.ds(pl.multiple_of(group * PAD, 16), PAD), :]

    uses = [(2, q) for q in range(4)] + [(1, q) for q in range(4)] + [(0, 3), (0, 0), (0, 1), (0, 2)]
    coming = {}

    def fetch(n):
        if n < len(uses):
            copy = pltpu.make_async_copy(weights_ref.at[uses[n]], block.at[n % 2], block_sem.at[n % 2])
            copy.start()
            coming[n] = copy

    def take(n):
        coming[n].wait()
        return block[n % 2]

    going = {}

    def put(n, left, right, target):
        if n - 2 in going:
            going.pop(n - 2).wait()

        def body(i, carry):
            columns = pl.ds(pl.multiple_of(i * 384, 128), 384)
            part[n % 2, columns, :] = product_by_rows(left[:, columns], right[...]).astype(jnp.bfloat16)
            return carry

        lax.fori_loop(0, width // 384, body, 0)
        going[n] = pltpu.make_async_copy(part.at[n % 2], target, part_sem.at[n % 2])
        going[n].start()

    quads = {}

    def slopes(q):
        quads[q] = pltpu.make_async_copy(slope_ref.at[q], quad.at[q], quad_sem.at[q])
        quads[q].start()
        quads["active", q] = pltpu.make_async_copy(active_ref.at[q], lows.at[q], low_sem.at[q])
        quads["active", q].start()

    def through_down(q):
        quads.pop(("active", q)).wait()
        value = product(lows[q], take(q))
        grad_middle[...] = grad_middle[...] + value if q else value
        work[...] = product_by_columns(grad_mlp_ref[...], block[q % 2])
        fetch(q + 2)
        quads[q].wait()

        def body(at):
            lows[q, at, :] = (work[at, :] * quad[q, at, :]).astype(jnp.bfloat16)

        chunks(count, body)
        if q < 2:
            source = (middle_ref, attended_ref)[q]
            quads[q] = pltpu.make_async_copy(source, quad.at[q], quad_sem.at[q])
            quads[q].start()

    def up_grad(q):
        put(q, hidden_two_ref, lows.at[q], up_part_ref.at[q])

    def through_up(q):
        value = product_by_columns(lows[q], take(4 + q))
        work[...] = work[...] + value if q else value
        fetch(6 + q)

    def norm_pull(grad, value, inverse):
        return inverse * (
            grad
            - jnp.mean(grad, axis=-1, keepdims=True)
            - value * jnp.mean(grad * value, axis=-1, keepdims=True)
        )

    def add_sums(segments, which, value):
        for crop in range(CROPS):
            kept = jnp.where(segments == crop, value, 0.0)
            sums[which, crop] = sums[which, crop] + kept[:8] + kept[8:]

    def second_norm(half):
        if half == 0:
            for q in range(2):
                quads[q].wait()
            sums[...] = jnp.zeros_like(sums)

        def body(at):
            segments = seg_col_ref[at, :1]
            grad = work[at, :]
            middle, mlp = quad[0, at, :], grad_middle[at, :]
            value, inverse = normed(middle)
            gate = pick(segments, table_ref, 4, 2, width)
            leave[0, at, :] = (middle + gate * mlp).astype(jnp.bfloat16)
            level = level_ref[3:4, :1]
            for crop in (2, 1, 0):
                level = jnp.where(segments == crop, level_ref[crop : crop + 1, :1], level)
            grad_out = cot_ref[at, :].astype(jnp.float32) * level
            add_sums(segments, 3, grad)
            add_sums(segments, 4, grad * value)
            add_sums(segments, 5, grad_out * mlp)
            scaled = grad * (1.0 + pick(segments, table_ref, 4, 1, width))
            total = grad_out + norm_pull(scaled, value, inverse)
            grad_middle[at, :] = total
            add_sums(segments, 2, total * quad[1, at, :])
            lows[3, at, :] = (total * pick(segments, table_ref, 0, 2, width)).astype(jnp.bfloat16)

        chunks(count // 2, body, half * (count // 2))
        if half:
            quads["out"] = pltpu.make_async_copy(leave.at[0], out_ref, out_sem)
            quads["out"].start()

    def context_grad():
        grad_context[...] = product_by_columns(lows[3], take(8)).astype(jnp.bfloat16)
        fetch(10)

    def out_grad():
        put(4, context_ref, lows.at[3], mixer_part_ref.at[3])
        for h in (0, 1):
            same = seg_col_ref[:, :1] == seg_all_ref[h][:1, :]
            bias[:, h * count : (h + 1) * count] = jnp.where(same, 0.0, LARGE_NEGATIVE)

    def attend_back(first, last):
        size = width // HEADS
        scale = 1.0 / math.sqrt(size)

        def body(head, carry):
            columns, inside = window_of(head, size, width)
            query, keys = query_ref[:, columns], sides_ref[0, :, columns]
            grad = grad_context[:, columns]
            scores = product_by_columns(jnp.where(inside, query, jnp.zeros_like(query)), keys)
            lane = lax.broadcasted_iota(jnp.int32, (1, 128), 1)
            total = jnp.sum(jnp.where(lane == head, total_ref[...], 0.0), axis=-1, keepdims=True)
            chance = jnp.exp(scores * scale + bias[...] - total)
            pulled = product_by_columns(
                jnp.where(inside, grad, jnp.zeros_like(grad)), sides_ref[1, :, columns]
            )
            inner = jnp.sum(chance * pulled, axis=-1, keepdims=True)
            grad_scores = (chance * (pulled - inner)).astype(jnp.bfloat16)
            grad_query = (product(grad_scores, keys) * scale).astype(jnp.bfloat16)
            lows[0, :, columns] = jnp.where(inside, grad_query, lows[0, :, columns])
            grad_key = product_by_rows(grad_scores, query) * scale
            grad_value = product_by_rows(chance.astype(jnp.bfloat16), grad)
            for h in (0, 1):
                here = slice(h * count, (h + 1) * count)
                quad[h, :, columns] = jnp.where(inside, grad_key[here], quad[h, :, columns])
                quad[2 + h, :, columns] = jnp.where(inside, grad_value[here], quad[2 + h, :, columns])
            return carry

        lax.fori_loop(first, last, body, 0)

    def swap_sides():
        quads["out"].wait()
        for j in (0, 1):
            leave[j] = quad[2 * j + 1 - c].astype(jnp.bfloat16)
            send("end", leave.at[j], enter.at[j], side_send.at[j], side_recv.at[j], c_peer)

    def query_grad():
        put(5, hidden_ref, lows.at[0], mixer_part_ref.at[0])

    def side_grad(j):
        arrive(enter.at[j], side_recv.at[j], c_peer)

        def body(at):
            total = quad[2 * j + c, at, :] + enter[j, at, :].astype(jnp.float32)
            lows[1 + j, at, :] = total.astype(jnp.bfloat16)

        chunks(count, body)
        put(6 + j, hidden_ref, lows.at[1 + j], mixer_part_ref.at[1 + j])

    def through_qkv(q):
        value = product_by_columns(lows[q], take(9 + q))
        work[...] = work[...] + value if q else value
        fetch(11 + q)

    def first_norm(half):
        def body(at):
            segments = seg_col_ref[at, :1]
            grad = work[at, :]
            value, inverse = normed(tokens_ref[at, :].astype(jnp.float32))
            add_sums(segments, 0, grad)
            add_sums(segments, 1, grad * value)
            scaled = grad * (1.0 + pick(segments, table_ref, 0, 1, width))
            tokens_grad_ref[at, :] = grad_middle[at, :] + norm_pull(scaled, value, inverse)

        chunks(count // 2, body, half * (count // 2))

    def sums_leave():
        for which in range(6):
            for crop in range(CROPS):
                row = which // 3 * CROPS + crop
                columns = slice(which % 3 * width, (which % 3 + 1) * width)
                sums_row[row : row + 1, columns] = jnp.sum(sums[which, crop], axis=0, keepdims=True)
        send("end", sums_row, sums_core, m_send, m_recv, c_peer)

    side = sums_row.shape[1]

    def place(k, other_y, other_x):
        zz = (z - k + 4) % 4
        yy = 1 - y if other_y else y
        xx = 1 - x if other_x else x
        return band.at[c, pl.ds(pl.multiple_of((zz * 4 + yy * 2 + xx) * 16, 16), 16)]

    def sums_start():
        arrive(sums_core, m_recv, c_peer)
        near = pl.ds(pl.multiple_of(c * (side - BAND), 128), BAND)
        total = sums_row[:, near] + sums_core[:, near]
        total = jnp.concatenate([total[:, : BAND // 2], total[:, BAND // 2 :]], axis=0)
        band[c, pl.ds(pl.multiple_of(me * 16, 16), 16), :] = total.astype(jnp.bfloat16)
        mine = place(0, 0, 0)
        for k in (1, 2, 3):
            send("end", mine, mine, mz_send.at[k - 1], mz_recv.at[k - 1], device((z + k) % 4, y, x, c))
        send("end", mine, mine, mx_send.at[0], mx_recv.at[0], x_peer)
        send("end", mine, mine, my_send.at[0], my_recv.at[0], y_peer)

    def sums_line():
        for k in (1, 2, 3):
            piece = place(k, 0, 0)
            arrive(piece, mz_recv.at[k - 1], device((z - k + 4) % 4, y, x, c))
            send("end", piece, piece, mx_send.at[k], mx_recv.at[k], x_peer)
            send("end", piece, piece, my_send.at[k], my_recv.at[k], y_peer)

    def sums_plane():
        for k in range(4):
            from_side, from_up = place(k, 0, 1), place(k, 1, 0)
            arrive(from_side, mx_recv.at[k], x_peer)
            arrive(from_up, my_recv.at[k], y_peer)
            if k % 2:
                send("end", from_side, from_side, md_send.at[k], md_recv.at[k], y_peer)
            else:
                send("end", from_up, from_up, md_send.at[k], md_recv.at[k], x_peer)

    def sums_cores():
        for k in range(4):
            arrive(place(k, 1, 1), md_recv.at[k], y_peer if k % 2 else x_peer)
        send("end", band.at[c], band.at[c], mc_send, mc_recv, c_peer)

    def condition(source):
        if source == 0:
            arrive(band.at[1 - c], mc_recv, c_peer)
            silu_side[...] = jnp.zeros_like(silu_side)
        acts = conds_ref[:, :8, :].astype(jnp.float32).reshape(CHIPS * 8, 128)
        row = lax.broadcasted_iota(jnp.int32, acts.shape, 0) % 8
        acts = jnp.where(row < CROPS, acts, 0.0)
        upper = acts.astype(jnp.bfloat16)
        lower = pltpu.roll(acts, CROPS, 0).astype(jnp.bfloat16)
        for half in (0, 1):
            first = source * (side - BAND) + half * (BAND // 2)
            skip = max(0, source * BAND - first)
            term = band[source].astype(jnp.float32).reshape(CHIPS, 16, BAND // 2)
            term = term[:, half * 8 : (half + 1) * 8, skip:].reshape(CHIPS * 8, BAND // 2 - skip)
            term = term.astype(jnp.bfloat16)
            for which, act in enumerate((upper, lower)):
                columns = slice(which * side + first + skip, which * side + first + BAND // 2)
                ada_grad_ref[:, columns] = product_by_rows(act, term)[: ada_grad_ref.shape[0]]
                value = product_by_columns(term, ada_ref[:, columns])
                silu_side[which, :, :PAD] = silu_side[which, :, :PAD] + value
        if source == 0:
            return
        silu_part[...] = silu_side[0] + pltpu.roll(silu_side[1], CHIPS * 8 - CROPS, 0)
        silu_ref[c, me] = silu_part[pl.ds(pl.multiple_of(me * 8, 8), 8), :]
        for k in range(1, CHIPS):
            to = (me + k) % CHIPS
            src = silu_part.at[pl.ds(pl.multiple_of(to * 8, 8), 8)]
            send("end", src, silu_ref.at[c, me], s_send.at[k - 1], s_recv.at[k - 1], (to, c))

    def condition_cores():
        for k in range(1, CHIPS):
            source = (me - k + CHIPS) % CHIPS
            arrive(silu_ref.at[c, source], s_recv.at[k - 1], (source, c))
        send("end", silu_ref.at[c], silu_ref.at[c], sc_send, sc_recv, c_peer)

    kinds = [begin] + [partial(pair, pos=pos) for pos in range(4)]
    kinds += [diag_along, relay_x, relay_y, plane, piece_along]
    steps = [partial(kinds[n % 10], n // 10) for n in BACKWARD_STEPS]
    layer = [partial(through_down, q) for q in range(4)] + [partial(up_grad, q) for q in range(4)]
    layer += [partial(through_up, q) for q in range(4)] + [partial(second_norm, h) for h in (0, 1)]
    layer += [context_grad, out_grad] + [partial(attend_back, h, h + 2) for h in range(0, HEADS, 2)]
    layer += [swap_sides, query_grad, partial(side_grad, 0), partial(side_grad, 1)]
    layer += [partial(through_qkv, q) for q in range(3)] + [partial(first_norm, h) for h in (0, 1)]
    layer += [sums_leave, sums_start, sums_line, sums_plane, sums_cores]
    layer += [partial(condition, 0), partial(condition, 1), condition_cores]
    begin(0)
    for q in range(4):
        slopes(q)
    fetch(0)
    fetch(1)
    interleave(steps, layer, BACKWARD_AFTER)
    for a in range(2):
        for j, (px, pc) in enumerate(partners):
            arrive(rows_ref.at[a, px * 2 + pc], group_recv.at[a, j], device(z, y, px, pc))
    arrive(silu_ref.at[1 - c], sc_recv, c_peer)
    for owner in list(sends):
        finish_sends(owner)


def run_backward(given, share):
    (weights, down_part, slope, middle, attended, active, hidden, query, sides, total, context, hidden_two,
     grad_mlp, table, conds, level, seg_all, seg_col, tokens, cot, ada) = given
    count, width = tokens.shape
    rows, side = 4 * share, ada.shape[1] // 2
    dma = pltpu.SemaphoreType.DMA
    low, wide = jnp.bfloat16, jnp.float32
    vmem, any_ = pl.BlockSpec(memory_space=pltpu.VMEM), pl.BlockSpec(memory_space=pl.ANY)
    out, buffer = jax.ShapeDtypeStruct, pltpu.VMEM
    slots = 12
    return pl.pallas_call(
        partial(backward_kernel, share),
        out_shape=(
            out((4, width, width), low),
            out((4, width, width), low),
            out((2, 4, PAD, width), low),
            out((rows, width), wide),
            out((count, width), wide),
            out((-(-share // 8) * 8, ada.shape[1]), wide),
            out((2, CHIPS, 8, 128), wide),
            out((count, width), low),
        ),
        in_specs=[any_] * 6 + [vmem] * 15,
        out_specs=[any_] * 2 + [vmem] * 5 + [any_],
        scratch_shapes=[
            buffer((HELD, 4, rows, width), low),
            buffer((4, 4, rows, width), low),
            buffer((5, rows, width), low),
            buffer((6, rows, width), low),
            buffer((6, rows, width), low),
            buffer((2, 5, rows, width), low),
            buffer((2, 5, rows - FAR[0] - FAR[1], width), low),
            buffer((2, 4 * PAD, width), low),
            buffer((2, width, width), low),
            buffer((2, width, width), low),
            buffer((4, count, width), wide),
            buffer((4, count, width), low),
            buffer((count, width), wide),
            buffer((count, width), wide),
            buffer((count, width), low),
            buffer((2, count, width), low),
            buffer((2, count, width), low),
            buffer((count, 2 * count), wide),
            buffer((6, CROPS, 8, width), wide),
            buffer((8, side), wide),
            buffer((8, side), wide),
            buffer((2, CHIPS * 16, BAND // 2), low),
            buffer((CHIPS * 8, 128), wide),
            buffer((2, CHIPS * 8, 128), wide),
            dma((slots, 4)), dma((slots, 4)), dma((slots, 4)),
            dma((slots,)), dma((slots,)), dma((slots,)), dma((slots,)),
            dma((slots, 2)), dma((slots, 2)), dma((slots, 2)), dma((slots, 2)),
            dma((3, 4)), dma((3, 5)), dma((3, 4)), dma((3, 5)),
            dma((2, 3)), dma((2, 3)), dma((2,)), dma((2,)), dma((4,)), dma((4,)), dma,
            dma((2,)), dma((2,)), dma, dma, dma((3,)), dma((3,)), dma((4,)), dma((4,)), dma((4,)), dma((4,)),
            dma((4,)), dma((4,)), dma, dma, dma((CHIPS - 1,)), dma((CHIPS - 1,)), dma, dma,
        ],
        compiler_params=pltpu.CompilerParams(
            collective_id=1, has_side_effects=True, vmem_limit_bytes=63 * 2**20 + 2**19
        ),
        name="backward",
    )(*given)


def finish_kernel(share, rows_ref, ada_given_ref, silu_ref, cond_ref, down_given, tokens_grad_given, out_given,
                  qkv_ref, out_grad_ref, up_ref, ada_ref, cond_grad_ref, down_ref, tokens_grad_ref, out_ref):
    for given, ref in ((down_given, down_ref), (tokens_grad_given, tokens_grad_ref), (out_given, out_ref)):

        def body(at):
            ref[at, :] = given[at, :]

        chunks(ref.shape[0], body)
    width = rows_ref.shape[-1]
    for q in range(4):
        value = rows_ref[0, q].astype(jnp.float32)[:share]
        if q == 3:
            out_grad_ref[...] = value
        else:
            qkv_ref[:, q * width : (q + 1) * width] = value
        up_ref[:, q * width : (q + 1) * width] = rows_ref[1, q].astype(jnp.float32)[:share]
    ada_ref[...] = ada_given_ref[...][:share]
    lane = lax.broadcasted_iota(jnp.int32, (8, 128), 1)
    tiles = [jnp.zeros((8, 128), jnp.float32)] * (width // 128)
    for number in range(2 * CHIPS):
        tile, offset = divmod(number * share, 128)
        value = jnp.where(lane < share, silu_ref[number % 2, number // 2], 0.0)
        if offset:
            value = pltpu.roll(value, offset, 1)
        tiles[tile] = tiles[tile] + jnp.where(lane >= offset, value, 0.0)
        if offset + share > 128:
            tiles[tile + 1] = tiles[tile + 1] + jnp.where(lane < offset, value, 0.0)
    grad = jnp.concatenate(tiles, axis=1)[:CROPS]
    cond = cond_ref[...].astype(jnp.float32)
    chance = 1.0 / (1.0 + jnp.exp(-cond))
    cond_grad_ref[...] = grad * (chance * (1.0 + cond * (1.0 - chance)))


def run_finish(rows, ada_grad, silu_part, cond, down_grad, tokens_grad, tokens_out, share):
    width = rows.shape[-1]
    wide = jnp.float32
    vmem, out = pl.BlockSpec(memory_space=pltpu.VMEM), jax.ShapeDtypeStruct
    return pl.pallas_call(
        partial(finish_kernel, share),
        out_shape=(
            out((share, 3 * width), wide),
            out((share, width), wide),
            out((share, 4 * width), wide),
            out((share, ada_grad.shape[1]), wide),
            out(cond.shape, wide),
            out(down_grad.shape, wide),
            out(tokens_grad.shape, wide),
            out(tokens_out.shape, tokens_out.dtype),
        ),
        in_specs=[vmem] * 7,
        out_specs=[vmem] * 8,
        compiler_params=pltpu.CompilerParams(vmem_limit_bytes=63 * 2**20),
        name="finish",
    )(rows, ada_grad, silu_part, cond, down_grad, tokens_grad, tokens_out)


def layer_norm(values):
    center = values - jnp.mean(values, axis=-1, keepdims=True)
    inverse = lax.rsqrt(jnp.mean(center * center, axis=-1, keepdims=True) + EPSILON)
    return (center * inverse, inverse)


def norm_back(grad_normed, normed, inverse):
    return inverse * (
        grad_normed
        - jnp.mean(grad_normed, axis=-1, keepdims=True)
        - normed * jnp.mean(grad_normed * normed, axis=-1, keepdims=True)
    )


def to_heads(array):
    return array.reshape(array.shape[0], HEADS, array.shape[1] // HEADS)


def dots(spec, left, right):
    return jnp.einsum(spec, left, right, preferred_element_type=jnp.float32)


def masked_scores(query_heads, key_heads, same_crop):
    scale_factor = 1.0 / math.sqrt(query_heads.shape[-1])
    scores = dots("qhd,khd->hqk", query_heads, key_heads) * scale_factor
    return jnp.where(same_crop[None], scores, LARGE_NEGATIVE)


def attend(query_seq, key_seq, value_seq, same_crop):
    scores = masked_scores(to_heads(query_seq), to_heads(key_seq), same_crop)
    row_max = jnp.max(scores, axis=-1, keepdims=True)
    raised = jnp.exp(scores - row_max)
    row_total = jnp.sum(raised, axis=-1, keepdims=True)
    probability = (raised / row_total).astype(jnp.bfloat16)
    context = dots("hqk,khd->qhd", probability, to_heads(value_seq))
    return (context.reshape(query_seq.shape[0], -1), (row_max + jnp.log(row_total))[..., 0])


def attend_back(query_seq, key_seq, value_seq, same_crop, log_total, grad_seq):
    query_heads = to_heads(query_seq)
    key_heads = to_heads(key_seq)
    value_heads = to_heads(value_seq)
    grad_heads = to_heads(grad_seq)
    scale_factor = 1.0 / math.sqrt(query_heads.shape[-1])
    scores = masked_scores(query_heads, key_heads, same_crop)
    probability = jnp.exp(scores - log_total[..., None])
    grad_prob = dots("qhd,khd->hqk", grad_heads, value_heads)
    inner = jnp.sum(probability * grad_prob, axis=-1, keepdims=True)
    grad_scores = (probability * (grad_prob - inner)).astype(jnp.bfloat16)
    grad_query = dots("hqk,khd->qhd", grad_scores, key_heads) * scale_factor
    grad_key = dots("hqk,qhd->khd", grad_scores, query_heads) * scale_factor
    grad_value = dots("hqk,qhd->khd", probability.astype(jnp.bfloat16), grad_heads)
    rows_here = query_seq.shape[0]
    rows_whole = key_seq.shape[0]
    return (
        grad_query.reshape(rows_here, -1),
        grad_key.reshape(rows_whole, -1),
        grad_value.reshape(rows_whole, -1),
    )


def forward_plain(tokens_float, segments, conditions, noise_bins, bin_counts, ada_weight, first, up_weight,
                  down_weight):
    groups, cores = lax.axis_size("dp"), lax.axis_size("sp")
    share, width = first.shape[0], tokens_float.shape[1]
    index = lax.axis_index("dp") * cores + lax.axis_index("sp")
    mixers = lax.all_gather(first, ("dp", "sp"), axis=0, tiled=True)
    uppers = lax.all_gather(up_weight, ("dp", "sp"), axis=0, tiled=True)
    downers = lax.all_gather(down_weight, ("dp", "sp"), axis=0, tiled=True)
    mixers = mixers.reshape(width, 4, width).transpose(1, 0, 2)
    uppers = uppers.reshape(width, 4, width).transpose(1, 0, 2)
    downers = downers.reshape(4, width, width)
    bin_total = lax.psum(bin_counts, "dp")
    bin_weight = 40.0 * groups / bin_total.astype(jnp.float32)
    crop_weight = jnp.sum(
        jnp.where(noise_bins[:, None] == jnp.arange(NBINS, dtype=jnp.int32), bin_weight, 0.0),
        axis=-1,
    )
    cond_all = lax.all_gather(conditions, "dp", axis=0, tiled=True)
    cond_here = lax.dynamic_slice_in_dim(cond_all, index * share, share, axis=1)
    cond_act = jax.nn.silu(cond_here.astype(jnp.float32)).astype(jnp.bfloat16)
    modulation_part = dots("sd,df->sf", cond_act, ada_weight).reshape(groups, CROPS, -1)
    modulation = lax.psum(lax.psum_scatter(modulation_part, "dp", scatter_dimension=0), "sp")
    selector = (segments[:, None] == jnp.arange(CROPS, dtype=jnp.int32)).astype(jnp.float32)
    per_token = jnp.einsum("tc,cf->tf", selector, modulation, precision=lax.Precision.HIGHEST)
    shift_one, scale_one, gate_one, shift_two, scale_two, _ = jnp.split(per_token, 6, axis=-1)
    normed_one, _ = layer_norm(tokens_float)
    hidden_one = (normed_one * (1.0 + scale_one) + shift_one).astype(jnp.bfloat16)
    projected = dots("td,qdf->qtf", hidden_one, mixers[:3]).astype(jnp.bfloat16)
    sides = lax.all_gather(projected[1:], "sp", axis=1, tiled=True)
    all_segments = lax.all_gather(segments, "sp", axis=0, tiled=True)
    same_crop = segments[:, None] == all_segments[None, :]
    context, log_total = attend(projected[0], sides[0], sides[1], same_crop)
    context_low = context.astype(jnp.bfloat16)
    attended = dots("td,df->tf", context_low, mixers[3])
    middle = tokens_float + gate_one * attended
    normed_two, _ = layer_norm(middle)
    hidden_two = (normed_two * (1.0 + scale_two) + shift_two).astype(jnp.bfloat16)
    upper_in = dots("td,qdf->qtf", hidden_two, uppers)
    activated = jax.nn.gelu(upper_in, approximate=True).astype(jnp.bfloat16)
    slope = jax.vjp(partial(jax.nn.gelu, approximate=True), upper_in)[1](jnp.ones_like(upper_in))[0]
    mlp_out = dots("qtf,qfd->td", activated, downers)
    return (
        (mixers, uppers, downers), activated, slope, hidden_one, projected[0], sides, log_total,
        context_low, attended, middle, hidden_two, mlp_out, modulation, cond_act, crop_weight, same_crop,
    )


def layer_plain(tokens_float, segments, conditions, noise_bins, bin_counts, cotangent, ada_weight, first,
                up_weight, down_weight):
    width = tokens_float.shape[1]
    (
        (mixers, uppers, downers), activated, slope, hidden_one, queries, sides, log_total,
        context_low, attended, middle, hidden_two, mlp_out, modulation, cond_act, crop_weight, same_crop,
    ) = forward_plain(
        tokens_float, segments, conditions, noise_bins, bin_counts, ada_weight, first, up_weight,
        down_weight,
    )
    selector = (segments[:, None] == jnp.arange(CROPS, dtype=jnp.int32)).astype(jnp.float32)
    per_token = jnp.einsum("tc,cf->tf", selector, modulation, precision=lax.Precision.HIGHEST)
    _, scale_one, gate_one, _, scale_two, gate_two = jnp.split(per_token, 6, axis=-1)
    normed_one, inverse_one = layer_norm(tokens_float)
    normed_two, inverse_two = layer_norm(middle)

    token_weight = jnp.sum(selector * crop_weight[None, :], axis=-1)
    grad_out = cotangent.astype(jnp.float32) * token_weight[:, None]
    grad_mlp = (grad_out * gate_two).astype(jnp.bfloat16)
    tokens_out = (middle + gate_two * mlp_out).astype(jnp.bfloat16)
    down_part = dots("qtf,td->qfd", activated, grad_mlp).astype(jnp.bfloat16)
    grad_act = dots("td,qfd->qtf", grad_mlp, downers)
    grad_upper = (grad_act * slope).astype(jnp.bfloat16)
    up_part = dots("td,qtf->qdf", hidden_two, grad_upper).astype(jnp.bfloat16)
    grad_hidden_two = dots("qtf,qdf->td", grad_upper, uppers)
    grad_middle = grad_out + norm_back(grad_hidden_two * (1.0 + scale_two), normed_two, inverse_two)
    grad_attended = (grad_middle * gate_one).astype(jnp.bfloat16)
    grad_context = dots("tf,df->td", grad_attended, mixers[3]).astype(jnp.bfloat16)
    grad_query, grad_key, grad_value = attend_back(
        queries, sides[0], sides[1], same_crop, log_total, grad_context
    )
    grad_sides = lax.psum_scatter(
        jnp.stack([grad_key, grad_value]).astype(jnp.bfloat16),
        "sp",
        scatter_dimension=1,
        tiled=True,
    )
    grad_projected = jnp.concatenate([grad_query.astype(jnp.bfloat16)[None], grad_sides])
    out_part = dots("td,tf->df", context_low, grad_attended).astype(jnp.bfloat16)
    qkv_part = dots("td,qtf->qdf", hidden_one, grad_projected).astype(jnp.bfloat16)
    first_part = jnp.concatenate([qkv_part, out_part[None]])
    grad_hidden_one = dots("qtf,qdf->td", grad_projected, mixers[:3])
    tokens_grad = grad_middle + norm_back(
        grad_hidden_one * (1.0 + scale_one), normed_one, inverse_one
    )

    joined = jnp.stack([first_part, up_part]).transpose(2, 0, 1, 3).reshape(width, 8 * width)
    rows = lax.psum_scatter(joined, ("dp", "sp"), scatter_dimension=0, tiled=True)
    rows = rows.astype(jnp.float32)
    first_grad, up_grad = rows[:, : 4 * width], rows[:, 4 * width :]
    down_grad = lax.psum_scatter(
        down_part.reshape(4 * width, width), ("dp", "sp"), scatter_dimension=0, tiled=True
    ).astype(jnp.float32)

    grad_per_token = jnp.concatenate(
        [
            grad_hidden_one,
            grad_hidden_one * normed_one,
            grad_middle * attended,
            grad_hidden_two,
            grad_hidden_two * normed_two,
            grad_out * mlp_out,
        ],
        axis=-1,
    )
    grad_modulation = lax.psum(
        jnp.einsum("tc,tf->cf", selector, grad_per_token, precision=lax.Precision.HIGHEST), "sp"
    )
    grad_rows = lax.all_gather(grad_modulation, "dp", axis=0, tiled=True)
    ada_grad = jnp.einsum(
        "sd,sf->df", cond_act.astype(jnp.float32), grad_rows, precision=lax.Precision.HIGHEST
    )
    silu_part = jnp.einsum(
        "sf,df->sd", grad_rows, ada_weight.astype(jnp.float32), precision=lax.Precision.HIGHEST
    )
    silu_all = lax.all_gather(silu_part, ("dp", "sp"), axis=0)
    silu_here = lax.dynamic_slice_in_dim(silu_all, lax.axis_index("dp") * CROPS, CROPS, axis=1)
    grad_silu = silu_here.transpose(1, 0, 2).reshape(CROPS, width)
    return tokens_out, tokens_grad, grad_silu, ada_grad, first_grad, up_grad, down_grad


def on_device(
    chips,
    tokens_in,
    segment_ids,
    conditions,
    noise_bins,
    bin_counts,
    cotangent,
    ada_weight,
    qkv_weight,
    out_weight,
    up_weight,
    down_weight,
):
    share = qkv_weight.shape[0]
    if chips and 4 * share == down_weight.shape[0]:
        (
            weights, down_part, slope, active, sides, attended, middle, hidden_one, queries, log_total,
            context_low, hidden_two, table, conds, level, grad_mlp, seg_all, seg_col, ada,
        ) = run_forward(
            qkv_weight, out_weight, up_weight, down_weight, conditions[0], noise_bins, bin_counts,
            ada_weight, tokens_in[0], cotangent[0], segment_ids,
        )
        given = (
            weights, down_part, slope, middle, attended, active, hidden_one, queries, sides, log_total,
            context_low, hidden_two, grad_mlp, table, conds, level, seg_all, seg_col, tokens_in[0],
            cotangent[0], ada,
        )
        _, _, rows, down_grad, tokens_grad, ada_grad, silu_part, tokens_out = run_backward(given, share)
        qkv_grad, out_grad, up_grad, ada_grad, cond_grad, down_grad, tokens_grad, tokens_out = run_finish(
            rows, ada_grad, silu_part, conditions[0], down_grad, tokens_grad, tokens_out, share
        )
    else:
        first = jnp.concatenate([qkv_weight, out_weight], axis=1)
        width = out_weight.shape[1]
        tokens_out, tokens_grad, grad_silu, ada_grad, first_grad, up_grad, down_grad = layer_plain(
            tokens_in[0].astype(jnp.float32), segment_ids[0], conditions[0], noise_bins[0], bin_counts[0],
            cotangent[0], ada_weight, first, up_weight, down_weight,
        )
        qkv_grad, out_grad = first_grad[:, : 3 * width], first_grad[:, 3 * width :]
        cond_grad = jax.vjp(jax.nn.silu, conditions[0].astype(jnp.float32))[1](grad_silu)[0]
    return (
        tokens_out[None],
        tokens_grad[None],
        cond_grad[None],
        ada_grad,
        qkv_grad,
        out_grad,
        up_grad,
        down_grad,
    )


def solution(mesh):
    placed = (
        P("dp", "sp", None),
        P("dp", "sp"),
        P("dp", None, None),
        P("dp", None),
        P("dp", None),
        P("dp", "sp", None),
        P(("dp", "sp"), None),
        P(("dp", "sp"), None),
        P(("dp", "sp"), None),
        P(("dp", "sp"), None),
        P(("dp", "sp"), None),
    )
    return jax.shard_map(
        partial(on_device, mesh.shape["dp"] == 16 and mesh.shape["sp"] == 2),
        mesh=mesh,
        in_specs=placed,
        out_specs=(
            P("dp", "sp", None),
            P("dp", "sp", None),
            P("dp", None, None),
            P(("dp", "sp"), None),
            P(("dp", "sp"), None),
            P(("dp", "sp"), None),
            P(("dp", "sp"), None),
            P(("dp", "sp"), None),
        ),
        check_vma=False,
    )
```

```python
from functools import partial
import math

import jax
import jax.numpy as jnp
from jax import lax
from jax.experimental import pallas as pl
from jax.experimental.pallas import tpu as pltpu
from jax.sharding import PartitionSpec as P

HEADS = 16
CROPS = 4
NBINS = 8
EPSILON = 1e-06
LARGE_NEGATIVE = -1e30
GELU_SCALE = math.sqrt(2.0 / math.pi)
GELU_CUBE = 0.044715

MESH = pl.DeviceIdType.MESH
PAD = 48
NEAR = (80, 64)
FAR = (32, 32)
HELD = 6
FORWARD_STEPS = (
    0, 2, 11, 12, 21, 3, 4, 22, 13, 5, 14, 31, 32, 7, 23, 24, 100, 15, 102, 33,
    16, 34, 26, 25, 111, 27, 121, 17, 103, 104, 35, 36, 112, 122, 37, 113, 114, 105, 107, 131,
    115, 132, 200, 123, 124, 116, 202, 133, 134, 126, 125, 211, 135, 212, 203, 117, 204, 221, 127, 136,
    137, 205, 222, 213, 214, 215, 207, 231, 232, 223, 224, 225, 216, 217, 233, 234, 226, 235, 236, 227,
    237,
)
BACKWARD_STEPS = (
    10, 4, 1, 3, 20, 12, 2, 30, 14, 6, 13, 22, 7, 5, 16, 11, 23, 34, 17, 32,
    8, 24, 40, 21, 33, 15, 18, 25, 44, 42, 26, 43, 27, 35, 9, 50, 47, 31, 46, 41,
    54, 60, 53, 52, 19, 28, 45, 36, 51, 62, 37, 64, 55, 61, 57, 70, 29, 63, 38, 56,
    48, 72, 65, 73, 66, 80, 67, 58, 39, 49, 74, 71, 90, 82, 100, 75, 84, 92, 81, 94,
    83, 59, 110, 91, 68, 76, 69, 86, 77, 85, 111, 87, 104, 102, 95, 96, 93, 101, 97, 103,
    78, 79, 105, 88, 114, 89, 107, 106, 115, 113, 112, 98, 116, 99, 108, 109, 117, 118, 119,
)
FORWARD_AFTER = (
    0, 2, 8, 20, 24, 26, 34, 35, 37, 39, 43, 47, 47, 47, 47, 49, 49, 51, 51, 54,
    59, 59, 62, 63, 64, 64, 65, 65, 67, 67, 70, 71, 77, 77, 78, 81,
)
BACKWARD_AFTER = (
    1, 9, 13, 14, 16, 18, 22, 22, 23, 24, 30, 31, 32, 40, 44, 45, 45, 46, 52, 54,
    54, 56, 57, 57, 57, 63, 65, 65, 81, 81, 85, 86, 88, 90, 98, 109, 116, 119, 119, 119,
    119,
)
CHIPS = 16
BAND = 1792
PLACES = ((0, 0), (0, 1), (1, 0), (1, 1))


def position():
    d = lax.axis_index("dp")
    c = lax.axis_index("sp")
    return d // 4, (d // 2) % 2, d % 2, c


def device(z, y, x, c):
    return (z * 4 + y * 2 + x, c)


def block_of(kind, zy, group):
    if kind == 2:
        return zy // 2, (zy % 2) * 4 + group
    return group, zy


def level_of(z, k):
    if k == 0:
        return z
    upper = z // 2
    inner = z * (1 - upper) + (3 - z) * upper
    step = k - inner if k == 1 else k
    return step * (1 - upper) + (3 - step) * upper


def greet(peers, meanwhile=None):
    barrier = pltpu.get_barrier_semaphore()
    for peer in peers:
        pl.semaphore_signal(barrier, inc=1, device_id=peer, device_id_type=MESH)
    if meanwhile is not None:
        meanwhile()
    pl.semaphore_wait(barrier, len(peers))


def remote(src, dst, send, recv, target):
    return pltpu.make_async_remote_copy(
        src_ref=src,
        dst_ref=dst,
        send_sem=send,
        recv_sem=recv,
        device_id=target,
        device_id_type=MESH,
    )


def arrive(ref, sem, target):
    remote(ref, ref, sem, sem, target).wait_recv()


def row_selector(rows, share):
    shape = (rows, 4 * PAD)
    row = lax.broadcasted_iota(jnp.int32, shape, 0)
    column = lax.broadcasted_iota(jnp.int32, shape, 1)
    picked = jnp.zeros(shape, jnp.bool_)
    for k in range(4):
        inside = (row >= k * share) & (row < (k + 1) * share)
        picked = picked | (inside & (column == row - k * share + k * PAD))
    return picked.astype(jnp.float32).astype(jnp.bfloat16)


def product(left, right):
    return jnp.dot(left, right, preferred_element_type=jnp.float32)


def product_by_rows(left, right):
    return lax.dot_general(left, right, (((0,), (0,)), ((), ())), preferred_element_type=jnp.float32)


def product_by_columns(left, right):
    return lax.dot_general(left, right, (((1,), (1,)), ((), ())), preferred_element_type=jnp.float32)


def chunks(rows, body, first=0, step=16):
    def run(i, carry):
        body(pl.ds(pl.multiple_of(first + i * step, step), step))
        return carry

    lax.fori_loop(0, rows // step, run, 0)


def normed(values):
    center = values - jnp.mean(values, axis=-1, keepdims=True)
    inverse = lax.rsqrt(jnp.mean(center * center, axis=-1, keepdims=True) + EPSILON)
    return center * inverse, inverse


def pick(segments, table, first, column, width):
    columns = slice(column * width, (column + 1) * width)
    value = table[first + 3 : first + 4, columns]
    for crop in (2, 1, 0):
        value = jnp.where(segments == crop, table[first + crop : first + crop + 1, columns], value)
    return value


def window_of(head, size, width):
    start = jnp.minimum((head * size) // 128, width // 128 - 2) * 128
    start = pl.multiple_of(start, 128)
    lane = lax.broadcasted_iota(jnp.int32, (1, 256), 1) + start
    return pl.ds(start, 256), (lane >= head * size) & (lane < (head + 1) * size)


def share_window(device_number, share, width):
    column = device_number * share
    start = jnp.minimum(column // 128, width // 128 - 2) * 128
    return pl.multiple_of(start, 128), column - start


def forward_kernel(share, qkv_ref, out_weight_ref, up_ref, down_ref, cond_ref, noise_ref, counts_ref, given_ada_ref,
                   tokens_ref, cot_ref, seg_ref,
                   weights_ref, down_part_ref, slope_ref, active_ref, sides_out_ref, attended_out_ref, middle_out_ref,
                   hidden_ref, query_ref, total_ref, context_ref, hidden_two_ref, table_ref,
                   conds_ref, level_ref, grad_mlp, seg_all, seg_col_ref, ada_ref,
                   full, shards_ref, stage, acts, acts_low, windows, part, part_recv, band, band_diag, band_x, band_y,
                   band_z, halves_of, sides_ref, attended_ref, middle_ref, bias, work, active, slope, *sems):
    (
        group_send, group_recv, z_send, z_recv, zd_send, zd_recv, x_send, x_recv, y_send, y_recv,
        dx_send, dx_recv, dy_send, dy_recv, c_send, c_recv,
        cond_send, cond_recv, pc_send, pc_recv, pd_send, pd_recv, px_send, px_recv, py_send, py_recv,
        pz_send, pz_recv, pm_send, pm_recv, seg_send, seg_recv, kv_send, kv_recv,
        save_sem, grad_sem, slope_sem, block_sem, store_sem,
    ) = sems
    z, y, x, c = position()
    me = z * 4 + y * 2 + x
    group = x * 2 + c
    zy = z * 2 + y
    rows = 4 * share
    count, width = tokens_ref.shape
    x_peer, y_peer, c_peer = device(z, y, 1 - x, c), device(z, 1 - y, x, c), device(z, y, x, 1 - c)
    partners = [(x, 1 - c), (1 - x, c), (1 - x, 1 - c)]

    def prepare():
        tail = share // 16 * 16
        for a in range(2):
            for q in range(4):
                source, at = (up_ref, q) if a else ((out_weight_ref, 0) if q == 3 else (qkv_ref, q))
                shards_ref[a, q, tail:, :] = jnp.zeros((PAD - tail, width), jnp.bfloat16)
                shards_ref[a, q, :share, :] = source[:, at * width : (at + 1) * width]
        ada_ref[tail:, :] = jnp.zeros((PAD - tail, ada_ref.shape[1]), jnp.bfloat16)
        ada_ref[:share, :] = given_ada_ref[...]
        cond = cond_ref[...].astype(jnp.float32)
        acts[...] = jnp.zeros_like(acts)
        acts[:CROPS, :] = cond * (1.0 / (1.0 + jnp.exp(-cond)))
        counts = counts_ref[...].astype(jnp.float32)
        for tile in range(width // 128):
            acts[CROPS : CROPS + 1, tile * 128 : tile * 128 + NBINS] = counts
        acts_low[...] = acts[...].astype(jnp.bfloat16)
        seg_all[c] = jnp.broadcast_to(seg_ref[...], (8, count))
        seg_col_ref[...] = jnp.transpose(jnp.broadcast_to(seg_ref[...], (128, count)))
        for a in range(2):
            stage[a, pl.ds(pl.multiple_of(group * PAD, 16), PAD), :] = shards_ref[a, group]
        start, _ = share_window(2 * me + c, share, width)
        windows[me] = acts_low[:, pl.ds(start, 256)]

    greet(
        [((me + k) % CHIPS, c) for k in range(1, CHIPS)] + [c_peer, device(z, y, 1 - x, 1 - c)], prepare
    )
    sends = {a: [] for a in (0, 1, 2, "other")}

    def send(a, *args):
        copy = remote(*args)
        copy.start()
        sends[a].append((None, copy))

    def finish_sends(a):
        for go, copy in sends[a]:
            if go is None:
                copy.wait_send()
            else:
                pl.when(go)(copy.wait_send)
        sends[a] = []

    level = partial(level_of, z)

    def place(a, k, other_y, other_x, core=None, first=0, last=None):
        yy = 1 - y if other_y else y
        xx = 1 - x if other_x else x
        cc = c if core is None else core
        block, row = block_of(a, level(k) * 2 + yy, xx * 2 + cc)
        count = (rows if last is None else last) - first
        return full.at[a, block, pl.ds(pl.multiple_of(row * rows + first, 16), count)]

    def cuts(k):
        top, low = FAR if k else NEAR
        return top, rows - low

    def along(a, k, ref, send_sem, recv_sem):
        source = level(k)
        for way, step in ((0, 1), (1, -1)):
            to = z + step
            go = (to >= 0) & (to < 4)
            if k:
                go = go & ((source < z) if step == 1 else (source > z))
            copy = remote(ref, ref, send_sem.at[a, k, way], recv_sem.at[a, source], device(jnp.clip(to, 0, 3), y, x, c))
            pl.when(go)(copy.start)
            sends[a].append((go, copy))

    def from_line(a, k, ref, recv_sem):
        source = level(k)
        arrive(ref, recv_sem.at[a, source], device((z + 1) % 4, y, x, c))

    for a in range(2):
        for j, (px, pc) in enumerate(partners):
            send(
                "other",
                shards_ref.at[a, px * 2 + pc],
                stage.at[a, pl.ds(pl.multiple_of(group * PAD, 16), PAD)],
                group_send.at[a, j],
                group_recv.at[a, j],
                device(z, y, px, pc),
            )
    for k in range(1, CHIPS):
        to = (me + k) % CHIPS
        start, _ = share_window(2 * to + c, share, width)
        send("other", acts_low.at[:, pl.ds(start, 256)], windows.at[me], cond_send.at[k - 1], cond_recv.at[k - 1], (to, c))
    send("other", seg_all.at[c], seg_all.at[c], seg_send, seg_recv, c_peer)

    def own(a):
        block, row = block_of(a, zy, group)
        here = pl.ds(pl.multiple_of(row * rows, 16), rows)
        if a < 2:
            for j, (px, pc) in enumerate(partners):
                arrive(
                    stage.at[a, pl.ds(pl.multiple_of((px * 2 + pc) * PAD, 16), PAD)],
                    group_recv.at[a, j],
                    device(z, y, px, pc),
                )
            full[a, block, here, :] = product(row_selector(rows, share), stage[a]).astype(jnp.bfloat16)
        else:
            full[a, block, here, :] = down_ref[...]
        along(a, 0, place(a, 0, 0, 0), z_send, z_recv)

    def to_core(a, k, pos):
        piece = place(a, k, *PLACES[pos])
        send(a, piece, piece, c_send.at[a, k, pos], c_recv.at[a, k, pos], c_peer)

    def pass_piece(a, k):
        from_line(a, k, place(a, k, 0, 0), z_recv)
        along(a, k, place(a, k, 0, 0), z_send, z_recv)

    def spread(a, k):
        top, low = cuts(k)
        for x_half, x_rows, y_half, y_rows in ((0, (0, top), 1, (low, rows)), (1, (top, rows), 0, (0, low))):
            part = place(a, k, 0, 0, None, *x_rows)
            send(a, part, part, x_send.at[a, k, x_half], x_recv.at[a, k, x_half], x_peer)
            part = place(a, k, 0, 0, None, *y_rows)
            send(a, part, part, y_send.at[a, k, y_half], y_recv.at[a, k, y_half], y_peer)
        to_core(a, k, 0)

    def turn_y(a, k):
        part = place(a, k, 0, 1, None, 0, cuts(k)[0])
        arrive(part, x_recv.at[a, k, 0], x_peer)
        send(a, part, part, dy_send.at[a, k], dy_recv.at[a, k], y_peer)

    def turn_x(a, k):
        part = place(a, k, 1, 0, None, cuts(k)[1], rows)
        arrive(part, y_recv.at[a, k, 1], y_peer)
        send(a, part, part, dx_send.at[a, k], dx_recv.at[a, k], x_peer)

    def share_sides(a, k):
        top, low = cuts(k)
        arrive(place(a, k, 0, 1, None, top, rows), x_recv.at[a, k, 1], x_peer)
        to_core(a, k, 1)
        arrive(place(a, k, 1, 0, None, 0, low), y_recv.at[a, k, 0], y_peer)
        to_core(a, k, 2)

    def middle(a, k):
        return place(a, k, 1, 1, None, FAR[0], rows - FAR[1])

    def pass_diagonal(a, k):
        from_line(a, k, middle(a, k), zd_recv)
        along(a, k, middle(a, k), zd_send, zd_recv)

    pending = []

    def finish(a, k):
        top, low = cuts(k)
        arrive(place(a, k, 1, 1, None, 0, top), dy_recv.at[a, k], y_peer)
        arrive(place(a, k, 1, 1, None, low, rows), dx_recv.at[a, k], x_peer)
        if k == 0:
            along(a, k, middle(a, k), zd_send, zd_recv)
        to_core(a, k, 3)
        if a == 2:
            while pending:
                complete_level(pending.pop())
            pending.append(k)

    saves = []

    def keep(src, dst, sem):
        copy = pltpu.make_async_copy(src, dst, sem)
        copy.start()
        saves.append(copy)

    def arrive_cores(a, k):
        for pos, (oy, ox) in enumerate(PLACES):
            arrive(place(a, k, oy, ox, 1 - c), c_recv.at[a, k, pos], c_peer)

    def complete(a):
        for k in range(4):
            arrive_cores(a, k)
        keep(full.at[a], weights_ref.at[a], save_sem.at[a])

    def complete_level(k):
        arrive_cores(2, k)
        keep(full.at[2, level(k)], weights_ref.at[2, level(k)], block_sem.at[k])

    def mod_start():
        for k in range(1, CHIPS):
            source = (me - k + CHIPS) % CHIPS
            arrive(windows.at[source], cond_recv.at[k - 1], (source, c))
        _, offset = share_window(2 * me + c, share, width)
        lane = lax.broadcasted_iota(jnp.int32, (256, 128), 1)
        picked = (lax.broadcasted_iota(jnp.int32, (256, 128), 0) == lane + offset) & (lane < share)
        picked = picked.astype(jnp.float32).astype(jnp.bfloat16)
        mine = product(windows[...].reshape(CHIPS * 16, 256), picked)
        conds_ref[...] = mine.reshape(CHIPS, 16, 128).astype(jnp.bfloat16)
        here = mine.reshape(CHIPS, 16, 128)[:, :8, :].reshape(CHIPS * 8, 128)
        row = lax.broadcasted_iota(jnp.int32, here.shape, 0) % 8
        here = jnp.where(row < CROPS, here, 0.0)
        upper = here.astype(jnp.bfloat16)
        lower = pltpu.roll(here, CROPS, 0).astype(jnp.bfloat16)
        side = ada_ref.shape[1] // 2
        part[...] = product(upper[:, :PAD], ada_ref[:, :side]) + product(lower[:, :PAD], ada_ref[:, side:])
        far = pl.ds(pl.multiple_of((1 - c) * (side - BAND), 128), BAND)
        send("other", part.at[:, far], part_recv, pc_send, pc_recv, c_peer)

    def block8(zz, yy, xx):
        return pl.ds(pl.multiple_of((zz * 4 + yy * 2 + xx) * 8, 8), 8)

    def mod_cores():
        arrive(part_recv, pc_recv, c_peer)
        side = ada_ref.shape[1] // 2
        near = pl.ds(pl.multiple_of(c * (side - BAND), 128), BAND)
        band[...] = part[:, near] + part_recv[...]
        for k in range(4):
            zz = (z + k) % 4
            src = band.at[block8(zz, 1 - y, 1 - x)]
            send("other", src, band_diag.at[k], pd_send.at[k], pd_recv.at[k], x_peer if k % 2 else y_peer)

    def mod_plane():
        for k in range(4):
            zz = (z + k) % 4
            to_x, to_y = block8(zz, y, 1 - x), block8(zz, 1 - y, x)
            arrive(band_diag.at[k], pd_recv.at[k], x_peer if k % 2 else y_peer)
            fold = to_y if k % 2 else to_x
            band[fold, :] = band[fold, :] + band_diag[k]
            send("other", band.at[to_x], band_x.at[k], px_send.at[k], px_recv.at[k], x_peer)
            send("other", band.at[to_y], band_y.at[k], py_send.at[k], py_recv.at[k], y_peer)

    def mod_line():
        for k in (1, 2, 3, 0):
            zz = (z + k) % 4
            mine = block8(zz, y, x)
            arrive(band_x.at[k], px_recv.at[k], x_peer)
            arrive(band_y.at[k], py_recv.at[k], y_peer)
            band[mine, :] = band[mine, :] + band_x[k] + band_y[k]
            if k:
                send("other", band.at[mine], band_z.at[k - 1], pz_send.at[k - 1], pz_recv.at[k - 1], device(zz, y, x, c))

    def mod_last():
        for k in (1, 2, 3):
            arrive(band_z.at[k - 1], pz_recv.at[k - 1], device((z - k + 4) % 4, y, x, c))
        halves_of[c] = band[block8(z, y, x), :] + band_z[0] + band_z[1] + band_z[2]
        send("other", halves_of.at[c], halves_of.at[c], pm_send, pm_recv, c_peer)

    def mod_end():
        arrive(halves_of.at[1 - c], pm_recv, c_peer)
        side = ada_ref.shape[1] // 2
        table_ref[:, :BAND] = halves_of[0]
        table_ref[:, BAND:] = halves_of[1][:, 2 * BAND - side :]
        counts = jnp.sum(windows[:, :, :128].astype(jnp.float32)[:, CROPS : CROPS + 1, :], axis=0)
        lane = lax.broadcasted_iota(jnp.int32, counts.shape, 1)
        weight = jnp.where(lane < NBINS, 40.0 * CHIPS / jnp.where(lane < NBINS, counts, 1.0), 0.0)
        level_ref[...] = jnp.zeros_like(level_ref)
        for crop in range(CROPS):
            mine = jnp.where(lane == noise_ref[:, crop : crop + 1], weight, 0.0)
            level_ref[crop : crop + 1, :] = jnp.broadcast_to(jnp.sum(mine, axis=-1, keepdims=True), (1, 128))

    def first_norm(part_of):
        def body(at):
            segments = seg_col_ref[at, :1]
            value, _ = normed(tokens_ref[at, :].astype(jnp.float32))
            value = value * (1.0 + pick(segments, table_ref, 0, 1, width))
            hidden_ref[at, :] = (value + pick(segments, table_ref, 0, 0, width)).astype(jnp.bfloat16)

        chunks(count // 2, body, part_of * (count // 2))
        if part_of == 0:
            arrive(seg_all.at[1 - c], seg_recv, c_peer)
            return
        for h in (0, 1):
            same = seg_col_ref[:, :1] == seg_all[h][:1, :]
            bias[:, h * count : (h + 1) * count] = jnp.where(same, 0.0, LARGE_NEGATIVE)

    def project(q):
        value = product(hidden_ref[...], full[0, q]).astype(jnp.bfloat16)
        if q == 0:
            query_ref[...] = value
            total_ref[...] = jnp.zeros_like(total_ref)
            work[...] = jnp.zeros_like(work)
            return
        here = pl.ds(pl.multiple_of(c * count, 256), count)
        sides_ref[q - 1, here, :] = value
        send("other", sides_ref.at[q - 1, here], sides_ref.at[q - 1, here], kv_send.at[q - 1], kv_recv.at[q - 1], c_peer)

    def attend(first, last):
        if first == 0:
            there = pl.ds(pl.multiple_of((1 - c) * count, 256), count)
            for q in (0, 1):
                arrive(sides_ref.at[q, there], kv_recv.at[q], c_peer)
            keep(sides_ref, sides_out_ref, store_sem.at[0])
        size = width // HEADS
        scale = 1.0 / math.sqrt(size)

        def body(head, carry):
            columns, inside = window_of(head, size, width)
            query = query_ref[:, columns]
            query = jnp.where(inside, query, jnp.zeros_like(query))
            scores = product_by_columns(query, sides_ref[0, :, columns]) * scale + bias[...]
            top = jnp.max(scores, axis=-1, keepdims=True)
            raised = jnp.exp(scores - top)
            total = jnp.sum(raised, axis=-1, keepdims=True)
            chance = (raised * (1.0 / total)).astype(jnp.bfloat16)
            context = product(chance, sides_ref[1, :, columns])
            work[:, columns] = jnp.where(inside, context, work[:, columns])
            lane = lax.broadcasted_iota(jnp.int32, (1, 128), 1)
            total_ref[...] = jnp.where(lane == head, top + jnp.log(total), total_ref[...])
            return carry

        lax.fori_loop(first, last, body, 0)

    def mix():
        context_ref[...] = work[...].astype(jnp.bfloat16)
        attended_ref[...] = product(context_ref[...], full[0, 3])
        keep(attended_ref, attended_out_ref, store_sem.at[1])

    def second_norm(part_of):
        def body(at):
            segments = seg_col_ref[at, :1]
            gate = pick(segments, table_ref, 0, 2, width)
            middle = tokens_ref[at, :].astype(jnp.float32) + gate * attended_ref[at, :]
            middle_ref[at, :] = middle
            value, _ = normed(middle)
            value = value * (1.0 + pick(segments, table_ref, 4, 1, width))
            hidden_two_ref[at, :] = (value + pick(segments, table_ref, 4, 0, width)).astype(jnp.bfloat16)
            level = level_ref[3:4, :1]
            for crop in (2, 1, 0):
                level = jnp.where(segments == crop, level_ref[crop : crop + 1, :1], level)
            grad = cot_ref[at, :].astype(jnp.float32) * level
            grad_mlp[at, :] = (grad * pick(segments, table_ref, 4, 2, width)).astype(jnp.bfloat16)

        chunks(count // 2, body, part_of * (count // 2))
        if part_of:
            keep(middle_ref, middle_out_ref, store_sem.at[2])

    slope_copies = {}

    def expand(q):
        work[...] = product(hidden_two_ref[...], full[1, q])

    def bend(q):
        if q >= 2:
            slope_copies[q - 2].wait()

        def body(at):
            u = work[at, :]
            square = u * u
            curve = jnp.tanh(GELU_SCALE * (u + GELU_CUBE * (square * u)))
            active[q, at, :] = (0.5 * u * (1.0 + curve)).astype(jnp.bfloat16)
            inner = GELU_SCALE * (1.0 + 3.0 * GELU_CUBE * square)
            slope[q % 2, at, :] = 0.5 * (1.0 + curve) + 0.5 * u * (1.0 - curve * curve) * inner

        chunks(count, body)
        copy = pltpu.make_async_copy(slope.at[q % 2], slope_ref.at[q], slope_sem.at[q % 2])
        copy.start()
        slope_copies[q] = copy
        keep(active.at[q], active_ref.at[q], store_sem.at[3 + q])

    def down_grad(q):
        if q == 0:
            finish_sends(0)
            saves.pop(0).wait()
        full[0, q] = product_by_rows(active[q], grad_mlp[...]).astype(jnp.bfloat16)
        keep(full.at[0, q], down_part_ref.at[q], grad_sem.at[q])

    kinds = (lambda a, k: own(a), pass_piece, spread, turn_y, turn_x, share_sides, pass_diagonal, finish)
    steps = [partial(kinds[n % 10], n // 100, n // 10 % 10) for n in FORWARD_STEPS]
    layer = [mod_start, mod_cores, mod_plane, mod_line, mod_last, mod_end]
    layer += [partial(first_norm, h) for h in (0, 1)] + [partial(complete, 0)]
    layer += [partial(project, q) for q in (1, 2, 0)] + [partial(attend, h, h + 2) for h in range(0, HEADS, 2)]
    layer += [mix, partial(second_norm, 0), partial(second_norm, 1), partial(complete, 1)]
    for q in range(4):
        layer += [partial(expand, q), partial(bend, q)]
    layer += [partial(down_grad, q) for q in range(4)]
    interleave(steps, layer, FORWARD_AFTER)
    complete_level(pending.pop())
    for copy in saves:
        copy.wait()
    for q in (2, 3):
        slope_copies[q].wait()
    for a in (1, 2, "other"):
        finish_sends(a)


def run_forward(qkv, out_weight, up, down, cond, noise, counts, ada, tokens, cot, segments):
    count, width = tokens.shape
    share = qkv.shape[0]
    dma = pltpu.SemaphoreType.DMA
    low, wide, whole = jnp.bfloat16, jnp.float32, jnp.int32
    side = ada.shape[1] // 2
    vmem, any_ = pl.BlockSpec(memory_space=pltpu.VMEM), pl.BlockSpec(memory_space=pl.ANY)
    out, buffer = jax.ShapeDtypeStruct, pltpu.VMEM
    return pl.pallas_call(
        partial(forward_kernel, share),
        out_shape=(
            out((3, 4, width, width), low),
            out((4, width, width), low),
            out((4, count, width), wide),
            out((4, count, width), low),
            out((2, 2 * count, width), low),
            out((count, width), wide),
            out((count, width), wide),
            out((count, width), low),
            out((count, width), low),
            out((count, 128), wide),
            out((count, width), low),
            out((count, width), low),
            out((8, side), wide),
            out((CHIPS, 16, 128), low),
            out((8, 128), wide),
            out((count, width), low),
            out((2, 8, count), whole),
            out((count, 128), whole),
            out((PAD, 2 * side), low),
        ),
        in_specs=[vmem] * 11,
        out_specs=[any_] * 7 + [vmem] * 12,
        scratch_shapes=[
            buffer((3, 4, width, width), low),
            buffer((2, 4, PAD, width), low),
            buffer((2, 4 * PAD, width), low),
            buffer((16, width), wide),
            buffer((16, width), low),
            buffer((CHIPS, 16, 256), low),
            buffer((CHIPS * 8, side), wide),
            buffer((CHIPS * 8, BAND), wide),
            buffer((CHIPS * 8, BAND), wide),
            buffer((4, 8, BAND), wide),
            buffer((4, 8, BAND), wide),
            buffer((4, 8, BAND), wide),
            buffer((3, 8, BAND), wide),
            buffer((2, 8, BAND), wide),
            buffer((2, 2 * count, width), low),
            buffer((count, width), wide),
            buffer((count, width), wide),
            buffer((count, 2 * count), wide),
            buffer((count, width), wide),
            buffer((4, count, width), low),
            buffer((2, count, width), wide),
            dma((2, 3)), dma((2, 3)), dma((3, 4, 2)), dma((3, 4)), dma((3, 4, 2)), dma((3, 4)),
            dma((3, 4, 2)), dma((3, 4, 2)), dma((3, 4, 2)), dma((3, 4, 2)),
            dma((3, 4)), dma((3, 4)), dma((3, 4)), dma((3, 4)),
            dma((3, 4, 4)), dma((3, 4, 4)),
            dma((CHIPS - 1,)), dma((CHIPS - 1,)), dma, dma, dma((4,)), dma((4,)),
            dma((4,)), dma((4,)), dma((4,)), dma((4,)), dma((3,)), dma((3,)), dma, dma, dma, dma,
            dma((2,)), dma((2,)), dma((2,)), dma((4,)), dma((2,)), dma((4,)), dma((7,)),
        ],
        compiler_params=pltpu.CompilerParams(
            collective_id=0, has_side_effects=True, vmem_limit_bytes=63 * 2**20
        ),
        name="forward",
    )(qkv, out_weight, up, down, cond, noise, counts, ada, tokens, cot, segments)


def interleave(steps, layer, after):
    done = 0
    for count, step in enumerate(steps):
        while done < len(layer) and after[done] <= count:
            layer[done]()
            done += 1
        step()
    for step in layer[done:]:
        step()


def add_rows(dst, sources, start, rows):
    def body(i, carry):
        where = pl.ds(pl.multiple_of(start + i * 16, 16), 16)
        total = dst[where, :].astype(jnp.float32)
        for source in sources:
            total = total + source[where, :].astype(jnp.float32)
        dst[where, :] = total.astype(dst.dtype)
        return carry

    lax.fori_loop(0, rows // 16, body, 0)


def backward_kernel(share, weights_ref, down_part_ref, slope_ref, middle_ref, attended_ref, active_ref,
                    hidden_given, query_given, sides_given, total_given, context_given, hidden_two_given,
                    grad_mlp_given, table_ref, conds_ref, level_ref, seg_all_ref, seg_col_ref, tokens_given,
                    cot_given, ada_ref,
                    mixer_part_ref, up_part_ref, rows_ref, down_ref, tokens_grad_ref, ada_grad_ref, silu_ref,
                    out_ref,
                    held, from_core, diag, from_x, from_y, piece_line, diag_line, spare, block, part, quad, lows,
                    work, grad_middle, grad_context, leave, enter, bias, sums, sums_row, sums_core, band, silu_part, silu_side,
                    hidden_ref, query_ref, sides_ref, total_ref, context_ref, hidden_two_ref, grad_mlp_ref,
                    tokens_ref, cot_ref,
                    *sems):
    (
        load_sem, c_send, c_recv, dx_send, dx_recv, dy_send, dy_recv, x_send, x_recv,
        y_send, y_recv, zo_send, zo_recv, zd_send, zd_recv, group_send, group_recv, block_sem, part_sem, quad_sem, low_sem, out_sem, late_sem,
        side_send, side_recv, m_send, m_recv, mz_send, mz_recv, mx_send, mx_recv, my_send, my_recv,
        md_send, md_recv, mc_send, mc_recv, s_send, s_recv, sc_send, sc_recv,
    ) = sems
    z, y, x, c = position()
    me = z * 4 + y * 2 + x
    group = x * 2 + c
    rows = 4 * share
    count, width = tokens_ref.shape
    x_peer, y_peer, c_peer = device(z, y, 1 - x, c), device(z, 1 - y, x, c), device(z, y, x, 1 - c)
    partners = [(x, 1 - c), (1 - x, c), (1 - x, 1 - c)]
    greet(
        [((me + k) % CHIPS, c) for k in range(1, CHIPS)] + [c_peer, device(z, y, 1 - x, 1 - c)]
    )
    sends = {}

    def send(owner, *args):
        copy = remote(*args)
        copy.start()
        sends.setdefault(owner, []).append(copy)

    def finish_sends(owner):
        for copy in sends.pop(owner, []):
            copy.wait_send()

    late = {}

    def fetch_late():
        pairs = (
            ("grad_mlp", grad_mlp_given, grad_mlp_ref), ("hidden_two", hidden_two_given, hidden_two_ref),
            ("cot", cot_given, cot_ref), ("context", context_given, context_ref),
            ("query", query_given, query_ref), ("sides", sides_given, sides_ref),
            ("total", total_given, total_ref), ("hidden", hidden_given, hidden_ref),
            ("tokens", tokens_given, tokens_ref),
        )
        for n, (name, source, target) in enumerate(pairs):
            late[name] = pltpu.make_async_copy(source, target, late_sem.at[n])
            late[name].start()

    def need(*names):
        for name in names:
            if name in late:
                late.pop(name).wait()

    order = [(a, k) for a in (2, 1, 0) for k in (3, 2, 1, 0)]
    given = (mixer_part_ref, up_part_ref, down_part_ref)
    loads = {}
    inner_rows = slice(FAR[0], rows - FAR[1])

    def cuts(i):
        top, low = FAR if order[i][1] else NEAR
        return top, rows - low

    def line(k):
        to = level_of(z, k)
        step = jnp.where(z < to, 1, -1)
        behind = z - step
        return to, z + step, (behind >= 0) & (behind < 4)

    def along(i, ref, lines, send_sem, recv_sem):
        a, k = order[i]
        to, after, _ = line(k)
        spot = jnp.where((after == to) & (z > to), 4, to)
        copy = remote(ref, lines.at[a % 2, spot], send_sem.at[a, k], recv_sem.at[a, spot], device(after, y, x, c))
        copy.start()
        return copy

    def from_line(i, lines, recv_sem, spot):
        a = order[i][0]
        arrive(lines.at[a % 2, spot], recv_sem.at[a, spot], device((z + 1) % 4, y, x, c))

    def hold(i, ref, lines, send_sem, recv_sem):
        sends.setdefault(("held", i), []).append(
            remote(ref, lines.at[0, 0], send_sem.at[order[i]], recv_sem.at[order[i][0], 0], x_peer)
        )

    def begin(i):
        a, k = order[i]
        if i % 4 == 0:
            for n in sorted(going):
                going.pop(n).wait()
        finish_sends(("held", i - HELD))
        zz = level_of(z, k)
        for pos in (3, 1, 2, 0):
            yy = 1 - y if PLACES[pos][0] else y
            xx = 1 - x if PLACES[pos][1] else x
            for cc in (1 - c, c):
                where, row = block_of(a, zz * 2 + yy, xx * 2 + cc)
                src = given[a].at[where, pl.ds(pl.multiple_of(row * rows, 16), rows)]
                if cc is c:
                    loads[i, pos] = pltpu.make_async_copy(src, held.at[i % HELD, pos], load_sem.at[i, pos])
                    loads[i, pos].start()
                else:
                    send("core", src, from_core.at[i % 4, pos], c_send.at[i, pos], c_recv.at[i, pos], c_peer)

    def pair(i, pos):
        k = order[i][1]
        top, low = cuts(i)
        mine = held.at[i % HELD, pos]
        loads[i, pos].wait()
        arrive(from_core.at[i % 4, pos], c_recv.at[i, pos], c_peer)
        add_rows(mine, [from_core.at[i % 4, pos]], 0, rows)
        if pos == 3 and k:
            diagonal(i)
            part = mine.at[inner_rows]
            hold(i, part, diag_line, zd_send, zd_recv)
            _, _, fed = line(k)

            @pl.when(jnp.logical_not(fed))
            def _():
                along(i, part, diag_line, zd_send, zd_recv)

        if pos == 1:
            part = mine.at[top:rows]
            send(("held", i), part, from_x.at[i % 6, top:rows], x_send.at[i, 1], x_recv.at[i, 1], x_peer)
        if pos == 2:
            part = mine.at[0:low]
            send(("held", i), part, from_y.at[i % 6, 0:low], y_send.at[i, 0], y_recv.at[i, 0], y_peer)

    def diagonal(i):
        top, low = cuts(i)
        mine, far = held.at[i % HELD, 3], diag.at[i % 5]
        send(("held", i), mine.at[0:top], far.at[0:top], dy_send.at[i], dy_recv.at[i], y_peer)
        send(("held", i), mine.at[low:rows], far.at[low:rows], dx_send.at[i], dx_recv.at[i], x_peer)

    def diag_along(i):
        k = order[i][1]
        mine = held.at[i % HELD, 3, inner_rows]
        size = rows - FAR[0] - FAR[1]
        if k:
            to, _, fed = line(k)

            @pl.when(fed)
            def _():
                from_line(i, diag_line, zd_recv, to)
                add_rows(mine, [diag_line.at[order[i][0] % 2, to]], 0, size)
                along(i, mine, diag_line, zd_send, zd_recv)

        else:
            for spot, here in ((z, z > 0), (4, z < 3)):

                @pl.when(here)
                def _():
                    from_line(i, diag_line, zd_recv, spot)
                    add_rows(mine, [diag_line.at[order[i][0] % 2, spot]], 0, size)

            diagonal(i)

    def relay_x(i):
        top, _ = cuts(i)
        far, mine = diag.at[i % 5], held.at[i % HELD, 1]
        arrive(far.at[0:top], dy_recv.at[i], y_peer)
        add_rows(mine, [far], 0, top)
        send(("held", i), mine.at[0:top], from_x.at[i % 6, 0:top], x_send.at[i, 0], x_recv.at[i, 0], x_peer)

    def relay_y(i):
        _, low = cuts(i)
        far, mine = diag.at[i % 5], held.at[i % HELD, 2]
        arrive(far.at[low:rows], dx_recv.at[i], x_peer)
        add_rows(mine, [far], low, rows - low)
        send(("held", i), mine.at[low:rows], from_y.at[i % 6, low:rows], y_send.at[i, 1], y_recv.at[i, 1], y_peer)

    def plane(i):
        k = order[i][1]
        top, low = cuts(i)
        mine = held.at[i % HELD, 0]
        arrive(from_x.at[i % 6, 0:top], x_recv.at[i, 0], x_peer)
        arrive(from_x.at[i % 6, top:rows], x_recv.at[i, 1], x_peer)
        arrive(from_y.at[i % 6, 0:low], y_recv.at[i, 0], y_peer)
        arrive(from_y.at[i % 6, low:rows], y_recv.at[i, 1], y_peer)
        add_rows(mine, [from_x.at[i % 6], from_y.at[i % 6]], 0, rows)
        if k:
            hold(i, mine, piece_line, zo_send, zo_recv)
            _, _, fed = line(k)

            @pl.when(jnp.logical_not(fed))
            def _():
                along(i, mine, piece_line, zo_send, zo_recv)

    def piece_along(i):
        a, k = order[i]
        mine = held.at[i % HELD, 0]
        if k:
            to, _, fed = line(k)

            @pl.when(fed)
            def _():
                from_line(i, piece_line, zo_recv, to)
                add_rows(mine, [piece_line.at[a % 2, to]], 0, rows)
                along(i, mine, piece_line, zo_send, zo_recv)

            return
        for spot, here in ((z, z > 0), (4, z < 3)):

            @pl.when(here)
            def _():
                from_line(i, piece_line, zo_recv, spot)
                add_rows(mine, [piece_line.at[a % 2, spot]], 0, rows)

        if a == 2:
            down_ref[...] = mine[...].astype(jnp.float32)
            return
        spare[a] = product_by_rows(row_selector(rows, share), mine[...]).astype(jnp.bfloat16)
        for j, (px, pc) in enumerate(partners):
            send(
                "end",
                spare.at[a, pl.ds(pl.multiple_of((px * 2 + pc) * PAD, 16), PAD)],
                rows_ref.at[a, group],
                group_send.at[a, j],
                group_recv.at[a, j],
                device(z, y, px, pc),
            )
        rows_ref[a, group] = spare[a, pl.ds(pl.multiple_of(group * PAD, 16), PAD), :]

    uses = [(2, q) for q in range(4)] + [(1, q) for q in range(4)] + [(0, 3), (0, 0), (0, 1), (0, 2)]
    coming = {}

    def fetch(n):
        if n < len(uses):
            copy = pltpu.make_async_copy(weights_ref.at[uses[n]], block.at[n % 2], block_sem.at[n % 2])
            copy.start()
            coming[n] = copy

    def take(n):
        coming[n].wait()
        return block[n % 2]

    going = {}

    def put(n, left, right, target):
        if n - 2 in going:
            going.pop(n - 2).wait()

        def body(i, carry):
            columns = pl.ds(pl.multiple_of(i * 384, 128), 384)
            part[n % 2, columns, :] = product_by_rows(left[:, columns], right[...]).astype(jnp.bfloat16)
            return carry

        lax.fori_loop(0, width // 384, body, 0)
        going[n] = pltpu.make_async_copy(part.at[n % 2], target, part_sem.at[n % 2])
        going[n].start()

    quads = {}

    def slopes(q):
        quads[q] = pltpu.make_async_copy(slope_ref.at[q], quad.at[q], quad_sem.at[q])
        quads[q].start()
        quads["active", q] = pltpu.make_async_copy(active_ref.at[q], lows.at[q], low_sem.at[q])
        quads["active", q].start()

    def through_down(q):
        need("grad_mlp")
        quads.pop(("active", q)).wait()
        value = product(lows[q], take(q))
        grad_middle[...] = grad_middle[...] + value if q else value
        work[...] = product_by_columns(grad_mlp_ref[...], block[q % 2])
        fetch(q + 2)
        quads[q].wait()

        def body(at):
            lows[q, at, :] = (work[at, :] * quad[q, at, :]).astype(jnp.bfloat16)

        chunks(count, body)
        if q < 2:
            source = (middle_ref, attended_ref)[q]
            quads[q] = pltpu.make_async_copy(source, quad.at[q], quad_sem.at[q])
            quads[q].start()

    def up_grad(q):
        need("hidden_two")
        put(q, hidden_two_ref, lows.at[q], up_part_ref.at[q])

    def through_up(q):
        value = product_by_columns(lows[q], take(4 + q))
        work[...] = work[...] + value if q else value
        fetch(6 + q)

    def norm_pull(grad, value, inverse):
        return inverse * (
            grad
            - jnp.mean(grad, axis=-1, keepdims=True)
            - value * jnp.mean(grad * value, axis=-1, keepdims=True)
        )

    def add_sums(segments, which, value):
        for crop in range(CROPS):
            kept = jnp.where(segments == crop, value, 0.0)
            sums[which, crop] = sums[which, crop] + kept[:8] + kept[8:]

    def second_norm(half):
        if half == 0:
            for q in range(2):
                quads[q].wait()
            sums[...] = jnp.zeros_like(sums)
            need("cot")

        def body(at):
            segments = seg_col_ref[at, :1]
            grad = work[at, :]
            middle, mlp = quad[0, at, :], grad_middle[at, :]
            value, inverse = normed(middle)
            gate = pick(segments, table_ref, 4, 2, width)
            leave[0, at, :] = (middle + gate * mlp).astype(jnp.bfloat16)
            level = level_ref[3:4, :1]
            for crop in (2, 1, 0):
                level = jnp.where(segments == crop, level_ref[crop : crop + 1, :1], level)
            grad_out = cot_ref[at, :].astype(jnp.float32) * level
            add_sums(segments, 3, grad)
            add_sums(segments, 4, grad * value)
            add_sums(segments, 5, grad_out * mlp)
            scaled = grad * (1.0 + pick(segments, table_ref, 4, 1, width))
            total = grad_out + norm_pull(scaled, value, inverse)
            grad_middle[at, :] = total
            add_sums(segments, 2, total * quad[1, at, :])
            lows[3, at, :] = (total * pick(segments, table_ref, 0, 2, width)).astype(jnp.bfloat16)

        chunks(count // 2, body, half * (count // 2))
        if half:
            quads["out"] = pltpu.make_async_copy(leave.at[0], out_ref, out_sem)
            quads["out"].start()

    def context_grad():
        grad_context[...] = product_by_columns(lows[3], take(8)).astype(jnp.bfloat16)
        fetch(10)

    def out_grad():
        need("context")
        put(4, context_ref, lows.at[3], mixer_part_ref.at[3])
        for h in (0, 1):
            same = seg_col_ref[:, :1] == seg_all_ref[h][:1, :]
            bias[:, h * count : (h + 1) * count] = jnp.where(same, 0.0, LARGE_NEGATIVE)

    def attend_back(first, last):
        need("query", "sides", "total")
        size = width // HEADS
        scale = 1.0 / math.sqrt(size)

        def body(head, carry):
            columns, inside = window_of(head, size, width)
            query, keys = query_ref[:, columns], sides_ref[0, :, columns]
            grad = grad_context[:, columns]
            scores = product_by_columns(jnp.where(inside, query, jnp.zeros_like(query)), keys)
            lane = lax.broadcasted_iota(jnp.int32, (1, 128), 1)
            total = jnp.sum(jnp.where(lane == head, total_ref[...], 0.0), axis=-1, keepdims=True)
            chance = jnp.exp(scores * scale + bias[...] - total)
            pulled = product_by_columns(
                jnp.where(inside, grad, jnp.zeros_like(grad)), sides_ref[1, :, columns]
            )
            inner = jnp.sum(chance * pulled, axis=-1, keepdims=True)
            grad_scores = (chance * (pulled - inner)).astype(jnp.bfloat16)
            grad_query = (product(grad_scores, keys) * scale).astype(jnp.bfloat16)
            lows[0, :, columns] = jnp.where(inside, grad_query, lows[0, :, columns])
            grad_key = product_by_rows(grad_scores, query) * scale
            grad_value = product_by_rows(chance.astype(jnp.bfloat16), grad)
            for h in (0, 1):
                here = slice(h * count, (h + 1) * count)
                quad[h, :, columns] = jnp.where(inside, grad_key[here], quad[h, :, columns])
                quad[2 + h, :, columns] = jnp.where(inside, grad_value[here], quad[2 + h, :, columns])
            return carry

        lax.fori_loop(first, last, body, 0)

    def swap_sides():
        quads["out"].wait()
        for j in (0, 1):
            leave[j] = quad[2 * j + 1 - c].astype(jnp.bfloat16)
            send("end", leave.at[j], enter.at[j], side_send.at[j], side_recv.at[j], c_peer)

    def query_grad():
        need("hidden")
        put(5, hidden_ref, lows.at[0], mixer_part_ref.at[0])

    def side_grad(j):
        arrive(enter.at[j], side_recv.at[j], c_peer)

        def body(at):
            total = quad[2 * j + c, at, :] + enter[j, at, :].astype(jnp.float32)
            lows[1 + j, at, :] = total.astype(jnp.bfloat16)

        chunks(count, body)
        put(6 + j, hidden_ref, lows.at[1 + j], mixer_part_ref.at[1 + j])

    def through_qkv(q):
        value = product_by_columns(lows[q], take(9 + q))
        work[...] = work[...] + value if q else value
        fetch(11 + q)

    def first_norm(half):
        need("tokens")

        def body(at):
            segments = seg_col_ref[at, :1]
            grad = work[at, :]
            value, inverse = normed(tokens_ref[at, :].astype(jnp.float32))
            add_sums(segments, 0, grad)
            add_sums(segments, 1, grad * value)
            scaled = grad * (1.0 + pick(segments, table_ref, 0, 1, width))
            tokens_grad_ref[at, :] = grad_middle[at, :] + norm_pull(scaled, value, inverse)

        chunks(count // 2, body, half * (count // 2))

    def sums_leave():
        for which in range(6):
            for crop in range(CROPS):
                row = which // 3 * CROPS + crop
                columns = slice(which % 3 * width, (which % 3 + 1) * width)
                sums_row[row : row + 1, columns] = jnp.sum(sums[which, crop], axis=0, keepdims=True)
        send("end", sums_row, sums_core, m_send, m_recv, c_peer)

    side = sums_row.shape[1]

    def place(k, other_y, other_x):
        zz = (z - k + 4) % 4
        yy = 1 - y if other_y else y
        xx = 1 - x if other_x else x
        return band.at[c, pl.ds(pl.multiple_of((zz * 4 + yy * 2 + xx) * 16, 16), 16)]

    def sums_start():
        arrive(sums_core, m_recv, c_peer)
        near = pl.ds(pl.multiple_of(c * (side - BAND), 128), BAND)
        total = sums_row[:, near] + sums_core[:, near]
        total = jnp.concatenate([total[:, : BAND // 2], total[:, BAND // 2 :]], axis=0)
        band[c, pl.ds(pl.multiple_of(me * 16, 16), 16), :] = total.astype(jnp.bfloat16)
        mine = place(0, 0, 0)
        for k in (1, 2, 3):
            send("end", mine, mine, mz_send.at[k - 1], mz_recv.at[k - 1], device((z + k) % 4, y, x, c))
        send("end", mine, mine, mx_send.at[0], mx_recv.at[0], x_peer)
        send("end", mine, mine, my_send.at[0], my_recv.at[0], y_peer)

    def sums_line():
        for k in (1, 2, 3):
            piece = place(k, 0, 0)
            arrive(piece, mz_recv.at[k - 1], device((z - k + 4) % 4, y, x, c))
            send("end", piece, piece, mx_send.at[k], mx_recv.at[k], x_peer)
            send("end", piece, piece, my_send.at[k], my_recv.at[k], y_peer)

    def sums_plane():
        for k in range(4):
            from_side, from_up = place(k, 0, 1), place(k, 1, 0)
            arrive(from_side, mx_recv.at[k], x_peer)
            arrive(from_up, my_recv.at[k], y_peer)
            if k % 2:
                send("end", from_side, from_side, md_send.at[k], md_recv.at[k], y_peer)
            else:
                send("end", from_up, from_up, md_send.at[k], md_recv.at[k], x_peer)

    def sums_cores():
        for k in range(4):
            arrive(place(k, 1, 1), md_recv.at[k], y_peer if k % 2 else x_peer)
        send("end", band.at[c], band.at[c], mc_send, mc_recv, c_peer)

    def condition(source):
        if source == 0:
            arrive(band.at[1 - c], mc_recv, c_peer)
            silu_side[...] = jnp.zeros_like(silu_side)
        acts = conds_ref[:, :8, :].astype(jnp.float32).reshape(CHIPS * 8, 128)
        row = lax.broadcasted_iota(jnp.int32, acts.shape, 0) % 8
        acts = jnp.where(row < CROPS, acts, 0.0)
        upper = acts.astype(jnp.bfloat16)
        lower = pltpu.roll(acts, CROPS, 0).astype(jnp.bfloat16)
        for half in (0, 1):
            first = source * (side - BAND) + half * (BAND // 2)
            skip = max(0, source * BAND - first)
            term = band[source].astype(jnp.float32).reshape(CHIPS, 16, BAND // 2)
            term = term[:, half * 8 : (half + 1) * 8, skip:].reshape(CHIPS * 8, BAND // 2 - skip)
            term = term.astype(jnp.bfloat16)
            for which, act in enumerate((upper, lower)):
                columns = slice(which * side + first + skip, which * side + first + BAND // 2)
                ada_grad_ref[:, columns] = product_by_rows(act, term)[: ada_grad_ref.shape[0]]
                value = product_by_columns(term, ada_ref[:, columns])
                silu_side[which, :, :PAD] = silu_side[which, :, :PAD] + value
        if source == 0:
            return
        silu_part[...] = silu_side[0] + pltpu.roll(silu_side[1], CHIPS * 8 - CROPS, 0)
        silu_ref[c, me] = silu_part[pl.ds(pl.multiple_of(me * 8, 8), 8), :]
        for k in range(1, CHIPS):
            to = (me + k) % CHIPS
            src = silu_part.at[pl.ds(pl.multiple_of(to * 8, 8), 8)]
            send("end", src, silu_ref.at[c, me], s_send.at[k - 1], s_recv.at[k - 1], (to, c))

    def condition_cores():
        for k in range(1, CHIPS):
            source = (me - k + CHIPS) % CHIPS
            arrive(silu_ref.at[c, source], s_recv.at[k - 1], (source, c))
        send("end", silu_ref.at[c], silu_ref.at[c], sc_send, sc_recv, c_peer)

    kinds = [begin] + [partial(pair, pos=pos) for pos in range(4)]
    kinds += [diag_along, relay_x, relay_y, plane, piece_along]
    steps = [partial(kinds[n % 10], n // 10) for n in BACKWARD_STEPS]
    layer = [partial(through_down, q) for q in range(4)] + [partial(up_grad, q) for q in range(4)]
    layer += [partial(through_up, q) for q in range(4)] + [partial(second_norm, h) for h in (0, 1)]
    layer += [context_grad, out_grad] + [partial(attend_back, h, h + 2) for h in range(0, HEADS, 2)]
    layer += [swap_sides, query_grad, partial(side_grad, 0), partial(side_grad, 1)]
    layer += [partial(through_qkv, q) for q in range(3)] + [partial(first_norm, h) for h in (0, 1)]
    layer += [sums_leave, sums_start, sums_line, sums_plane, sums_cores]
    layer += [partial(condition, 0), partial(condition, 1), condition_cores]
    begin(0)
    fetch(0)
    fetch_late()
    for q in range(4):
        slopes(q)
    fetch(1)
    interleave(steps, layer, BACKWARD_AFTER)
    for a in range(2):
        for j, (px, pc) in enumerate(partners):
            arrive(rows_ref.at[a, px * 2 + pc], group_recv.at[a, j], device(z, y, px, pc))
    arrive(silu_ref.at[1 - c], sc_recv, c_peer)
    for owner in list(sends):
        finish_sends(owner)


def run_backward(given, share):
    (weights, down_part, slope, middle, attended, active, hidden, query, sides, total, context, hidden_two,
     grad_mlp, table, conds, level, seg_all, seg_col, tokens, cot, ada) = given
    count, width = tokens.shape
    rows, side = 4 * share, ada.shape[1] // 2
    dma = pltpu.SemaphoreType.DMA
    low, wide = jnp.bfloat16, jnp.float32
    vmem, any_ = pl.BlockSpec(memory_space=pltpu.VMEM), pl.BlockSpec(memory_space=pl.ANY)
    out, buffer = jax.ShapeDtypeStruct, pltpu.VMEM
    slots = 12
    return pl.pallas_call(
        partial(backward_kernel, share),
        out_shape=(
            out((4, width, width), low),
            out((4, width, width), low),
            out((2, 4, PAD, width), low),
            out((rows, width), wide),
            out((count, width), wide),
            out((-(-share // 8) * 8, ada.shape[1]), wide),
            out((2, CHIPS, 8, 128), wide),
            out((count, width), low),
        ),
        in_specs=[any_] * 13 + [vmem] * 5 + [any_] * 2 + [vmem],
        out_specs=[any_] * 2 + [vmem] * 5 + [any_],
        scratch_shapes=[
            buffer((HELD, 4, rows, width), low),
            buffer((4, 4, rows, width), low),
            buffer((5, rows, width), low),
            buffer((6, rows, width), low),
            buffer((6, rows, width), low),
            buffer((2, 5, rows, width), low),
            buffer((2, 5, rows - FAR[0] - FAR[1], width), low),
            buffer((2, 4 * PAD, width), low),
            buffer((2, width, width), low),
            buffer((2, width, width), low),
            buffer((4, count, width), wide),
            buffer((4, count, width), low),
            buffer((count, width), wide),
            buffer((count, width), wide),
            buffer((count, width), low),
            buffer((2, count, width), low),
            buffer((2, count, width), low),
            buffer((count, 2 * count), wide),
            buffer((6, CROPS, 8, width), wide),
            buffer((8, side), wide),
            buffer((8, side), wide),
            buffer((2, CHIPS * 16, BAND // 2), low),
            buffer((CHIPS * 8, 128), wide),
            buffer((2, CHIPS * 8, 128), wide),
            buffer((count, width), low),
            buffer((count, width), low),
            buffer((2, 2 * count, width), low),
            buffer((count, 128), wide),
            buffer((count, width), low),
            buffer((count, width), low),
            buffer((count, width), low),
            buffer((count, width), low),
            buffer((count, width), low),
            dma((slots, 4)), dma((slots, 4)), dma((slots, 4)),
            dma((slots,)), dma((slots,)), dma((slots,)), dma((slots,)),
            dma((slots, 2)), dma((slots, 2)), dma((slots, 2)), dma((slots, 2)),
            dma((3, 4)), dma((3, 5)), dma((3, 4)), dma((3, 5)),
            dma((2, 3)), dma((2, 3)), dma((2,)), dma((2,)), dma((4,)), dma((4,)), dma, dma((9,)),
            dma((2,)), dma((2,)), dma, dma, dma((3,)), dma((3,)), dma((4,)), dma((4,)), dma((4,)), dma((4,)),
            dma((4,)), dma((4,)), dma, dma, dma((CHIPS - 1,)), dma((CHIPS - 1,)), dma, dma,
        ],
        compiler_params=pltpu.CompilerParams(
            collective_id=1, has_side_effects=True, vmem_limit_bytes=63 * 2**20 + 2**19
        ),
        name="backward",
    )(*given)


def finish_kernel(share, rows_ref, ada_given_ref, silu_ref, cond_ref, down_given, tokens_grad_given, out_given,
                  qkv_ref, out_grad_ref, up_ref, ada_ref, cond_grad_ref, down_ref, tokens_grad_ref, out_ref):
    for given, ref in ((down_given, down_ref), (tokens_grad_given, tokens_grad_ref), (out_given, out_ref)):

        def body(at):
            ref[at, :] = given[at, :]

        chunks(ref.shape[0], body)
    width = rows_ref.shape[-1]
    for q in range(4):
        value = rows_ref[0, q].astype(jnp.float32)[:share]
        if q == 3:
            out_grad_ref[...] = value
        else:
            qkv_ref[:, q * width : (q + 1) * width] = value
        up_ref[:, q * width : (q + 1) * width] = rows_ref[1, q].astype(jnp.float32)[:share]
    ada_ref[...] = ada_given_ref[...][:share]
    lane = lax.broadcasted_iota(jnp.int32, (8, 128), 1)
    tiles = [jnp.zeros((8, 128), jnp.float32)] * (width // 128)
    for number in range(2 * CHIPS):
        tile, offset = divmod(number * share, 128)
        value = jnp.where(lane < share, silu_ref[number % 2, number // 2], 0.0)
        if offset:
            value = pltpu.roll(value, offset, 1)
        tiles[tile] = tiles[tile] + jnp.where(lane >= offset, value, 0.0)
        if offset + share > 128:
            tiles[tile + 1] = tiles[tile + 1] + jnp.where(lane < offset, value, 0.0)
    grad = jnp.concatenate(tiles, axis=1)[:CROPS]
    cond = cond_ref[...].astype(jnp.float32)
    chance = 1.0 / (1.0 + jnp.exp(-cond))
    cond_grad_ref[...] = grad * (chance * (1.0 + cond * (1.0 - chance)))


def run_finish(rows, ada_grad, silu_part, cond, down_grad, tokens_grad, tokens_out, share):
    width = rows.shape[-1]
    wide = jnp.float32
    vmem, out = pl.BlockSpec(memory_space=pltpu.VMEM), jax.ShapeDtypeStruct
    return pl.pallas_call(
        partial(finish_kernel, share),
        out_shape=(
            out((share, 3 * width), wide),
            out((share, width), wide),
            out((share, 4 * width), wide),
            out((share, ada_grad.shape[1]), wide),
            out(cond.shape, wide),
            out(down_grad.shape, wide),
            out(tokens_grad.shape, wide),
            out(tokens_out.shape, tokens_out.dtype),
        ),
        in_specs=[vmem] * 7,
        out_specs=[vmem] * 8,
        compiler_params=pltpu.CompilerParams(vmem_limit_bytes=63 * 2**20),
        name="finish",
    )(rows, ada_grad, silu_part, cond, down_grad, tokens_grad, tokens_out)


def layer_norm(values):
    center = values - jnp.mean(values, axis=-1, keepdims=True)
    inverse = lax.rsqrt(jnp.mean(center * center, axis=-1, keepdims=True) + EPSILON)
    return (center * inverse, inverse)


def norm_back(grad_normed, normed, inverse):
    return inverse * (
        grad_normed
        - jnp.mean(grad_normed, axis=-1, keepdims=True)
        - normed * jnp.mean(grad_normed * normed, axis=-1, keepdims=True)
    )


def to_heads(array):
    return array.reshape(array.shape[0], HEADS, array.shape[1] // HEADS)


def dots(spec, left, right):
    return jnp.einsum(spec, left, right, preferred_element_type=jnp.float32)


def masked_scores(query_heads, key_heads, same_crop):
    scale_factor = 1.0 / math.sqrt(query_heads.shape[-1])
    scores = dots("qhd,khd->hqk", query_heads, key_heads) * scale_factor
    return jnp.where(same_crop[None], scores, LARGE_NEGATIVE)


def attend(query_seq, key_seq, value_seq, same_crop):
    scores = masked_scores(to_heads(query_seq), to_heads(key_seq), same_crop)
    row_max = jnp.max(scores, axis=-1, keepdims=True)
    raised = jnp.exp(scores - row_max)
    row_total = jnp.sum(raised, axis=-1, keepdims=True)
    probability = (raised / row_total).astype(jnp.bfloat16)
    context = dots("hqk,khd->qhd", probability, to_heads(value_seq))
    return (context.reshape(query_seq.shape[0], -1), (row_max + jnp.log(row_total))[..., 0])


def attend_back(query_seq, key_seq, value_seq, same_crop, log_total, grad_seq):
    query_heads = to_heads(query_seq)
    key_heads = to_heads(key_seq)
    value_heads = to_heads(value_seq)
    grad_heads = to_heads(grad_seq)
    scale_factor = 1.0 / math.sqrt(query_heads.shape[-1])
    scores = masked_scores(query_heads, key_heads, same_crop)
    probability = jnp.exp(scores - log_total[..., None])
    grad_prob = dots("qhd,khd->hqk", grad_heads, value_heads)
    inner = jnp.sum(probability * grad_prob, axis=-1, keepdims=True)
    grad_scores = (probability * (grad_prob - inner)).astype(jnp.bfloat16)
    grad_query = dots("hqk,khd->qhd", grad_scores, key_heads) * scale_factor
    grad_key = dots("hqk,qhd->khd", grad_scores, query_heads) * scale_factor
    grad_value = dots("hqk,qhd->khd", probability.astype(jnp.bfloat16), grad_heads)
    rows_here = query_seq.shape[0]
    rows_whole = key_seq.shape[0]
    return (
        grad_query.reshape(rows_here, -1),
        grad_key.reshape(rows_whole, -1),
        grad_value.reshape(rows_whole, -1),
    )


def forward_plain(tokens_float, segments, conditions, noise_bins, bin_counts, ada_weight, first, up_weight,
                  down_weight):
    groups, cores = lax.axis_size("dp"), lax.axis_size("sp")
    share, width = first.shape[0], tokens_float.shape[1]
    index = lax.axis_index("dp") * cores + lax.axis_index("sp")
    mixers = lax.all_gather(first, ("dp", "sp"), axis=0, tiled=True)
    uppers = lax.all_gather(up_weight, ("dp", "sp"), axis=0, tiled=True)
    downers = lax.all_gather(down_weight, ("dp", "sp"), axis=0, tiled=True)
    mixers = mixers.reshape(width, 4, width).transpose(1, 0, 2)
    uppers = uppers.reshape(width, 4, width).transpose(1, 0, 2)
    downers = downers.reshape(4, width, width)
    bin_total = lax.psum(bin_counts, "dp")
    bin_weight = 40.0 * groups / bin_total.astype(jnp.float32)
    crop_weight = jnp.sum(
        jnp.where(noise_bins[:, None] == jnp.arange(NBINS, dtype=jnp.int32), bin_weight, 0.0),
        axis=-1,
    )
    cond_all = lax.all_gather(conditions, "dp", axis=0, tiled=True)
    cond_here = lax.dynamic_slice_in_dim(cond_all, index * share, share, axis=1)
    cond_act = jax.nn.silu(cond_here.astype(jnp.float32)).astype(jnp.bfloat16)
    modulation_part = dots("sd,df->sf", cond_act, ada_weight).reshape(groups, CROPS, -1)
    modulation = lax.psum(lax.psum_scatter(modulation_part, "dp", scatter_dimension=0), "sp")
    selector = (segments[:, None] == jnp.arange(CROPS, dtype=jnp.int32)).astype(jnp.float32)
    per_token = jnp.einsum("tc,cf->tf", selector, modulation, precision=lax.Precision.HIGHEST)
    shift_one, scale_one, gate_one, shift_two, scale_two, _ = jnp.split(per_token, 6, axis=-1)
    normed_one, _ = layer_norm(tokens_float)
    hidden_one = (normed_one * (1.0 + scale_one) + shift_one).astype(jnp.bfloat16)
    projected = dots("td,qdf->qtf", hidden_one, mixers[:3]).astype(jnp.bfloat16)
    sides = lax.all_gather(projected[1:], "sp", axis=1, tiled=True)
    all_segments = lax.all_gather(segments, "sp", axis=0, tiled=True)
    same_crop = segments[:, None] == all_segments[None, :]
    context, log_total = attend(projected[0], sides[0], sides[1], same_crop)
    context_low = context.astype(jnp.bfloat16)
    attended = dots("td,df->tf", context_low, mixers[3])
    middle = tokens_float + gate_one * attended
    normed_two, _ = layer_norm(middle)
    hidden_two = (normed_two * (1.0 + scale_two) + shift_two).astype(jnp.bfloat16)
    upper_in = dots("td,qdf->qtf", hidden_two, uppers)
    activated = jax.nn.gelu(upper_in, approximate=True).astype(jnp.bfloat16)
    slope = jax.vjp(partial(jax.nn.gelu, approximate=True), upper_in)[1](jnp.ones_like(upper_in))[0]
    mlp_out = dots("qtf,qfd->td", activated, downers)
    return (
        (mixers, uppers, downers), activated, slope, hidden_one, projected[0], sides, log_total,
        context_low, attended, middle, hidden_two, mlp_out, modulation, cond_act, crop_weight, same_crop,
    )


def layer_plain(tokens_float, segments, conditions, noise_bins, bin_counts, cotangent, ada_weight, first,
                up_weight, down_weight):
    width = tokens_float.shape[1]
    (
        (mixers, uppers, downers), activated, slope, hidden_one, queries, sides, log_total,
        context_low, attended, middle, hidden_two, mlp_out, modulation, cond_act, crop_weight, same_crop,
    ) = forward_plain(
        tokens_float, segments, conditions, noise_bins, bin_counts, ada_weight, first, up_weight,
        down_weight,
    )
    selector = (segments[:, None] == jnp.arange(CROPS, dtype=jnp.int32)).astype(jnp.float32)
    per_token = jnp.einsum("tc,cf->tf", selector, modulation, precision=lax.Precision.HIGHEST)
    _, scale_one, gate_one, _, scale_two, gate_two = jnp.split(per_token, 6, axis=-1)
    normed_one, inverse_one = layer_norm(tokens_float)
    normed_two, inverse_two = layer_norm(middle)

    token_weight = jnp.sum(selector * crop_weight[None, :], axis=-1)
    grad_out = cotangent.astype(jnp.float32) * token_weight[:, None]
    grad_mlp = (grad_out * gate_two).astype(jnp.bfloat16)
    tokens_out = (middle + gate_two * mlp_out).astype(jnp.bfloat16)
    down_part = dots("qtf,td->qfd", activated, grad_mlp).astype(jnp.bfloat16)
    grad_act = dots("td,qfd->qtf", grad_mlp, downers)
    grad_upper = (grad_act * slope).astype(jnp.bfloat16)
    up_part = dots("td,qtf->qdf", hidden_two, grad_upper).astype(jnp.bfloat16)
    grad_hidden_two = dots("qtf,qdf->td", grad_upper, uppers)
    grad_middle = grad_out + norm_back(grad_hidden_two * (1.0 + scale_two), normed_two, inverse_two)
    grad_attended = (grad_middle * gate_one).astype(jnp.bfloat16)
    grad_context = dots("tf,df->td", grad_attended, mixers[3]).astype(jnp.bfloat16)
    grad_query, grad_key, grad_value = attend_back(
        queries, sides[0], sides[1], same_crop, log_total, grad_context
    )
    grad_sides = lax.psum_scatter(
        jnp.stack([grad_key, grad_value]).astype(jnp.bfloat16),
        "sp",
        scatter_dimension=1,
        tiled=True,
    )
    grad_projected = jnp.concatenate([grad_query.astype(jnp.bfloat16)[None], grad_sides])
    out_part = dots("td,tf->df", context_low, grad_attended).astype(jnp.bfloat16)
    qkv_part = dots("td,qtf->qdf", hidden_one, grad_projected).astype(jnp.bfloat16)
    first_part = jnp.concatenate([qkv_part, out_part[None]])
    grad_hidden_one = dots("qtf,qdf->td", grad_projected, mixers[:3])
    tokens_grad = grad_middle + norm_back(
        grad_hidden_one * (1.0 + scale_one), normed_one, inverse_one
    )

    joined = jnp.stack([first_part, up_part]).transpose(2, 0, 1, 3).reshape(width, 8 * width)
    rows = lax.psum_scatter(joined, ("dp", "sp"), scatter_dimension=0, tiled=True)
    rows = rows.astype(jnp.float32)
    first_grad, up_grad = rows[:, : 4 * width], rows[:, 4 * width :]
    down_grad = lax.psum_scatter(
        down_part.reshape(4 * width, width), ("dp", "sp"), scatter_dimension=0, tiled=True
    ).astype(jnp.float32)

    grad_per_token = jnp.concatenate(
        [
            grad_hidden_one,
            grad_hidden_one * normed_one,
            grad_middle * attended,
            grad_hidden_two,
            grad_hidden_two * normed_two,
            grad_out * mlp_out,
        ],
        axis=-1,
    )
    grad_modulation = lax.psum(
        jnp.einsum("tc,tf->cf", selector, grad_per_token, precision=lax.Precision.HIGHEST), "sp"
    )
    grad_rows = lax.all_gather(grad_modulation, "dp", axis=0, tiled=True)
    ada_grad = jnp.einsum(
        "sd,sf->df", cond_act.astype(jnp.float32), grad_rows, precision=lax.Precision.HIGHEST
    )
    silu_part = jnp.einsum(
        "sf,df->sd", grad_rows, ada_weight.astype(jnp.float32), precision=lax.Precision.HIGHEST
    )
    silu_all = lax.all_gather(silu_part, ("dp", "sp"), axis=0)
    silu_here = lax.dynamic_slice_in_dim(silu_all, lax.axis_index("dp") * CROPS, CROPS, axis=1)
    grad_silu = silu_here.transpose(1, 0, 2).reshape(CROPS, width)
    return tokens_out, tokens_grad, grad_silu, ada_grad, first_grad, up_grad, down_grad


def on_device(
    chips,
    tokens_in,
    segment_ids,
    conditions,
    noise_bins,
    bin_counts,
    cotangent,
    ada_weight,
    qkv_weight,
    out_weight,
    up_weight,
    down_weight,
):
    share = qkv_weight.shape[0]
    if chips and 4 * share == down_weight.shape[0]:
        (
            weights, down_part, slope, active, sides, attended, middle, hidden_one, queries, log_total,
            context_low, hidden_two, table, conds, level, grad_mlp, seg_all, seg_col, ada,
        ) = run_forward(
            qkv_weight, out_weight, up_weight, down_weight, conditions[0], noise_bins, bin_counts,
            ada_weight, tokens_in[0], cotangent[0], segment_ids,
        )
        given = (
            weights, down_part, slope, middle, attended, active, hidden_one, queries, sides, log_total,
            context_low, hidden_two, grad_mlp, table, conds, level, seg_all, seg_col, tokens_in[0],
            cotangent[0], ada,
        )
        _, _, rows, down_grad, tokens_grad, ada_grad, silu_part, tokens_out = run_backward(given, share)
        qkv_grad, out_grad, up_grad, ada_grad, cond_grad, down_grad, tokens_grad, tokens_out = run_finish(
            rows, ada_grad, silu_part, conditions[0], down_grad, tokens_grad, tokens_out, share
        )
    else:
        first = jnp.concatenate([qkv_weight, out_weight], axis=1)
        width = out_weight.shape[1]
        tokens_out, tokens_grad, grad_silu, ada_grad, first_grad, up_grad, down_grad = layer_plain(
            tokens_in[0].astype(jnp.float32), segment_ids[0], conditions[0], noise_bins[0], bin_counts[0],
            cotangent[0], ada_weight, first, up_weight, down_weight,
        )
        qkv_grad, out_grad = first_grad[:, : 3 * width], first_grad[:, 3 * width :]
        cond_grad = jax.vjp(jax.nn.silu, conditions[0].astype(jnp.float32))[1](grad_silu)[0]
    return (
        tokens_out[None],
        tokens_grad[None],
        cond_grad[None],
        ada_grad,
        qkv_grad,
        out_grad,
        up_grad,
        down_grad,
    )


def solution(mesh):
    placed = (
        P("dp", "sp", None),
        P("dp", "sp"),
        P("dp", None, None),
        P("dp", None),
        P("dp", None),
        P("dp", "sp", None),
        P(("dp", "sp"), None),
        P(("dp", "sp"), None),
        P(("dp", "sp"), None),
        P(("dp", "sp"), None),
        P(("dp", "sp"), None),
    )
    return jax.shard_map(
        partial(on_device, mesh.shape["dp"] == 16 and mesh.shape["sp"] == 2),
        mesh=mesh,
        in_specs=placed,
        out_specs=(
            P("dp", "sp", None),
            P("dp", "sp", None),
            P("dp", None, None),
            P(("dp", "sp"), None),
            P(("dp", "sp"), None),
            P(("dp", "sp"), None),
            P(("dp", "sp"), None),
            P(("dp", "sp"), None),
        ),
        check_vma=False,
    )
```

```python
from functools import partial
import math

import jax
import jax.numpy as jnp
from jax import lax
from jax.experimental import pallas as pl
from jax.experimental.pallas import tpu as pltpu
from jax.sharding import PartitionSpec as P

HEADS = 16
CROPS = 4
NBINS = 8
EPSILON = 1e-06
LARGE_NEGATIVE = -1e30
GELU_SCALE = math.sqrt(2.0 / math.pi)
GELU_CUBE = 0.044715

MESH = pl.DeviceIdType.MESH
PAD = 48
NEAR = (80, 64)
FAR = (32, 32)
HELD = 6
FORWARD_STEPS = (
    0, 2, 11, 12, 21, 3, 4, 22, 13, 5, 14, 31, 32, 7, 23, 24, 100, 15, 102, 33,
    16, 34, 26, 25, 111, 27, 121, 17, 103, 104, 35, 36, 112, 122, 37, 113, 114, 105, 107, 131,
    115, 132, 200, 123, 124, 116, 202, 133, 134, 126, 125, 211, 135, 212, 203, 117, 204, 221, 127, 136,
    137, 205, 222, 213, 214, 215, 207, 231, 232, 223, 224, 225, 216, 217, 233, 234, 226, 235, 236, 227,
    237,
)
BACKWARD_STEPS = (
    10, 4, 1, 3, 20, 12, 2, 30, 14, 6, 13, 22, 7, 5, 16, 11, 23, 34, 17, 32,
    8, 24, 40, 21, 33, 15, 18, 25, 44, 42, 26, 43, 27, 35, 9, 50, 47, 31, 46, 41,
    54, 60, 53, 52, 19, 28, 45, 36, 51, 62, 37, 64, 55, 61, 57, 70, 29, 63, 38, 56,
    48, 72, 65, 73, 66, 80, 67, 58, 39, 49, 74, 71, 90, 82, 100, 75, 84, 92, 81, 94,
    83, 59, 110, 91, 68, 76, 69, 86, 77, 85, 111, 87, 104, 102, 95, 96, 93, 101, 97, 103,
    78, 79, 105, 88, 114, 89, 107, 106, 115, 113, 112, 98, 116, 99, 108, 109, 117, 118, 119,
)
FORWARD_AFTER = (
    0, 2, 8, 20, 24, 26, 34, 35, 37, 39, 43, 47, 47, 47, 47, 49, 49, 51, 51, 54,
    59, 59, 62, 63, 64, 64, 65, 65, 67, 67, 70, 71, 77, 77, 78, 81,
)
BACKWARD_AFTER = (
    1, 9, 13, 14, 16, 18, 22, 22, 23, 24, 30, 31, 32, 40, 44, 45, 45, 46, 52, 54,
    54, 56, 57, 57, 57, 63, 65, 65, 81, 81, 85, 86, 88, 90, 98, 109, 116, 119, 119, 119,
    119,
)
CHIPS = 16
BAND = 1792
PLACES = ((0, 0), (0, 1), (1, 0), (1, 1))


def position():
    d = lax.axis_index("dp")
    c = lax.axis_index("sp")
    return d // 4, (d // 2) % 2, d % 2, c


def device(z, y, x, c):
    return (z * 4 + y * 2 + x, c)


def block_of(kind, zy, group):
    if kind == 2:
        return zy // 2, (zy % 2) * 4 + group
    return group, zy


def level_of(z, k):
    if k == 0:
        return z
    upper = z // 2
    inner = z * (1 - upper) + (3 - z) * upper
    step = k - inner if k == 1 else k
    return step * (1 - upper) + (3 - step) * upper


def greet(peers, meanwhile=None):
    barrier = pltpu.get_barrier_semaphore()
    for peer in peers:
        pl.semaphore_signal(barrier, inc=1, device_id=peer, device_id_type=MESH)
    if meanwhile is not None:
        meanwhile()
    pl.semaphore_wait(barrier, len(peers))


def remote(src, dst, send, recv, target):
    return pltpu.make_async_remote_copy(
        src_ref=src,
        dst_ref=dst,
        send_sem=send,
        recv_sem=recv,
        device_id=target,
        device_id_type=MESH,
    )


def arrive(ref, sem, target):
    remote(ref, ref, sem, sem, target).wait_recv()


def row_selector(rows, share):
    shape = (rows, 4 * PAD)
    row = lax.broadcasted_iota(jnp.int32, shape, 0)
    column = lax.broadcasted_iota(jnp.int32, shape, 1)
    picked = jnp.zeros(shape, jnp.bool_)
    for k in range(4):
        inside = (row >= k * share) & (row < (k + 1) * share)
        picked = picked | (inside & (column == row - k * share + k * PAD))
    return picked.astype(jnp.float32).astype(jnp.bfloat16)


def product(left, right):
    return jnp.dot(left, right, preferred_element_type=jnp.float32)


def product_by_rows(left, right):
    return lax.dot_general(left, right, (((0,), (0,)), ((), ())), preferred_element_type=jnp.float32)


def product_by_columns(left, right):
    return lax.dot_general(left, right, (((1,), (1,)), ((), ())), preferred_element_type=jnp.float32)


def chunks(rows, body, first=0, step=16):
    def run(i, carry):
        body(pl.ds(pl.multiple_of(first + i * step, step), step))
        return carry

    lax.fori_loop(0, rows // step, run, 0)


def normed(values):
    center = values - jnp.mean(values, axis=-1, keepdims=True)
    inverse = lax.rsqrt(jnp.mean(center * center, axis=-1, keepdims=True) + EPSILON)
    return center * inverse, inverse


def pick(segments, table, first, column, width):
    columns = slice(column * width, (column + 1) * width)
    value = table[first + 3 : first + 4, columns]
    for crop in (2, 1, 0):
        value = jnp.where(segments == crop, table[first + crop : first + crop + 1, columns], value)
    return value


def window_of(head, size, width):
    start = jnp.minimum((head * size) // 128, width // 128 - 2) * 128
    start = pl.multiple_of(start, 128)
    lane = lax.broadcasted_iota(jnp.int32, (1, 256), 1) + start
    return pl.ds(start, 256), (lane >= head * size) & (lane < (head + 1) * size)


def share_window(device_number, share, width):
    column = device_number * share
    start = jnp.minimum(column // 128, width // 128 - 2) * 128
    return pl.multiple_of(start, 128), column - start


def forward_kernel(share, qkv_ref, out_weight_ref, up_ref, down_ref, cond_ref, noise_ref, counts_ref, given_ada_ref,
                   tokens_ref, cot_ref, seg_ref,
                   weights_ref, down_part_ref, slope_ref, active_ref, sides_out_ref, attended_out_ref, middle_out_ref,
                   hidden_out_ref, query_out_ref, total_ref, context_out_ref, hidden_two_out_ref, table_ref,
                   conds_ref, level_ref, grad_mlp_out_ref, seg_all, seg_col_ref, ada_out_ref,
                   full, shards_ref, stage, acts, acts_low, windows, part, part_recv, band, band_diag, band_x, band_y,
                   band_z, halves_of, sides_ref, attended_ref, middle_ref, bias, work, active, slope,
                   hidden_ref, query_ref, context_ref, hidden_two_ref, grad_mlp, ada_ref, *sems):
    (
        group_send, group_recv, z_send, z_recv, zd_send, zd_recv, x_send, x_recv, y_send, y_recv,
        dx_send, dx_recv, dy_send, dy_recv, c_send, c_recv,
        cond_send, cond_recv, pc_send, pc_recv, pd_send, pd_recv, px_send, px_recv, py_send, py_recv,
        pz_send, pz_recv, pm_send, pm_recv, seg_send, seg_recv, kv_send, kv_recv,
        save_sem, grad_sem, slope_sem, block_sem, store_sem,
    ) = sems
    z, y, x, c = position()
    me = z * 4 + y * 2 + x
    group = x * 2 + c
    zy = z * 2 + y
    rows = 4 * share
    count, width = tokens_ref.shape
    x_peer, y_peer, c_peer = device(z, y, 1 - x, c), device(z, 1 - y, x, c), device(z, y, x, 1 - c)
    partners = [(x, 1 - c), (1 - x, c), (1 - x, 1 - c)]

    def prepare():
        tail = share // 16 * 16
        for a in range(2):
            for q in range(4):
                source, at = (up_ref, q) if a else ((out_weight_ref, 0) if q == 3 else (qkv_ref, q))
                shards_ref[a, q, tail:, :] = jnp.zeros((PAD - tail, width), jnp.bfloat16)
                shards_ref[a, q, :share, :] = source[:, at * width : (at + 1) * width]
        ada_ref[tail:, :] = jnp.zeros((PAD - tail, ada_ref.shape[1]), jnp.bfloat16)
        ada_ref[:share, :] = given_ada_ref[...]
        cond = cond_ref[...].astype(jnp.float32)
        acts[...] = jnp.zeros_like(acts)
        acts[:CROPS, :] = cond * (1.0 / (1.0 + jnp.exp(-cond)))
        counts = counts_ref[...].astype(jnp.float32)
        for tile in range(width // 128):
            acts[CROPS : CROPS + 1, tile * 128 : tile * 128 + NBINS] = counts
        acts_low[...] = acts[...].astype(jnp.bfloat16)
        seg_all[c] = jnp.broadcast_to(seg_ref[...], (8, count))
        seg_col_ref[...] = jnp.transpose(jnp.broadcast_to(seg_ref[...], (128, count)))
        for a in range(2):
            stage[a, pl.ds(pl.multiple_of(group * PAD, 16), PAD), :] = shards_ref[a, group]
        start, _ = share_window(2 * me + c, share, width)
        windows[me] = acts_low[:, pl.ds(start, 256)]

    greet(
        [((me + k) % CHIPS, c) for k in range(1, CHIPS)] + [c_peer, device(z, y, 1 - x, 1 - c)], prepare
    )
    sends = {a: [] for a in (0, 1, 2, "other")}

    def send(a, *args):
        copy = remote(*args)
        copy.start()
        sends[a].append((None, copy))

    def finish_sends(a):
        for go, copy in sends[a]:
            if go is None:
                copy.wait_send()
            else:
                pl.when(go)(copy.wait_send)
        sends[a] = []

    level = partial(level_of, z)

    def place(a, k, other_y, other_x, core=None, first=0, last=None):
        yy = 1 - y if other_y else y
        xx = 1 - x if other_x else x
        cc = c if core is None else core
        block, row = block_of(a, level(k) * 2 + yy, xx * 2 + cc)
        count = (rows if last is None else last) - first
        return full.at[a, block, pl.ds(pl.multiple_of(row * rows + first, 16), count)]

    def cuts(k):
        top, low = FAR if k else NEAR
        return top, rows - low

    def along(a, k, ref, send_sem, recv_sem):
        source = level(k)
        for way, step in ((0, 1), (1, -1)):
            to = z + step
            go = (to >= 0) & (to < 4)
            if k:
                go = go & ((source < z) if step == 1 else (source > z))
            copy = remote(ref, ref, send_sem.at[a, k, way], recv_sem.at[a, source], device(jnp.clip(to, 0, 3), y, x, c))
            pl.when(go)(copy.start)
            sends[a].append((go, copy))

    def from_line(a, k, ref, recv_sem):
        source = level(k)
        arrive(ref, recv_sem.at[a, source], device((z + 1) % 4, y, x, c))

    for a in range(2):
        for j, (px, pc) in enumerate(partners):
            send(
                "other",
                shards_ref.at[a, px * 2 + pc],
                stage.at[a, pl.ds(pl.multiple_of(group * PAD, 16), PAD)],
                group_send.at[a, j],
                group_recv.at[a, j],
                device(z, y, px, pc),
            )
    for k in range(1, CHIPS):
        to = (me + k) % CHIPS
        start, _ = share_window(2 * to + c, share, width)
        send("other", acts_low.at[:, pl.ds(start, 256)], windows.at[me], cond_send.at[k - 1], cond_recv.at[k - 1], (to, c))
    send("other", seg_all.at[c], seg_all.at[c], seg_send, seg_recv, c_peer)

    def own(a):
        block, row = block_of(a, zy, group)
        here = pl.ds(pl.multiple_of(row * rows, 16), rows)
        if a < 2:
            for j, (px, pc) in enumerate(partners):
                arrive(
                    stage.at[a, pl.ds(pl.multiple_of((px * 2 + pc) * PAD, 16), PAD)],
                    group_recv.at[a, j],
                    device(z, y, px, pc),
                )
            full[a, block, here, :] = product(row_selector(rows, share), stage[a]).astype(jnp.bfloat16)
        else:
            full[a, block, here, :] = down_ref[...]
        along(a, 0, place(a, 0, 0, 0), z_send, z_recv)

    def to_core(a, k, pos):
        piece = place(a, k, *PLACES[pos])
        send(a, piece, piece, c_send.at[a, k, pos], c_recv.at[a, k, pos], c_peer)

    def pass_piece(a, k):
        from_line(a, k, place(a, k, 0, 0), z_recv)
        along(a, k, place(a, k, 0, 0), z_send, z_recv)

    def spread(a, k):
        top, low = cuts(k)
        for x_half, x_rows, y_half, y_rows in ((0, (0, top), 1, (low, rows)), (1, (top, rows), 0, (0, low))):
            part = place(a, k, 0, 0, None, *x_rows)
            send(a, part, part, x_send.at[a, k, x_half], x_recv.at[a, k, x_half], x_peer)
            part = place(a, k, 0, 0, None, *y_rows)
            send(a, part, part, y_send.at[a, k, y_half], y_recv.at[a, k, y_half], y_peer)
        to_core(a, k, 0)

    def turn_y(a, k):
        part = place(a, k, 0, 1, None, 0, cuts(k)[0])
        arrive(part, x_recv.at[a, k, 0], x_peer)
        send(a, part, part, dy_send.at[a, k], dy_recv.at[a, k], y_peer)

    def turn_x(a, k):
        part = place(a, k, 1, 0, None, cuts(k)[1], rows)
        arrive(part, y_recv.at[a, k, 1], y_peer)
        send(a, part, part, dx_send.at[a, k], dx_recv.at[a, k], x_peer)

    def share_sides(a, k):
        top, low = cuts(k)
        arrive(place(a, k, 0, 1, None, top, rows), x_recv.at[a, k, 1], x_peer)
        to_core(a, k, 1)
        arrive(place(a, k, 1, 0, None, 0, low), y_recv.at[a, k, 0], y_peer)
        to_core(a, k, 2)

    def middle(a, k):
        return place(a, k, 1, 1, None, FAR[0], rows - FAR[1])

    def pass_diagonal(a, k):
        from_line(a, k, middle(a, k), zd_recv)
        along(a, k, middle(a, k), zd_send, zd_recv)

    pending = []

    def finish(a, k):
        top, low = cuts(k)
        arrive(place(a, k, 1, 1, None, 0, top), dy_recv.at[a, k], y_peer)
        arrive(place(a, k, 1, 1, None, low, rows), dx_recv.at[a, k], x_peer)
        if k == 0:
            along(a, k, middle(a, k), zd_send, zd_recv)
        to_core(a, k, 3)
        if a == 2:
            while pending:
                complete_level(pending.pop())
            pending.append(k)

    saves, mixers_saved = [], []

    def keep(src, dst, sem):
        copy = pltpu.make_async_copy(src, dst, sem)
        copy.start()
        saves.append(copy)

    keep(ada_ref, ada_out_ref, store_sem.at[7])

    def arrive_cores(a, k):
        for pos, (oy, ox) in enumerate(PLACES):
            arrive(place(a, k, oy, ox, 1 - c), c_recv.at[a, k, pos], c_peer)

    def complete(a):
        for k in range(4):
            arrive_cores(a, k)
        copy = pltpu.make_async_copy(full.at[a], weights_ref.at[a], save_sem.at[a])
        copy.start()
        (saves if a else mixers_saved).append(copy)

    def complete_level(k):
        arrive_cores(2, k)
        keep(full.at[2, level(k)], weights_ref.at[2, level(k)], block_sem.at[k])

    def mod_start():
        for k in range(1, CHIPS):
            source = (me - k + CHIPS) % CHIPS
            arrive(windows.at[source], cond_recv.at[k - 1], (source, c))
        _, offset = share_window(2 * me + c, share, width)
        lane = lax.broadcasted_iota(jnp.int32, (256, 128), 1)
        picked = (lax.broadcasted_iota(jnp.int32, (256, 128), 0) == lane + offset) & (lane < share)
        picked = picked.astype(jnp.float32).astype(jnp.bfloat16)
        mine = product(windows[...].reshape(CHIPS * 16, 256), picked)
        conds_ref[...] = mine.reshape(CHIPS, 16, 128).astype(jnp.bfloat16)
        here = mine.reshape(CHIPS, 16, 128)[:, :8, :].reshape(CHIPS * 8, 128)
        row = lax.broadcasted_iota(jnp.int32, here.shape, 0) % 8
        here = jnp.where(row < CROPS, here, 0.0)
        upper = here.astype(jnp.bfloat16)
        lower = pltpu.roll(here, CROPS, 0).astype(jnp.bfloat16)
        side = ada_ref.shape[1] // 2
        part[...] = product(upper[:, :PAD], ada_ref[:, :side]) + product(lower[:, :PAD], ada_ref[:, side:])
        far = pl.ds(pl.multiple_of((1 - c) * (side - BAND), 128), BAND)
        send("other", part.at[:, far], part_recv, pc_send, pc_recv, c_peer)

    def block8(zz, yy, xx):
        return pl.ds(pl.multiple_of((zz * 4 + yy * 2 + xx) * 8, 8), 8)

    def mod_cores():
        arrive(part_recv, pc_recv, c_peer)
        side = ada_ref.shape[1] // 2
        near = pl.ds(pl.multiple_of(c * (side - BAND), 128), BAND)
        band[...] = part[:, near] + part_recv[...]
        for k in range(4):
            zz = (z + k) % 4
            src = band.at[block8(zz, 1 - y, 1 - x)]
            send("other", src, band_diag.at[k], pd_send.at[k], pd_recv.at[k], x_peer if k % 2 else y_peer)

    def mod_plane():
        for k in range(4):
            zz = (z + k) % 4
            to_x, to_y = block8(zz, y, 1 - x), block8(zz, 1 - y, x)
            arrive(band_diag.at[k], pd_recv.at[k], x_peer if k % 2 else y_peer)
            fold = to_y if k % 2 else to_x
            band[fold, :] = band[fold, :] + band_diag[k]
            send("other", band.at[to_x], band_x.at[k], px_send.at[k], px_recv.at[k], x_peer)
            send("other", band.at[to_y], band_y.at[k], py_send.at[k], py_recv.at[k], y_peer)

    def mod_line():
        for k in (1, 2, 3, 0):
            zz = (z + k) % 4
            mine = block8(zz, y, x)
            arrive(band_x.at[k], px_recv.at[k], x_peer)
            arrive(band_y.at[k], py_recv.at[k], y_peer)
            band[mine, :] = band[mine, :] + band_x[k] + band_y[k]
            if k:
                send("other", band.at[mine], band_z.at[k - 1], pz_send.at[k - 1], pz_recv.at[k - 1], device(zz, y, x, c))

    def mod_last():
        for k in (1, 2, 3):
            arrive(band_z.at[k - 1], pz_recv.at[k - 1], device((z - k + 4) % 4, y, x, c))
        halves_of[c] = band[block8(z, y, x), :] + band_z[0] + band_z[1] + band_z[2]
        send("other", halves_of.at[c], halves_of.at[c], pm_send, pm_recv, c_peer)

    def mod_end():
        arrive(halves_of.at[1 - c], pm_recv, c_peer)
        side = ada_ref.shape[1] // 2
        table_ref[:, :BAND] = halves_of[0]
        table_ref[:, BAND:] = halves_of[1][:, 2 * BAND - side :]
        counts = jnp.sum(windows[:, :, :128].astype(jnp.float32)[:, CROPS : CROPS + 1, :], axis=0)
        lane = lax.broadcasted_iota(jnp.int32, counts.shape, 1)
        weight = jnp.where(lane < NBINS, 40.0 * CHIPS / jnp.where(lane < NBINS, counts, 1.0), 0.0)
        level_ref[...] = jnp.zeros_like(level_ref)
        for crop in range(CROPS):
            mine = jnp.where(lane == noise_ref[:, crop : crop + 1], weight, 0.0)
            level_ref[crop : crop + 1, :] = jnp.broadcast_to(jnp.sum(mine, axis=-1, keepdims=True), (1, 128))

    def first_norm(part_of):
        def body(at):
            segments = seg_col_ref[at, :1]
            value, _ = normed(tokens_ref[at, :].astype(jnp.float32))
            value = value * (1.0 + pick(segments, table_ref, 0, 1, width))
            hidden_ref[at, :] = (value + pick(segments, table_ref, 0, 0, width)).astype(jnp.bfloat16)

        chunks(count // 2, body, part_of * (count // 2))
        if part_of == 0:
            arrive(seg_all.at[1 - c], seg_recv, c_peer)
            return
        keep(hidden_ref, hidden_out_ref, store_sem.at[8])
        for h in (0, 1):
            same = seg_col_ref[:, :1] == seg_all[h][:1, :]
            bias[:, h * count : (h + 1) * count] = jnp.where(same, 0.0, LARGE_NEGATIVE)

    def project(q):
        value = product(hidden_ref[...], full[0, q]).astype(jnp.bfloat16)
        if q == 0:
            query_ref[...] = value
            keep(query_ref, query_out_ref, store_sem.at[9])
            total_ref[...] = jnp.zeros_like(total_ref)
            work[...] = jnp.zeros_like(work)
            return
        here = pl.ds(pl.multiple_of(c * count, 256), count)
        sides_ref[q - 1, here, :] = value
        send("other", sides_ref.at[q - 1, here], sides_ref.at[q - 1, here], kv_send.at[q - 1], kv_recv.at[q - 1], c_peer)

    def attend(first, last):
        if first == 0:
            there = pl.ds(pl.multiple_of((1 - c) * count, 256), count)
            for q in (0, 1):
                arrive(sides_ref.at[q, there], kv_recv.at[q], c_peer)
            keep(sides_ref, sides_out_ref, store_sem.at[0])
        size = width // HEADS
        scale = 1.0 / math.sqrt(size)

        def body(head, carry):
            columns, inside = window_of(head, size, width)
            query = query_ref[:, columns]
            query = jnp.where(inside, query, jnp.zeros_like(query))
            scores = product_by_columns(query, sides_ref[0, :, columns]) * scale + bias[...]
            top = jnp.max(scores, axis=-1, keepdims=True)
            raised = jnp.exp(scores - top)
            total = jnp.sum(raised, axis=-1, keepdims=True)
            chance = (raised * (1.0 / total)).astype(jnp.bfloat16)
            context = product(chance, sides_ref[1, :, columns])
            work[:, columns] = jnp.where(inside, context, work[:, columns])
            lane = lax.broadcasted_iota(jnp.int32, (1, 128), 1)
            total_ref[...] = jnp.where(lane == head, top + jnp.log(total), total_ref[...])
            return carry

        lax.fori_loop(first, last, body, 0)

    def mix():
        context_ref[...] = work[...].astype(jnp.bfloat16)
        keep(context_ref, context_out_ref, store_sem.at[10])
        attended_ref[...] = product(context_ref[...], full[0, 3])
        keep(attended_ref, attended_out_ref, store_sem.at[1])

    def second_norm(part_of):
        def body(at):
            segments = seg_col_ref[at, :1]
            gate = pick(segments, table_ref, 0, 2, width)
            middle = tokens_ref[at, :].astype(jnp.float32) + gate * attended_ref[at, :]
            middle_ref[at, :] = middle
            value, _ = normed(middle)
            value = value * (1.0 + pick(segments, table_ref, 4, 1, width))
            hidden_two_ref[at, :] = (value + pick(segments, table_ref, 4, 0, width)).astype(jnp.bfloat16)
            level = level_ref[3:4, :1]
            for crop in (2, 1, 0):
                level = jnp.where(segments == crop, level_ref[crop : crop + 1, :1], level)
            grad = cot_ref[at, :].astype(jnp.float32) * level
            grad_mlp[at, :] = (grad * pick(segments, table_ref, 4, 2, width)).astype(jnp.bfloat16)

        chunks(count // 2, body, part_of * (count // 2))
        if part_of:
            keep(middle_ref, middle_out_ref, store_sem.at[2])
            keep(hidden_two_ref, hidden_two_out_ref, store_sem.at[11])
            keep(grad_mlp, grad_mlp_out_ref, store_sem.at[12])

    slope_copies = {}

    def expand(q):
        work[...] = product(hidden_two_ref[...], full[1, q])

    def bend(q):
        if q >= 2:
            slope_copies[q - 2].wait()

        def body(at):
            u = work[at, :]
            square = u * u
            curve = jnp.tanh(GELU_SCALE * (u + GELU_CUBE * (square * u)))
            active[q, at, :] = (0.5 * u * (1.0 + curve)).astype(jnp.bfloat16)
            inner = GELU_SCALE * (1.0 + 3.0 * GELU_CUBE * square)
            slope[q % 2, at, :] = 0.5 * (1.0 + curve) + 0.5 * u * (1.0 - curve * curve) * inner

        chunks(count, body)
        copy = pltpu.make_async_copy(slope.at[q % 2], slope_ref.at[q], slope_sem.at[q % 2])
        copy.start()
        slope_copies[q] = copy
        keep(active.at[q], active_ref.at[q], store_sem.at[3 + q])

    def down_grad(q):
        if q == 0:
            finish_sends(0)
            mixers_saved.pop().wait()
        full[0, q] = product_by_rows(active[q], grad_mlp[...]).astype(jnp.bfloat16)
        keep(full.at[0, q], down_part_ref.at[q], grad_sem.at[q])

    kinds = (lambda a, k: own(a), pass_piece, spread, turn_y, turn_x, share_sides, pass_diagonal, finish)
    steps = [partial(kinds[n % 10], n // 100, n // 10 % 10) for n in FORWARD_STEPS]
    layer = [mod_start, mod_cores, mod_plane, mod_line, mod_last, mod_end]
    layer += [partial(first_norm, h) for h in (0, 1)] + [partial(complete, 0)]
    layer += [partial(project, q) for q in (1, 2, 0)] + [partial(attend, h, h + 2) for h in range(0, HEADS, 2)]
    layer += [mix, partial(second_norm, 0), partial(second_norm, 1), partial(complete, 1)]
    for q in range(4):
        layer += [partial(expand, q), partial(bend, q)]
    layer += [partial(down_grad, q) for q in range(4)]
    interleave(steps, layer, FORWARD_AFTER)
    complete_level(pending.pop())
    for copy in saves:
        copy.wait()
    for q in (2, 3):
        slope_copies[q].wait()
    for a in (1, 2, "other"):
        finish_sends(a)


def run_forward(qkv, out_weight, up, down, cond, noise, counts, ada, tokens, cot, segments):
    count, width = tokens.shape
    share = qkv.shape[0]
    dma = pltpu.SemaphoreType.DMA
    low, wide, whole = jnp.bfloat16, jnp.float32, jnp.int32
    side = ada.shape[1] // 2
    vmem, any_ = pl.BlockSpec(memory_space=pltpu.VMEM), pl.BlockSpec(memory_space=pl.ANY)
    out, buffer = jax.ShapeDtypeStruct, pltpu.VMEM
    return pl.pallas_call(
        partial(forward_kernel, share),
        out_shape=(
            out((3, 4, width, width), low),
            out((4, width, width), low),
            out((4, count, width), wide),
            out((4, count, width), low),
            out((2, 2 * count, width), low),
            out((count, width), wide),
            out((count, width), wide),
            out((count, width), low),
            out((count, width), low),
            out((count, 128), wide),
            out((count, width), low),
            out((count, width), low),
            out((8, side), wide),
            out((CHIPS, 16, 128), low),
            out((8, 128), wide),
            out((count, width), low),
            out((2, 8, count), whole),
            out((count, 128), whole),
            out((PAD, 2 * side), low),
        ),
        in_specs=[vmem] * 11,
        out_specs=[any_] * 9 + [vmem] + [any_] * 2 + [vmem] * 3 + [any_] + [vmem] * 2 + [any_],
        scratch_shapes=[
            buffer((3, 4, width, width), low),
            buffer((2, 4, PAD, width), low),
            buffer((2, 4 * PAD, width), low),
            buffer((16, width), wide),
            buffer((16, width), low),
            buffer((CHIPS, 16, 256), low),
            buffer((CHIPS * 8, side), wide),
            buffer((CHIPS * 8, BAND), wide),
            buffer((CHIPS * 8, BAND), wide),
            buffer((4, 8, BAND), wide),
            buffer((4, 8, BAND), wide),
            buffer((4, 8, BAND), wide),
            buffer((3, 8, BAND), wide),
            buffer((2, 8, BAND), wide),
            buffer((2, 2 * count, width), low),
            buffer((count, width), wide),
            buffer((count, width), wide),
            buffer((count, 2 * count), wide),
            buffer((count, width), wide),
            buffer((4, count, width), low),
            buffer((2, count, width), wide),
            buffer((count, width), low),
            buffer((count, width), low),
            buffer((count, width), low),
            buffer((count, width), low),
            buffer((count, width), low),
            buffer((PAD, 2 * side), low),
            dma((2, 3)), dma((2, 3)), dma((3, 4, 2)), dma((3, 4)), dma((3, 4, 2)), dma((3, 4)),
            dma((3, 4, 2)), dma((3, 4, 2)), dma((3, 4, 2)), dma((3, 4, 2)),
            dma((3, 4)), dma((3, 4)), dma((3, 4)), dma((3, 4)),
            dma((3, 4, 4)), dma((3, 4, 4)),
            dma((CHIPS - 1,)), dma((CHIPS - 1,)), dma, dma, dma((4,)), dma((4,)),
            dma((4,)), dma((4,)), dma((4,)), dma((4,)), dma((3,)), dma((3,)), dma, dma, dma, dma,
            dma((2,)), dma((2,)), dma((2,)), dma((4,)), dma((2,)), dma((4,)), dma((13,)),
        ],
        compiler_params=pltpu.CompilerParams(
            collective_id=0, has_side_effects=True, vmem_limit_bytes=63 * 2**20
        ),
        name="forward",
    )(qkv, out_weight, up, down, cond, noise, counts, ada, tokens, cot, segments)


def interleave(steps, layer, after):
    done = 0
    for count, step in enumerate(steps):
        while done < len(layer) and after[done] <= count:
            layer[done]()
            done += 1
        step()
    for step in layer[done:]:
        step()


def add_rows(dst, sources, start, rows):
    def body(i, carry):
        where = pl.ds(pl.multiple_of(start + i * 16, 16), 16)
        total = dst[where, :].astype(jnp.float32)
        for source in sources:
            total = total + source[where, :].astype(jnp.float32)
        dst[where, :] = total.astype(dst.dtype)
        return carry

    lax.fori_loop(0, rows // 16, body, 0)


def backward_kernel(share, weights_ref, down_part_ref, slope_ref, middle_ref, attended_ref, active_ref,
                    hidden_given, query_given, sides_given, total_given, context_given, hidden_two_given,
                    grad_mlp_given, table_ref, conds_ref, level_ref, seg_all_ref, seg_col_ref, tokens_given,
                    cot_given, ada_ref,
                    mixer_part_ref, up_part_ref, rows_ref, down_out_ref, tokens_grad_out_ref, ada_grad_ref, silu_ref,
                    out_ref,
                    held, from_core, diag, from_x, from_y, piece_line, diag_line, spare, block, part, quad, lows,
                    work, grad_middle, grad_context, leave, enter, bias, sums, sums_row, sums_core, band, silu_part, silu_side,
                    hidden_ref, query_ref, sides_ref, total_ref, context_ref, hidden_two_ref, grad_mlp_ref,
                    tokens_ref, cot_ref, down_ref, tokens_grad_ref,
                    *sems):
    (
        load_sem, c_send, c_recv, dx_send, dx_recv, dy_send, dy_recv, x_send, x_recv,
        y_send, y_recv, zo_send, zo_recv, zd_send, zd_recv, group_send, group_recv, block_sem, part_sem, quad_sem, low_sem, out_sem, late_sem, early_sem,
        side_send, side_recv, m_send, m_recv, mz_send, mz_recv, mx_send, mx_recv, my_send, my_recv,
        md_send, md_recv, mc_send, mc_recv, s_send, s_recv, sc_send, sc_recv,
    ) = sems
    z, y, x, c = position()
    me = z * 4 + y * 2 + x
    group = x * 2 + c
    rows = 4 * share
    count, width = tokens_ref.shape
    x_peer, y_peer, c_peer = device(z, y, 1 - x, c), device(z, 1 - y, x, c), device(z, y, x, 1 - c)
    partners = [(x, 1 - c), (1 - x, c), (1 - x, 1 - c)]
    greet(
        [((me + k) % CHIPS, c) for k in range(1, CHIPS)] + [c_peer, device(z, y, 1 - x, 1 - c)]
    )
    sends = {}

    def send(owner, *args):
        copy = remote(*args)
        copy.start()
        sends.setdefault(owner, []).append(copy)

    def finish_sends(owner):
        for copy in sends.pop(owner, []):
            copy.wait_send()

    late = {}

    def fetch_late():
        pairs = (
            ("grad_mlp", grad_mlp_given, grad_mlp_ref), ("hidden_two", hidden_two_given, hidden_two_ref),
            ("cot", cot_given, cot_ref), ("context", context_given, context_ref),
            ("query", query_given, query_ref), ("sides", sides_given, sides_ref),
            ("total", total_given, total_ref), ("hidden", hidden_given, hidden_ref),
            ("tokens", tokens_given, tokens_ref),
        )
        for n, (name, source, target) in enumerate(pairs):
            late[name] = pltpu.make_async_copy(source, target, late_sem.at[n])
            late[name].start()

    def need(*names):
        for name in names:
            if name in late:
                late.pop(name).wait()

    order = [(a, k) for a in (2, 1, 0) for k in (3, 2, 1, 0)]
    given = (mixer_part_ref, up_part_ref, down_part_ref)
    loads = {}
    inner_rows = slice(FAR[0], rows - FAR[1])

    def cuts(i):
        top, low = FAR if order[i][1] else NEAR
        return top, rows - low

    def line(k):
        to = level_of(z, k)
        step = jnp.where(z < to, 1, -1)
        behind = z - step
        return to, z + step, (behind >= 0) & (behind < 4)

    def along(i, ref, lines, send_sem, recv_sem):
        a, k = order[i]
        to, after, _ = line(k)
        spot = jnp.where((after == to) & (z > to), 4, to)
        copy = remote(ref, lines.at[a % 2, spot], send_sem.at[a, k], recv_sem.at[a, spot], device(after, y, x, c))
        copy.start()
        return copy

    def from_line(i, lines, recv_sem, spot):
        a = order[i][0]
        arrive(lines.at[a % 2, spot], recv_sem.at[a, spot], device((z + 1) % 4, y, x, c))

    def hold(i, ref, lines, send_sem, recv_sem):
        sends.setdefault(("held", i), []).append(
            remote(ref, lines.at[0, 0], send_sem.at[order[i]], recv_sem.at[order[i][0], 0], x_peer)
        )

    def begin(i):
        a, k = order[i]
        if i % 4 == 0:
            for n in sorted(going):
                going.pop(n).wait()
        finish_sends(("held", i - HELD))
        zz = level_of(z, k)
        for pos in (3, 1, 2, 0):
            yy = 1 - y if PLACES[pos][0] else y
            xx = 1 - x if PLACES[pos][1] else x
            for cc in (1 - c, c):
                where, row = block_of(a, zz * 2 + yy, xx * 2 + cc)
                src = given[a].at[where, pl.ds(pl.multiple_of(row * rows, 16), rows)]
                if cc is c:
                    loads[i, pos] = pltpu.make_async_copy(src, held.at[i % HELD, pos], load_sem.at[i, pos])
                    loads[i, pos].start()
                else:
                    send("core", src, from_core.at[i % 4, pos], c_send.at[i, pos], c_recv.at[i, pos], c_peer)

    def pair(i, pos):
        k = order[i][1]
        top, low = cuts(i)
        mine = held.at[i % HELD, pos]
        loads[i, pos].wait()
        arrive(from_core.at[i % 4, pos], c_recv.at[i, pos], c_peer)
        add_rows(mine, [from_core.at[i % 4, pos]], 0, rows)
        if pos == 3 and k:
            diagonal(i)
            part = mine.at[inner_rows]
            hold(i, part, diag_line, zd_send, zd_recv)
            _, _, fed = line(k)

            @pl.when(jnp.logical_not(fed))
            def _():
                along(i, part, diag_line, zd_send, zd_recv)

        if pos == 1:
            part = mine.at[top:rows]
            send(("held", i), part, from_x.at[i % 6, top:rows], x_send.at[i, 1], x_recv.at[i, 1], x_peer)
        if pos == 2:
            part = mine.at[0:low]
            send(("held", i), part, from_y.at[i % 6, 0:low], y_send.at[i, 0], y_recv.at[i, 0], y_peer)

    def diagonal(i):
        top, low = cuts(i)
        mine, far = held.at[i % HELD, 3], diag.at[i % 5]
        send(("held", i), mine.at[0:top], far.at[0:top], dy_send.at[i], dy_recv.at[i], y_peer)
        send(("held", i), mine.at[low:rows], far.at[low:rows], dx_send.at[i], dx_recv.at[i], x_peer)

    def diag_along(i):
        k = order[i][1]
        mine = held.at[i % HELD, 3, inner_rows]
        size = rows - FAR[0] - FAR[1]
        if k:
            to, _, fed = line(k)

            @pl.when(fed)
            def _():
                from_line(i, diag_line, zd_recv, to)
                add_rows(mine, [diag_line.at[order[i][0] % 2, to]], 0, size)
                along(i, mine, diag_line, zd_send, zd_recv)

        else:
            for spot, here in ((z, z > 0), (4, z < 3)):

                @pl.when(here)
                def _():
                    from_line(i, diag_line, zd_recv, spot)
                    add_rows(mine, [diag_line.at[order[i][0] % 2, spot]], 0, size)

            diagonal(i)

    def relay_x(i):
        top, _ = cuts(i)
        far, mine = diag.at[i % 5], held.at[i % HELD, 1]
        arrive(far.at[0:top], dy_recv.at[i], y_peer)
        add_rows(mine, [far], 0, top)
        send(("held", i), mine.at[0:top], from_x.at[i % 6, 0:top], x_send.at[i, 0], x_recv.at[i, 0], x_peer)

    def relay_y(i):
        _, low = cuts(i)
        far, mine = diag.at[i % 5], held.at[i % HELD, 2]
        arrive(far.at[low:rows], dx_recv.at[i], x_peer)
        add_rows(mine, [far], low, rows - low)
        send(("held", i), mine.at[low:rows], from_y.at[i % 6, low:rows], y_send.at[i, 1], y_recv.at[i, 1], y_peer)

    def plane(i):
        k = order[i][1]
        top, low = cuts(i)
        mine = held.at[i % HELD, 0]
        arrive(from_x.at[i % 6, 0:top], x_recv.at[i, 0], x_peer)
        arrive(from_x.at[i % 6, top:rows], x_recv.at[i, 1], x_peer)
        arrive(from_y.at[i % 6, 0:low], y_recv.at[i, 0], y_peer)
        arrive(from_y.at[i % 6, low:rows], y_recv.at[i, 1], y_peer)
        add_rows(mine, [from_x.at[i % 6], from_y.at[i % 6]], 0, rows)
        if k:
            hold(i, mine, piece_line, zo_send, zo_recv)
            _, _, fed = line(k)

            @pl.when(jnp.logical_not(fed))
            def _():
                along(i, mine, piece_line, zo_send, zo_recv)

    def piece_along(i):
        a, k = order[i]
        mine = held.at[i % HELD, 0]
        if k:
            to, _, fed = line(k)

            @pl.when(fed)
            def _():
                from_line(i, piece_line, zo_recv, to)
                add_rows(mine, [piece_line.at[a % 2, to]], 0, rows)
                along(i, mine, piece_line, zo_send, zo_recv)

            return
        for spot, here in ((z, z > 0), (4, z < 3)):

            @pl.when(here)
            def _():
                from_line(i, piece_line, zo_recv, spot)
                add_rows(mine, [piece_line.at[a % 2, spot]], 0, rows)

        if a == 2:
            down_ref[...] = mine[...].astype(jnp.float32)
            quads["down"] = pltpu.make_async_copy(down_ref, down_out_ref, early_sem.at[0])
            quads["down"].start()
            return
        spare[a] = product_by_rows(row_selector(rows, share), mine[...]).astype(jnp.bfloat16)
        for j, (px, pc) in enumerate(partners):
            send(
                "end",
                spare.at[a, pl.ds(pl.multiple_of((px * 2 + pc) * PAD, 16), PAD)],
                rows_ref.at[a, group],
                group_send.at[a, j],
                group_recv.at[a, j],
                device(z, y, px, pc),
            )
        rows_ref[a, group] = spare[a, pl.ds(pl.multiple_of(group * PAD, 16), PAD), :]

    uses = [(2, q) for q in range(4)] + [(1, q) for q in range(4)] + [(0, 3), (0, 0), (0, 1), (0, 2)]
    coming = {}

    def fetch(n):
        if n < len(uses):
            copy = pltpu.make_async_copy(weights_ref.at[uses[n]], block.at[n % 2], block_sem.at[n % 2])
            copy.start()
            coming[n] = copy

    def take(n):
        coming[n].wait()
        return block[n % 2]

    going = {}

    def put(n, left, right, target):
        if n - 2 in going:
            going.pop(n - 2).wait()

        def body(i, carry):
            columns = pl.ds(pl.multiple_of(i * 384, 128), 384)
            part[n % 2, columns, :] = product_by_rows(left[:, columns], right[...]).astype(jnp.bfloat16)
            return carry

        lax.fori_loop(0, width // 384, body, 0)
        going[n] = pltpu.make_async_copy(part.at[n % 2], target, part_sem.at[n % 2])
        going[n].start()

    quads = {}

    def slopes(q):
        quads[q] = pltpu.make_async_copy(slope_ref.at[q], quad.at[q], quad_sem.at[q])
        quads[q].start()
        quads["active", q] = pltpu.make_async_copy(active_ref.at[q], lows.at[q], low_sem.at[q])
        quads["active", q].start()

    def through_down(q):
        need("grad_mlp")
        quads.pop(("active", q)).wait()
        value = product(lows[q], take(q))
        grad_middle[...] = grad_middle[...] + value if q else value
        work[...] = product_by_columns(grad_mlp_ref[...], block[q % 2])
        fetch(q + 2)
        quads[q].wait()

        def body(at):
            lows[q, at, :] = (work[at, :] * quad[q, at, :]).astype(jnp.bfloat16)

        chunks(count, body)
        if q < 2:
            source = (middle_ref, attended_ref)[q]
            quads[q] = pltpu.make_async_copy(source, quad.at[q], quad_sem.at[q])
            quads[q].start()

    def up_grad(q):
        need("hidden_two")
        put(q, hidden_two_ref, lows.at[q], up_part_ref.at[q])

    def through_up(q):
        value = product_by_columns(lows[q], take(4 + q))
        work[...] = work[...] + value if q else value
        fetch(6 + q)

    def norm_pull(grad, value, inverse):
        return inverse * (
            grad
            - jnp.mean(grad, axis=-1, keepdims=True)
            - value * jnp.mean(grad * value, axis=-1, keepdims=True)
        )

    def add_sums(segments, which, value):
        for crop in range(CROPS):
            kept = jnp.where(segments == crop, value, 0.0)
            sums[which, crop] = sums[which, crop] + kept[:8] + kept[8:]

    def second_norm(half):
        if half == 0:
            for q in range(2):
                quads[q].wait()
            sums[...] = jnp.zeros_like(sums)
            need("cot")

        def body(at):
            segments = seg_col_ref[at, :1]
            grad = work[at, :]
            middle, mlp = quad[0, at, :], grad_middle[at, :]
            value, inverse = normed(middle)
            gate = pick(segments, table_ref, 4, 2, width)
            leave[0, at, :] = (middle + gate * mlp).astype(jnp.bfloat16)
            level = level_ref[3:4, :1]
            for crop in (2, 1, 0):
                level = jnp.where(segments == crop, level_ref[crop : crop + 1, :1], level)
            grad_out = cot_ref[at, :].astype(jnp.float32) * level
            add_sums(segments, 3, grad)
            add_sums(segments, 4, grad * value)
            add_sums(segments, 5, grad_out * mlp)
            scaled = grad * (1.0 + pick(segments, table_ref, 4, 1, width))
            total = grad_out + norm_pull(scaled, value, inverse)
            grad_middle[at, :] = total
            add_sums(segments, 2, total * quad[1, at, :])
            lows[3, at, :] = (total * pick(segments, table_ref, 0, 2, width)).astype(jnp.bfloat16)

        chunks(count // 2, body, half * (count // 2))
        if half:
            quads["out"] = pltpu.make_async_copy(leave.at[0], out_ref, out_sem)
            quads["out"].start()

    def context_grad():
        grad_context[...] = product_by_columns(lows[3], take(8)).astype(jnp.bfloat16)
        fetch(10)

    def out_grad():
        need("context")
        put(4, context_ref, lows.at[3], mixer_part_ref.at[3])
        for h in (0, 1):
            same = seg_col_ref[:, :1] == seg_all_ref[h][:1, :]
            bias[:, h * count : (h + 1) * count] = jnp.where(same, 0.0, LARGE_NEGATIVE)

    def attend_back(first, last):
        need("query", "sides", "total")
        size = width // HEADS
        scale = 1.0 / math.sqrt(size)

        def body(head, carry):
            columns, inside = window_of(head, size, width)
            query, keys = query_ref[:, columns], sides_ref[0, :, columns]
            grad = grad_context[:, columns]
            scores = product_by_columns(jnp.where(inside, query, jnp.zeros_like(query)), keys)
            lane = lax.broadcasted_iota(jnp.int32, (1, 128), 1)
            total = jnp.sum(jnp.where(lane == head, total_ref[...], 0.0), axis=-1, keepdims=True)
            chance = jnp.exp(scores * scale + bias[...] - total)
            pulled = product_by_columns(
                jnp.where(inside, grad, jnp.zeros_like(grad)), sides_ref[1, :, columns]
            )
            inner = jnp.sum(chance * pulled, axis=-1, keepdims=True)
            grad_scores = (chance * (pulled - inner)).astype(jnp.bfloat16)
            grad_query = (product(grad_scores, keys) * scale).astype(jnp.bfloat16)
            lows[0, :, columns] = jnp.where(inside, grad_query, lows[0, :, columns])
            grad_key = product_by_rows(grad_scores, query) * scale
            grad_value = product_by_rows(chance.astype(jnp.bfloat16), grad)
            for h in (0, 1):
                here = slice(h * count, (h + 1) * count)
                quad[h, :, columns] = jnp.where(inside, grad_key[here], quad[h, :, columns])
                quad[2 + h, :, columns] = jnp.where(inside, grad_value[here], quad[2 + h, :, columns])
            return carry

        lax.fori_loop(first, last, body, 0)

    def swap_sides():
        quads["out"].wait()
        for j in (0, 1):
            leave[j] = quad[2 * j + 1 - c].astype(jnp.bfloat16)
            send("end", leave.at[j], enter.at[j], side_send.at[j], side_recv.at[j], c_peer)

    def query_grad():
        need("hidden")
        put(5, hidden_ref, lows.at[0], mixer_part_ref.at[0])

    def side_grad(j):
        arrive(enter.at[j], side_recv.at[j], c_peer)

        def body(at):
            total = quad[2 * j + c, at, :] + enter[j, at, :].astype(jnp.float32)
            lows[1 + j, at, :] = total.astype(jnp.bfloat16)

        chunks(count, body)
        put(6 + j, hidden_ref, lows.at[1 + j], mixer_part_ref.at[1 + j])

    def through_qkv(q):
        value = product_by_columns(lows[q], take(9 + q))
        work[...] = work[...] + value if q else value
        fetch(11 + q)

    def first_norm(half):
        need("tokens")

        def body(at):
            segments = seg_col_ref[at, :1]
            grad = work[at, :]
            value, inverse = normed(tokens_ref[at, :].astype(jnp.float32))
            add_sums(segments, 0, grad)
            add_sums(segments, 1, grad * value)
            scaled = grad * (1.0 + pick(segments, table_ref, 0, 1, width))
            tokens_grad_ref[at, :] = grad_middle[at, :] + norm_pull(scaled, value, inverse)

        chunks(count // 2, body, half * (count // 2))
        if half:
            quads["tokens"] = pltpu.make_async_copy(tokens_grad_ref, tokens_grad_out_ref, early_sem.at[1])
            quads["tokens"].start()

    def sums_leave():
        for which in range(6):
            for crop in range(CROPS):
                row = which // 3 * CROPS + crop
                columns = slice(which % 3 * width, (which % 3 + 1) * width)
                sums_row[row : row + 1, columns] = jnp.sum(sums[which, crop], axis=0, keepdims=True)
        send("end", sums_row, sums_core, m_send, m_recv, c_peer)

    side = sums_row.shape[1]

    def place(k, other_y, other_x):
        zz = (z - k + 4) % 4
        yy = 1 - y if other_y else y
        xx = 1 - x if other_x else x
        return band.at[c, pl.ds(pl.multiple_of((zz * 4 + yy * 2 + xx) * 16, 16), 16)]

    def sums_start():
        arrive(sums_core, m_recv, c_peer)
        near = pl.ds(pl.multiple_of(c * (side - BAND), 128), BAND)
        total = sums_row[:, near] + sums_core[:, near]
        total = jnp.concatenate([total[:, : BAND // 2], total[:, BAND // 2 :]], axis=0)
        band[c, pl.ds(pl.multiple_of(me * 16, 16), 16), :] = total.astype(jnp.bfloat16)
        mine = place(0, 0, 0)
        for k in (1, 2, 3):
            send("end", mine, mine, mz_send.at[k - 1], mz_recv.at[k - 1], device((z + k) % 4, y, x, c))
        send("end", mine, mine, mx_send.at[0], mx_recv.at[0], x_peer)
        send("end", mine, mine, my_send.at[0], my_recv.at[0], y_peer)

    def sums_line():
        for k in (1, 2, 3):
            piece = place(k, 0, 0)
            arrive(piece, mz_recv.at[k - 1], device((z - k + 4) % 4, y, x, c))
            send("end", piece, piece, mx_send.at[k], mx_recv.at[k], x_peer)
            send("end", piece, piece, my_send.at[k], my_recv.at[k], y_peer)

    def sums_plane():
        for k in range(4):
            from_side, from_up = place(k, 0, 1), place(k, 1, 0)
            arrive(from_side, mx_recv.at[k], x_peer)
            arrive(from_up, my_recv.at[k], y_peer)
            if k % 2:
                send("end", from_side, from_side, md_send.at[k], md_recv.at[k], y_peer)
            else:
                send("end", from_up, from_up, md_send.at[k], md_recv.at[k], x_peer)

    def sums_cores():
        for k in range(4):
            arrive(place(k, 1, 1), md_recv.at[k], y_peer if k % 2 else x_peer)
        send("end", band.at[c], band.at[c], mc_send, mc_recv, c_peer)

    def condition(source):
        if source == 0:
            arrive(band.at[1 - c], mc_recv, c_peer)
            silu_side[...] = jnp.zeros_like(silu_side)
        acts = conds_ref[:, :8, :].astype(jnp.float32).reshape(CHIPS * 8, 128)
        row = lax.broadcasted_iota(jnp.int32, acts.shape, 0) % 8
        acts = jnp.where(row < CROPS, acts, 0.0)
        upper = acts.astype(jnp.bfloat16)
        lower = pltpu.roll(acts, CROPS, 0).astype(jnp.bfloat16)
        for half in (0, 1):
            first = source * (side - BAND) + half * (BAND // 2)
            skip = max(0, source * BAND - first)
            term = band[source].astype(jnp.float32).reshape(CHIPS, 16, BAND // 2)
            term = term[:, half * 8 : (half + 1) * 8, skip:].reshape(CHIPS * 8, BAND // 2 - skip)
            term = term.astype(jnp.bfloat16)
            for which, act in enumerate((upper, lower)):
                columns = slice(which * side + first + skip, which * side + first + BAND // 2)
                ada_grad_ref[:, columns] = product_by_rows(act, term)[: ada_grad_ref.shape[0]]
                value = product_by_columns(term, ada_ref[:, columns])
                silu_side[which, :, :PAD] = silu_side[which, :, :PAD] + value
        if source == 0:
            return
        silu_part[...] = silu_side[0] + pltpu.roll(silu_side[1], CHIPS * 8 - CROPS, 0)
        silu_ref[c, me] = silu_part[pl.ds(pl.multiple_of(me * 8, 8), 8), :]
        for k in range(1, CHIPS):
            to = (me + k) % CHIPS
            src = silu_part.at[pl.ds(pl.multiple_of(to * 8, 8), 8)]
            send("end", src, silu_ref.at[c, me], s_send.at[k - 1], s_recv.at[k - 1], (to, c))

    def condition_cores():
        for k in range(1, CHIPS):
            source = (me - k + CHIPS) % CHIPS
            arrive(silu_ref.at[c, source], s_recv.at[k - 1], (source, c))
        send("end", silu_ref.at[c], silu_ref.at[c], sc_send, sc_recv, c_peer)

    kinds = [begin] + [partial(pair, pos=pos) for pos in range(4)]
    kinds += [diag_along, relay_x, relay_y, plane, piece_along]
    steps = [partial(kinds[n % 10], n // 10) for n in BACKWARD_STEPS]
    layer = [partial(through_down, q) for q in range(4)] + [partial(up_grad, q) for q in range(4)]
    layer += [partial(through_up, q) for q in range(4)] + [partial(second_norm, h) for h in (0, 1)]
    layer += [context_grad, out_grad] + [partial(attend_back, h, h + 2) for h in range(0, HEADS, 2)]
    layer += [swap_sides, query_grad, partial(side_grad, 0), partial(side_grad, 1)]
    layer += [partial(through_qkv, q) for q in range(3)] + [partial(first_norm, h) for h in (0, 1)]
    layer += [sums_leave, sums_start, sums_line, sums_plane, sums_cores]
    layer += [partial(condition, 0), partial(condition, 1), condition_cores]
    begin(0)
    fetch(0)
    fetch_late()
    for q in range(4):
        slopes(q)
    fetch(1)
    interleave(steps, layer, BACKWARD_AFTER)
    for a in range(2):
        for j, (px, pc) in enumerate(partners):
            arrive(rows_ref.at[a, px * 2 + pc], group_recv.at[a, j], device(z, y, px, pc))
    arrive(silu_ref.at[1 - c], sc_recv, c_peer)
    for name in ("down", "tokens"):
        quads[name].wait()
    for owner in list(sends):
        finish_sends(owner)


def run_backward(given, share):
    (weights, down_part, slope, middle, attended, active, hidden, query, sides, total, context, hidden_two,
     grad_mlp, table, conds, level, seg_all, seg_col, tokens, cot, ada) = given
    count, width = tokens.shape
    rows, side = 4 * share, ada.shape[1] // 2
    dma = pltpu.SemaphoreType.DMA
    low, wide = jnp.bfloat16, jnp.float32
    vmem, any_ = pl.BlockSpec(memory_space=pltpu.VMEM), pl.BlockSpec(memory_space=pl.ANY)
    out, buffer = jax.ShapeDtypeStruct, pltpu.VMEM
    slots = 12
    return pl.pallas_call(
        partial(backward_kernel, share),
        out_shape=(
            out((4, width, width), low),
            out((4, width, width), low),
            out((2, 4, PAD, width), low),
            out((rows, width), wide),
            out((count, width), wide),
            out((-(-share // 8) * 8, ada.shape[1]), wide),
            out((2, CHIPS, 8, 128), wide),
            out((count, width), low),
        ),
        in_specs=[any_] * 13 + [vmem] * 5 + [any_] * 2 + [vmem],
        out_specs=[any_] * 2 + [vmem] + [any_] * 2 + [vmem] * 2 + [any_],
        scratch_shapes=[
            buffer((HELD, 4, rows, width), low),
            buffer((4, 4, rows, width), low),
            buffer((5, rows, width), low),
            buffer((6, rows, width), low),
            buffer((6, rows, width), low),
            buffer((2, 5, rows, width), low),
            buffer((2, 5, rows - FAR[0] - FAR[1], width), low),
            buffer((2, 4 * PAD, width), low),
            buffer((2, width, width), low),
            buffer((2, width, width), low),
            buffer((4, count, width), wide),
            buffer((4, count, width), low),
            buffer((count, width), wide),
            buffer((count, width), wide),
            buffer((count, width), low),
            buffer((2, count, width), low),
            buffer((2, count, width), low),
            buffer((count, 2 * count), wide),
            buffer((6, CROPS, 8, width), wide),
            buffer((8, side), wide),
            buffer((8, side), wide),
            buffer((2, CHIPS * 16, BAND // 2), low),
            buffer((CHIPS * 8, 128), wide),
            buffer((2, CHIPS * 8, 128), wide),
            buffer((count, width), low),
            buffer((count, width), low),
            buffer((2, 2 * count, width), low),
            buffer((count, 128), wide),
            buffer((count, width), low),
            buffer((count, width), low),
            buffer((count, width), low),
            buffer((count, width), low),
            buffer((count, width), low),
            buffer((rows, width), wide),
            buffer((count, width), wide),
            dma((slots, 4)), dma((slots, 4)), dma((slots, 4)),
            dma((slots,)), dma((slots,)), dma((slots,)), dma((slots,)),
            dma((slots, 2)), dma((slots, 2)), dma((slots, 2)), dma((slots, 2)),
            dma((3, 4)), dma((3, 5)), dma((3, 4)), dma((3, 5)),
            dma((2, 3)), dma((2, 3)), dma((2,)), dma((2,)), dma((4,)), dma((4,)), dma, dma((9,)), dma((2,)),
            dma((2,)), dma((2,)), dma, dma, dma((3,)), dma((3,)), dma((4,)), dma((4,)), dma((4,)), dma((4,)),
            dma((4,)), dma((4,)), dma, dma, dma((CHIPS - 1,)), dma((CHIPS - 1,)), dma, dma,
        ],
        compiler_params=pltpu.CompilerParams(
            collective_id=1, has_side_effects=True, vmem_limit_bytes=63 * 2**20 + 2**19
        ),
        name="backward",
    )(*given)


def finish_kernel(share, rows_ref, ada_given_ref, silu_ref, cond_ref, down_given, tokens_grad_given, out_given,
                  qkv_ref, out_grad_ref, up_ref, ada_ref, cond_grad_ref, down_ref, tokens_grad_ref, out_ref):
    for given, ref in ((down_given, down_ref), (tokens_grad_given, tokens_grad_ref), (out_given, out_ref)):

        def body(at):
            ref[at, :] = given[at, :]

        chunks(ref.shape[0], body)
    width = rows_ref.shape[-1]
    for q in range(4):
        value = rows_ref[0, q].astype(jnp.float32)[:share]
        if q == 3:
            out_grad_ref[...] = value
        else:
            qkv_ref[:, q * width : (q + 1) * width] = value
        up_ref[:, q * width : (q + 1) * width] = rows_ref[1, q].astype(jnp.float32)[:share]
    ada_ref[...] = ada_given_ref[...][:share]
    lane = lax.broadcasted_iota(jnp.int32, (8, 128), 1)
    tiles = [jnp.zeros((8, 128), jnp.float32)] * (width // 128)
    for number in range(2 * CHIPS):
        tile, offset = divmod(number * share, 128)
        value = jnp.where(lane < share, silu_ref[number % 2, number // 2], 0.0)
        if offset:
            value = pltpu.roll(value, offset, 1)
        tiles[tile] = tiles[tile] + jnp.where(lane >= offset, value, 0.0)
        if offset + share > 128:
            tiles[tile + 1] = tiles[tile + 1] + jnp.where(lane < offset, value, 0.0)
    grad = jnp.concatenate(tiles, axis=1)[:CROPS]
    cond = cond_ref[...].astype(jnp.float32)
    chance = 1.0 / (1.0 + jnp.exp(-cond))
    cond_grad_ref[...] = grad * (chance * (1.0 + cond * (1.0 - chance)))


def run_finish(rows, ada_grad, silu_part, cond, down_grad, tokens_grad, tokens_out, share):
    width = rows.shape[-1]
    wide = jnp.float32
    vmem, out = pl.BlockSpec(memory_space=pltpu.VMEM), jax.ShapeDtypeStruct
    return pl.pallas_call(
        partial(finish_kernel, share),
        out_shape=(
            out((share, 3 * width), wide),
            out((share, width), wide),
            out((share, 4 * width), wide),
            out((share, ada_grad.shape[1]), wide),
            out(cond.shape, wide),
            out(down_grad.shape, wide),
            out(tokens_grad.shape, wide),
            out(tokens_out.shape, tokens_out.dtype),
        ),
        in_specs=[vmem] * 7,
        out_specs=[vmem] * 8,
        compiler_params=pltpu.CompilerParams(vmem_limit_bytes=63 * 2**20),
        name="finish",
    )(rows, ada_grad, silu_part, cond, down_grad, tokens_grad, tokens_out)


def layer_norm(values):
    center = values - jnp.mean(values, axis=-1, keepdims=True)
    inverse = lax.rsqrt(jnp.mean(center * center, axis=-1, keepdims=True) + EPSILON)
    return (center * inverse, inverse)


def norm_back(grad_normed, normed, inverse):
    return inverse * (
        grad_normed
        - jnp.mean(grad_normed, axis=-1, keepdims=True)
        - normed * jnp.mean(grad_normed * normed, axis=-1, keepdims=True)
    )


def to_heads(array):
    return array.reshape(array.shape[0], HEADS, array.shape[1] // HEADS)


def dots(spec, left, right):
    return jnp.einsum(spec, left, right, preferred_element_type=jnp.float32)


def masked_scores(query_heads, key_heads, same_crop):
    scale_factor = 1.0 / math.sqrt(query_heads.shape[-1])
    scores = dots("qhd,khd->hqk", query_heads, key_heads) * scale_factor
    return jnp.where(same_crop[None], scores, LARGE_NEGATIVE)


def attend(query_seq, key_seq, value_seq, same_crop):
    scores = masked_scores(to_heads(query_seq), to_heads(key_seq), same_crop)
    row_max = jnp.max(scores, axis=-1, keepdims=True)
    raised = jnp.exp(scores - row_max)
    row_total = jnp.sum(raised, axis=-1, keepdims=True)
    probability = (raised / row_total).astype(jnp.bfloat16)
    context = dots("hqk,khd->qhd", probability, to_heads(value_seq))
    return (context.reshape(query_seq.shape[0], -1), (row_max + jnp.log(row_total))[..., 0])


def attend_back(query_seq, key_seq, value_seq, same_crop, log_total, grad_seq):
    query_heads = to_heads(query_seq)
    key_heads = to_heads(key_seq)
    value_heads = to_heads(value_seq)
    grad_heads = to_heads(grad_seq)
    scale_factor = 1.0 / math.sqrt(query_heads.shape[-1])
    scores = masked_scores(query_heads, key_heads, same_crop)
    probability = jnp.exp(scores - log_total[..., None])
    grad_prob = dots("qhd,khd->hqk", grad_heads, value_heads)
    inner = jnp.sum(probability * grad_prob, axis=-1, keepdims=True)
    grad_scores = (probability * (grad_prob - inner)).astype(jnp.bfloat16)
    grad_query = dots("hqk,khd->qhd", grad_scores, key_heads) * scale_factor
    grad_key = dots("hqk,qhd->khd", grad_scores, query_heads) * scale_factor
    grad_value = dots("hqk,qhd->khd", probability.astype(jnp.bfloat16), grad_heads)
    rows_here = query_seq.shape[0]
    rows_whole = key_seq.shape[0]
    return (
        grad_query.reshape(rows_here, -1),
        grad_key.reshape(rows_whole, -1),
        grad_value.reshape(rows_whole, -1),
    )


def forward_plain(tokens_float, segments, conditions, noise_bins, bin_counts, ada_weight, first, up_weight,
                  down_weight):
    groups, cores = lax.axis_size("dp"), lax.axis_size("sp")
    share, width = first.shape[0], tokens_float.shape[1]
    index = lax.axis_index("dp") * cores + lax.axis_index("sp")
    mixers = lax.all_gather(first, ("dp", "sp"), axis=0, tiled=True)
    uppers = lax.all_gather(up_weight, ("dp", "sp"), axis=0, tiled=True)
    downers = lax.all_gather(down_weight, ("dp", "sp"), axis=0, tiled=True)
    mixers = mixers.reshape(width, 4, width).transpose(1, 0, 2)
    uppers = uppers.reshape(width, 4, width).transpose(1, 0, 2)
    downers = downers.reshape(4, width, width)
    bin_total = lax.psum(bin_counts, "dp")
    bin_weight = 40.0 * groups / bin_total.astype(jnp.float32)
    crop_weight = jnp.sum(
        jnp.where(noise_bins[:, None] == jnp.arange(NBINS, dtype=jnp.int32), bin_weight, 0.0),
        axis=-1,
    )
    cond_all = lax.all_gather(conditions, "dp", axis=0, tiled=True)
    cond_here = lax.dynamic_slice_in_dim(cond_all, index * share, share, axis=1)
    cond_act = jax.nn.silu(cond_here.astype(jnp.float32)).astype(jnp.bfloat16)
    modulation_part = dots("sd,df->sf", cond_act, ada_weight).reshape(groups, CROPS, -1)
    modulation = lax.psum(lax.psum_scatter(modulation_part, "dp", scatter_dimension=0), "sp")
    selector = (segments[:, None] == jnp.arange(CROPS, dtype=jnp.int32)).astype(jnp.float32)
    per_token = jnp.einsum("tc,cf->tf", selector, modulation, precision=lax.Precision.HIGHEST)
    shift_one, scale_one, gate_one, shift_two, scale_two, _ = jnp.split(per_token, 6, axis=-1)
    normed_one, _ = layer_norm(tokens_float)
    hidden_one = (normed_one * (1.0 + scale_one) + shift_one).astype(jnp.bfloat16)
    projected = dots("td,qdf->qtf", hidden_one, mixers[:3]).astype(jnp.bfloat16)
    sides = lax.all_gather(projected[1:], "sp", axis=1, tiled=True)
    all_segments = lax.all_gather(segments, "sp", axis=0, tiled=True)
    same_crop = segments[:, None] == all_segments[None, :]
    context, log_total = attend(projected[0], sides[0], sides[1], same_crop)
    context_low = context.astype(jnp.bfloat16)
    attended = dots("td,df->tf", context_low, mixers[3])
    middle = tokens_float + gate_one * attended
    normed_two, _ = layer_norm(middle)
    hidden_two = (normed_two * (1.0 + scale_two) + shift_two).astype(jnp.bfloat16)
    upper_in = dots("td,qdf->qtf", hidden_two, uppers)
    activated = jax.nn.gelu(upper_in, approximate=True).astype(jnp.bfloat16)
    slope = jax.vjp(partial(jax.nn.gelu, approximate=True), upper_in)[1](jnp.ones_like(upper_in))[0]
    mlp_out = dots("qtf,qfd->td", activated, downers)
    return (
        (mixers, uppers, downers), activated, slope, hidden_one, projected[0], sides, log_total,
        context_low, attended, middle, hidden_two, mlp_out, modulation, cond_act, crop_weight, same_crop,
    )


def layer_plain(tokens_float, segments, conditions, noise_bins, bin_counts, cotangent, ada_weight, first,
                up_weight, down_weight):
    width = tokens_float.shape[1]
    (
        (mixers, uppers, downers), activated, slope, hidden_one, queries, sides, log_total,
        context_low, attended, middle, hidden_two, mlp_out, modulation, cond_act, crop_weight, same_crop,
    ) = forward_plain(
        tokens_float, segments, conditions, noise_bins, bin_counts, ada_weight, first, up_weight,
        down_weight,
    )
    selector = (segments[:, None] == jnp.arange(CROPS, dtype=jnp.int32)).astype(jnp.float32)
    per_token = jnp.einsum("tc,cf->tf", selector, modulation, precision=lax.Precision.HIGHEST)
    _, scale_one, gate_one, _, scale_two, gate_two = jnp.split(per_token, 6, axis=-1)
    normed_one, inverse_one = layer_norm(tokens_float)
    normed_two, inverse_two = layer_norm(middle)

    token_weight = jnp.sum(selector * crop_weight[None, :], axis=-1)
    grad_out = cotangent.astype(jnp.float32) * token_weight[:, None]
    grad_mlp = (grad_out * gate_two).astype(jnp.bfloat16)
    tokens_out = (middle + gate_two * mlp_out).astype(jnp.bfloat16)
    down_part = dots("qtf,td->qfd", activated, grad_mlp).astype(jnp.bfloat16)
    grad_act = dots("td,qfd->qtf", grad_mlp, downers)
    grad_upper = (grad_act * slope).astype(jnp.bfloat16)
    up_part = dots("td,qtf->qdf", hidden_two, grad_upper).astype(jnp.bfloat16)
    grad_hidden_two = dots("qtf,qdf->td", grad_upper, uppers)
    grad_middle = grad_out + norm_back(grad_hidden_two * (1.0 + scale_two), normed_two, inverse_two)
    grad_attended = (grad_middle * gate_one).astype(jnp.bfloat16)
    grad_context = dots("tf,df->td", grad_attended, mixers[3]).astype(jnp.bfloat16)
    grad_query, grad_key, grad_value = attend_back(
        queries, sides[0], sides[1], same_crop, log_total, grad_context
    )
    grad_sides = lax.psum_scatter(
        jnp.stack([grad_key, grad_value]).astype(jnp.bfloat16),
        "sp",
        scatter_dimension=1,
        tiled=True,
    )
    grad_projected = jnp.concatenate([grad_query.astype(jnp.bfloat16)[None], grad_sides])
    out_part = dots("td,tf->df", context_low, grad_attended).astype(jnp.bfloat16)
    qkv_part = dots("td,qtf->qdf", hidden_one, grad_projected).astype(jnp.bfloat16)
    first_part = jnp.concatenate([qkv_part, out_part[None]])
    grad_hidden_one = dots("qtf,qdf->td", grad_projected, mixers[:3])
    tokens_grad = grad_middle + norm_back(
        grad_hidden_one * (1.0 + scale_one), normed_one, inverse_one
    )

    joined = jnp.stack([first_part, up_part]).transpose(2, 0, 1, 3).reshape(width, 8 * width)
    rows = lax.psum_scatter(joined, ("dp", "sp"), scatter_dimension=0, tiled=True)
    rows = rows.astype(jnp.float32)
    first_grad, up_grad = rows[:, : 4 * width], rows[:, 4 * width :]
    down_grad = lax.psum_scatter(
        down_part.reshape(4 * width, width), ("dp", "sp"), scatter_dimension=0, tiled=True
    ).astype(jnp.float32)

    grad_per_token = jnp.concatenate(
        [
            grad_hidden_one,
            grad_hidden_one * normed_one,
            grad_middle * attended,
            grad_hidden_two,
            grad_hidden_two * normed_two,
            grad_out * mlp_out,
        ],
        axis=-1,
    )
    grad_modulation = lax.psum(
        jnp.einsum("tc,tf->cf", selector, grad_per_token, precision=lax.Precision.HIGHEST), "sp"
    )
    grad_rows = lax.all_gather(grad_modulation, "dp", axis=0, tiled=True)
    ada_grad = jnp.einsum(
        "sd,sf->df", cond_act.astype(jnp.float32), grad_rows, precision=lax.Precision.HIGHEST
    )
    silu_part = jnp.einsum(
        "sf,df->sd", grad_rows, ada_weight.astype(jnp.float32), precision=lax.Precision.HIGHEST
    )
    silu_all = lax.all_gather(silu_part, ("dp", "sp"), axis=0)
    silu_here = lax.dynamic_slice_in_dim(silu_all, lax.axis_index("dp") * CROPS, CROPS, axis=1)
    grad_silu = silu_here.transpose(1, 0, 2).reshape(CROPS, width)
    return tokens_out, tokens_grad, grad_silu, ada_grad, first_grad, up_grad, down_grad


def on_device(
    chips,
    tokens_in,
    segment_ids,
    conditions,
    noise_bins,
    bin_counts,
    cotangent,
    ada_weight,
    qkv_weight,
    out_weight,
    up_weight,
    down_weight,
):
    share = qkv_weight.shape[0]
    if chips and 4 * share == down_weight.shape[0]:
        (
            weights, down_part, slope, active, sides, attended, middle, hidden_one, queries, log_total,
            context_low, hidden_two, table, conds, level, grad_mlp, seg_all, seg_col, ada,
        ) = run_forward(
            qkv_weight, out_weight, up_weight, down_weight, conditions[0], noise_bins, bin_counts,
            ada_weight, tokens_in[0], cotangent[0], segment_ids,
        )
        given = (
            weights, down_part, slope, middle, attended, active, hidden_one, queries, sides, log_total,
            context_low, hidden_two, grad_mlp, table, conds, level, seg_all, seg_col, tokens_in[0],
            cotangent[0], ada,
        )
        _, _, rows, down_grad, tokens_grad, ada_grad, silu_part, tokens_out = run_backward(given, share)
        qkv_grad, out_grad, up_grad, ada_grad, cond_grad, down_grad, tokens_grad, tokens_out = run_finish(
            rows, ada_grad, silu_part, conditions[0], down_grad, tokens_grad, tokens_out, share
        )
    else:
        first = jnp.concatenate([qkv_weight, out_weight], axis=1)
        width = out_weight.shape[1]
        tokens_out, tokens_grad, grad_silu, ada_grad, first_grad, up_grad, down_grad = layer_plain(
            tokens_in[0].astype(jnp.float32), segment_ids[0], conditions[0], noise_bins[0], bin_counts[0],
            cotangent[0], ada_weight, first, up_weight, down_weight,
        )
        qkv_grad, out_grad = first_grad[:, : 3 * width], first_grad[:, 3 * width :]
        cond_grad = jax.vjp(jax.nn.silu, conditions[0].astype(jnp.float32))[1](grad_silu)[0]
    return (
        tokens_out[None],
        tokens_grad[None],
        cond_grad[None],
        ada_grad,
        qkv_grad,
        out_grad,
        up_grad,
        down_grad,
    )


def solution(mesh):
    placed = (
        P("dp", "sp", None),
        P("dp", "sp"),
        P("dp", None, None),
        P("dp", None),
        P("dp", None),
        P("dp", "sp", None),
        P(("dp", "sp"), None),
        P(("dp", "sp"), None),
        P(("dp", "sp"), None),
        P(("dp", "sp"), None),
        P(("dp", "sp"), None),
    )
    return jax.shard_map(
        partial(on_device, mesh.shape["dp"] == 16 and mesh.shape["sp"] == 2),
        mesh=mesh,
        in_specs=placed,
        out_specs=(
            P("dp", "sp", None),
            P("dp", "sp", None),
            P("dp", None, None),
            P(("dp", "sp"), None),
            P(("dp", "sp"), None),
            P(("dp", "sp"), None),
            P(("dp", "sp"), None),
            P(("dp", "sp"), None),
        ),
        check_vma=False,
    )
```
